32 devices in a mesh: slab: 2 (over y), pulse: 4 (over z), rx: 2 (over x), rng: 2 (over core).
Axes of the slice: x: 2, y: 2, z: 4, core: 2. Of those that a mesh axis runs over, the one named last changes fastest.
Arguments:
- echoes: bfloat16 [2, 64, 16, 4096], P(None, ('slab', 'pulse'), 'rx', 'rng'), parts along dimension 1, may hold values from -6 to 6
- beam_angle: int32 [64], replicated, may hold values from 0 to 1023
- interp_table: int32 [32, 2, 64], replicated, may hold values from 0 to 11
Outputs:
- focused: float32 [2, 128, 4096], P(None, 'slab', ('rng', 'rx', 'pulse')), parts along dimension 1
The draws below stay inside these ranges and needn't reach their ends.
There are 2 independent parts, one for each index of `slab`. The reference program is written for one: setup_inputs(seed, part) draws one part's arguments, and reference() takes and returns one part's arrays. A program takes and returns all parts, laid end to end along the dimension named above; an argument that names none is the same for every part. Nothing has to cross between parts.
All inputs are finite; a program needn't handle non-finite values.
Results may differ from the reference program's by a relative error of at most 0.0059.
Values may be sent and summed in bfloat16 or wider, within the bound.
No kernel may reach another device: no remote copies, remote signals or barrier semaphores. Data moves between devices by JAX's collectives and lax.ppermute only.
A program may use at most 64 MiB of HBM per device.

```python
import math
import jax
import jax.numpy as jnp
from jax import lax

BEAMS = 64
RXS = 16
RTAPS = 64
CTAPS = 512
P_DEV = 8
R_DEV = 2048
PULSES = 32
R = 4096
N_RNG = 2


def place_ends(result, rng, low, top_value):
    longest = result.shape.index(max(result.shape))
    spots = []
    for shift in (0, 1):
        where = [jax.random.randint(jax.random.fold_in(rng, axis), (), 0, length) for axis, length in enumerate(result.shape)]
        where[longest] = (where[longest] + shift) % result.shape[longest]
        spots.append(tuple(where))
    return result.at[spots[0]].set(low).at[spots[1]].set(top_value)


def steps_of(own_key, dims, split, least, high):
    factor_of = 1.0
    for dim, parts in split:
        heights = jax.random.uniform(jax.random.fold_in(jax.random.fold_in(own_key, 6), dim), (parts,), jnp.float32, least / len(split), high / len(split))
        factor_of = factor_of * jnp.repeat(jnp.exp(heights), dims[dim] // parts).reshape((-1,) + (1,) * (len(dims) - 1 - dim))
    return factor_of


def noise(own_key, shape, deviation, reach, shards=(), kind=jnp.bfloat16):
    gain = steps_of(own_key, shape, shards, -0.22, 0.18) if shards else 1.0
    drawn = jax.random.normal(own_key, shape, jnp.float32) * deviation * gain
    return jnp.minimum(jnp.maximum(drawn, -reach), reach).astype(kind)


def setup_inputs(seed: int = 0, part: int = 0) -> dict:
    splits = jax.random.split(jax.random.key(seed), 4)
    own_keys = jax.random.split(jax.random.fold_in(splits[3], part), 4)
    return {
        "echoes": noise(own_keys[0], (2, PULSES, RXS, R), 1.0, 6.0, ((1, 4), (2, 2), (3, 2))),
        "beam_angle": place_ends(jax.random.randint(splits[1], (BEAMS,), 0, 1024), jax.random.fold_in(splits[1], 1), 0, 1023).astype(jnp.int32),
        "interp_table": place_ends(jax.random.randint(splits[2], (PULSES, 2, BEAMS), 0, 12), jax.random.fold_in(splits[2], 1), 0, 11).astype(jnp.int32),
    }


half_root = 0.7071067811865476
full_turn = 2.0 * math.pi

def receiver_taps(channel_ids, tap_count):
    tap_index = jnp.arange(tap_count, dtype=jnp.float32)
    window = 0.5 - 0.5 * jnp.cos(full_turn * (tap_index + 0.5) / tap_count)
    window = window / jnp.sqrt(jnp.sum(window * window))
    channel = channel_ids.astype(jnp.float32)[:, None] + 1.0
    angle = full_turn * channel * (tap_index - tap_count // 2) / (4 * tap_count)
    return ((window * jnp.cos(angle)).astype(jnp.bfloat16), (window * jnp.sin(angle)).astype(jnp.bfloat16))

def chirp_taps(tap_count):
    offset = jnp.arange(tap_count, dtype=jnp.int32) - tap_count // 2
    phase_step = jnp.mod(offset * offset, 2 * tap_count).astype(jnp.float32)
    angle = math.pi * phase_step / tap_count
    scale = 1.0 / math.sqrt(tap_count)
    return ((jnp.cos(angle) * scale).astype(jnp.bfloat16), (-jnp.sin(angle) * scale).astype(jnp.bfloat16))

def steering(beam_angle, receivers):
    channel = jnp.arange(receivers, dtype=jnp.int32)
    turns = jnp.mod(beam_angle[:, None] * channel[None, :], 1024).astype(jnp.float32)
    angle = full_turn * turns / 1024.0
    scale = 1.0 / math.sqrt(receivers)
    return ((jnp.cos(angle) * scale).astype(jnp.bfloat16), (-jnp.sin(angle) * scale).astype(jnp.bfloat16))

def interp_matrices(codes, beam_count):
    shifted = codes // 4 - 1
    fraction = jnp.mod(codes, 4).astype(jnp.float32) / 4.0
    weights = (-fraction * (fraction - 1.0) * (fraction - 2.0) / 6.0, (fraction + 1.0) * (fraction - 1.0) * (fraction - 2.0) / 2.0, -(fraction + 1.0) * fraction * (fraction - 2.0) / 2.0, (fraction + 1.0) * fraction * (fraction - 1.0) / 6.0)
    columns = jnp.arange(beam_count, dtype=jnp.int32)
    matrices = jnp.zeros(codes.shape + (beam_count,), jnp.float32)
    for tap_index in range(4):
        target = jnp.mod(columns + shifted + tap_index - 1, beam_count)
        matrices = matrices + weights[tap_index][..., None] * (target[..., None] == columns).astype(jnp.float32)
    return matrices

def phases(node_ids, positions, beam_angle, side):
    base = jnp.mod(beam_angle[:, None] * (positions[None, :] + 1), 1024)
    factor = 2 * node_ids + side + 1
    turns = jnp.mod(base[:, None, :] * factor[None, :, None], 1024).astype(jnp.float32)
    angle = full_turn * turns / 1024.0
    return (jnp.cos(angle), jnp.sin(angle))

def side_term(picture, matrices, cosine, sine):
    moved = jnp.einsum('gqa,cagr->cqgr', matrices, picture, precision=lax.Precision.HIGHEST)
    return (cosine * moved[0] - sine * moved[1], sine * moved[0] + cosine * moved[1])

def merge_pair(left_image, right_image, node_ids, positions, beam_angle, interp_table):
    matrices = interp_matrices(interp_table[node_ids], left_image.shape[1])
    left_cos, left_sin = phases(node_ids, positions, beam_angle, 0)
    right_cos, right_sin = phases(node_ids, positions, beam_angle, 1)
    left_re, left_im = side_term(left_image, matrices[:, 0], left_cos, left_sin)
    right_re, right_im = side_term(right_image, matrices[:, 1], right_cos, right_sin)
    return jnp.stack([(left_re + right_re) * half_root, (left_im + right_im) * half_root])

def correlate(signal_re, signal_im, taps_re, taps_im):
    tap_count = taps_re.shape[-1]
    length = signal_re.shape[-1]
    total = length + tap_count
    signal = signal_re + 1j * signal_im
    kernel = (taps_re + 1j * taps_im)[..., ::-1]
    product = jnp.fft.ifft(jnp.fft.fft(signal, total) * jnp.fft.fft(kernel, total))
    start = tap_count // 2 - 1
    window = product[..., start:start + length]
    return (jnp.real(window), jnp.imag(window))

def settle(values):
    return lax.optimization_barrier(values.astype(jnp.bfloat16)).astype(jnp.float32)

def reference(echoes, beam_angle, interp_table):
    group_count = PULSES // P_DEV
    length = R_DEV * N_RNG
    rx_re, rx_im = receiver_taps(jnp.arange(RXS, dtype=jnp.int32), RTAPS)
    rx_re = rx_re.astype(jnp.float32)
    rx_im = rx_im.astype(jnp.float32)
    chirp_re, chirp_im = chirp_taps(CTAPS)
    chirp_re = chirp_re.astype(jnp.float32)
    chirp_im = chirp_im.astype(jnp.float32)
    steering_real, steering_imaginary = steering(beam_angle, RXS)
    steering_real = steering_real.astype(jnp.float32)
    steering_imaginary = steering_imaginary.astype(jnp.float32)
    positions = jnp.arange(length, dtype=jnp.int32)
    grouped = jnp.moveaxis(echoes.reshape(2, group_count, P_DEV, RXS, length), 1, 0)
    local_levels = P_DEV.bit_length() - 1
    highest_precision = lax.Precision.HIGHEST

    def one_group(packed):
        block, group_index = packed
        filtered_re, filtered_im = correlate(block[0].astype(jnp.float32), block[1].astype(jnp.float32), rx_re, rx_im)
        filtered_re = settle(filtered_re)
        filtered_im = settle(filtered_im)
        compressed_real_part, compressed_imaginary_part = correlate(filtered_re, filtered_im, chirp_re, chirp_im)
        compressed_real_part = settle(compressed_real_part)
        compressed_imaginary_part = settle(compressed_imaginary_part)
        beam_output_real = jnp.einsum('lx,yxd->lyd', steering_real, compressed_real_part, precision=highest_precision) - jnp.einsum('lx,yxd->lyd', steering_imaginary, compressed_imaginary_part, precision=highest_precision)
        beam_output_imaginary = jnp.einsum('lx,yxd->lyd', steering_imaginary, compressed_real_part, precision=highest_precision) + jnp.einsum('lx,yxd->lyd', steering_real, compressed_imaginary_part, precision=highest_precision)
        picture = jnp.stack([beam_output_real, beam_output_imaginary])
        for level in range(local_levels):
            groups_now = P_DEV >> level + 1
            node_ids = (group_count + group_index) * groups_now + jnp.arange(groups_now, dtype=jnp.int32)
            paired = picture.reshape(2, BEAMS, groups_now, 2, length)
            picture = merge_pair(paired[:, :, :, 0], paired[:, :, :, 1], node_ids, positions, beam_angle, interp_table)
        return picture[:, :, 0]
    pictures = lax.map(one_group, (grouped, jnp.arange(group_count, dtype=jnp.int32)))
    picture = jnp.moveaxis(pictures, 0, 2)
    for level in range(group_count.bit_length() - 1):
        groups_now = group_count >> level + 1
        node_ids = groups_now + jnp.arange(groups_now, dtype=jnp.int32)
        paired = picture.reshape(2, BEAMS, groups_now, 2, length)
        picture = merge_pair(paired[:, :, :, 0], paired[:, :, :, 1], node_ids, positions, beam_angle, interp_table)
    return picture[:, :, 0]
```

```python
import functools
import math

import jax
import jax.numpy as jnp
import ml_dtypes
import numpy as np
from jax import lax
from jax.experimental import pallas as pl
from jax.experimental.pallas import tpu as pltpu
from jax.sharding import PartitionSpec as P

RTAPS = 64
CTAPS = 512


half_root = 0.7071067811865476
full_turn = 2.0 * math.pi


def extended_2(block, sides, width):
    for axis, dim in sides:
        count = lax.axis_size(axis)
        forward = [(i, i + 1) for i in range(count - 1)]
        backward = [(target, source) for source, target in forward]
        low = lax.ppermute(
            lax.slice_in_dim(block, block.shape[dim] - width, None, axis=dim), axis, forward
        )
        high = lax.ppermute(lax.slice_in_dim(block, 0, width, axis=dim), axis, backward)
        block = jnp.concatenate([low, block, high], axis=dim)
    return block


def swapped(x, axis, distance):
    return lax.ppermute(x, axis, [(i, i ^ 1 << distance) for i in range(lax.axis_size(axis))])


def receiver_taps(channel_ids, tap_count):
    tap_index = jnp.arange(tap_count, dtype=jnp.float32)
    window = 0.5 - 0.5 * jnp.cos(full_turn * (tap_index + 0.5) / tap_count)
    window = window / jnp.sqrt(jnp.sum(window * window))
    channel = channel_ids.astype(jnp.float32)[:, None] + 1.0
    angle = full_turn * channel * (tap_index - tap_count // 2) / (4 * tap_count)
    return (
        (window * jnp.cos(angle)).astype(jnp.bfloat16),
        (window * jnp.sin(angle)).astype(jnp.bfloat16),
    )


def chirp_taps(tap_count):
    offset = jnp.arange(tap_count, dtype=jnp.int32) - tap_count // 2
    phase_step = jnp.mod(offset * offset, 2 * tap_count).astype(jnp.float32)
    angle = math.pi * phase_step / tap_count
    scale = 1.0 / math.sqrt(tap_count)
    return (
        (jnp.cos(angle) * scale).astype(jnp.bfloat16),
        (-jnp.sin(angle) * scale).astype(jnp.bfloat16),
    )


def steering(beam_angle, receivers):
    channel = jnp.arange(receivers, dtype=jnp.int32)
    turns = jnp.mod(beam_angle[:, None] * channel[None, :], 1024).astype(jnp.float32)
    angle = full_turn * turns / 1024.0
    scale = 1.0 / math.sqrt(receivers)
    return (
        (jnp.cos(angle) * scale).astype(jnp.bfloat16),
        (-jnp.sin(angle) * scale).astype(jnp.bfloat16),
    )


def interp_matrices(codes, beam_count):
    shifted = codes // 4 - 1
    fraction = jnp.mod(codes, 4).astype(jnp.float32) / 4.0
    weights = (
        -fraction * (fraction - 1.0) * (fraction - 2.0) / 6.0,
        (fraction + 1.0) * (fraction - 1.0) * (fraction - 2.0) / 2.0,
        -(fraction + 1.0) * fraction * (fraction - 2.0) / 2.0,
        (fraction + 1.0) * fraction * (fraction - 1.0) / 6.0,
    )
    columns = jnp.arange(beam_count, dtype=jnp.int32)
    matrices = jnp.zeros(codes.shape + (beam_count,), jnp.float32)
    for tap_index in range(4):
        target = jnp.mod(columns + shifted + tap_index - 1, beam_count)
        matrices = matrices + weights[tap_index][..., None] * (target[..., None] == columns).astype(
            jnp.float32
        )
    return matrices


def phases(node_ids, positions, beam_angle, side):
    base = jnp.mod(beam_angle[:, None] * (positions[None, :] + 1), 1024)
    factor = 2 * node_ids + side + 1
    turns = jnp.mod(base[:, None, :] * factor[None, :, None], 1024).astype(jnp.float32)
    angle = full_turn * turns / 1024.0
    return (jnp.cos(angle), jnp.sin(angle))


def side_term(picture, matrices, cosine, sine):
    moved = jnp.einsum("gqa,cagr->cqgr", matrices, picture, precision=lax.Precision.HIGHEST)
    return (cosine * moved[0] - sine * moved[1], sine * moved[0] + cosine * moved[1])


def merge_pair(left_image, right_image, node_ids, positions, beam_angle, interp_table):
    matrices = interp_matrices(interp_table[node_ids], left_image.shape[1])
    left_cos, left_sin = phases(node_ids, positions, beam_angle, 0)
    right_cos, right_sin = phases(node_ids, positions, beam_angle, 1)
    left_re, left_im = side_term(left_image, matrices[:, 0], left_cos, left_sin)
    right_re, right_im = side_term(right_image, matrices[:, 1], right_cos, right_sin)
    return jnp.stack([(left_re + right_re) * half_root, (left_im + right_im) * half_root])


def toeplitz_blocks(taps_re, taps_im):
    tap_count = taps_re.shape[-1]
    leading = taps_re.shape[:-1]

    def lay_out(taps):
        padded = jnp.concatenate([taps, jnp.zeros(leading + (tap_count + 1,), taps.dtype)], axis=-1)
        tiled = jnp.tile(padded, (1,) * len(leading) + (tap_count,))
        banded = tiled[..., : 2 * tap_count * tap_count].reshape(
            leading + (tap_count, 2 * tap_count)
        )
        return jnp.swapaxes(banded, -1, -2)

    real_band = lay_out(taps_re)
    imag_band = lay_out(taps_im)
    upper = jnp.concatenate([real_band, imag_band], axis=-1)
    lower = jnp.concatenate([-imag_band, real_band], axis=-1)
    return jnp.concatenate([upper, lower], axis=-2)


def block_filter(extended, matrices, tap_count, per_channel):
    pulses, channels, length = extended.shape[1:]
    blocks = length // tap_count - 1
    pieces = extended.reshape(2, pulses, channels, blocks + 1, tap_count)
    windows = jnp.concatenate([pieces[:, :, :, :-1], pieces[:, :, :, 1:]], axis=4)
    windows = jnp.transpose(windows, (1, 2, 3, 0, 4)).reshape(
        pulses, channels, blocks, 4 * tap_count
    )
    if per_channel:
        output = jnp.einsum("pcnw,cwo->pcno", windows, matrices, preferred_element_type=jnp.float32)
    else:
        output = jnp.einsum("pcnw,wo->pcno", windows, matrices, preferred_element_type=jnp.float32)
    output = output.reshape(pulses, channels, blocks, 2, tap_count)
    return jnp.transpose(output, (3, 0, 1, 2, 4)).reshape(2, pulses, channels, blocks * tap_count)


def local(echoes, beam_angle, interp_table):
    rx_count = lax.axis_size("rx")
    pulse_count = lax.axis_size("pulse")
    rng_place = lax.axis_index("rng")
    rx_place = lax.axis_index("rx")
    pulse_place = lax.axis_index("pulse")
    pulses, channels, length = echoes.shape[1:]
    beam_count = beam_angle.shape[0]
    receivers = channels * rx_count
    channel_ids = rx_place * channels + jnp.arange(channels, dtype=jnp.int32)
    rx_re, rx_im = receiver_taps(channel_ids, RTAPS)
    rx_bands = toeplitz_blocks(rx_re, rx_im)
    chirp_re, chirp_im = chirp_taps(CTAPS)
    chirp_band = toeplitz_blocks(chirp_re, chirp_im)
    extended = extended_2(echoes, (("rng", 3),), RTAPS // 2)
    filtered = block_filter(extended, rx_bands, RTAPS, True).astype(jnp.bfloat16)
    filtered = extended_2(filtered, (("rng", 3),), CTAPS // 2)
    compressed = block_filter(filtered, chirp_band, CTAPS, False).astype(jnp.bfloat16)
    steering_real, steering_imaginary = steering(beam_angle, receivers)
    steer_matrix = jnp.concatenate(
        [
            jnp.concatenate([steering_real, -steering_imaginary], axis=1),
            jnp.concatenate([steering_imaginary, steering_real], axis=1),
        ],
        axis=0,
    )
    arrived = lax.all_to_all(compressed, "rx", split_axis=3, concat_axis=2, tiled=True)
    item_count, recv_count, owned_cols = arrived.shape[1:]
    stacked = jnp.transpose(arrived, (0, 2, 1, 3)).reshape(2 * recv_count, item_count * owned_cols)
    formed = jnp.dot(steer_matrix, stacked, preferred_element_type=jnp.float32)
    picture = formed.reshape(2, beam_count, item_count, owned_cols)
    owned_width = length // rx_count
    positions = (
        rng_place * length + rx_place * owned_width + jnp.arange(owned_width, dtype=jnp.int32)
    )
    for level in range(pulses.bit_length() - 1):
        groups_now = pulses >> level + 1
        node_ids = (pulse_count + pulse_place) * groups_now + jnp.arange(
            groups_now, dtype=jnp.int32
        )
        paired = picture.reshape(2, beam_count, groups_now, 2, owned_width)
        picture = merge_pair(
            paired[:, :, :, 0], paired[:, :, :, 1], node_ids, positions, beam_angle, interp_table
        )
    picture = picture[:, :, 0]
    cross_levels = pulse_count.bit_length() - 1
    piece_width = owned_width // pulse_count
    pieces = picture.reshape(2, beam_count, pulse_count, piece_width)
    spots = positions.reshape(pulse_count, piece_width)
    for level in range(cross_levels):
        parity = jnp.right_shift(pulse_place, level) & 1
        count_now = pieces.shape[2]
        paired = pieces.reshape(2, beam_count, count_now // 2, 2, piece_width)
        kept_half = lax.dynamic_index_in_dim(paired, parity, 3, keepdims=False)
        sent_half = lax.dynamic_index_in_dim(paired, 1 - parity, 3, keepdims=False)
        partner = swapped(sent_half, "pulse", level)
        spot_pairs = spots.reshape(count_now // 2, 2, piece_width)
        spots = lax.dynamic_index_in_dim(spot_pairs, parity, 1, keepdims=False)
        own_part = kept_half.reshape(2, beam_count, -1)
        other_part = partner.reshape(2, beam_count, -1)
        left_image = jnp.where(parity == 0, own_part, other_part)
        right_image = jnp.where(parity == 0, other_part, own_part)
        combine_node_ids = jnp.reshape(
            (pulse_count >> level + 1) + jnp.right_shift(pulse_place, level + 1), (1,)
        )
        merged = merge_pair(
            left_image[:, :, None],
            right_image[:, :, None],
            combine_node_ids,
            spots.reshape(-1),
            beam_angle,
            interp_table,
        )
        flat = merged[:, :, 0]
        pieces = flat.reshape(2, beam_count, count_now // 2, piece_width)
    picture = pieces.reshape(2, beam_count, piece_width)
    return picture


LANES = 128
RX_TILE = 2 * LANES
CHIRP_TILE = 6 * LANES
HALO_TILES = 3
HALO = HALO_TILES * LANES


def vmem():
    return pl.BlockSpec(memory_space=pltpu.VMEM)


def rx_bands_table(receivers):
    step = np.arange(RTAPS, dtype=np.float64)
    window = 0.5 - 0.5 * np.cos(full_turn * (step + 0.5) / RTAPS)
    window = window / np.sqrt(np.sum(window * window))
    channel = np.arange(receivers, dtype=np.float64)[:, None] + 1.0
    angle = full_turn * channel * (step - RTAPS // 2) / (4 * RTAPS)
    offset = np.arange(RX_TILE)[:, None] - np.arange(LANES)[None, :]
    inside = (offset >= 0) & (offset < RTAPS)
    place = np.clip(offset, 0, RTAPS - 1)
    bands = [
        np.where(inside, taps[:, place], 0.0) for taps in (window * np.cos(angle), window * np.sin(angle))
    ]
    return np.concatenate(bands, axis=-1).astype(ml_dtypes.bfloat16)


def chirp_bands_table():
    offset = np.arange(CTAPS) - CTAPS // 2
    angle = math.pi * np.mod(offset * offset, 2 * CTAPS) / CTAPS
    scale = 1.0 / math.sqrt(CTAPS)
    offset = np.arange(CHIRP_TILE)[:, None] - np.arange(LANES)[None, :] - (LANES - RTAPS // 2)
    inside = (offset >= 0) & (offset < CTAPS)
    place = np.clip(offset, 0, CTAPS - 1)
    bands = [
        np.where(inside, taps[place], 0.0) for taps in (np.cos(angle) * scale, -np.sin(angle) * scale)
    ]
    return np.concatenate(bands, axis=-1).astype(ml_dtypes.bfloat16)


def chirp_piece(filtered_ref, chirp_ref, starts, out_ref):
    windows = [filtered_ref[:, pl.ds(start, CHIRP_TILE)] for start in starts]
    product = jnp.dot(
        jnp.concatenate(windows, axis=0), chirp_ref[...], preferred_element_type=jnp.float32
    )
    pulses, rows, _ = out_ref.shape
    channels = rows // 2
    product = product.reshape(len(starts), pulses, rows, 2 * LANES)
    for tile in range(len(starts)):
        block = product[tile]
        real = block[:, :channels, :LANES] - block[:, channels:, LANES:]
        imag = block[:, :channels, LANES:] + block[:, channels:, :LANES]
        out_ref[:, :, tile * LANES : (tile + 1) * LANES] = jnp.concatenate(
            [real, imag], axis=1
        ).astype(jnp.bfloat16)


def filter_kernel(sizes, echo_ref, edge_ref, bands_hbm, chirp_ref, *rest):
    rng_count, piece_count, piece_tiles = sizes
    send_refs, (filtered_ref, rows_in, rows_out, bands_ref, arrived) = (
        rest[:piece_count],
        rest[piece_count:],
    )
    _, pulses, channels, length = echo_ref.shape
    rng_place = lax.axis_index("rng")
    rx_place = lax.axis_index("rx")
    pulse_place = lax.axis_index("pulse")
    fetch = pltpu.make_async_copy(
        bands_hbm.at[pl.ds(rx_place * channels, channels)], bands_ref, arrived
    )
    fetch.start()
    tiles = length // LANES
    group = 2 * pulses
    has_low = jnp.where(rng_place > 0, 1.0, 0.0).astype(jnp.float32)
    has_high = jnp.where(rng_place < rng_count - 1, 1.0, 0.0).astype(jnp.float32)
    for part in range(2):
        for pulse in range(pulses):
            where = pl.ds(part * pulses + pulse, channels, stride=group)
            edge = edge_ref[part, pulse].astype(jnp.float32)
            block = echo_ref[part, pulse].astype(jnp.float32)
            for tile in range(HALO_TILES):
                span = edge[:, tile * LANES : (tile + 1) * LANES]
                rows_in[tile, where, :] = span * has_low
                rows_in[HALO_TILES + tiles + tile, where, :] = span * has_high
            for tile in range(tiles):
                span = block[:, tile * LANES : (tile + 1) * LANES]
                rows_in[HALO_TILES + tile, where, :] = span
    fetch.wait()
    out_tiles = tiles + 2 * HALO_TILES - 1
    lane = lax.broadcasted_iota(jnp.int32, (1, LANES), 1)
    total = rng_count * length
    for channel in range(channels):
        rows = rows_in[:, channel * group : (channel + 1) * group, :].astype(jnp.bfloat16)
        windows = jnp.concatenate(
            [
                rows[:-1].reshape(out_tiles * group, LANES),
                rows[1:].reshape(out_tiles * group, LANES),
            ],
            axis=1,
        )
        product = jnp.dot(windows, bands_ref[channel], preferred_element_type=jnp.float32)
        product = product.reshape(out_tiles, group, 2 * LANES)
        for tile in range(out_tiles):
            block = product[tile]
            real = block[:pulses, :LANES] - block[pulses:, LANES:]
            imag = block[:pulses, LANES:] + block[pulses:, :LANES]
            if tile <= HALO_TILES - 1 or tile >= out_tiles - HALO_TILES:
                spot = rng_place * length + (tile - HALO_TILES) * LANES + RTAPS // 2 + lane
                inside = (spot >= 0) & (spot < total)
                real = jnp.where(inside, real, 0.0)
                imag = jnp.where(inside, imag, 0.0)
            rows_out[tile, pl.ds(channel, pulses, stride=2 * channels), :] = real
            rows_out[tile, pl.ds(channels + channel, pulses, stride=2 * channels), :] = imag
    for tile in range(out_tiles):
        filtered_ref[:, tile * LANES : (tile + 1) * LANES] = rows_out[tile].astype(jnp.bfloat16)
    base = (1 - rx_place) * (piece_count * piece_tiles)
    for distance in range(piece_count):
        piece = jnp.bitwise_xor(pulse_place, distance)
        first = base + piece * piece_tiles
        starts = [pl.multiple_of((first + t) * LANES, LANES) for t in range(piece_tiles)]
        chirp_piece(filtered_ref, chirp_ref, starts, send_refs[distance])


def keep_kernel(sizes, filtered_ref, chirp_ref, *keep_refs):
    piece_count, piece_tiles = sizes
    rx_place = lax.axis_index("rx")
    pulse_place = lax.axis_index("pulse")
    base = rx_place * (piece_count * piece_tiles)
    for distance in range(piece_count):
        piece = jnp.bitwise_xor(pulse_place, distance)
        first = base + piece * piece_tiles
        starts = [pl.multiple_of((first + t) * LANES, LANES) for t in range(piece_tiles)]
        chirp_piece(filtered_ref, chirp_ref, starts, keep_refs[distance])


def turn_parts(step):
    shifted = step + 128
    angle = (jnp.bitwise_and(shifted, 255) - 128).astype(jnp.float32) * (full_turn / 1024.0)
    quarter = jnp.right_shift(shifted, 8)
    square = angle * angle
    cosine = 1.0 + square * (-1 / 2 + square * (1 / 24 + square * (-1 / 720 + square * (1 / 40320))))
    sine = angle * (1.0 + square * (-1 / 6 + square * (1 / 120 + square * (-1 / 5040))))
    odd = jnp.bitwise_and(quarter, 1) == 1
    real = jnp.where(odd, sine, cosine)
    imag = jnp.where(odd, cosine, sine)
    real = jnp.where(jnp.bitwise_and(quarter + 1, 2) == 2, -real, real)
    imag = jnp.where(jnp.bitwise_and(quarter, 2) == 2, -imag, imag)
    return real, imag


def as_column(row):
    count = row.shape[1]
    first = lax.broadcasted_iota(jnp.int32, (count, count), 0)
    second = lax.broadcasted_iota(jnp.int32, (count, count), 1)
    spread = jnp.where(first == second, row.astype(jnp.float32), 0.0)
    return jnp.sum(spread, axis=1, keepdims=True).astype(jnp.int32)


def interp_matrix(codes_ref, row):
    code = as_column(codes_ref[pl.ds(row, 1), :])
    beams = codes_ref.shape[1]
    shift = jnp.right_shift(code, 2) - 1
    part = jnp.bitwise_and(code, 3).astype(jnp.float32) * 0.25
    weights = (
        -part * (part - 1.0) * (part - 2.0) * (1.0 / 6.0),
        (part + 1.0) * (part - 1.0) * (part - 2.0) * 0.5,
        -(part + 1.0) * part * (part - 2.0) * 0.5,
        (part + 1.0) * part * (part - 1.0) * (1.0 / 6.0),
    )
    angle_bin = lax.broadcasted_iota(jnp.int32, (beams, beams), 0)
    column = lax.broadcasted_iota(jnp.int32, (beams, beams), 1)
    tap = jnp.bitwise_and(column - angle_bin - shift + 1, beams - 1)
    matrix = jnp.zeros((beams, beams), jnp.float32)
    for index in range(4):
        matrix = jnp.where(tap == index, weights[index], matrix)
    return matrix.astype(jnp.bfloat16)


def tables_kernel(
    sizes, angle_ref, codes_ref, first_ref, inner_ref, outer_ref, phase_ref, outer_phase_ref
):
    pulses, channels, rx_count, width = sizes
    rng_place = lax.axis_index("rng")
    rx_place = lax.axis_index("rx")
    pulse_place = lax.axis_index("pulse")
    beams = angle_ref.shape[1]
    piece_count = phase_ref.shape[0]
    piece_width = phase_ref.shape[4]
    images = pulses * piece_count
    angle = as_column(angle_ref[...])
    column = lax.broadcasted_iota(jnp.int32, (1, 4 * channels * 2), 1)
    within = jnp.bitwise_and(column, 4 * channels - 1)
    owner = jnp.bitwise_xor(rx_place, jnp.where(within >= 2 * channels, 1, 0))
    receiver = owner * channels + jnp.bitwise_and(column, channels - 1)
    is_imag = jnp.bitwise_and(within, channels) != 0
    scale = 1.0 / math.sqrt(channels * rx_count)
    steer_re, steer_im = turn_parts(jnp.bitwise_and(angle * receiver, 1023))
    steer_re = (steer_re * scale).astype(jnp.bfloat16).astype(jnp.float32)
    steer_im = (-steer_im * scale).astype(jnp.bfloat16).astype(jnp.float32)
    steer = jnp.concatenate(
        [
            jnp.where(is_imag, -steer_im, steer_re).astype(jnp.bfloat16),
            jnp.where(is_imag, steer_re, steer_im).astype(jnp.bfloat16),
        ],
        axis=1,
    )
    low_half = column >= 4 * channels
    entries = 8 * channels
    for index in range(pulses):
        matrix = interp_matrix(codes_ref, images + pulse_place * pulses + index)
        composed = jnp.dot(matrix, steer, preferred_element_type=jnp.float32)
        for part in range(2):
            value = composed[:, part * entries : (part + 1) * entries]
            high = value.astype(jnp.bfloat16)
            low = (value - high.astype(jnp.float32)).astype(jnp.bfloat16)
            first_ref[index, part * beams : (part + 1) * beams, :] = jnp.where(
                low_half, low.astype(jnp.float32), high.astype(jnp.float32)
            ).astype(jnp.bfloat16)
    factors = []
    slot = 0
    now = pulses
    while now > 1:
        factors.extend(now * piece_count + pulse_place * now + i + 1 for i in range(now))
        if now < pulses:
            for index in range(now):
                inner_ref[slot] = interp_matrix(
                    codes_ref, now * piece_count + pulse_place * now + index
                )
                slot += 1
        now //= 2
    lane = lax.broadcasted_iota(jnp.int32, (1, piece_width), 1)
    block = (rng_place * rx_count + rx_place) * width + 1

    def one_piece(distance, carry):
        piece = jnp.bitwise_xor(pulse_place, distance)
        base = jnp.bitwise_and(angle * (block + piece * piece_width + lane), 1023)
        for index, factor in enumerate(factors):
            real, imag = turn_parts(jnp.bitwise_and(base * factor, 1023))
            phase_ref[distance, index, 0] = real * half_root
            phase_ref[distance, index, 1] = imag * half_root
        return carry

    lax.fori_loop(0, piece_count, one_piece, 0)
    base = jnp.bitwise_and(angle * (block + pulse_place * piece_width + lane), 1023)
    slot = 0
    now = piece_count
    while now > 1:
        for index in range(now):
            outer_ref[slot] = interp_matrix(codes_ref, now + index)
            real, imag = turn_parts(jnp.bitwise_and(base * (now + index + 1), 1023))
            outer_phase_ref[slot, 0] = real * half_root
            outer_phase_ref[slot, 1] = imag * half_root
            slot += 1
        now //= 2


def turned(real, imag, phase_re, phase_im):
    return phase_re * real - phase_im * imag, phase_im * real + phase_re * imag


def inner_kernel(own_ref, other_ref, first_ref, inner_ref, phase_ref, out_ref):
    pulses = own_ref.shape[0]
    beams = inner_ref.shape[1]
    terms = []
    for index in range(pulses):
        rows = jnp.concatenate([own_ref[index], other_ref[index]], axis=0)
        moved = jnp.dot(
            first_ref[index],
            jnp.concatenate([rows, rows], axis=0),
            preferred_element_type=jnp.float32,
        )
        terms.append(
            turned(moved[:beams], moved[beams:], phase_ref[0, index, 0], phase_ref[0, index, 1])
        )
        if index & 1:
            right, left = terms.pop(), terms.pop()
            terms.append((left[0] + right[0], left[1] + right[1]))
    slot = 0
    phase_slot = pulses
    while len(terms) > 1:
        pictures, terms = terms, []
        for index, (real, imag) in enumerate(pictures):
            matrix = inner_ref[slot]
            moved_re = jnp.dot(
                matrix, real.astype(jnp.bfloat16), preferred_element_type=jnp.float32
            )
            moved_im = jnp.dot(
                matrix, imag.astype(jnp.bfloat16), preferred_element_type=jnp.float32
            )
            terms.append(
                turned(moved_re, moved_im, phase_ref[0, phase_slot, 0], phase_ref[0, phase_slot, 1])
            )
            if index & 1:
                right, left = terms.pop(), terms.pop()
                terms.append((left[0] + right[0], left[1] + right[1]))
            slot += 1
            phase_slot += 1
    out_ref[0] = terms[0][0].astype(jnp.bfloat16)
    out_ref[1] = terms[0][1].astype(jnp.bfloat16)


def outer_kernel(outer_ref, phase_ref, *rest):
    image_refs, out_ref = rest[:-1], rest[-1]
    pulse_place = lax.axis_index("pulse")
    pictures = [(ref[0], ref[1]) for ref in image_refs]
    base = 0
    level = 0
    while len(pictures) > 1:
        count = len(pictures)
        place = jnp.right_shift(pulse_place, level)
        merged = []
        for distance, (real, imag) in enumerate(pictures):
            slot = base + jnp.bitwise_xor(place, distance)
            matrix = outer_ref[slot]
            moved_re = jnp.dot(
                matrix, real.astype(jnp.bfloat16), preferred_element_type=jnp.float32
            )
            moved_im = jnp.dot(
                matrix, imag.astype(jnp.bfloat16), preferred_element_type=jnp.float32
            )
            merged.append(turned(moved_re, moved_im, phase_ref[slot, 0], phase_ref[slot, 1]))
            if distance & 1:
                right, left = merged.pop(), merged.pop()
                merged.append((left[0] + right[0], left[1] + right[1]))
        pictures = merged
        base += count
        level += 1
    out_ref[0] = pictures[0][0]
    out_ref[1] = pictures[0][1]


PARAMS = dict(compiler_params=pltpu.CompilerParams(vmem_limit_bytes=48 * 1024 * 1024))


def fast(echoes, beam_angle, interp_table):
    rng_count = lax.axis_size("rng")
    rx_count = lax.axis_size("rx")
    pulse_count = lax.axis_size("pulse")
    rng_place = lax.axis_index("rng")
    _, pulses, channels, length = echoes.shape
    beams = beam_angle.shape[0]
    width = length // rx_count
    piece_width = width // pulse_count
    piece_tiles = piece_width // LANES
    rows = 2 * channels
    bands = jnp.asarray(rx_bands_table(channels * rx_count))
    chirp = jnp.asarray(chirp_bands_table())
    bf16 = jnp.bfloat16
    f32 = jnp.float32
    edge = jnp.where(rng_place == 0, echoes[..., length - HALO :], echoes[..., :HALO])
    edge = swapped(edge, "rng", 0)
    shape = jax.ShapeDtypeStruct
    piece_shape = shape((pulses, rows, piece_width), bf16)
    tiles = length // LANES + 2 * HALO_TILES
    filtered_shape = shape((rows * pulses, (tiles - 1) * LANES), bf16)
    *sent, filtered = pl.pallas_call(
        functools.partial(filter_kernel, (rng_count, pulse_count, piece_tiles)),
        out_shape=[piece_shape] * pulse_count + [filtered_shape],
        in_specs=[vmem(), vmem(), pl.BlockSpec(memory_space=pl.ANY), vmem()],
        out_specs=[vmem()] * (pulse_count + 1),
        scratch_shapes=[
            pltpu.VMEM((tiles, rows * pulses, LANES), f32),
            pltpu.VMEM((tiles - 1, rows * pulses, LANES), f32),
            pltpu.VMEM((channels,) + bands.shape[1:], bf16),
            pltpu.SemaphoreType.DMA,
        ],
        name="filter",
        **PARAMS,
    )(echoes, edge, bands, chirp)
    received = [swapped(piece, "rx", 0) for piece in sent]
    kept = pl.pallas_call(
        functools.partial(keep_kernel, (pulse_count, piece_tiles)),
        out_shape=[piece_shape] * pulse_count,
        in_specs=[vmem()] * 2,
        out_specs=[vmem()] * pulse_count,
        name="keep",
        **PARAMS,
    )(filtered, chirp)
    inner_count = pulses - 2
    outer_count = 2 * pulse_count - 2
    first, inner, outer, phase, outer_phase = pl.pallas_call(
        functools.partial(tables_kernel, (pulses, channels, rx_count, width)),
        out_shape=[
            shape((pulses, 2 * beams, 8 * channels), bf16),
            shape((inner_count, beams, beams), bf16),
            shape((outer_count, beams, beams), bf16),
            shape((pulse_count, 2 * pulses - 2, 2, beams, piece_width), f32),
            shape((outer_count, 2, beams, piece_width), f32),
        ],
        in_specs=[vmem()] * 2,
        out_specs=[vmem()] * 5,
        name="tables",
        **PARAMS,
    )(beam_angle.reshape(1, beams), interp_table.reshape(-1, beams))
    images = []
    for distance in reversed(range(pulse_count)):
        image = pl.pallas_call(
            inner_kernel,
            out_shape=shape((2, beams, piece_width), bf16),
            grid=(1,),
            in_specs=[
                vmem(),
                vmem(),
                vmem(),
                vmem(),
                pl.BlockSpec(
                    (1,) + phase.shape[1:], lambda step, distance=distance: (distance, 0, 0, 0, 0)
                ),
            ],
            out_specs=vmem(),
            name="inner",
            **PARAMS,
        )(kept[distance], received[distance], first, inner, phase)
        if distance:
            image = lax.ppermute(
                image, "pulse", [(i, i ^ distance) for i in range(pulse_count)]
            )
        images.insert(0, image)
    return pl.pallas_call(
        outer_kernel,
        out_shape=shape((2, beams, piece_width), f32),
        in_specs=[vmem()] * (2 + pulse_count),
        out_specs=vmem(),
        name="outer",
        **PARAMS,
    )(outer, outer_phase, *images)


def power_of_two(count):
    return count > 0 and count & (count - 1) == 0


def per_device(echoes, beam_angle, interp_table):
    _, pulses, channels, length = echoes.shape
    rx_count = lax.axis_size("rx")
    pulse_count = lax.axis_size("pulse")
    piece_width = length // (rx_count * pulse_count)
    if (
        lax.axis_size("rng") == 2
        and rx_count == 2
        and channels == 8
        and pulses == 8
        and power_of_two(pulse_count)
        and pulse_count > 1
        and power_of_two(beam_angle.shape[0])
        and beam_angle.shape[0] % 16 == 0
        and piece_width % LANES == 0
    ):
        return fast(echoes, beam_angle, interp_table)
    return local(echoes, beam_angle, interp_table)


def solution(mesh):
    placed = (P(None, ("slab", "pulse"), "rx", "rng"), P(), P())
    return jax.shard_map(
        per_device,
        mesh=mesh,
        in_specs=placed,
        out_specs=P(None, "slab", ("rng", "rx", "pulse")),
        check_vma=False,
    )
```

```python
import functools
import math

import jax
import jax.numpy as jnp
import ml_dtypes
import numpy as np
from jax import lax
from jax.experimental import pallas as pl
from jax.experimental.pallas import tpu as pltpu
from jax.sharding import PartitionSpec as P

RTAPS = 64
CTAPS = 512


half_root = 0.7071067811865476
full_turn = 2.0 * math.pi


def extended_2(block, sides, width):
    for axis, dim in sides:
        count = lax.axis_size(axis)
        forward = [(i, i + 1) for i in range(count - 1)]
        backward = [(target, source) for source, target in forward]
        low = lax.ppermute(
            lax.slice_in_dim(block, block.shape[dim] - width, None, axis=dim), axis, forward
        )
        high = lax.ppermute(lax.slice_in_dim(block, 0, width, axis=dim), axis, backward)
        block = jnp.concatenate([low, block, high], axis=dim)
    return block


def swapped(x, axis, distance):
    return lax.ppermute(x, axis, [(i, i ^ 1 << distance) for i in range(lax.axis_size(axis))])


def receiver_taps(channel_ids, tap_count):
    tap_index = jnp.arange(tap_count, dtype=jnp.float32)
    window = 0.5 - 0.5 * jnp.cos(full_turn * (tap_index + 0.5) / tap_count)
    window = window / jnp.sqrt(jnp.sum(window * window))
    channel = channel_ids.astype(jnp.float32)[:, None] + 1.0
    angle = full_turn * channel * (tap_index - tap_count // 2) / (4 * tap_count)
    return (
        (window * jnp.cos(angle)).astype(jnp.bfloat16),
        (window * jnp.sin(angle)).astype(jnp.bfloat16),
    )


def chirp_taps(tap_count):
    offset = jnp.arange(tap_count, dtype=jnp.int32) - tap_count // 2
    phase_step = jnp.mod(offset * offset, 2 * tap_count).astype(jnp.float32)
    angle = math.pi * phase_step / tap_count
    scale = 1.0 / math.sqrt(tap_count)
    return (
        (jnp.cos(angle) * scale).astype(jnp.bfloat16),
        (-jnp.sin(angle) * scale).astype(jnp.bfloat16),
    )


def steering(beam_angle, receivers):
    channel = jnp.arange(receivers, dtype=jnp.int32)
    turns = jnp.mod(beam_angle[:, None] * channel[None, :], 1024).astype(jnp.float32)
    angle = full_turn * turns / 1024.0
    scale = 1.0 / math.sqrt(receivers)
    return (
        (jnp.cos(angle) * scale).astype(jnp.bfloat16),
        (-jnp.sin(angle) * scale).astype(jnp.bfloat16),
    )


def interp_matrices(codes, beam_count):
    shifted = codes // 4 - 1
    fraction = jnp.mod(codes, 4).astype(jnp.float32) / 4.0
    weights = (
        -fraction * (fraction - 1.0) * (fraction - 2.0) / 6.0,
        (fraction + 1.0) * (fraction - 1.0) * (fraction - 2.0) / 2.0,
        -(fraction + 1.0) * fraction * (fraction - 2.0) / 2.0,
        (fraction + 1.0) * fraction * (fraction - 1.0) / 6.0,
    )
    columns = jnp.arange(beam_count, dtype=jnp.int32)
    matrices = jnp.zeros(codes.shape + (beam_count,), jnp.float32)
    for tap_index in range(4):
        target = jnp.mod(columns + shifted + tap_index - 1, beam_count)
        matrices = matrices + weights[tap_index][..., None] * (target[..., None] == columns).astype(
            jnp.float32
        )
    return matrices


def phases(node_ids, positions, beam_angle, side):
    base = jnp.mod(beam_angle[:, None] * (positions[None, :] + 1), 1024)
    factor = 2 * node_ids + side + 1
    turns = jnp.mod(base[:, None, :] * factor[None, :, None], 1024).astype(jnp.float32)
    angle = full_turn * turns / 1024.0
    return (jnp.cos(angle), jnp.sin(angle))


def side_term(picture, matrices, cosine, sine):
    moved = jnp.einsum("gqa,cagr->cqgr", matrices, picture, precision=lax.Precision.HIGHEST)
    return (cosine * moved[0] - sine * moved[1], sine * moved[0] + cosine * moved[1])


def merge_pair(left_image, right_image, node_ids, positions, beam_angle, interp_table):
    matrices = interp_matrices(interp_table[node_ids], left_image.shape[1])
    left_cos, left_sin = phases(node_ids, positions, beam_angle, 0)
    right_cos, right_sin = phases(node_ids, positions, beam_angle, 1)
    left_re, left_im = side_term(left_image, matrices[:, 0], left_cos, left_sin)
    right_re, right_im = side_term(right_image, matrices[:, 1], right_cos, right_sin)
    return jnp.stack([(left_re + right_re) * half_root, (left_im + right_im) * half_root])


def toeplitz_blocks(taps_re, taps_im):
    tap_count = taps_re.shape[-1]
    leading = taps_re.shape[:-1]

    def lay_out(taps):
        padded = jnp.concatenate([taps, jnp.zeros(leading + (tap_count + 1,), taps.dtype)], axis=-1)
        tiled = jnp.tile(padded, (1,) * len(leading) + (tap_count,))
        banded = tiled[..., : 2 * tap_count * tap_count].reshape(
            leading + (tap_count, 2 * tap_count)
        )
        return jnp.swapaxes(banded, -1, -2)

    real_band = lay_out(taps_re)
    imag_band = lay_out(taps_im)
    upper = jnp.concatenate([real_band, imag_band], axis=-1)
    lower = jnp.concatenate([-imag_band, real_band], axis=-1)
    return jnp.concatenate([upper, lower], axis=-2)


def block_filter(extended, matrices, tap_count, per_channel):
    pulses, channels, length = extended.shape[1:]
    blocks = length // tap_count - 1
    pieces = extended.reshape(2, pulses, channels, blocks + 1, tap_count)
    windows = jnp.concatenate([pieces[:, :, :, :-1], pieces[:, :, :, 1:]], axis=4)
    windows = jnp.transpose(windows, (1, 2, 3, 0, 4)).reshape(
        pulses, channels, blocks, 4 * tap_count
    )
    if per_channel:
        output = jnp.einsum("pcnw,cwo->pcno", windows, matrices, preferred_element_type=jnp.float32)
    else:
        output = jnp.einsum("pcnw,wo->pcno", windows, matrices, preferred_element_type=jnp.float32)
    output = output.reshape(pulses, channels, blocks, 2, tap_count)
    return jnp.transpose(output, (3, 0, 1, 2, 4)).reshape(2, pulses, channels, blocks * tap_count)


def local(echoes, beam_angle, interp_table):
    rx_count = lax.axis_size("rx")
    pulse_count = lax.axis_size("pulse")
    rng_place = lax.axis_index("rng")
    rx_place = lax.axis_index("rx")
    pulse_place = lax.axis_index("pulse")
    pulses, channels, length = echoes.shape[1:]
    beam_count = beam_angle.shape[0]
    receivers = channels * rx_count
    channel_ids = rx_place * channels + jnp.arange(channels, dtype=jnp.int32)
    rx_re, rx_im = receiver_taps(channel_ids, RTAPS)
    rx_bands = toeplitz_blocks(rx_re, rx_im)
    chirp_re, chirp_im = chirp_taps(CTAPS)
    chirp_band = toeplitz_blocks(chirp_re, chirp_im)
    extended = extended_2(echoes, (("rng", 3),), RTAPS // 2)
    filtered = block_filter(extended, rx_bands, RTAPS, True).astype(jnp.bfloat16)
    filtered = extended_2(filtered, (("rng", 3),), CTAPS // 2)
    compressed = block_filter(filtered, chirp_band, CTAPS, False).astype(jnp.bfloat16)
    steering_real, steering_imaginary = steering(beam_angle, receivers)
    steer_matrix = jnp.concatenate(
        [
            jnp.concatenate([steering_real, -steering_imaginary], axis=1),
            jnp.concatenate([steering_imaginary, steering_real], axis=1),
        ],
        axis=0,
    )
    arrived = lax.all_to_all(compressed, "rx", split_axis=3, concat_axis=2, tiled=True)
    item_count, recv_count, owned_cols = arrived.shape[1:]
    stacked = jnp.transpose(arrived, (0, 2, 1, 3)).reshape(2 * recv_count, item_count * owned_cols)
    formed = jnp.dot(steer_matrix, stacked, preferred_element_type=jnp.float32)
    picture = formed.reshape(2, beam_count, item_count, owned_cols)
    owned_width = length // rx_count
    positions = (
        rng_place * length + rx_place * owned_width + jnp.arange(owned_width, dtype=jnp.int32)
    )
    for level in range(pulses.bit_length() - 1):
        groups_now = pulses >> level + 1
        node_ids = (pulse_count + pulse_place) * groups_now + jnp.arange(
            groups_now, dtype=jnp.int32
        )
        paired = picture.reshape(2, beam_count, groups_now, 2, owned_width)
        picture = merge_pair(
            paired[:, :, :, 0], paired[:, :, :, 1], node_ids, positions, beam_angle, interp_table
        )
    picture = picture[:, :, 0]
    cross_levels = pulse_count.bit_length() - 1
    piece_width = owned_width // pulse_count
    pieces = picture.reshape(2, beam_count, pulse_count, piece_width)
    spots = positions.reshape(pulse_count, piece_width)
    for level in range(cross_levels):
        parity = jnp.right_shift(pulse_place, level) & 1
        count_now = pieces.shape[2]
        paired = pieces.reshape(2, beam_count, count_now // 2, 2, piece_width)
        kept_half = lax.dynamic_index_in_dim(paired, parity, 3, keepdims=False)
        sent_half = lax.dynamic_index_in_dim(paired, 1 - parity, 3, keepdims=False)
        partner = swapped(sent_half, "pulse", level)
        spot_pairs = spots.reshape(count_now // 2, 2, piece_width)
        spots = lax.dynamic_index_in_dim(spot_pairs, parity, 1, keepdims=False)
        own_part = kept_half.reshape(2, beam_count, -1)
        other_part = partner.reshape(2, beam_count, -1)
        left_image = jnp.where(parity == 0, own_part, other_part)
        right_image = jnp.where(parity == 0, other_part, own_part)
        combine_node_ids = jnp.reshape(
            (pulse_count >> level + 1) + jnp.right_shift(pulse_place, level + 1), (1,)
        )
        merged = merge_pair(
            left_image[:, :, None],
            right_image[:, :, None],
            combine_node_ids,
            spots.reshape(-1),
            beam_angle,
            interp_table,
        )
        flat = merged[:, :, 0]
        pieces = flat.reshape(2, beam_count, count_now // 2, piece_width)
    picture = pieces.reshape(2, beam_count, piece_width)
    return picture


LANES = 128
RX_TILE = 2 * LANES
CHIRP_TILE = 6 * LANES
HALO_TILES = 3
HALO = HALO_TILES * LANES


def vmem():
    return pl.BlockSpec(memory_space=pltpu.VMEM)


def hbm():
    return pl.BlockSpec(memory_space=pltpu.HBM)


def anywhere():
    return pl.BlockSpec(memory_space=pl.ANY)


def rx_bands_table(receivers):
    step = np.arange(RTAPS, dtype=np.float64)
    window = 0.5 - 0.5 * np.cos(full_turn * (step + 0.5) / RTAPS)
    window = window / np.sqrt(np.sum(window * window))
    channel = np.arange(receivers, dtype=np.float64)[:, None] + 1.0
    angle = full_turn * channel * (step - RTAPS // 2) / (4 * RTAPS)
    offset = np.arange(RX_TILE)[:, None] - np.arange(LANES)[None, :]
    inside = (offset >= 0) & (offset < RTAPS)
    place = np.clip(offset, 0, RTAPS - 1)
    bands = [
        np.where(inside, taps[:, place], 0.0)
        for taps in (window * np.cos(angle), window * np.sin(angle))
    ]
    return np.concatenate(bands, axis=-1).astype(ml_dtypes.bfloat16)


def chirp_bands_table():
    offset = np.arange(CTAPS) - CTAPS // 2
    angle = math.pi * np.mod(offset * offset, 2 * CTAPS) / CTAPS
    scale = 1.0 / math.sqrt(CTAPS)
    offset = np.arange(CHIRP_TILE)[:, None] - np.arange(LANES)[None, :] - (LANES - RTAPS // 2)
    inside = (offset >= 0) & (offset < CTAPS)
    place = np.clip(offset, 0, CTAPS - 1)
    bands = [
        np.where(inside, taps[place], 0.0)
        for taps in (np.cos(angle) * scale, -np.sin(angle) * scale)
    ]
    return np.concatenate(bands, axis=-1).astype(ml_dtypes.bfloat16)


def edge_kernel(echo_hbm, edge_ref, echo_ref, arrived):
    length = echo_hbm.shape[3]
    start = jnp.where(lax.axis_index("rng") == 0, length - HALO, 0)
    start = pl.multiple_of(start, LANES)
    edge = pltpu.make_async_copy(
        echo_hbm.at[:, :, :, pl.ds(start, HALO)], edge_ref, arrived.at[0]
    )
    edge.start()
    whole = pltpu.make_async_copy(echo_hbm, echo_ref, arrived.at[1])
    whole.start()
    edge.wait()
    whole.wait()


def filter_channel(windows, bands, pulses):
    product = jnp.dot(windows, bands, preferred_element_type=jnp.float32)
    product = product.reshape(-1, 2, pulses, 2 * LANES)
    real = product[:, 0, :, :LANES] - product[:, 1, :, LANES:]
    imag = product[:, 0, :, LANES:] + product[:, 1, :, :LANES]
    return real, imag


def interior_kernel(echo_ref, bands_hbm, filtered_ref, rows_in, rows_out, bands_ref, arrived):
    _, pulses, channels, length = echo_ref.shape
    rx_place = lax.axis_index("rx")
    fetch = pltpu.make_async_copy(
        bands_hbm.at[pl.ds(rx_place * channels, channels)], bands_ref, arrived
    )
    fetch.start()
    tiles = length // LANES
    group = 2 * pulses
    empty = jnp.zeros(rows_in.shape[1:], jnp.float32)
    rows_in[0] = empty
    rows_in[tiles + 1] = empty
    for part in range(2):
        for pulse in range(pulses):
            where = pl.ds(part * pulses + pulse, channels, stride=group)
            block = echo_ref[part, pulse].astype(jnp.float32)
            for tile in range(tiles):
                rows_in[tile + 1, where, :] = block[:, tile * LANES : (tile + 1) * LANES]
    fetch.wait()
    lane = lax.broadcasted_iota(jnp.int32, (1, LANES), 1)
    for channel in range(channels):
        rows = rows_in[:, channel * group : (channel + 1) * group, :].astype(jnp.bfloat16)
        windows = jnp.concatenate(
            [rows[:-1].reshape(-1, LANES), rows[1:].reshape(-1, LANES)], axis=1
        )
        real, imag = filter_channel(windows, bands_ref[channel], pulses)
        for tile in range(tiles + 1):
            tile_re, tile_im = real[tile], imag[tile]
            if tile == 0:
                tile_re = jnp.where(lane >= LANES - RTAPS // 2, tile_re, 0.0)
                tile_im = jnp.where(lane >= LANES - RTAPS // 2, tile_im, 0.0)
            if tile == tiles:
                tile_re = jnp.where(lane < LANES - RTAPS // 2, tile_re, 0.0)
                tile_im = jnp.where(lane < LANES - RTAPS // 2, tile_im, 0.0)
            rows_out[tile, pl.ds(channel, pulses, stride=2 * channels), :] = tile_re
            rows_out[tile, pl.ds(channels + channel, pulses, stride=2 * channels), :] = tile_im
    rows = filtered_ref.shape[0]
    nothing = jnp.zeros((rows, (HALO_TILES - 1) * LANES), jnp.bfloat16)
    filtered_ref[:, : (HALO_TILES - 1) * LANES] = nothing
    filtered_ref[:, (HALO_TILES + tiles) * LANES :] = nothing
    for tile in range(tiles + 1):
        spot = (HALO_TILES - 1 + tile) * LANES
        filtered_ref[:, spot : spot + LANES] = rows_out[tile].astype(jnp.bfloat16)


def chirp_piece(filtered_ref, chirp_ref, starts, out_ref):
    windows = [filtered_ref[:, pl.ds(start, CHIRP_TILE)] for start in starts]
    product = jnp.dot(
        jnp.concatenate(windows, axis=0), chirp_ref[...], preferred_element_type=jnp.float32
    )
    pulses, rows, _ = out_ref.shape
    channels = rows // 2
    product = product.reshape(len(starts), pulses, rows, 2 * LANES)
    for tile in range(len(starts)):
        block = product[tile]
        real = block[:, :channels, :LANES] - block[:, channels:, LANES:]
        imag = block[:, :channels, LANES:] + block[:, channels:, :LANES]
        out_ref[:, :, tile * LANES : (tile + 1) * LANES] = jnp.concatenate(
            [real, imag], axis=1
        ).astype(jnp.bfloat16)


def chirp_half(filtered_ref, chirp_ref, owner, piece_tiles, out_refs):
    pulse_place = lax.axis_index("pulse")
    piece_count = sum(ref.shape[0] for ref in out_refs)
    distance = piece_count - 1
    for out_ref in out_refs:
        for index in range(out_ref.shape[0]):
            piece = jnp.bitwise_xor(pulse_place, distance)
            first = owner * (piece_count * piece_tiles) + piece * piece_tiles
            starts = [pl.multiple_of((first + t) * LANES, LANES) for t in range(piece_tiles)]
            chirp_piece(filtered_ref, chirp_ref, starts, out_ref.at[index])
            distance -= 1


def send_kernel(piece_tiles, inner_ref, echo_ref, edge_ref, bands_hbm, chirp_hbm, *rest):
    *send_refs, filtered_ref, chirp_ref, rows_in, rows_out, bands_ref, arrived = rest
    _, pulses, channels, length = echo_ref.shape
    rng_place = lax.axis_index("rng")
    rx_place = lax.axis_index("rx")
    fetch = pltpu.make_async_copy(
        bands_hbm.at[pl.ds(rx_place * channels, channels)], bands_ref, arrived.at[0]
    )
    fetch.start()
    fetch_chirp = pltpu.make_async_copy(chirp_hbm, chirp_ref, arrived.at[1])
    fetch_chirp.start()
    filtered_ref[...] = inner_ref[...]
    tiles = length // LANES
    group = 2 * pulses
    lowest = rng_place == 0
    for part in range(2):
        for pulse in range(pulses):
            where = pl.ds(part * pulses + pulse, channels, stride=group)
            edge = edge_ref[part, pulse].astype(jnp.float32)
            near_low = echo_ref[part, pulse, :, :LANES].astype(jnp.float32)
            near_high = echo_ref[part, pulse, :, length - LANES :].astype(jnp.float32)
            pieces = [edge[:, t * LANES : (t + 1) * LANES] for t in range(HALO_TILES)]
            for tile in range(HALO_TILES + 1):
                high = near_high if tile == 0 else pieces[tile - 1]
                low = near_low if tile == HALO_TILES else pieces[tile]
                rows_in[tile, where, :] = jnp.where(lowest, high, low)
    fetch.wait()
    for channel in range(channels):
        rows = rows_in[:, channel * group : (channel + 1) * group, :].astype(jnp.bfloat16)
        windows = jnp.concatenate(
            [rows[:-1].reshape(-1, LANES), rows[1:].reshape(-1, LANES)], axis=1
        )
        real, imag = filter_channel(windows, bands_ref[channel], pulses)
        for tile in range(HALO_TILES):
            rows_out[tile, pl.ds(channel, pulses, stride=2 * channels), :] = real[tile]
            rows_out[tile, pl.ds(channels + channel, pulses, stride=2 * channels), :] = imag[tile]
    first = jnp.where(lowest, tiles + HALO_TILES - 1, 0)
    for tile in range(HALO_TILES):
        start = pl.multiple_of((first + tile) * LANES, LANES)
        filtered_ref[:, pl.ds(start, LANES)] = rows_out[tile].astype(jnp.bfloat16)
    fetch_chirp.wait()
    chirp_half(filtered_ref, chirp_ref, 1 - rx_place, piece_tiles, send_refs)


def keep_kernel(piece_tiles, filtered_ref, chirp_ref, keep_ref):
    chirp_half(filtered_ref, chirp_ref, lax.axis_index("rx"), piece_tiles, [keep_ref])


def turn_parts(step):
    shifted = step + 128
    angle = (jnp.bitwise_and(shifted, 255) - 128).astype(jnp.float32) * (full_turn / 1024.0)
    quarter = jnp.right_shift(shifted, 8)
    square = angle * angle
    cosine = 1.0 + square * (-1 / 2 + square * (1 / 24 + square * (-1 / 720 + square * (1 / 40320))))
    sine = angle * (1.0 + square * (-1 / 6 + square * (1 / 120 + square * (-1 / 5040))))
    odd = jnp.bitwise_and(quarter, 1) == 1
    real = jnp.where(odd, sine, cosine)
    imag = jnp.where(odd, cosine, sine)
    real = jnp.where(jnp.bitwise_and(quarter + 1, 2) == 2, -real, real)
    imag = jnp.where(jnp.bitwise_and(quarter, 2) == 2, -imag, imag)
    return real, imag


def as_column(row):
    count = row.shape[1]
    first = lax.broadcasted_iota(jnp.int32, (count, count), 0)
    second = lax.broadcasted_iota(jnp.int32, (count, count), 1)
    spread = jnp.where(first == second, row.astype(jnp.float32), 0.0)
    return jnp.sum(spread, axis=1, keepdims=True).astype(jnp.int32)


def interp_matrix(codes_ref, row):
    beams = codes_ref.shape[1]
    code = as_column(codes_ref[pl.ds(row, 1), :])
    angle_bin = lax.broadcasted_iota(jnp.int32, (beams, beams), 0)
    column = lax.broadcasted_iota(jnp.int32, (beams, beams), 1)
    half = 2 * beams
    away = jnp.bitwise_and(4 * (column - angle_bin + 1) - code + half, 4 * beams - 1) - half
    away = jnp.abs(away.astype(jnp.float32)) * 0.25
    near = (1.0 - away * away) * (2.0 - away) * 0.5
    far = (1.0 - away) * (2.0 - away) * (3.0 - away) * (1.0 / 6.0)
    matrix = jnp.where(away < 1.0, near, jnp.where(away < 2.0, far, 0.0))
    return matrix.astype(jnp.bfloat16)


def tables_kernel(sizes, angle_ref, codes_ref, first_ref, inner_ref, phase_ref):
    pulses, channels, rx_count, width = sizes
    rng_place = lax.axis_index("rng")
    rx_place = lax.axis_index("rx")
    pulse_place = lax.axis_index("pulse")
    beams = angle_ref.shape[1]
    piece_count = phase_ref.shape[0]
    piece_width = phase_ref.shape[4]
    images = pulses * piece_count
    angle = as_column(angle_ref[...])
    column = lax.broadcasted_iota(jnp.int32, (1, 4 * channels * 2), 1)
    within = jnp.bitwise_and(column, 4 * channels - 1)
    owner = jnp.bitwise_xor(rx_place, jnp.where(within >= 2 * channels, 1, 0))
    receiver = owner * channels + jnp.bitwise_and(column, channels - 1)
    is_imag = jnp.bitwise_and(within, channels) != 0
    scale = 1.0 / math.sqrt(channels * rx_count)
    steer_re, steer_im = turn_parts(jnp.bitwise_and(angle * receiver, 1023))
    steer_re = (steer_re * scale).astype(jnp.bfloat16).astype(jnp.float32)
    steer_im = (-steer_im * scale).astype(jnp.bfloat16).astype(jnp.float32)
    steer = jnp.concatenate(
        [
            jnp.where(is_imag, -steer_im, steer_re).astype(jnp.bfloat16),
            jnp.where(is_imag, steer_re, steer_im).astype(jnp.bfloat16),
        ],
        axis=1,
    )
    low_half = column >= 4 * channels
    entries = 8 * channels
    for index in range(pulses):
        matrix = interp_matrix(codes_ref, images + pulse_place * pulses + index)
        composed = jnp.dot(matrix, steer, preferred_element_type=jnp.float32)
        for part in range(2):
            value = composed[:, part * entries : (part + 1) * entries]
            high = value.astype(jnp.bfloat16)
            low = (value - high.astype(jnp.float32)).astype(jnp.bfloat16)
            first_ref[index, part * beams : (part + 1) * beams, :] = jnp.where(
                low_half, low.astype(jnp.float32), high.astype(jnp.float32)
            ).astype(jnp.bfloat16)
    factors = []
    slot = 0
    now = pulses
    while now > 1:
        factors.append(now * piece_count + pulse_place * now + 1)
        if now < pulses:
            for index in range(now):
                inner_ref[slot] = interp_matrix(
                    codes_ref, now * piece_count + pulse_place * now + index
                )
                slot += 1
        now //= 2
    lane = lax.broadcasted_iota(jnp.int32, (1, piece_width), 1)
    block = (rng_place * rx_count + rx_place) * width + 1
    for index in range(piece_count):
        piece = jnp.bitwise_xor(pulse_place, piece_count - 1 - index)
        base = jnp.bitwise_and(angle * (block + piece * piece_width + lane), 1023)
        real, imag = turn_parts(base)
        phase_ref[index, 0, 0] = real
        phase_ref[index, 0, 1] = imag
        for slot, factor in enumerate(factors):
            real, imag = turn_parts(jnp.bitwise_and(base * factor, 1023))
            phase_ref[index, slot + 1, 0] = real * half_root
            phase_ref[index, slot + 1, 1] = imag * half_root


def outer_tables_kernel(sizes, angle_ref, codes_ref, after_ref, outer_ref, phase_ref):
    rx_count, width, piece_count = sizes
    rng_place = lax.axis_index("rng")
    rx_place = lax.axis_index("rx")
    pulse_place = lax.axis_index("pulse")
    piece_width = phase_ref.shape[3]
    angle = as_column(angle_ref[...])
    lane = lax.broadcasted_iota(jnp.int32, (1, piece_width), 1)
    block = (rng_place * rx_count + rx_place) * width + 1
    base = jnp.bitwise_and(angle * (block + pulse_place * piece_width + lane), 1023)
    slot = 0
    now = piece_count
    while now > 1:
        for index in range(now):
            outer_ref[slot] = interp_matrix(codes_ref, now + index)
            real, imag = turn_parts(jnp.bitwise_and(base * (now + index + 1), 1023))
            phase_ref[slot, 0] = real * half_root
            phase_ref[slot, 1] = imag * half_root
            slot += 1
        now //= 2


def turned(real, imag, phase_re, phase_im):
    return phase_re * real - phase_im * imag, phase_im * real + phase_re * imag


ROWS = 8


def inner_kernel(index, keep_ref, other_ref, first_ref, inner_ref, phase_ref, *rest):
    out_ref, moved_ref, picture_ref, level_ref = rest[-4:]
    pulses = keep_ref.shape[1]
    beams = inner_ref.shape[1]
    columns = keep_ref.shape[3]
    other = index % other_ref.shape[0]
    for image in range(pulses):
        rows = jnp.concatenate([keep_ref[index, image], other_ref[other, image]], axis=0)
        moved_ref[image] = jnp.dot(
            first_ref[image],
            jnp.concatenate([rows, rows], axis=0),
            preferred_element_type=jnp.float32,
        )

    def merge(count, level, read, write):
        for row in range(0, beams, ROWS):
            span = slice(row, row + ROWS)
            step = (phase_ref[index, 0, 0, span], phase_ref[index, 0, 1, span])
            phase = (phase_ref[index, level, 0, span], phase_ref[index, level, 1, span])
            for image in range(count):
                term = turned(*read(image, row), *phase)
                if image & 1:
                    write(image // 2, row, left[0] + term[0], left[1] + term[1])
                left = term
                if image < count - 1:
                    phase = turned(*phase, *step)

    def write_picture(image, row, real, imag):
        picture_ref[image, row : row + ROWS, :columns] = real
        picture_ref[image, row : row + ROWS, columns:] = imag

    def write_out(image, row, real, imag):
        picture_ref[0, row : row + ROWS, :columns] = real
        picture_ref[0, row : row + ROWS, columns:] = imag

    merge(
        pulses,
        1,
        lambda image, row: (
            moved_ref[image, row : row + ROWS],
            moved_ref[image, beams + row : beams + row + ROWS],
        ),
        write_picture,
    )
    slot = 0
    level = 2
    count = pulses // 2
    while count > 1:
        for image in range(count):
            level_ref[image] = jnp.dot(
                inner_ref[slot],
                picture_ref[image].astype(jnp.bfloat16),
                preferred_element_type=jnp.float32,
            )
            slot += 1
        merge(
            count,
            level,
            lambda image, row: (
                level_ref[image, row : row + ROWS, :columns],
                level_ref[image, row : row + ROWS, columns:],
            ),
            write_picture,
        )
        count //= 2
        level += 1
    out_ref[0] = picture_ref[0, :, :columns].astype(jnp.bfloat16)
    out_ref[1] = picture_ref[0, :, columns:].astype(jnp.bfloat16)


def outer_kernel(outer_ref, phase_ref, *rest):
    image_refs, out_ref = rest[:-1], rest[-1]
    pulse_place = lax.axis_index("pulse")
    pictures = [(ref[0], ref[1]) for ref in image_refs]
    base = 0
    level = 0
    while len(pictures) > 1:
        count = len(pictures)
        place = jnp.right_shift(pulse_place, level)
        merged = []
        for distance, (real, imag) in enumerate(pictures):
            slot = base + jnp.bitwise_xor(place, distance)
            matrix = outer_ref[slot]
            moved_re = jnp.dot(
                matrix, real.astype(jnp.bfloat16), preferred_element_type=jnp.float32
            )
            moved_im = jnp.dot(
                matrix, imag.astype(jnp.bfloat16), preferred_element_type=jnp.float32
            )
            merged.append(turned(moved_re, moved_im, phase_ref[slot, 0], phase_ref[slot, 1]))
            if distance & 1:
                right, left = merged.pop(), merged.pop()
                merged.append((left[0] + right[0], left[1] + right[1]))
        pictures = merged
        base += count
        level += 1
    out_ref[0] = pictures[0][0]
    out_ref[1] = pictures[0][1]


PARAMS = dict(compiler_params=pltpu.CompilerParams(vmem_limit_bytes=40 * 1024 * 1024))


def fast(echoes, beam_angle, interp_table):
    rx_count = lax.axis_size("rx")
    pulse_count = lax.axis_size("pulse")
    _, pulses, channels, length = echoes.shape
    beams = beam_angle.shape[0]
    width = length // rx_count
    piece_width = width // pulse_count
    piece_tiles = piece_width // LANES
    rows = 2 * channels
    group = 2 * pulses
    bands = jnp.asarray(rx_bands_table(channels * rx_count))
    chirp = jnp.asarray(chirp_bands_table())
    angles = beam_angle.reshape(1, beams)
    codes = interp_table.reshape(-1, beams)
    bf16 = jnp.bfloat16
    f32 = jnp.float32
    shape = jax.ShapeDtypeStruct
    edge, echoes = pl.pallas_call(
        edge_kernel,
        out_shape=[shape(echoes.shape[:3] + (HALO,), bf16), shape(echoes.shape, bf16)],
        in_specs=[hbm()],
        out_specs=[vmem(), vmem()],
        scratch_shapes=[pltpu.SemaphoreType.DMA((2,))],
        name="edge",
        **PARAMS,
    )(echoes)
    edge = swapped(edge, "rng", 0)
    tiles = length // LANES
    filtered_shape = shape((rows * pulses, (tiles + 2 * HALO_TILES - 1) * LANES), bf16)
    bands_scratch = pltpu.VMEM((channels,) + bands.shape[1:], bf16)
    filtered = pl.pallas_call(
        interior_kernel,
        out_shape=filtered_shape,
        in_specs=[vmem(), hbm()],
        out_specs=vmem(),
        scratch_shapes=[
            pltpu.VMEM((tiles + 2, channels * group, LANES), f32),
            pltpu.VMEM((tiles + 1, rows * pulses, LANES), f32),
            bands_scratch,
            pltpu.SemaphoreType.DMA,
        ],
        name="interior",
        **PARAMS,
    )(echoes, bands)
    chunk = max(1, pulse_count // 2)
    piece_shape = (pulses, rows, piece_width)
    sent_shape = shape((chunk,) + piece_shape, bf16)
    *sent, filtered, chirp = pl.pallas_call(
        functools.partial(send_kernel, piece_tiles),
        out_shape=[sent_shape] * (pulse_count // chunk)
        + [filtered_shape, shape(chirp.shape, bf16)],
        in_specs=[vmem(), vmem(), vmem(), hbm(), hbm()],
        out_specs=[vmem()] * (pulse_count // chunk + 2),
        scratch_shapes=[
            pltpu.VMEM((HALO_TILES + 1, channels * group, LANES), f32),
            pltpu.VMEM((HALO_TILES, rows * pulses, LANES), f32),
            bands_scratch,
            pltpu.SemaphoreType.DMA((2,)),
        ],
        name="send",
        **PARAMS,
    )(filtered, echoes, edge, bands, chirp)
    received = [swapped(piece, "rx", 0) for piece in sent]
    kept = pl.pallas_call(
        functools.partial(keep_kernel, piece_tiles),
        out_shape=shape((pulse_count,) + piece_shape, bf16),
        in_specs=[vmem()] * 2,
        out_specs=vmem(),
        name="keep",
        **PARAMS,
    )(filtered, chirp)
    levels = pulses.bit_length() - 1
    first, inner, phase = pl.pallas_call(
        functools.partial(tables_kernel, (pulses, channels, rx_count, width)),
        out_shape=[
            shape((pulses, 2 * beams, 8 * channels), bf16),
            shape((pulses - 2, beams, beams), bf16),
            shape((pulse_count, levels + 1, 2, beams, piece_width), f32),
        ],
        in_specs=[vmem()] * 2,
        out_specs=[vmem()] * 3,
        name="tables",
        **PARAMS,
    )(angles, codes)
    images = []
    after = []
    for index in range(pulse_count):
        distance = pulse_count - 1 - index
        image = pl.pallas_call(
            functools.partial(inner_kernel, index),
            out_shape=shape((2, beams, piece_width), bf16),
            in_specs=[vmem()] * 5 + [anywhere()] * len(after),
            out_specs=vmem(),
            scratch_shapes=[
                pltpu.VMEM((pulses, 2 * beams, piece_width), f32),
                pltpu.VMEM((pulses // 2, beams, 2 * piece_width), f32),
                pltpu.VMEM((pulses // 2, beams, 2 * piece_width), f32),
            ],
            name="inner",
            **PARAMS,
        )(kept, received[index // chunk], first, inner, phase, *after)
        after = [image]
        if distance:
            image = lax.ppermute(image, "pulse", [(i, i ^ distance) for i in range(pulse_count)])
        images.insert(0, image)
    outer_count = 2 * pulse_count - 2
    outer, outer_phase = pl.pallas_call(
        functools.partial(outer_tables_kernel, (rx_count, width, pulse_count)),
        out_shape=[
            shape((outer_count, beams, beams), bf16),
            shape((outer_count, 2, beams, piece_width), f32),
        ],
        in_specs=[vmem(), vmem(), anywhere()],
        out_specs=[vmem()] * 2,
        name="outer_tables",
        **PARAMS,
    )(angles, codes, *after)
    return pl.pallas_call(
        outer_kernel,
        out_shape=shape((2, beams, piece_width), f32),
        in_specs=[vmem()] * (2 + pulse_count),
        out_specs=vmem(),
        name="outer",
        **PARAMS,
    )(outer, outer_phase, *images)


def power_of_two(count):
    return count > 0 and count & (count - 1) == 0


def per_device(echoes, beam_angle, interp_table):
    _, pulses, channels, length = echoes.shape
    rx_count = lax.axis_size("rx")
    pulse_count = lax.axis_size("pulse")
    piece_width = length // (rx_count * pulse_count)
    if (
        lax.axis_size("rng") == 2
        and rx_count == 2
        and channels == 8
        and pulses == 8
        and power_of_two(pulse_count)
        and pulse_count > 1
        and power_of_two(beam_angle.shape[0])
        and beam_angle.shape[0] % 16 == 0
        and piece_width % LANES == 0
    ):
        return fast(echoes, beam_angle, interp_table)
    return local(echoes, beam_angle, interp_table)


def solution(mesh):
    placed = (P(None, ("slab", "pulse"), "rx", "rng"), P(), P())
    return jax.shard_map(
        per_device,
        mesh=mesh,
        in_specs=placed,
        out_specs=P(None, "slab", ("rng", "rx", "pulse")),
        check_vma=False,
    )
```

```python
import functools
import math

import jax
import jax.numpy as jnp
import ml_dtypes
import numpy as np
from jax import lax
from jax.experimental import pallas as pl
from jax.experimental.pallas import tpu as pltpu
from jax.sharding import PartitionSpec as P

RTAPS = 64
CTAPS = 512


half_root = 0.7071067811865476
full_turn = 2.0 * math.pi


def extended_2(block, sides, width):
    for axis, dim in sides:
        count = lax.axis_size(axis)
        forward = [(i, i + 1) for i in range(count - 1)]
        backward = [(target, source) for source, target in forward]
        low = lax.ppermute(
            lax.slice_in_dim(block, block.shape[dim] - width, None, axis=dim), axis, forward
        )
        high = lax.ppermute(lax.slice_in_dim(block, 0, width, axis=dim), axis, backward)
        block = jnp.concatenate([low, block, high], axis=dim)
    return block


def swapped(x, axis, distance):
    return lax.ppermute(x, axis, [(i, i ^ 1 << distance) for i in range(lax.axis_size(axis))])


def receiver_taps(channel_ids, tap_count):
    tap_index = jnp.arange(tap_count, dtype=jnp.float32)
    window = 0.5 - 0.5 * jnp.cos(full_turn * (tap_index + 0.5) / tap_count)
    window = window / jnp.sqrt(jnp.sum(window * window))
    channel = channel_ids.astype(jnp.float32)[:, None] + 1.0
    angle = full_turn * channel * (tap_index - tap_count // 2) / (4 * tap_count)
    return (
        (window * jnp.cos(angle)).astype(jnp.bfloat16),
        (window * jnp.sin(angle)).astype(jnp.bfloat16),
    )


def chirp_taps(tap_count):
    offset = jnp.arange(tap_count, dtype=jnp.int32) - tap_count // 2
    phase_step = jnp.mod(offset * offset, 2 * tap_count).astype(jnp.float32)
    angle = math.pi * phase_step / tap_count
    scale = 1.0 / math.sqrt(tap_count)
    return (
        (jnp.cos(angle) * scale).astype(jnp.bfloat16),
        (-jnp.sin(angle) * scale).astype(jnp.bfloat16),
    )


def steering(beam_angle, receivers):
    channel = jnp.arange(receivers, dtype=jnp.int32)
    turns = jnp.mod(beam_angle[:, None] * channel[None, :], 1024).astype(jnp.float32)
    angle = full_turn * turns / 1024.0
    scale = 1.0 / math.sqrt(receivers)
    return (
        (jnp.cos(angle) * scale).astype(jnp.bfloat16),
        (-jnp.sin(angle) * scale).astype(jnp.bfloat16),
    )


def interp_matrices(codes, beam_count):
    shifted = codes // 4 - 1
    fraction = jnp.mod(codes, 4).astype(jnp.float32) / 4.0
    weights = (
        -fraction * (fraction - 1.0) * (fraction - 2.0) / 6.0,
        (fraction + 1.0) * (fraction - 1.0) * (fraction - 2.0) / 2.0,
        -(fraction + 1.0) * fraction * (fraction - 2.0) / 2.0,
        (fraction + 1.0) * fraction * (fraction - 1.0) / 6.0,
    )
    columns = jnp.arange(beam_count, dtype=jnp.int32)
    matrices = jnp.zeros(codes.shape + (beam_count,), jnp.float32)
    for tap_index in range(4):
        target = jnp.mod(columns + shifted + tap_index - 1, beam_count)
        matrices = matrices + weights[tap_index][..., None] * (target[..., None] == columns).astype(
            jnp.float32
        )
    return matrices


def phases(node_ids, positions, beam_angle, side):
    base = jnp.mod(beam_angle[:, None] * (positions[None, :] + 1), 1024)
    factor = 2 * node_ids + side + 1
    turns = jnp.mod(base[:, None, :] * factor[None, :, None], 1024).astype(jnp.float32)
    angle = full_turn * turns / 1024.0
    return (jnp.cos(angle), jnp.sin(angle))


def side_term(picture, matrices, cosine, sine):
    moved = jnp.einsum("gqa,cagr->cqgr", matrices, picture, precision=lax.Precision.HIGHEST)
    return (cosine * moved[0] - sine * moved[1], sine * moved[0] + cosine * moved[1])


def merge_pair(left_image, right_image, node_ids, positions, beam_angle, interp_table):
    matrices = interp_matrices(interp_table[node_ids], left_image.shape[1])
    left_cos, left_sin = phases(node_ids, positions, beam_angle, 0)
    right_cos, right_sin = phases(node_ids, positions, beam_angle, 1)
    left_re, left_im = side_term(left_image, matrices[:, 0], left_cos, left_sin)
    right_re, right_im = side_term(right_image, matrices[:, 1], right_cos, right_sin)
    return jnp.stack([(left_re + right_re) * half_root, (left_im + right_im) * half_root])


def toeplitz_blocks(taps_re, taps_im):
    tap_count = taps_re.shape[-1]
    leading = taps_re.shape[:-1]

    def lay_out(taps):
        padded = jnp.concatenate([taps, jnp.zeros(leading + (tap_count + 1,), taps.dtype)], axis=-1)
        tiled = jnp.tile(padded, (1,) * len(leading) + (tap_count,))
        banded = tiled[..., : 2 * tap_count * tap_count].reshape(
            leading + (tap_count, 2 * tap_count)
        )
        return jnp.swapaxes(banded, -1, -2)

    real_band = lay_out(taps_re)
    imag_band = lay_out(taps_im)
    upper = jnp.concatenate([real_band, imag_band], axis=-1)
    lower = jnp.concatenate([-imag_band, real_band], axis=-1)
    return jnp.concatenate([upper, lower], axis=-2)


def block_filter(extended, matrices, tap_count, per_channel):
    pulses, channels, length = extended.shape[1:]
    blocks = length // tap_count - 1
    pieces = extended.reshape(2, pulses, channels, blocks + 1, tap_count)
    windows = jnp.concatenate([pieces[:, :, :, :-1], pieces[:, :, :, 1:]], axis=4)
    windows = jnp.transpose(windows, (1, 2, 3, 0, 4)).reshape(
        pulses, channels, blocks, 4 * tap_count
    )
    if per_channel:
        output = jnp.einsum("pcnw,cwo->pcno", windows, matrices, preferred_element_type=jnp.float32)
    else:
        output = jnp.einsum("pcnw,wo->pcno", windows, matrices, preferred_element_type=jnp.float32)
    output = output.reshape(pulses, channels, blocks, 2, tap_count)
    return jnp.transpose(output, (3, 0, 1, 2, 4)).reshape(2, pulses, channels, blocks * tap_count)


def local(echoes, beam_angle, interp_table):
    rx_count = lax.axis_size("rx")
    pulse_count = lax.axis_size("pulse")
    rng_place = lax.axis_index("rng")
    rx_place = lax.axis_index("rx")
    pulse_place = lax.axis_index("pulse")
    pulses, channels, length = echoes.shape[1:]
    beam_count = beam_angle.shape[0]
    receivers = channels * rx_count
    channel_ids = rx_place * channels + jnp.arange(channels, dtype=jnp.int32)
    rx_re, rx_im = receiver_taps(channel_ids, RTAPS)
    rx_bands = toeplitz_blocks(rx_re, rx_im)
    chirp_re, chirp_im = chirp_taps(CTAPS)
    chirp_band = toeplitz_blocks(chirp_re, chirp_im)
    extended = extended_2(echoes, (("rng", 3),), RTAPS // 2)
    filtered = block_filter(extended, rx_bands, RTAPS, True).astype(jnp.bfloat16)
    filtered = extended_2(filtered, (("rng", 3),), CTAPS // 2)
    compressed = block_filter(filtered, chirp_band, CTAPS, False).astype(jnp.bfloat16)
    steering_real, steering_imaginary = steering(beam_angle, receivers)
    steer_matrix = jnp.concatenate(
        [
            jnp.concatenate([steering_real, -steering_imaginary], axis=1),
            jnp.concatenate([steering_imaginary, steering_real], axis=1),
        ],
        axis=0,
    )
    arrived = lax.all_to_all(compressed, "rx", split_axis=3, concat_axis=2, tiled=True)
    item_count, recv_count, owned_cols = arrived.shape[1:]
    stacked = jnp.transpose(arrived, (0, 2, 1, 3)).reshape(2 * recv_count, item_count * owned_cols)
    formed = jnp.dot(steer_matrix, stacked, preferred_element_type=jnp.float32)
    picture = formed.reshape(2, beam_count, item_count, owned_cols)
    owned_width = length // rx_count
    positions = (
        rng_place * length + rx_place * owned_width + jnp.arange(owned_width, dtype=jnp.int32)
    )
    for level in range(pulses.bit_length() - 1):
        groups_now = pulses >> level + 1
        node_ids = (pulse_count + pulse_place) * groups_now + jnp.arange(
            groups_now, dtype=jnp.int32
        )
        paired = picture.reshape(2, beam_count, groups_now, 2, owned_width)
        picture = merge_pair(
            paired[:, :, :, 0], paired[:, :, :, 1], node_ids, positions, beam_angle, interp_table
        )
    picture = picture[:, :, 0]
    cross_levels = pulse_count.bit_length() - 1
    piece_width = owned_width // pulse_count
    pieces = picture.reshape(2, beam_count, pulse_count, piece_width)
    spots = positions.reshape(pulse_count, piece_width)
    for level in range(cross_levels):
        parity = jnp.right_shift(pulse_place, level) & 1
        count_now = pieces.shape[2]
        paired = pieces.reshape(2, beam_count, count_now // 2, 2, piece_width)
        kept_half = lax.dynamic_index_in_dim(paired, parity, 3, keepdims=False)
        sent_half = lax.dynamic_index_in_dim(paired, 1 - parity, 3, keepdims=False)
        partner = swapped(sent_half, "pulse", level)
        spot_pairs = spots.reshape(count_now // 2, 2, piece_width)
        spots = lax.dynamic_index_in_dim(spot_pairs, parity, 1, keepdims=False)
        own_part = kept_half.reshape(2, beam_count, -1)
        other_part = partner.reshape(2, beam_count, -1)
        left_image = jnp.where(parity == 0, own_part, other_part)
        right_image = jnp.where(parity == 0, other_part, own_part)
        combine_node_ids = jnp.reshape(
            (pulse_count >> level + 1) + jnp.right_shift(pulse_place, level + 1), (1,)
        )
        merged = merge_pair(
            left_image[:, :, None],
            right_image[:, :, None],
            combine_node_ids,
            spots.reshape(-1),
            beam_angle,
            interp_table,
        )
        flat = merged[:, :, 0]
        pieces = flat.reshape(2, beam_count, count_now // 2, piece_width)
    picture = pieces.reshape(2, beam_count, piece_width)
    return picture


LANES = 128
RX_TILE = 2 * LANES
CHIRP_TILE = 6 * LANES
HALO_TILES = 3
HALO = HALO_TILES * LANES


def vmem():
    return pl.BlockSpec(memory_space=pltpu.VMEM)


def hbm():
    return pl.BlockSpec(memory_space=pltpu.HBM)


def anywhere():
    return pl.BlockSpec(memory_space=pl.ANY)


def rx_bands_table(receivers):
    step = np.arange(RTAPS, dtype=np.float64)
    window = 0.5 - 0.5 * np.cos(full_turn * (step + 0.5) / RTAPS)
    window = window / np.sqrt(np.sum(window * window))
    channel = np.arange(receivers, dtype=np.float64)[:, None] + 1.0
    angle = full_turn * channel * (step - RTAPS // 2) / (4 * RTAPS)
    offset = np.arange(RX_TILE)[:, None] - np.arange(LANES)[None, :]
    inside = (offset >= 0) & (offset < RTAPS)
    place = np.clip(offset, 0, RTAPS - 1)
    bands = [
        np.where(inside, taps[:, place], 0.0)
        for taps in (window * np.cos(angle), window * np.sin(angle))
    ]
    return np.concatenate(bands, axis=-1).astype(ml_dtypes.bfloat16)


def chirp_bands_table():
    offset = np.arange(CTAPS) - CTAPS // 2
    angle = math.pi * np.mod(offset * offset, 2 * CTAPS) / CTAPS
    scale = 1.0 / math.sqrt(CTAPS)
    offset = np.arange(CHIRP_TILE)[:, None] - np.arange(LANES)[None, :] - (LANES - RTAPS // 2)
    inside = (offset >= 0) & (offset < CTAPS)
    place = np.clip(offset, 0, CTAPS - 1)
    bands = [
        np.where(inside, taps[place], 0.0)
        for taps in (np.cos(angle) * scale, -np.sin(angle) * scale)
    ]
    return np.concatenate(bands, axis=-1).astype(ml_dtypes.bfloat16)


def edge_kernel(echo_hbm, edge_ref, echo_ref, arrived):
    length = echo_hbm.shape[3]
    start = jnp.where(lax.axis_index("rng") == 0, length - HALO, 0)
    start = pl.multiple_of(start, LANES)
    edge = pltpu.make_async_copy(
        echo_hbm.at[:, :, :, pl.ds(start, HALO)], edge_ref, arrived.at[0]
    )
    edge.start()
    whole = pltpu.make_async_copy(echo_hbm, echo_ref, arrived.at[1])
    whole.start()
    edge.wait()
    whole.wait()


def filter_channel(windows, bands, pulses):
    product = jnp.dot(windows, bands, preferred_element_type=jnp.float32)
    product = product.reshape(-1, 2, pulses, 2 * LANES)
    real = product[:, 0, :, :LANES] - product[:, 1, :, LANES:]
    imag = product[:, 0, :, LANES:] + product[:, 1, :, :LANES]
    return real, imag


def interior_kernel(echo_ref, bands_hbm, filtered_ref, rows_in, rows_out, bands_ref, arrived):
    _, pulses, channels, length = echo_ref.shape
    rx_place = lax.axis_index("rx")
    fetch = pltpu.make_async_copy(
        bands_hbm.at[pl.ds(rx_place * channels, channels)], bands_ref, arrived
    )
    fetch.start()
    tiles = length // LANES
    group = 2 * pulses
    empty = jnp.zeros(rows_in.shape[1:], jnp.float32)
    rows_in[0] = empty
    rows_in[tiles + 1] = empty
    for part in range(2):
        for pulse in range(pulses):
            where = pl.ds(part * pulses + pulse, channels, stride=group)
            block = echo_ref[part, pulse].astype(jnp.float32)
            for tile in range(tiles):
                rows_in[tile + 1, where, :] = block[:, tile * LANES : (tile + 1) * LANES]
    fetch.wait()
    lane = lax.broadcasted_iota(jnp.int32, (1, LANES), 1)
    for channel in range(channels):
        rows = rows_in[:, channel * group : (channel + 1) * group, :].astype(jnp.bfloat16)
        windows = jnp.concatenate(
            [rows[:-1].reshape(-1, LANES), rows[1:].reshape(-1, LANES)], axis=1
        )
        real, imag = filter_channel(windows, bands_ref[channel], pulses)
        for tile in range(tiles + 1):
            tile_re, tile_im = real[tile], imag[tile]
            if tile == 0:
                tile_re = jnp.where(lane >= LANES - RTAPS // 2, tile_re, 0.0)
                tile_im = jnp.where(lane >= LANES - RTAPS // 2, tile_im, 0.0)
            if tile == tiles:
                tile_re = jnp.where(lane < LANES - RTAPS // 2, tile_re, 0.0)
                tile_im = jnp.where(lane < LANES - RTAPS // 2, tile_im, 0.0)
            rows_out[tile, pl.ds(channel, pulses, stride=2 * channels), :] = tile_re
            rows_out[tile, pl.ds(channels + channel, pulses, stride=2 * channels), :] = tile_im
    rows = filtered_ref.shape[0]
    nothing = jnp.zeros((rows, (HALO_TILES - 1) * LANES), jnp.bfloat16)
    filtered_ref[:, : (HALO_TILES - 1) * LANES] = nothing
    filtered_ref[:, (HALO_TILES + tiles) * LANES :] = nothing
    for tile in range(tiles + 1):
        spot = (HALO_TILES - 1 + tile) * LANES
        filtered_ref[:, spot : spot + LANES] = rows_out[tile].astype(jnp.bfloat16)


def chirp_piece(filtered_ref, chirp_ref, starts, out_ref):
    windows = [filtered_ref[:, pl.ds(start, CHIRP_TILE)] for start in starts]
    product = jnp.dot(
        jnp.concatenate(windows, axis=0), chirp_ref[...], preferred_element_type=jnp.float32
    )
    pulses, rows, _ = out_ref.shape
    channels = rows // 2
    product = product.reshape(len(starts), pulses, rows, 2 * LANES)
    for tile in range(len(starts)):
        block = product[tile]
        real = block[:, :channels, :LANES] - block[:, channels:, LANES:]
        imag = block[:, :channels, LANES:] + block[:, channels:, :LANES]
        out_ref[:, :, tile * LANES : (tile + 1) * LANES] = jnp.concatenate(
            [real, imag], axis=1
        ).astype(jnp.bfloat16)


def chirp_half(filtered_ref, chirp_ref, owner, piece_tiles, out_refs):
    pulse_place = lax.axis_index("pulse")
    piece_count = sum(ref.shape[0] for ref in out_refs)
    distance = piece_count - 1
    for out_ref in out_refs:
        for index in range(out_ref.shape[0]):
            piece = jnp.bitwise_xor(pulse_place, distance)
            first = owner * (piece_count * piece_tiles) + piece * piece_tiles
            starts = [pl.multiple_of((first + t) * LANES, LANES) for t in range(piece_tiles)]
            chirp_piece(filtered_ref, chirp_ref, starts, out_ref.at[index])
            distance -= 1


def send_kernel(piece_tiles, inner_ref, echo_ref, edge_ref, bands_hbm, chirp_hbm, *rest):
    *send_refs, filtered_ref, chirp_ref, rows_in, rows_out, bands_ref, arrived = rest
    _, pulses, channels, length = echo_ref.shape
    rng_place = lax.axis_index("rng")
    rx_place = lax.axis_index("rx")
    fetch = pltpu.make_async_copy(
        bands_hbm.at[pl.ds(rx_place * channels, channels)], bands_ref, arrived.at[0]
    )
    fetch.start()
    fetch_chirp = pltpu.make_async_copy(chirp_hbm, chirp_ref, arrived.at[1])
    fetch_chirp.start()
    filtered_ref[...] = inner_ref[...]
    tiles = length // LANES
    group = 2 * pulses
    lowest = rng_place == 0
    for part in range(2):
        for pulse in range(pulses):
            where = pl.ds(part * pulses + pulse, channels, stride=group)
            edge = edge_ref[part, pulse].astype(jnp.float32)
            near_low = echo_ref[part, pulse, :, :LANES].astype(jnp.float32)
            near_high = echo_ref[part, pulse, :, length - LANES :].astype(jnp.float32)
            pieces = [edge[:, t * LANES : (t + 1) * LANES] for t in range(HALO_TILES)]
            for tile in range(HALO_TILES + 1):
                high = near_high if tile == 0 else pieces[tile - 1]
                low = near_low if tile == HALO_TILES else pieces[tile]
                rows_in[tile, where, :] = jnp.where(lowest, high, low)
    fetch.wait()
    for channel in range(channels):
        rows = rows_in[:, channel * group : (channel + 1) * group, :].astype(jnp.bfloat16)
        windows = jnp.concatenate(
            [rows[:-1].reshape(-1, LANES), rows[1:].reshape(-1, LANES)], axis=1
        )
        real, imag = filter_channel(windows, bands_ref[channel], pulses)
        for tile in range(HALO_TILES):
            rows_out[tile, pl.ds(channel, pulses, stride=2 * channels), :] = real[tile]
            rows_out[tile, pl.ds(channels + channel, pulses, stride=2 * channels), :] = imag[tile]
    first = jnp.where(lowest, tiles + HALO_TILES - 1, 0)
    for tile in range(HALO_TILES):
        start = pl.multiple_of((first + tile) * LANES, LANES)
        filtered_ref[:, pl.ds(start, LANES)] = rows_out[tile].astype(jnp.bfloat16)
    fetch_chirp.wait()
    chirp_half(filtered_ref, chirp_ref, 1 - rx_place, piece_tiles, send_refs)


def keep_kernel(piece_tiles, filtered_ref, chirp_ref, keep_ref):
    chirp_half(filtered_ref, chirp_ref, lax.axis_index("rx"), piece_tiles, [keep_ref])


def turn_parts(step):
    shifted = step + 128
    angle = (jnp.bitwise_and(shifted, 255) - 128).astype(jnp.float32) * (full_turn / 1024.0)
    quarter = jnp.right_shift(shifted, 8)
    square = angle * angle
    cosine = 1.0 + square * (-1 / 2 + square * (1 / 24 + square * (-1 / 720 + square * (1 / 40320))))
    sine = angle * (1.0 + square * (-1 / 6 + square * (1 / 120 + square * (-1 / 5040))))
    odd = jnp.bitwise_and(quarter, 1) == 1
    real = jnp.where(odd, sine, cosine)
    imag = jnp.where(odd, cosine, sine)
    real = jnp.where(jnp.bitwise_and(quarter + 1, 2) == 2, -real, real)
    imag = jnp.where(jnp.bitwise_and(quarter, 2) == 2, -imag, imag)
    return real, imag


def as_column(row):
    count = row.shape[1]
    first = lax.broadcasted_iota(jnp.int32, (count, count), 0)
    second = lax.broadcasted_iota(jnp.int32, (count, count), 1)
    spread = jnp.where(first == second, row.astype(jnp.float32), 0.0)
    return jnp.sum(spread, axis=1, keepdims=True).astype(jnp.int32)


def interp_matrix(codes_ref, row):
    beams = codes_ref.shape[1]
    code = as_column(codes_ref[pl.ds(row, 1), :])
    angle_bin = lax.broadcasted_iota(jnp.int32, (beams, beams), 0)
    column = lax.broadcasted_iota(jnp.int32, (beams, beams), 1)
    half = 2 * beams
    away = jnp.bitwise_and(4 * (column - angle_bin + 1) - code + half, 4 * beams - 1) - half
    away = jnp.abs(away.astype(jnp.float32)) * 0.25
    near = (1.0 - away * away) * (2.0 - away) * 0.5
    far = (1.0 - away) * (2.0 - away) * (3.0 - away) * (1.0 / 6.0)
    matrix = jnp.where(away < 1.0, near, jnp.where(away < 2.0, far, 0.0))
    return matrix.astype(jnp.bfloat16)


def tables_kernel(sizes, angle_ref, codes_ref, first_ref, inner_ref, phase_ref):
    pulses, channels, rx_count, width = sizes
    rng_place = lax.axis_index("rng")
    rx_place = lax.axis_index("rx")
    pulse_place = lax.axis_index("pulse")
    beams = angle_ref.shape[1]
    piece_count = phase_ref.shape[0]
    piece_width = phase_ref.shape[4]
    images = pulses * piece_count
    angle = as_column(angle_ref[...])
    column = lax.broadcasted_iota(jnp.int32, (1, 4 * channels * 2), 1)
    within = jnp.bitwise_and(column, 4 * channels - 1)
    owner = jnp.bitwise_xor(rx_place, jnp.where(within >= 2 * channels, 1, 0))
    receiver = owner * channels + jnp.bitwise_and(column, channels - 1)
    is_imag = jnp.bitwise_and(within, channels) != 0
    scale = 1.0 / math.sqrt(channels * rx_count)
    steer_re, steer_im = turn_parts(jnp.bitwise_and(angle * receiver, 1023))
    steer_re = (steer_re * scale).astype(jnp.bfloat16).astype(jnp.float32)
    steer_im = (-steer_im * scale).astype(jnp.bfloat16).astype(jnp.float32)
    steer = jnp.concatenate(
        [
            jnp.where(is_imag, -steer_im, steer_re).astype(jnp.bfloat16),
            jnp.where(is_imag, steer_re, steer_im).astype(jnp.bfloat16),
        ],
        axis=1,
    )
    low_half = column >= 4 * channels
    entries = 8 * channels
    for index in range(pulses):
        matrix = interp_matrix(codes_ref, images + pulse_place * pulses + index)
        composed = jnp.dot(matrix, steer, preferred_element_type=jnp.float32)
        for part in range(2):
            value = composed[:, part * entries : (part + 1) * entries]
            high = value.astype(jnp.bfloat16)
            low = (value - high.astype(jnp.float32)).astype(jnp.bfloat16)
            first_ref[index, part * beams : (part + 1) * beams, :] = jnp.where(
                low_half, low.astype(jnp.float32), high.astype(jnp.float32)
            ).astype(jnp.bfloat16)
    factors = []
    slot = 0
    now = pulses
    while now > 1:
        factors.append(now * piece_count + pulse_place * now + 1)
        if now < pulses:
            for index in range(now):
                inner_ref[slot] = interp_matrix(
                    codes_ref, now * piece_count + pulse_place * now + index
                )
                slot += 1
        now //= 2
    lane = lax.broadcasted_iota(jnp.int32, (1, piece_width), 1)
    block = (rng_place * rx_count + rx_place) * width + 1
    for index in range(piece_count):
        piece = jnp.bitwise_xor(pulse_place, piece_count - 1 - index)
        base = jnp.bitwise_and(angle * (block + piece * piece_width + lane), 1023)
        real, imag = turn_parts(base)
        phase_ref[index, 0, 0] = real
        phase_ref[index, 0, 1] = imag
        for slot, factor in enumerate(factors):
            real, imag = turn_parts(jnp.bitwise_and(base * factor, 1023))
            phase_ref[index, slot + 1, 0] = real * half_root
            phase_ref[index, slot + 1, 1] = imag * half_root


def outer_tables_kernel(sizes, angle_ref, codes_ref, after_ref, outer_ref, phase_ref):
    rx_count, width, piece_count = sizes
    rng_place = lax.axis_index("rng")
    rx_place = lax.axis_index("rx")
    pulse_place = lax.axis_index("pulse")
    piece_width = phase_ref.shape[3]
    angle = as_column(angle_ref[...])
    lane = lax.broadcasted_iota(jnp.int32, (1, piece_width), 1)
    block = (rng_place * rx_count + rx_place) * width + 1
    base = jnp.bitwise_and(angle * (block + pulse_place * piece_width + lane), 1023)
    slot = 0
    now = piece_count
    while now > 1:
        for index in range(now):
            outer_ref[slot] = interp_matrix(codes_ref, now + index)
            real, imag = turn_parts(jnp.bitwise_and(base * (now + index + 1), 1023))
            phase_ref[slot, 0] = real * half_root
            phase_ref[slot, 1] = imag * half_root
            slot += 1
        now //= 2


def turned(real, imag, phase_re, phase_im):
    return phase_re * real - phase_im * imag, phase_im * real + phase_re * imag


ROWS = 8


def inner_kernel(index, keep_ref, other_ref, first_ref, inner_ref, phase_ref, *rest):
    out_ref, moved_ref, picture_ref, level_ref = rest[-4:]
    pulses = keep_ref.shape[1]
    beams = inner_ref.shape[1]
    columns = keep_ref.shape[3]
    other = index % other_ref.shape[0]
    for image in range(pulses):
        rows = jnp.concatenate([keep_ref[index, image], other_ref[other, image]], axis=0)
        moved_ref[image] = jnp.dot(
            first_ref[image],
            jnp.concatenate([rows, rows], axis=0),
            preferred_element_type=jnp.float32,
        )

    def merge(count, level, read, write):
        for row in range(0, beams, ROWS):
            span = slice(row, row + ROWS)
            step = (phase_ref[index, 0, 0, span], phase_ref[index, 0, 1, span])
            phase = (phase_ref[index, level, 0, span], phase_ref[index, level, 1, span])
            for image in range(count):
                term = turned(*read(image, row), *phase)
                if image & 1:
                    write(image // 2, row, left[0] + term[0], left[1] + term[1])
                left = term
                if image < count - 1:
                    phase = turned(*phase, *step)

    def write_picture(image, row, real, imag):
        picture_ref[image, row : row + ROWS, :columns] = real
        picture_ref[image, row : row + ROWS, columns:] = imag

    def write_out(image, row, real, imag):
        picture_ref[0, row : row + ROWS, :columns] = real
        picture_ref[0, row : row + ROWS, columns:] = imag

    merge(
        pulses,
        1,
        lambda image, row: (
            moved_ref[image, row : row + ROWS],
            moved_ref[image, beams + row : beams + row + ROWS],
        ),
        write_picture,
    )
    slot = 0
    level = 2
    count = pulses // 2
    while count > 1:
        for image in range(count):
            level_ref[image] = jnp.dot(
                inner_ref[slot],
                picture_ref[image].astype(jnp.bfloat16),
                preferred_element_type=jnp.float32,
            )
            slot += 1
        merge(
            count,
            level,
            lambda image, row: (
                level_ref[image, row : row + ROWS, :columns],
                level_ref[image, row : row + ROWS, columns:],
            ),
            write_picture,
        )
        count //= 2
        level += 1
    out_ref[0] = picture_ref[0, :, :columns].astype(jnp.bfloat16)
    out_ref[1] = picture_ref[0, :, columns:].astype(jnp.bfloat16)


def outer_kernel(outer_ref, phase_ref, *rest):
    image_refs, out_ref = rest[:-1], rest[-1]
    pulse_place = lax.axis_index("pulse")
    pictures = [(ref[0], ref[1]) for ref in image_refs]
    base = 0
    level = 0
    while len(pictures) > 1:
        count = len(pictures)
        place = jnp.right_shift(pulse_place, level)
        merged = []
        for distance, (real, imag) in enumerate(pictures):
            slot = base + jnp.bitwise_xor(place, distance)
            matrix = outer_ref[slot]
            moved_re = jnp.dot(
                matrix, real.astype(jnp.bfloat16), preferred_element_type=jnp.float32
            )
            moved_im = jnp.dot(
                matrix, imag.astype(jnp.bfloat16), preferred_element_type=jnp.float32
            )
            merged.append(turned(moved_re, moved_im, phase_ref[slot, 0], phase_ref[slot, 1]))
            if distance & 1:
                right, left = merged.pop(), merged.pop()
                merged.append((left[0] + right[0], left[1] + right[1]))
        pictures = merged
        base += count
        level += 1
    out_ref[0] = pictures[0][0]
    out_ref[1] = pictures[0][1]


PARAMS = dict(compiler_params=pltpu.CompilerParams(vmem_limit_bytes=40 * 1024 * 1024))


def fast(echoes, beam_angle, interp_table):
    rx_count = lax.axis_size("rx")
    pulse_count = lax.axis_size("pulse")
    _, pulses, channels, length = echoes.shape
    beams = beam_angle.shape[0]
    width = length // rx_count
    piece_width = width // pulse_count
    piece_tiles = piece_width // LANES
    rows = 2 * channels
    group = 2 * pulses
    bands = jnp.asarray(rx_bands_table(channels * rx_count))
    chirp = jnp.asarray(chirp_bands_table())
    angles = beam_angle.reshape(1, beams)
    codes = interp_table.reshape(-1, beams)
    bf16 = jnp.bfloat16
    f32 = jnp.float32
    shape = jax.ShapeDtypeStruct
    edge, echoes = pl.pallas_call(
        edge_kernel,
        out_shape=[shape(echoes.shape[:3] + (HALO,), bf16), shape(echoes.shape, bf16)],
        in_specs=[hbm()],
        out_specs=[vmem(), vmem()],
        scratch_shapes=[pltpu.SemaphoreType.DMA((2,))],
        name="edge",
        cost_estimate=pl.CostEstimate(flops=10**10, bytes_accessed=10**8, transcendentals=0),
        **PARAMS,
    )(echoes)
    edge = swapped(edge, "rng", 0)
    tiles = length // LANES
    filtered_shape = shape((rows * pulses, (tiles + 2 * HALO_TILES - 1) * LANES), bf16)
    bands_scratch = pltpu.VMEM((channels,) + bands.shape[1:], bf16)
    filtered = pl.pallas_call(
        interior_kernel,
        out_shape=filtered_shape,
        in_specs=[vmem(), hbm()],
        out_specs=vmem(),
        scratch_shapes=[
            pltpu.VMEM((tiles + 2, channels * group, LANES), f32),
            pltpu.VMEM((tiles + 1, rows * pulses, LANES), f32),
            bands_scratch,
            pltpu.SemaphoreType.DMA,
        ],
        name="interior",
        **PARAMS,
    )(echoes, bands)
    chunk = max(1, pulse_count // 2)
    piece_shape = (pulses, rows, piece_width)
    sent_shape = shape((chunk,) + piece_shape, bf16)
    *sent, filtered, chirp = pl.pallas_call(
        functools.partial(send_kernel, piece_tiles),
        out_shape=[sent_shape] * (pulse_count // chunk)
        + [filtered_shape, shape(chirp.shape, bf16)],
        in_specs=[vmem(), vmem(), vmem(), hbm(), hbm()],
        out_specs=[vmem()] * (pulse_count // chunk + 2),
        scratch_shapes=[
            pltpu.VMEM((HALO_TILES + 1, channels * group, LANES), f32),
            pltpu.VMEM((HALO_TILES, rows * pulses, LANES), f32),
            bands_scratch,
            pltpu.SemaphoreType.DMA((2,)),
        ],
        name="send",
        **PARAMS,
    )(filtered, echoes, edge, bands, chirp)
    received = [swapped(piece, "rx", 0) for piece in sent]
    kept = pl.pallas_call(
        functools.partial(keep_kernel, piece_tiles),
        out_shape=shape((pulse_count,) + piece_shape, bf16),
        in_specs=[vmem()] * 2,
        out_specs=vmem(),
        name="keep",
        **PARAMS,
    )(filtered, chirp)
    levels = pulses.bit_length() - 1
    first, inner, phase = pl.pallas_call(
        functools.partial(tables_kernel, (pulses, channels, rx_count, width)),
        out_shape=[
            shape((pulses, 2 * beams, 8 * channels), bf16),
            shape((pulses - 2, beams, beams), bf16),
            shape((pulse_count, levels + 1, 2, beams, piece_width), f32),
        ],
        in_specs=[vmem()] * 2,
        out_specs=[vmem()] * 3,
        name="tables",
        **PARAMS,
    )(angles, codes)
    images = [None] * pulse_count
    for distance in [*range(1, pulse_count), 0]:
        index = pulse_count - 1 - distance
        image = pl.pallas_call(
            functools.partial(inner_kernel, index),
            out_shape=shape((2, beams, piece_width), bf16),
            in_specs=[vmem()] * 5,
            out_specs=vmem(),
            scratch_shapes=[
                pltpu.VMEM((pulses, 2 * beams, piece_width), f32),
                pltpu.VMEM((pulses // 2, beams, 2 * piece_width), f32),
                pltpu.VMEM((pulses // 2, beams, 2 * piece_width), f32),
            ],
            name="inner",
            **PARAMS,
        )(kept, received[index // chunk], first, inner, phase)
        images[distance] = image
        if distance:
            pairs = [(i, i ^ distance) for i in range(pulse_count)]
            images[distance] = lax.ppermute(image, "pulse", pairs)
    outer_count = 2 * pulse_count - 2
    outer, outer_phase = pl.pallas_call(
        functools.partial(outer_tables_kernel, (rx_count, width, pulse_count)),
        out_shape=[
            shape((outer_count, beams, beams), bf16),
            shape((outer_count, 2, beams, piece_width), f32),
        ],
        in_specs=[vmem(), vmem(), anywhere()],
        out_specs=[vmem()] * 2,
        name="outer_tables",
        **PARAMS,
    )(angles, codes, images[0])
    return pl.pallas_call(
        outer_kernel,
        out_shape=shape((2, beams, piece_width), f32),
        in_specs=[vmem()] * (2 + pulse_count),
        out_specs=vmem(),
        name="outer",
        **PARAMS,
    )(outer, outer_phase, *images)


def power_of_two(count):
    return count > 0 and count & (count - 1) == 0


def per_device(echoes, beam_angle, interp_table):
    _, pulses, channels, length = echoes.shape
    rx_count = lax.axis_size("rx")
    pulse_count = lax.axis_size("pulse")
    piece_width = length // (rx_count * pulse_count)
    if (
        lax.axis_size("rng") == 2
        and rx_count == 2
        and channels == 8
        and pulses == 8
        and power_of_two(pulse_count)
        and pulse_count > 1
        and power_of_two(beam_angle.shape[0])
        and beam_angle.shape[0] % 16 == 0
        and piece_width % LANES == 0
    ):
        return fast(echoes, beam_angle, interp_table)
    return local(echoes, beam_angle, interp_table)


def solution(mesh):
    placed = (P(None, ("slab", "pulse"), "rx", "rng"), P(), P())
    return jax.shard_map(
        per_device,
        mesh=mesh,
        in_specs=placed,
        out_specs=P(None, "slab", ("rng", "rx", "pulse")),
        check_vma=False,
    )
```

```python
import functools
import math

import jax
import jax.numpy as jnp
import ml_dtypes
import numpy as np
from jax import lax
from jax.experimental import pallas as pl
from jax.experimental.pallas import tpu as pltpu
from jax.sharding import PartitionSpec as P

RTAPS = 64
CTAPS = 512


half_root = 0.7071067811865476
full_turn = 2.0 * math.pi


def extended_2(block, sides, width):
    for axis, dim in sides:
        count = lax.axis_size(axis)
        forward = [(i, i + 1) for i in range(count - 1)]
        backward = [(target, source) for source, target in forward]
        low = lax.ppermute(
            lax.slice_in_dim(block, block.shape[dim] - width, None, axis=dim), axis, forward
        )
        high = lax.ppermute(lax.slice_in_dim(block, 0, width, axis=dim), axis, backward)
        block = jnp.concatenate([low, block, high], axis=dim)
    return block


def swapped(x, axis, distance):
    return lax.ppermute(x, axis, [(i, i ^ 1 << distance) for i in range(lax.axis_size(axis))])


def receiver_taps(channel_ids, tap_count):
    tap_index = jnp.arange(tap_count, dtype=jnp.float32)
    window = 0.5 - 0.5 * jnp.cos(full_turn * (tap_index + 0.5) / tap_count)
    window = window / jnp.sqrt(jnp.sum(window * window))
    channel = channel_ids.astype(jnp.float32)[:, None] + 1.0
    angle = full_turn * channel * (tap_index - tap_count // 2) / (4 * tap_count)
    return (
        (window * jnp.cos(angle)).astype(jnp.bfloat16),
        (window * jnp.sin(angle)).astype(jnp.bfloat16),
    )


def chirp_taps(tap_count):
    offset = jnp.arange(tap_count, dtype=jnp.int32) - tap_count // 2
    phase_step = jnp.mod(offset * offset, 2 * tap_count).astype(jnp.float32)
    angle = math.pi * phase_step / tap_count
    scale = 1.0 / math.sqrt(tap_count)
    return (
        (jnp.cos(angle) * scale).astype(jnp.bfloat16),
        (-jnp.sin(angle) * scale).astype(jnp.bfloat16),
    )


def steering(beam_angle, receivers):
    channel = jnp.arange(receivers, dtype=jnp.int32)
    turns = jnp.mod(beam_angle[:, None] * channel[None, :], 1024).astype(jnp.float32)
    angle = full_turn * turns / 1024.0
    scale = 1.0 / math.sqrt(receivers)
    return (
        (jnp.cos(angle) * scale).astype(jnp.bfloat16),
        (-jnp.sin(angle) * scale).astype(jnp.bfloat16),
    )


def interp_matrices(codes, beam_count):
    shifted = codes // 4 - 1
    fraction = jnp.mod(codes, 4).astype(jnp.float32) / 4.0
    weights = (
        -fraction * (fraction - 1.0) * (fraction - 2.0) / 6.0,
        (fraction + 1.0) * (fraction - 1.0) * (fraction - 2.0) / 2.0,
        -(fraction + 1.0) * fraction * (fraction - 2.0) / 2.0,
        (fraction + 1.0) * fraction * (fraction - 1.0) / 6.0,
    )
    columns = jnp.arange(beam_count, dtype=jnp.int32)
    matrices = jnp.zeros(codes.shape + (beam_count,), jnp.float32)
    for tap_index in range(4):
        target = jnp.mod(columns + shifted + tap_index - 1, beam_count)
        matrices = matrices + weights[tap_index][..., None] * (target[..., None] == columns).astype(
            jnp.float32
        )
    return matrices


def phases(node_ids, positions, beam_angle, side):
    base = jnp.mod(beam_angle[:, None] * (positions[None, :] + 1), 1024)
    factor = 2 * node_ids + side + 1
    turns = jnp.mod(base[:, None, :] * factor[None, :, None], 1024).astype(jnp.float32)
    angle = full_turn * turns / 1024.0
    return (jnp.cos(angle), jnp.sin(angle))


def side_term(picture, matrices, cosine, sine):
    moved = jnp.einsum("gqa,cagr->cqgr", matrices, picture, precision=lax.Precision.HIGHEST)
    return (cosine * moved[0] - sine * moved[1], sine * moved[0] + cosine * moved[1])


def merge_pair(left_image, right_image, node_ids, positions, beam_angle, interp_table):
    matrices = interp_matrices(interp_table[node_ids], left_image.shape[1])
    left_cos, left_sin = phases(node_ids, positions, beam_angle, 0)
    right_cos, right_sin = phases(node_ids, positions, beam_angle, 1)
    left_re, left_im = side_term(left_image, matrices[:, 0], left_cos, left_sin)
    right_re, right_im = side_term(right_image, matrices[:, 1], right_cos, right_sin)
    return jnp.stack([(left_re + right_re) * half_root, (left_im + right_im) * half_root])


def toeplitz_blocks(taps_re, taps_im):
    tap_count = taps_re.shape[-1]
    leading = taps_re.shape[:-1]

    def lay_out(taps):
        padded = jnp.concatenate([taps, jnp.zeros(leading + (tap_count + 1,), taps.dtype)], axis=-1)
        tiled = jnp.tile(padded, (1,) * len(leading) + (tap_count,))
        banded = tiled[..., : 2 * tap_count * tap_count].reshape(
            leading + (tap_count, 2 * tap_count)
        )
        return jnp.swapaxes(banded, -1, -2)

    real_band = lay_out(taps_re)
    imag_band = lay_out(taps_im)
    upper = jnp.concatenate([real_band, imag_band], axis=-1)
    lower = jnp.concatenate([-imag_band, real_band], axis=-1)
    return jnp.concatenate([upper, lower], axis=-2)


def block_filter(extended, matrices, tap_count, per_channel):
    pulses, channels, length = extended.shape[1:]
    blocks = length // tap_count - 1
    pieces = extended.reshape(2, pulses, channels, blocks + 1, tap_count)
    windows = jnp.concatenate([pieces[:, :, :, :-1], pieces[:, :, :, 1:]], axis=4)
    windows = jnp.transpose(windows, (1, 2, 3, 0, 4)).reshape(
        pulses, channels, blocks, 4 * tap_count
    )
    if per_channel:
        output = jnp.einsum("pcnw,cwo->pcno", windows, matrices, preferred_element_type=jnp.float32)
    else:
        output = jnp.einsum("pcnw,wo->pcno", windows, matrices, preferred_element_type=jnp.float32)
    output = output.reshape(pulses, channels, blocks, 2, tap_count)
    return jnp.transpose(output, (3, 0, 1, 2, 4)).reshape(2, pulses, channels, blocks * tap_count)


def local(echoes, beam_angle, interp_table):
    rx_count = lax.axis_size("rx")
    pulse_count = lax.axis_size("pulse")
    rng_place = lax.axis_index("rng")
    rx_place = lax.axis_index("rx")
    pulse_place = lax.axis_index("pulse")
    pulses, channels, length = echoes.shape[1:]
    beam_count = beam_angle.shape[0]
    receivers = channels * rx_count
    channel_ids = rx_place * channels + jnp.arange(channels, dtype=jnp.int32)
    rx_re, rx_im = receiver_taps(channel_ids, RTAPS)
    rx_bands = toeplitz_blocks(rx_re, rx_im)
    chirp_re, chirp_im = chirp_taps(CTAPS)
    chirp_band = toeplitz_blocks(chirp_re, chirp_im)
    extended = extended_2(echoes, (("rng", 3),), RTAPS // 2)
    filtered = block_filter(extended, rx_bands, RTAPS, True).astype(jnp.bfloat16)
    filtered = extended_2(filtered, (("rng", 3),), CTAPS // 2)
    compressed = block_filter(filtered, chirp_band, CTAPS, False).astype(jnp.bfloat16)
    steering_real, steering_imaginary = steering(beam_angle, receivers)
    steer_matrix = jnp.concatenate(
        [
            jnp.concatenate([steering_real, -steering_imaginary], axis=1),
            jnp.concatenate([steering_imaginary, steering_real], axis=1),
        ],
        axis=0,
    )
    arrived = lax.all_to_all(compressed, "rx", split_axis=3, concat_axis=2, tiled=True)
    item_count, recv_count, owned_cols = arrived.shape[1:]
    stacked = jnp.transpose(arrived, (0, 2, 1, 3)).reshape(2 * recv_count, item_count * owned_cols)
    formed = jnp.dot(steer_matrix, stacked, preferred_element_type=jnp.float32)
    picture = formed.reshape(2, beam_count, item_count, owned_cols)
    owned_width = length // rx_count
    positions = (
        rng_place * length + rx_place * owned_width + jnp.arange(owned_width, dtype=jnp.int32)
    )
    for level in range(pulses.bit_length() - 1):
        groups_now = pulses >> level + 1
        node_ids = (pulse_count + pulse_place) * groups_now + jnp.arange(
            groups_now, dtype=jnp.int32
        )
        paired = picture.reshape(2, beam_count, groups_now, 2, owned_width)
        picture = merge_pair(
            paired[:, :, :, 0], paired[:, :, :, 1], node_ids, positions, beam_angle, interp_table
        )
    picture = picture[:, :, 0]
    cross_levels = pulse_count.bit_length() - 1
    piece_width = owned_width // pulse_count
    pieces = picture.reshape(2, beam_count, pulse_count, piece_width)
    spots = positions.reshape(pulse_count, piece_width)
    for level in range(cross_levels):
        parity = jnp.right_shift(pulse_place, level) & 1
        count_now = pieces.shape[2]
        paired = pieces.reshape(2, beam_count, count_now // 2, 2, piece_width)
        kept_half = lax.dynamic_index_in_dim(paired, parity, 3, keepdims=False)
        sent_half = lax.dynamic_index_in_dim(paired, 1 - parity, 3, keepdims=False)
        partner = swapped(sent_half, "pulse", level)
        spot_pairs = spots.reshape(count_now // 2, 2, piece_width)
        spots = lax.dynamic_index_in_dim(spot_pairs, parity, 1, keepdims=False)
        own_part = kept_half.reshape(2, beam_count, -1)
        other_part = partner.reshape(2, beam_count, -1)
        left_image = jnp.where(parity == 0, own_part, other_part)
        right_image = jnp.where(parity == 0, other_part, own_part)
        combine_node_ids = jnp.reshape(
            (pulse_count >> level + 1) + jnp.right_shift(pulse_place, level + 1), (1,)
        )
        merged = merge_pair(
            left_image[:, :, None],
            right_image[:, :, None],
            combine_node_ids,
            spots.reshape(-1),
            beam_angle,
            interp_table,
        )
        flat = merged[:, :, 0]
        pieces = flat.reshape(2, beam_count, count_now // 2, piece_width)
    picture = pieces.reshape(2, beam_count, piece_width)
    return picture


LANES = 128
RX_TILE = 2 * LANES
CHIRP_TILE = 6 * LANES
HALO_TILES = 3
HALO = HALO_TILES * LANES


def vmem():
    return pl.BlockSpec(memory_space=pltpu.VMEM)


def hbm():
    return pl.BlockSpec(memory_space=pltpu.HBM)


def anywhere():
    return pl.BlockSpec(memory_space=pl.ANY)


def rx_bands_table(receivers):
    step = np.arange(RTAPS, dtype=np.float64)
    window = 0.5 - 0.5 * np.cos(full_turn * (step + 0.5) / RTAPS)
    window = window / np.sqrt(np.sum(window * window))
    channel = np.arange(receivers, dtype=np.float64)[:, None] + 1.0
    angle = full_turn * channel * (step - RTAPS // 2) / (4 * RTAPS)
    offset = np.arange(RX_TILE)[:, None] - np.arange(LANES)[None, :]
    inside = (offset >= 0) & (offset < RTAPS)
    place = np.clip(offset, 0, RTAPS - 1)
    bands = [
        np.where(inside, taps[:, place], 0.0)
        for taps in (window * np.cos(angle), window * np.sin(angle))
    ]
    return np.concatenate(bands, axis=-1).astype(ml_dtypes.bfloat16)


def chirp_bands_table():
    offset = np.arange(CTAPS) - CTAPS // 2
    angle = math.pi * np.mod(offset * offset, 2 * CTAPS) / CTAPS
    scale = 1.0 / math.sqrt(CTAPS)
    offset = np.arange(CHIRP_TILE)[:, None] - np.arange(LANES)[None, :] - (LANES - RTAPS // 2)
    inside = (offset >= 0) & (offset < CTAPS)
    place = np.clip(offset, 0, CTAPS - 1)
    bands = [
        np.where(inside, taps[place], 0.0)
        for taps in (np.cos(angle) * scale, -np.sin(angle) * scale)
    ]
    return np.concatenate(bands, axis=-1).astype(ml_dtypes.bfloat16)


def edge_kernel(echo_hbm, edge_ref, echo_ref, arrived):
    length = echo_hbm.shape[3]
    start = jnp.where(lax.axis_index("rng") == 0, length - HALO, 0)
    start = pl.multiple_of(start, LANES)
    edge = pltpu.make_async_copy(
        echo_hbm.at[:, :, :, pl.ds(start, HALO)], edge_ref, arrived.at[0]
    )
    edge.start()
    whole = pltpu.make_async_copy(echo_hbm, echo_ref, arrived.at[1])
    whole.start()
    edge.wait()
    whole.wait()


def filter_channel(windows, bands, pulses):
    product = jnp.dot(windows, bands, preferred_element_type=jnp.float32)
    product = product.reshape(-1, 2, pulses, 2 * LANES)
    real = product[:, 0, :, :LANES] - product[:, 1, :, LANES:]
    imag = product[:, 0, :, LANES:] + product[:, 1, :, :LANES]
    return real, imag


def interior_kernel(echo_ref, bands_ref, filtered_ref, rows_in, rows_out):
    _, pulses, channels, length = echo_ref.shape
    first_channel = lax.axis_index("rx") * channels
    tiles = length // LANES
    group = 2 * pulses
    empty = jnp.zeros(rows_in.shape[1:], jnp.float32)
    rows_in[0] = empty
    rows_in[tiles + 1] = empty
    for part in range(2):
        for pulse in range(pulses):
            where = pl.ds(part * pulses + pulse, channels, stride=group)
            block = echo_ref[part, pulse].astype(jnp.float32)
            for tile in range(tiles):
                rows_in[tile + 1, where, :] = block[:, tile * LANES : (tile + 1) * LANES]
    lane = lax.broadcasted_iota(jnp.int32, (1, LANES), 1)
    for channel in range(channels):
        rows = rows_in[:, channel * group : (channel + 1) * group, :].astype(jnp.bfloat16)
        windows = jnp.concatenate(
            [rows[:-1].reshape(-1, LANES), rows[1:].reshape(-1, LANES)], axis=1
        )
        real, imag = filter_channel(windows, bands_ref[first_channel + channel], pulses)
        for tile in range(tiles + 1):
            tile_re, tile_im = real[tile], imag[tile]
            if tile == 0:
                tile_re = jnp.where(lane >= LANES - RTAPS // 2, tile_re, 0.0)
                tile_im = jnp.where(lane >= LANES - RTAPS // 2, tile_im, 0.0)
            if tile == tiles:
                tile_re = jnp.where(lane < LANES - RTAPS // 2, tile_re, 0.0)
                tile_im = jnp.where(lane < LANES - RTAPS // 2, tile_im, 0.0)
            rows_out[tile, pl.ds(channel, pulses, stride=2 * channels), :] = tile_re
            rows_out[tile, pl.ds(channels + channel, pulses, stride=2 * channels), :] = tile_im
    rows = filtered_ref.shape[0]
    nothing = jnp.zeros((rows, (HALO_TILES - 1) * LANES), jnp.bfloat16)
    filtered_ref[:, : (HALO_TILES - 1) * LANES] = nothing
    filtered_ref[:, (HALO_TILES + tiles) * LANES :] = nothing
    for tile in range(tiles + 1):
        spot = (HALO_TILES - 1 + tile) * LANES
        filtered_ref[:, spot : spot + LANES] = rows_out[tile].astype(jnp.bfloat16)


def chirp_piece(filtered_ref, chirp_ref, starts, out_ref):
    windows = [filtered_ref[:, pl.ds(start, CHIRP_TILE)] for start in starts]
    product = jnp.dot(
        jnp.concatenate(windows, axis=0), chirp_ref[...], preferred_element_type=jnp.float32
    )
    pulses, rows, _ = out_ref.shape
    channels = rows // 2
    product = product.reshape(len(starts), pulses, rows, 2 * LANES)
    for tile in range(len(starts)):
        block = product[tile]
        real = block[:, :channels, :LANES] - block[:, channels:, LANES:]
        imag = block[:, :channels, LANES:] + block[:, channels:, :LANES]
        out_ref[:, :, tile * LANES : (tile + 1) * LANES] = jnp.concatenate(
            [real, imag], axis=1
        ).astype(jnp.bfloat16)


def chirp_pieces(filtered_ref, chirp_ref, owner, piece_count, distances, out_ref):
    pulse_place = lax.axis_index("pulse")
    piece_tiles = out_ref.shape[3] // LANES
    for index, distance in enumerate(distances):
        piece = jnp.bitwise_xor(pulse_place, distance)
        first = (owner * piece_count + piece) * piece_tiles
        starts = [pl.multiple_of((first + t) * LANES, LANES) for t in range(piece_tiles)]
        chirp_piece(filtered_ref, chirp_ref, starts, out_ref.at[index])


def edges_kernel(
    plan, inner_ref, echo_ref, edge_ref, bands_ref, chirp_ref, filtered_ref, *rest
):
    *send_refs, rows_in, rows_out = rest
    del inner_ref
    _, pulses, channels, length = echo_ref.shape
    first_channel = lax.axis_index("rx") * channels
    tiles = length // LANES
    group = 2 * pulses
    lowest = lax.axis_index("rng") == 0
    for part in range(2):
        for pulse in range(pulses):
            where = pl.ds(part * pulses + pulse, channels, stride=group)
            edge = edge_ref[part, pulse].astype(jnp.float32)
            near_low = echo_ref[part, pulse, :, :LANES].astype(jnp.float32)
            near_high = echo_ref[part, pulse, :, length - LANES :].astype(jnp.float32)
            pieces = [edge[:, t * LANES : (t + 1) * LANES] for t in range(HALO_TILES)]
            for tile in range(HALO_TILES + 1):
                high = near_high if tile == 0 else pieces[tile - 1]
                low = near_low if tile == HALO_TILES else pieces[tile]
                rows_in[tile, where, :] = jnp.where(lowest, high, low)
    for channel in range(channels):
        rows = rows_in[:, channel * group : (channel + 1) * group, :].astype(jnp.bfloat16)
        windows = jnp.concatenate(
            [rows[:-1].reshape(-1, LANES), rows[1:].reshape(-1, LANES)], axis=1
        )
        real, imag = filter_channel(windows, bands_ref[first_channel + channel], pulses)
        for tile in range(HALO_TILES):
            rows_out[tile, pl.ds(channel, pulses, stride=2 * channels), :] = real[tile]
            rows_out[tile, pl.ds(channels + channel, pulses, stride=2 * channels), :] = imag[tile]
    first = jnp.where(lowest, tiles + HALO_TILES - 1, 0)
    for tile in range(HALO_TILES):
        start = pl.multiple_of((first + tile) * LANES, LANES)
        filtered_ref[:, pl.ds(start, LANES)] = rows_out[tile].astype(jnp.bfloat16)
    piece_count, groups = plan
    for distances, send_ref in zip(groups, send_refs):
        chirp_pieces(
            filtered_ref, chirp_ref, 1 - lax.axis_index("rx"), piece_count, distances, send_ref
        )


def chirp_kernel(partner, piece_count, groups, filtered_ref, chirp_ref, *out_refs):
    out_refs = out_refs[len(out_refs) - len(groups) :]
    rx_place = lax.axis_index("rx")
    owner = 1 - rx_place if partner else rx_place
    for distances, out_ref in zip(groups, out_refs):
        chirp_pieces(filtered_ref, chirp_ref, owner, piece_count, distances, out_ref)


def turn_parts(step):
    shifted = step + 128
    angle = (jnp.bitwise_and(shifted, 255) - 128).astype(jnp.float32) * (full_turn / 1024.0)
    quarter = jnp.right_shift(shifted, 8)
    square = angle * angle
    cosine = 1.0 + square * (-1 / 2 + square * (1 / 24 + square * (-1 / 720 + square * (1 / 40320))))
    sine = angle * (1.0 + square * (-1 / 6 + square * (1 / 120 + square * (-1 / 5040))))
    odd = jnp.bitwise_and(quarter, 1) == 1
    real = jnp.where(odd, sine, cosine)
    imag = jnp.where(odd, cosine, sine)
    real = jnp.where(jnp.bitwise_and(quarter + 1, 2) == 2, -real, real)
    imag = jnp.where(jnp.bitwise_and(quarter, 2) == 2, -imag, imag)
    return real, imag


def turned(real, imag, phase_re, phase_im):
    return phase_re * real - phase_im * imag, phase_im * real + phase_re * imag


def as_column(row):
    count = row.shape[1]
    first = lax.broadcasted_iota(jnp.int32, (count, count), 0)
    second = lax.broadcasted_iota(jnp.int32, (count, count), 1)
    spread = jnp.where(first == second, row.astype(jnp.float32), 0.0)
    return jnp.sum(spread, axis=1, keepdims=True).astype(jnp.int32)


def interp_matrix(code):
    beams = code.shape[0]
    angle_bin = lax.broadcasted_iota(jnp.int32, (beams, beams), 0)
    column = lax.broadcasted_iota(jnp.int32, (beams, beams), 1)
    half = 2 * beams
    away = jnp.bitwise_and(4 * (column - angle_bin + 1) - code + half, 4 * beams - 1) - half
    away = jnp.abs(away.astype(jnp.float32)) * 0.25
    near = (1.0 - away * away) * (2.0 - away) * 0.5
    far = (1.0 - away) * (2.0 - away) * (3.0 - away) * (1.0 / 6.0)
    matrix = jnp.where(away < 1.0, near, jnp.where(away < 2.0, far, 0.0))
    return matrix.astype(jnp.bfloat16)


def code_columns(codes_ref, rows):
    picked = [codes_ref[pl.ds(row, 1), :] for row in rows]
    picked = jnp.concatenate(picked, axis=0).astype(jnp.float32)
    spare = -len(rows) % 8
    if spare:
        picked = jnp.concatenate([picked, jnp.zeros((spare, picked.shape[1]), jnp.float32)], axis=0)
    return picked.T.astype(jnp.int32)


def tables_kernel(sizes, angle_ref, codes_ref, first_ref, inner_ref, phase_ref):
    pulses, channels, rx_count, width = sizes
    rng_place = lax.axis_index("rng")
    rx_place = lax.axis_index("rx")
    pulse_place = lax.axis_index("pulse")
    beams = angle_ref.shape[1]
    piece_count = phase_ref.shape[0]
    piece_tiles = phase_ref.shape[4] // LANES
    angle = as_column(angle_ref[...])
    factors = []
    rows = []
    now = pulses
    while now > 1:
        base = now * piece_count + pulse_place * now
        factors.append(base + 1)
        rows.extend(base + index for index in range(now))
        now //= 2
    codes = code_columns(codes_ref, rows)
    column = lax.broadcasted_iota(jnp.int32, (1, 4 * channels * 2), 1)
    within = jnp.bitwise_and(column, 4 * channels - 1)
    owner = jnp.bitwise_xor(rx_place, jnp.where(within >= 2 * channels, 1, 0))
    receiver = owner * channels + jnp.bitwise_and(column, channels - 1)
    is_imag = jnp.bitwise_and(within, channels) != 0
    scale = 1.0 / math.sqrt(channels * rx_count)
    steer_re, steer_im = turn_parts(jnp.bitwise_and(angle * receiver, 1023))
    steer_re = (steer_re * scale).astype(jnp.bfloat16).astype(jnp.float32)
    steer_im = (-steer_im * scale).astype(jnp.bfloat16).astype(jnp.float32)
    steer = jnp.concatenate(
        [
            jnp.where(is_imag, -steer_im, steer_re).astype(jnp.bfloat16),
            jnp.where(is_imag, steer_re, steer_im).astype(jnp.bfloat16),
        ],
        axis=1,
    )
    low_half = column >= 4 * channels
    entries = 8 * channels
    matrices = [interp_matrix(codes[:, index : index + 1]) for index in range(len(rows))]
    composed = jnp.dot(
        jnp.concatenate(matrices[:pulses], axis=0), steer, preferred_element_type=jnp.float32
    )
    for index in range(pulses):
        for part in range(2):
            value = composed[
                index * beams : (index + 1) * beams, part * entries : (part + 1) * entries
            ]
            high = value.astype(jnp.bfloat16).astype(jnp.float32)
            first_ref[index, part * beams : (part + 1) * beams, :] = jnp.where(
                low_half, value - high, high
            ).astype(jnp.bfloat16)
    for index, matrix in enumerate(matrices[pulses:]):
        inner_ref[index] = matrix
    lane = lax.broadcasted_iota(jnp.int32, (1, LANES), 1)
    block = (rng_place * rx_count + rx_place) * width + 1
    base = jnp.bitwise_and(angle * (block + lane), 1023)
    for slot, factor in enumerate([1, *factors]):
        scale = half_root if slot else 1.0
        real, imag = turn_parts(jnp.bitwise_and(base * factor, 1023))
        real, imag = real * scale, imag * scale
        step = turn_parts(jnp.bitwise_and(angle * (factor * LANES), 1023))
        for tile in range(piece_count * piece_tiles):
            index = piece_count - 1 - jnp.bitwise_xor(pulse_place, tile // piece_tiles)
            start = tile % piece_tiles * LANES
            phase_ref[index, slot, 0, :, start : start + LANES] = real
            phase_ref[index, slot, 1, :, start : start + LANES] = imag
            real, imag = turned(real, imag, *step)


def outer_levels(piece_count):
    return [piece_count >> level for level in range(piece_count.bit_length() - 1)]


def outer_tables_kernel(sizes, angle_ref, codes_ref, after_ref, outer_ref, phase_ref):
    rx_count, width, piece_count = sizes
    rng_place = lax.axis_index("rng")
    rx_place = lax.axis_index("rx")
    pulse_place = lax.axis_index("pulse")
    piece_width = phase_ref.shape[3]
    angle = as_column(angle_ref[...])
    lane = lax.broadcasted_iota(jnp.int32, (1, piece_width), 1)
    block = (rng_place * rx_count + rx_place) * width + 1
    base = jnp.bitwise_and(angle * (block + pulse_place * piece_width + lane), 1023)
    rows = [row + level for level in outer_levels(piece_count) for row in range(level)]
    codes = code_columns(codes_ref, rows)
    slot = 0
    now = piece_count
    while now > 1:
        for index in range(now):
            outer_ref[slot] = interp_matrix(codes[:, slot : slot + 1])
            real, imag = turn_parts(jnp.bitwise_and(base * (now + index + 1), 1023))
            phase_ref[slot, 0] = real * half_root
            phase_ref[slot, 1] = imag * half_root
            slot += 1
        now //= 2


ROWS = 8


def inner_kernel(index, other, keep_ref, other_ref, first_ref, inner_ref, phase_ref, *rest):
    out_ref, moved_ref, picture_ref, level_ref = rest[-4:]
    pulses = keep_ref.shape[1]
    beams = inner_ref.shape[1]
    columns = keep_ref.shape[3]
    for image in range(pulses):
        rows = jnp.concatenate([keep_ref[index, image], other_ref[other, image]], axis=0)
        moved_ref[image] = jnp.dot(
            first_ref[image],
            jnp.concatenate([rows, rows], axis=0),
            preferred_element_type=jnp.float32,
        )

    def merge(count, level, read, write):
        for row in range(0, beams, ROWS):
            span = slice(row, row + ROWS)
            step = (phase_ref[index, 0, 0, span], phase_ref[index, 0, 1, span])
            phase = (phase_ref[index, level, 0, span], phase_ref[index, level, 1, span])
            for image in range(count):
                term = turned(*read(image, row), *phase)
                if image & 1:
                    write(image // 2, row, left[0] + term[0], left[1] + term[1])
                left = term
                if image < count - 1:
                    phase = turned(*phase, *step)

    def write_picture(image, row, real, imag):
        picture_ref[image, row : row + ROWS, :columns] = real
        picture_ref[image, row : row + ROWS, columns:] = imag

    def write_out(image, row, real, imag):
        picture_ref[0, row : row + ROWS, :columns] = real
        picture_ref[0, row : row + ROWS, columns:] = imag

    merge(
        pulses,
        1,
        lambda image, row: (
            moved_ref[image, row : row + ROWS],
            moved_ref[image, beams + row : beams + row + ROWS],
        ),
        write_picture,
    )
    slot = 0
    level = 2
    count = pulses // 2
    while count > 1:
        for image in range(count):
            level_ref[image] = jnp.dot(
                inner_ref[slot],
                picture_ref[image].astype(jnp.bfloat16),
                preferred_element_type=jnp.float32,
            )
            slot += 1
        merge(
            count,
            level,
            lambda image, row: (
                level_ref[image, row : row + ROWS, :columns],
                level_ref[image, row : row + ROWS, columns:],
            ),
            write_picture,
        )
        count //= 2
        level += 1
    out_ref[0] = picture_ref[0, :, :columns].astype(jnp.bfloat16)
    out_ref[1] = picture_ref[0, :, columns:].astype(jnp.bfloat16)


def outer_kernel(outer_ref, phase_ref, *rest):
    image_refs, out_ref = rest[-2::-1], rest[-1]
    pulse_place = lax.axis_index("pulse")
    pictures = [(ref[0], ref[1]) for ref in image_refs]
    base = 0
    level = 0
    while len(pictures) > 1:
        count = len(pictures)
        place = jnp.right_shift(pulse_place, level)
        merged = []
        for distance, (real, imag) in enumerate(pictures):
            slot = base + jnp.bitwise_xor(place, distance)
            matrix = outer_ref[slot]
            moved_re = jnp.dot(
                matrix, real.astype(jnp.bfloat16), preferred_element_type=jnp.float32
            )
            moved_im = jnp.dot(
                matrix, imag.astype(jnp.bfloat16), preferred_element_type=jnp.float32
            )
            merged.append(turned(moved_re, moved_im, phase_ref[slot, 0], phase_ref[slot, 1]))
            if distance & 1:
                right, left = merged.pop(), merged.pop()
                merged.append((left[0] + right[0], left[1] + right[1]))
        pictures = merged
        base += count
        level += 1
    out_ref[0] = pictures[0][0]
    out_ref[1] = pictures[0][1]


PARAMS = dict(compiler_params=pltpu.CompilerParams(vmem_limit_bytes=40 * 1024 * 1024))


def send_groups(pulse_count):
    last = pulse_count - 1
    if pulse_count < 4:
        return [[distance] for distance in range(last, -1, -1)]
    return [[distance] for distance in range(last, -1, -1)]


def fast(echoes, beam_angle, interp_table):
    rx_count = lax.axis_size("rx")
    pulse_count = lax.axis_size("pulse")
    _, pulses, channels, length = echoes.shape
    beams = beam_angle.shape[0]
    width = length // rx_count
    piece_width = width // pulse_count
    piece_tiles = piece_width // LANES
    rows = 2 * channels
    group = 2 * pulses
    bands = jnp.asarray(rx_bands_table(channels * rx_count))
    chirp = jnp.asarray(chirp_bands_table())
    angles = beam_angle.reshape(1, beams)
    codes = interp_table.reshape(-1, beams)
    bf16 = jnp.bfloat16
    f32 = jnp.float32
    shape = jax.ShapeDtypeStruct
    edge, echoes = pl.pallas_call(
        edge_kernel,
        out_shape=[shape(echoes.shape[:3] + (HALO,), bf16), shape(echoes.shape, bf16)],
        in_specs=[hbm()],
        out_specs=[vmem(), vmem()],
        scratch_shapes=[pltpu.SemaphoreType.DMA((2,))],
        name="edge",
        cost_estimate=pl.CostEstimate(flops=10**10, bytes_accessed=10**8, transcendentals=0),
        **PARAMS,
    )(echoes)
    edge = swapped(edge, "rng", 0)
    tiles = length // LANES
    filtered_shape = shape((rows * pulses, (tiles + 2 * HALO_TILES - 1) * LANES), bf16)
    filtered = pl.pallas_call(
        interior_kernel,
        out_shape=filtered_shape,
        in_specs=[vmem()] * 2,
        out_specs=vmem(),
        scratch_shapes=[
            pltpu.VMEM((tiles + 2, channels * group, LANES), f32),
            pltpu.VMEM((tiles + 1, rows * pulses, LANES), f32),
        ],
        name="interior",
        **PARAMS,
    )(echoes, bands)

    def pieces(count):
        return shape((count, pulses, rows, piece_width), bf16)

    last = pulse_count - 1
    groups = send_groups(pulse_count)
    filtered, *sent = pl.pallas_call(
        functools.partial(edges_kernel, (pulse_count, groups)),
        out_shape=[filtered_shape] + [pieces(len(members)) for members in groups],
        in_specs=[vmem()] * 5,
        out_specs=[vmem()] * (1 + len(groups)),
        scratch_shapes=[
            pltpu.VMEM((HALO_TILES + 1, channels * group, LANES), f32),
            pltpu.VMEM((HALO_TILES, rows * pulses, LANES), f32),
        ],
        input_output_aliases={0: 0},
        name="edges",
        **PARAMS,
    )(filtered, echoes, edge, bands, chirp)
    received = {}

    def receive(members, piece):
        piece = swapped(piece, "rx", 0)
        for index, distance in enumerate(members):
            received[distance] = (piece, index)

    for index in [*range(len(groups) - 2, -1, -1), len(groups) - 1]:
        receive(groups[index], sent[index])
    kept = pl.pallas_call(
        functools.partial(
            chirp_kernel, False, pulse_count, [[last - index for index in range(pulse_count)]]
        ),
        out_shape=[pieces(pulse_count)],
        in_specs=[vmem()] * 2,
        out_specs=[vmem()],
        name="keep",
        **PARAMS,
    )(filtered, chirp)[0]
    levels = pulses.bit_length() - 1
    first, inner, phase = pl.pallas_call(
        functools.partial(tables_kernel, (pulses, channels, rx_count, width)),
        out_shape=[
            shape((pulses, 2 * beams, 8 * channels), bf16),
            shape((pulses - 2, beams, beams), bf16),
            shape((pulse_count, levels + 1, 2, beams, piece_width), f32),
        ],
        in_specs=[vmem()] * 2,
        out_specs=[vmem()] * 3,
        name="tables",
        **PARAMS,
    )(angles, codes)
    images = [None] * pulse_count

    def merge(distance):
        other, place = received[distance]
        return pl.pallas_call(
            functools.partial(inner_kernel, last - distance, place),
            out_shape=shape((2, beams, piece_width), bf16),
            in_specs=[vmem()] * 5,
            out_specs=vmem(),
            scratch_shapes=[
                pltpu.VMEM((pulses, 2 * beams, piece_width), f32),
                pltpu.VMEM((pulses // 2, beams, 2 * piece_width), f32),
                pltpu.VMEM((pulses // 2, beams, 2 * piece_width), f32),
            ],
            name="inner",
            **PARAMS,
        )(kept, other, first, inner, phase)

    for distance in [*range(1, pulse_count), 0]:
        images[distance] = merge(distance)
    for distance in range(1, pulse_count):
        pairs = [(i, i ^ distance) for i in range(pulse_count)]
        images[distance] = lax.ppermute(images[distance], "pulse", pairs)
    outer_count = 2 * pulse_count - 2
    outer, outer_phase = pl.pallas_call(
        functools.partial(outer_tables_kernel, (rx_count, width, pulse_count)),
        out_shape=[
            shape((outer_count, beams, beams), bf16),
            shape((outer_count, 2, beams, piece_width), f32),
        ],
        in_specs=[vmem(), vmem(), anywhere()],
        out_specs=[vmem()] * 2,
        name="outer_tables",
        **PARAMS,
    )(angles, codes, images[0])
    return pl.pallas_call(
        outer_kernel,
        out_shape=shape((2, beams, piece_width), f32),
        in_specs=[vmem()] * (2 + pulse_count),
        out_specs=vmem(),
        name="outer",
        **PARAMS,
    )(outer, outer_phase, *images[::-1])


def power_of_two(count):
    return count > 0 and count & (count - 1) == 0


def per_device(echoes, beam_angle, interp_table):
    _, pulses, channels, length = echoes.shape
    rx_count = lax.axis_size("rx")
    pulse_count = lax.axis_size("pulse")
    piece_width = length // (rx_count * pulse_count)
    if (
        lax.axis_size("rng") == 2
        and rx_count == 2
        and channels == 8
        and pulses == 8
        and power_of_two(pulse_count)
        and pulse_count > 1
        and power_of_two(beam_angle.shape[0])
        and beam_angle.shape[0] % 16 == 0
        and piece_width % LANES == 0
    ):
        return fast(echoes, beam_angle, interp_table)
    return local(echoes, beam_angle, interp_table)


def solution(mesh):
    placed = (P(None, ("slab", "pulse"), "rx", "rng"), P(), P())
    return jax.shard_map(
        per_device,
        mesh=mesh,
        in_specs=placed,
        out_specs=P(None, "slab", ("rng", "rx", "pulse")),
        check_vma=False,
    )
```

```python
import functools
import math

import jax
import jax.numpy as jnp
import ml_dtypes
import numpy as np
from jax import lax
from jax.experimental import pallas as pl
from jax.experimental.pallas import tpu as pltpu
from jax.sharding import PartitionSpec as P

RTAPS = 64
CTAPS = 512


half_root = 0.7071067811865476
full_turn = 2.0 * math.pi


def extended_2(block, sides, width):
    for axis, dim in sides:
        count = lax.axis_size(axis)
        forward = [(i, i + 1) for i in range(count - 1)]
        backward = [(target, source) for source, target in forward]
        low = lax.ppermute(
            lax.slice_in_dim(block, block.shape[dim] - width, None, axis=dim), axis, forward
        )
        high = lax.ppermute(lax.slice_in_dim(block, 0, width, axis=dim), axis, backward)
        block = jnp.concatenate([low, block, high], axis=dim)
    return block


def swapped(x, axis, distance):
    return lax.ppermute(x, axis, [(i, i ^ 1 << distance) for i in range(lax.axis_size(axis))])


def receiver_taps(channel_ids, tap_count):
    tap_index = jnp.arange(tap_count, dtype=jnp.float32)
    window = 0.5 - 0.5 * jnp.cos(full_turn * (tap_index + 0.5) / tap_count)
    window = window / jnp.sqrt(jnp.sum(window * window))
    channel = channel_ids.astype(jnp.float32)[:, None] + 1.0
    angle = full_turn * channel * (tap_index - tap_count // 2) / (4 * tap_count)
    return (
        (window * jnp.cos(angle)).astype(jnp.bfloat16),
        (window * jnp.sin(angle)).astype(jnp.bfloat16),
    )


def chirp_taps(tap_count):
    offset = jnp.arange(tap_count, dtype=jnp.int32) - tap_count // 2
    phase_step = jnp.mod(offset * offset, 2 * tap_count).astype(jnp.float32)
    angle = math.pi * phase_step / tap_count
    scale = 1.0 / math.sqrt(tap_count)
    return (
        (jnp.cos(angle) * scale).astype(jnp.bfloat16),
        (-jnp.sin(angle) * scale).astype(jnp.bfloat16),
    )


def steering(beam_angle, receivers):
    channel = jnp.arange(receivers, dtype=jnp.int32)
    turns = jnp.mod(beam_angle[:, None] * channel[None, :], 1024).astype(jnp.float32)
    angle = full_turn * turns / 1024.0
    scale = 1.0 / math.sqrt(receivers)
    return (
        (jnp.cos(angle) * scale).astype(jnp.bfloat16),
        (-jnp.sin(angle) * scale).astype(jnp.bfloat16),
    )


def interp_matrices(codes, beam_count):
    shifted = codes // 4 - 1
    fraction = jnp.mod(codes, 4).astype(jnp.float32) / 4.0
    weights = (
        -fraction * (fraction - 1.0) * (fraction - 2.0) / 6.0,
        (fraction + 1.0) * (fraction - 1.0) * (fraction - 2.0) / 2.0,
        -(fraction + 1.0) * fraction * (fraction - 2.0) / 2.0,
        (fraction + 1.0) * fraction * (fraction - 1.0) / 6.0,
    )
    columns = jnp.arange(beam_count, dtype=jnp.int32)
    matrices = jnp.zeros(codes.shape + (beam_count,), jnp.float32)
    for tap_index in range(4):
        target = jnp.mod(columns + shifted + tap_index - 1, beam_count)
        matrices = matrices + weights[tap_index][..., None] * (target[..., None] == columns).astype(
            jnp.float32
        )
    return matrices


def phases(node_ids, positions, beam_angle, side):
    base = jnp.mod(beam_angle[:, None] * (positions[None, :] + 1), 1024)
    factor = 2 * node_ids + side + 1
    turns = jnp.mod(base[:, None, :] * factor[None, :, None], 1024).astype(jnp.float32)
    angle = full_turn * turns / 1024.0
    return (jnp.cos(angle), jnp.sin(angle))


def side_term(picture, matrices, cosine, sine):
    moved = jnp.einsum("gqa,cagr->cqgr", matrices, picture, precision=lax.Precision.HIGHEST)
    return (cosine * moved[0] - sine * moved[1], sine * moved[0] + cosine * moved[1])


def merge_pair(left_image, right_image, node_ids, positions, beam_angle, interp_table):
    matrices = interp_matrices(interp_table[node_ids], left_image.shape[1])
    left_cos, left_sin = phases(node_ids, positions, beam_angle, 0)
    right_cos, right_sin = phases(node_ids, positions, beam_angle, 1)
    left_re, left_im = side_term(left_image, matrices[:, 0], left_cos, left_sin)
    right_re, right_im = side_term(right_image, matrices[:, 1], right_cos, right_sin)
    return jnp.stack([(left_re + right_re) * half_root, (left_im + right_im) * half_root])


def toeplitz_blocks(taps_re, taps_im):
    tap_count = taps_re.shape[-1]
    leading = taps_re.shape[:-1]

    def lay_out(taps):
        padded = jnp.concatenate([taps, jnp.zeros(leading + (tap_count + 1,), taps.dtype)], axis=-1)
        tiled = jnp.tile(padded, (1,) * len(leading) + (tap_count,))
        banded = tiled[..., : 2 * tap_count * tap_count].reshape(
            leading + (tap_count, 2 * tap_count)
        )
        return jnp.swapaxes(banded, -1, -2)

    real_band = lay_out(taps_re)
    imag_band = lay_out(taps_im)
    upper = jnp.concatenate([real_band, imag_band], axis=-1)
    lower = jnp.concatenate([-imag_band, real_band], axis=-1)
    return jnp.concatenate([upper, lower], axis=-2)


def block_filter(extended, matrices, tap_count, per_channel):
    pulses, channels, length = extended.shape[1:]
    blocks = length // tap_count - 1
    pieces = extended.reshape(2, pulses, channels, blocks + 1, tap_count)
    windows = jnp.concatenate([pieces[:, :, :, :-1], pieces[:, :, :, 1:]], axis=4)
    windows = jnp.transpose(windows, (1, 2, 3, 0, 4)).reshape(
        pulses, channels, blocks, 4 * tap_count
    )
    if per_channel:
        output = jnp.einsum("pcnw,cwo->pcno", windows, matrices, preferred_element_type=jnp.float32)
    else:
        output = jnp.einsum("pcnw,wo->pcno", windows, matrices, preferred_element_type=jnp.float32)
    output = output.reshape(pulses, channels, blocks, 2, tap_count)
    return jnp.transpose(output, (3, 0, 1, 2, 4)).reshape(2, pulses, channels, blocks * tap_count)


def local(echoes, beam_angle, interp_table):
    rx_count = lax.axis_size("rx")
    pulse_count = lax.axis_size("pulse")
    rng_place = lax.axis_index("rng")
    rx_place = lax.axis_index("rx")
    pulse_place = lax.axis_index("pulse")
    pulses, channels, length = echoes.shape[1:]
    beam_count = beam_angle.shape[0]
    receivers = channels * rx_count
    channel_ids = rx_place * channels + jnp.arange(channels, dtype=jnp.int32)
    rx_re, rx_im = receiver_taps(channel_ids, RTAPS)
    rx_bands = toeplitz_blocks(rx_re, rx_im)
    chirp_re, chirp_im = chirp_taps(CTAPS)
    chirp_band = toeplitz_blocks(chirp_re, chirp_im)
    extended = extended_2(echoes, (("rng", 3),), RTAPS // 2)
    filtered = block_filter(extended, rx_bands, RTAPS, True).astype(jnp.bfloat16)
    filtered = extended_2(filtered, (("rng", 3),), CTAPS // 2)
    compressed = block_filter(filtered, chirp_band, CTAPS, False).astype(jnp.bfloat16)
    steering_real, steering_imaginary = steering(beam_angle, receivers)
    steer_matrix = jnp.concatenate(
        [
            jnp.concatenate([steering_real, -steering_imaginary], axis=1),
            jnp.concatenate([steering_imaginary, steering_real], axis=1),
        ],
        axis=0,
    )
    arrived = lax.all_to_all(compressed, "rx", split_axis=3, concat_axis=2, tiled=True)
    item_count, recv_count, owned_cols = arrived.shape[1:]
    stacked = jnp.transpose(arrived, (0, 2, 1, 3)).reshape(2 * recv_count, item_count * owned_cols)
    formed = jnp.dot(steer_matrix, stacked, preferred_element_type=jnp.float32)
    picture = formed.reshape(2, beam_count, item_count, owned_cols)
    owned_width = length // rx_count
    positions = (
        rng_place * length + rx_place * owned_width + jnp.arange(owned_width, dtype=jnp.int32)
    )
    for level in range(pulses.bit_length() - 1):
        groups_now = pulses >> level + 1
        node_ids = (pulse_count + pulse_place) * groups_now + jnp.arange(
            groups_now, dtype=jnp.int32
        )
        paired = picture.reshape(2, beam_count, groups_now, 2, owned_width)
        picture = merge_pair(
            paired[:, :, :, 0], paired[:, :, :, 1], node_ids, positions, beam_angle, interp_table
        )
    picture = picture[:, :, 0]
    cross_levels = pulse_count.bit_length() - 1
    piece_width = owned_width // pulse_count
    pieces = picture.reshape(2, beam_count, pulse_count, piece_width)
    spots = positions.reshape(pulse_count, piece_width)
    for level in range(cross_levels):
        parity = jnp.right_shift(pulse_place, level) & 1
        count_now = pieces.shape[2]
        paired = pieces.reshape(2, beam_count, count_now // 2, 2, piece_width)
        kept_half = lax.dynamic_index_in_dim(paired, parity, 3, keepdims=False)
        sent_half = lax.dynamic_index_in_dim(paired, 1 - parity, 3, keepdims=False)
        partner = swapped(sent_half, "pulse", level)
        spot_pairs = spots.reshape(count_now // 2, 2, piece_width)
        spots = lax.dynamic_index_in_dim(spot_pairs, parity, 1, keepdims=False)
        own_part = kept_half.reshape(2, beam_count, -1)
        other_part = partner.reshape(2, beam_count, -1)
        left_image = jnp.where(parity == 0, own_part, other_part)
        right_image = jnp.where(parity == 0, other_part, own_part)
        combine_node_ids = jnp.reshape(
            (pulse_count >> level + 1) + jnp.right_shift(pulse_place, level + 1), (1,)
        )
        merged = merge_pair(
            left_image[:, :, None],
            right_image[:, :, None],
            combine_node_ids,
            spots.reshape(-1),
            beam_angle,
            interp_table,
        )
        flat = merged[:, :, 0]
        pieces = flat.reshape(2, beam_count, count_now // 2, piece_width)
    picture = pieces.reshape(2, beam_count, piece_width)
    return picture


LANES = 128
RX_TILE = 2 * LANES
CHIRP_TILE = 6 * LANES
HALO_TILES = 3
HALO = HALO_TILES * LANES


def vmem():
    return pl.BlockSpec(memory_space=pltpu.VMEM)


def hbm():
    return pl.BlockSpec(memory_space=pltpu.HBM)


def anywhere():
    return pl.BlockSpec(memory_space=pl.ANY)


def rx_bands_table(receivers):
    step = np.arange(RTAPS, dtype=np.float64)
    window = 0.5 - 0.5 * np.cos(full_turn * (step + 0.5) / RTAPS)
    window = window / np.sqrt(np.sum(window * window))
    channel = np.arange(receivers, dtype=np.float64)[:, None] + 1.0
    angle = full_turn * channel * (step - RTAPS // 2) / (4 * RTAPS)
    offset = np.arange(RX_TILE)[:, None] - np.arange(LANES)[None, :]
    inside = (offset >= 0) & (offset < RTAPS)
    place = np.clip(offset, 0, RTAPS - 1)
    bands = [
        np.where(inside, taps[:, place], 0.0)
        for taps in (window * np.cos(angle), window * np.sin(angle))
    ]
    return np.concatenate(bands, axis=-1).astype(ml_dtypes.bfloat16)


def chirp_bands_table():
    offset = np.arange(CTAPS) - CTAPS // 2
    angle = math.pi * np.mod(offset * offset, 2 * CTAPS) / CTAPS
    scale = 1.0 / math.sqrt(CTAPS)
    offset = np.arange(CHIRP_TILE)[:, None] - np.arange(LANES)[None, :] - (LANES - RTAPS // 2)
    inside = (offset >= 0) & (offset < CTAPS)
    place = np.clip(offset, 0, CTAPS - 1)
    bands = [
        np.where(inside, taps[place], 0.0)
        for taps in (np.cos(angle) * scale, -np.sin(angle) * scale)
    ]
    return np.concatenate(bands, axis=-1).astype(ml_dtypes.bfloat16)


def filter_channel(windows, bands, pulses):
    product = jnp.dot(windows, bands, preferred_element_type=jnp.float32)
    product = product.reshape(-1, 2, pulses, 2 * LANES)
    real = product[:, 0, :, :LANES] - product[:, 1, :, LANES:]
    imag = product[:, 0, :, LANES:] + product[:, 1, :, :LANES]
    return real, imag


def mask_kernel(mask_ref):
    lane = lax.broadcasted_iota(jnp.int32, mask_ref.shape, 1)
    mask_ref[...] = jnp.where(lane >= LANES - RTAPS // 2, 1.0, 0.0)


def interior_kernel(echo_ref, bands_ref, mask_ref, filtered_ref, rows_in, rows_out):
    _, pulses, channels, length = echo_ref.shape
    first_channel = lax.axis_index("rx") * channels
    tiles = length // LANES
    group = 2 * pulses
    empty = jnp.zeros(rows_in.shape[1:], jnp.float32)
    rows_in[0] = empty
    rows_in[tiles + 1] = empty
    for part in range(2):
        for pulse in range(pulses):
            where = pl.ds(part * pulses + pulse, channels, stride=group)
            block = echo_ref[part, pulse].astype(jnp.float32)
            for tile in range(tiles):
                rows_in[tile + 1, where, :] = block[:, tile * LANES : (tile + 1) * LANES]
    mask = mask_ref[...]
    for channel in range(channels):
        rows = rows_in[:, channel * group : (channel + 1) * group, :].astype(jnp.bfloat16)
        windows = jnp.concatenate(
            [rows[:-1].reshape(-1, LANES), rows[1:].reshape(-1, LANES)], axis=1
        )
        real, imag = filter_channel(windows, bands_ref[first_channel + channel], pulses)
        for tile in range(tiles + 1):
            tile_re, tile_im = real[tile], imag[tile]
            if tile == 0:
                tile_re, tile_im = tile_re * mask, tile_im * mask
            if tile == tiles:
                tile_re, tile_im = tile_re * (1.0 - mask), tile_im * (1.0 - mask)
            rows_out[tile, pl.ds(channel, pulses, stride=2 * channels), :] = tile_re
            rows_out[tile, pl.ds(channels + channel, pulses, stride=2 * channels), :] = tile_im
    rows = filtered_ref.shape[0]
    nothing = jnp.zeros((rows, (HALO_TILES - 1) * LANES), jnp.bfloat16)
    filtered_ref[:, : (HALO_TILES - 1) * LANES] = nothing
    filtered_ref[:, (HALO_TILES + tiles) * LANES :] = nothing
    for tile in range(tiles + 1):
        spot = (HALO_TILES - 1 + tile) * LANES
        filtered_ref[:, spot : spot + LANES] = rows_out[tile].astype(jnp.bfloat16)


def chirp_piece(filtered_ref, chirp_ref, starts, out_ref):
    windows = [filtered_ref[:, pl.ds(start, CHIRP_TILE)] for start in starts]
    product = jnp.dot(
        jnp.concatenate(windows, axis=0), chirp_ref[...], preferred_element_type=jnp.float32
    )
    pulses, rows, _ = out_ref.shape
    channels = rows // 2
    product = product.reshape(len(starts), pulses, rows, 2 * LANES)
    for tile in range(len(starts)):
        block = product[tile]
        real = block[:, :channels, :LANES] - block[:, channels:, LANES:]
        imag = block[:, :channels, LANES:] + block[:, channels:, :LANES]
        out_ref[:, :, tile * LANES : (tile + 1) * LANES] = jnp.concatenate(
            [real, imag], axis=1
        ).astype(jnp.bfloat16)


def chirp_pieces(filtered_ref, chirp_ref, owner, piece_count, distances, out_ref):
    pulse_place = lax.axis_index("pulse")
    piece_tiles = out_ref.shape[3] // LANES
    for index, distance in enumerate(distances):
        piece = jnp.bitwise_xor(pulse_place, distance)
        first = (owner * piece_count + piece) * piece_tiles
        starts = [pl.multiple_of((first + t) * LANES, LANES) for t in range(piece_tiles)]
        chirp_piece(filtered_ref, chirp_ref, starts, out_ref.at[index])


def edges_kernel(
    plan, inner_ref, echo_ref, across_ref, bands_ref, chirp_ref, filtered_ref, *rest
):
    *send_refs, rows_in, rows_out = rest
    del inner_ref
    _, pulses, channels, length = echo_ref.shape
    first_channel = lax.axis_index("rx") * channels
    tiles = length // LANES
    group = 2 * pulses
    lowest = lax.axis_index("rng") == 0
    far = pl.ds(pl.multiple_of(jnp.where(lowest, 0, length - HALO), LANES), HALO)
    for part in range(2):
        for pulse in range(pulses):
            where = pl.ds(part * pulses + pulse, channels, stride=group)
            edge = across_ref[part, pulse, :, far].astype(jnp.float32)
            near_low = echo_ref[part, pulse, :, :LANES].astype(jnp.float32)
            near_high = echo_ref[part, pulse, :, length - LANES :].astype(jnp.float32)
            pieces = [edge[:, t * LANES : (t + 1) * LANES] for t in range(HALO_TILES)]
            for tile in range(HALO_TILES + 1):
                high = near_high if tile == 0 else pieces[tile - 1]
                low = near_low if tile == HALO_TILES else pieces[tile]
                rows_in[tile, where, :] = jnp.where(lowest, high, low)
    for channel in range(channels):
        rows = rows_in[:, channel * group : (channel + 1) * group, :].astype(jnp.bfloat16)
        windows = jnp.concatenate(
            [rows[:-1].reshape(-1, LANES), rows[1:].reshape(-1, LANES)], axis=1
        )
        real, imag = filter_channel(windows, bands_ref[first_channel + channel], pulses)
        for tile in range(HALO_TILES):
            rows_out[tile, pl.ds(channel, pulses, stride=2 * channels), :] = real[tile]
            rows_out[tile, pl.ds(channels + channel, pulses, stride=2 * channels), :] = imag[tile]
    first = jnp.where(lowest, tiles + HALO_TILES - 1, 0)
    for tile in range(HALO_TILES):
        start = pl.multiple_of((first + tile) * LANES, LANES)
        filtered_ref[:, pl.ds(start, LANES)] = rows_out[tile].astype(jnp.bfloat16)
    piece_count, groups = plan
    for distances, send_ref in zip(groups, send_refs):
        chirp_pieces(
            filtered_ref, chirp_ref, 1 - lax.axis_index("rx"), piece_count, distances, send_ref
        )


def rest_kernel(piece_count, groups, filtered_ref, chirp_ref, after_ref, keep_ref, *send_refs):
    rx_place = lax.axis_index("rx")
    own = list(range(piece_count - 1, -1, -1))
    chirp_pieces(filtered_ref, chirp_ref, rx_place, piece_count, own, keep_ref)
    for distances, send_ref in zip(groups, send_refs):
        chirp_pieces(filtered_ref, chirp_ref, 1 - rx_place, piece_count, distances, send_ref)


def turn_parts(step):
    shifted = step + 128
    angle = (jnp.bitwise_and(shifted, 255) - 128).astype(jnp.float32) * (full_turn / 1024.0)
    quarter = jnp.right_shift(shifted, 8)
    square = angle * angle
    cosine = 1.0 + square * (-1 / 2 + square * (1 / 24 + square * (-1 / 720 + square * (1 / 40320))))
    sine = angle * (1.0 + square * (-1 / 6 + square * (1 / 120 + square * (-1 / 5040))))
    odd = jnp.bitwise_and(quarter, 1) == 1
    real = jnp.where(odd, sine, cosine)
    imag = jnp.where(odd, cosine, sine)
    real = jnp.where(jnp.bitwise_and(quarter + 1, 2) == 2, -real, real)
    imag = jnp.where(jnp.bitwise_and(quarter, 2) == 2, -imag, imag)
    return real, imag


def turned(real, imag, phase_re, phase_im):
    return phase_re * real - phase_im * imag, phase_im * real + phase_re * imag


def as_column(row):
    count = row.shape[1]
    first = lax.broadcasted_iota(jnp.int32, (count, count), 0)
    second = lax.broadcasted_iota(jnp.int32, (count, count), 1)
    spread = jnp.where(first == second, row.astype(jnp.float32), 0.0)
    return jnp.sum(spread, axis=1, keepdims=True).astype(jnp.int32)


def interp_matrix(code):
    beams = code.shape[0]
    angle_bin = lax.broadcasted_iota(jnp.int32, (beams, beams), 0)
    column = lax.broadcasted_iota(jnp.int32, (beams, beams), 1)
    half = 2 * beams
    away = jnp.bitwise_and(4 * (column - angle_bin + 1) - code + half, 4 * beams - 1) - half
    away = jnp.abs(away.astype(jnp.float32)) * 0.25
    near = (1.0 - away * away) * (2.0 - away) * 0.5
    far = (1.0 - away) * (2.0 - away) * (3.0 - away) * (1.0 / 6.0)
    matrix = jnp.where(away < 1.0, near, jnp.where(away < 2.0, far, 0.0))
    return matrix.astype(jnp.bfloat16)


def code_columns(codes_ref, rows):
    picked = [codes_ref[pl.ds(row, 1), :] for row in rows]
    picked = jnp.concatenate(picked, axis=0).astype(jnp.float32)
    spare = -len(rows) % 8
    if spare:
        picked = jnp.concatenate([picked, jnp.zeros((spare, picked.shape[1]), jnp.float32)], axis=0)
    return picked.T.astype(jnp.int32)


def tables_kernel(sizes, angle_ref, codes_ref, first_ref, inner_ref, phase_ref):
    pulses, channels, rx_count, width = sizes
    rng_place = lax.axis_index("rng")
    rx_place = lax.axis_index("rx")
    pulse_place = lax.axis_index("pulse")
    beams = angle_ref.shape[1]
    piece_count = phase_ref.shape[0]
    piece_tiles = phase_ref.shape[4] // LANES
    angle = as_column(angle_ref[...])
    factors = []
    rows = []
    now = pulses
    while now > 1:
        base = now * piece_count + pulse_place * now
        factors.append(base + 1)
        rows.extend(base + index for index in range(now))
        now //= 2
    codes = code_columns(codes_ref, rows)
    column = lax.broadcasted_iota(jnp.int32, (1, 4 * channels * 2), 1)
    within = jnp.bitwise_and(column, 4 * channels - 1)
    owner = jnp.bitwise_xor(rx_place, jnp.where(within >= 2 * channels, 1, 0))
    receiver = owner * channels + jnp.bitwise_and(column, channels - 1)
    is_imag = jnp.bitwise_and(within, channels) != 0
    scale = 1.0 / math.sqrt(channels * rx_count)
    steer_re, steer_im = turn_parts(jnp.bitwise_and(angle * receiver, 1023))
    steer_re = (steer_re * scale).astype(jnp.bfloat16).astype(jnp.float32)
    steer_im = (-steer_im * scale).astype(jnp.bfloat16).astype(jnp.float32)
    steer = jnp.concatenate(
        [
            jnp.where(is_imag, -steer_im, steer_re).astype(jnp.bfloat16),
            jnp.where(is_imag, steer_re, steer_im).astype(jnp.bfloat16),
        ],
        axis=1,
    )
    low_half = column >= 4 * channels
    entries = 8 * channels
    matrices = [interp_matrix(codes[:, index : index + 1]) for index in range(len(rows))]
    composed = jnp.dot(
        jnp.concatenate(matrices[:pulses], axis=0), steer, preferred_element_type=jnp.float32
    )
    for index in range(pulses):
        for part in range(2):
            value = composed[
                index * beams : (index + 1) * beams, part * entries : (part + 1) * entries
            ]
            high = value.astype(jnp.bfloat16).astype(jnp.float32)
            first_ref[index, part * beams : (part + 1) * beams, :] = jnp.where(
                low_half, value - high, high
            ).astype(jnp.bfloat16)
    for index, matrix in enumerate(matrices[pulses:]):
        inner_ref[index] = matrix
    lane = lax.broadcasted_iota(jnp.int32, (1, LANES), 1)
    block = (rng_place * rx_count + rx_place) * width + 1
    base = jnp.bitwise_and(angle * (block + lane), 1023)
    for slot, factor in enumerate([1, *factors]):
        scale = half_root if slot else 1.0
        real, imag = turn_parts(jnp.bitwise_and(base * factor, 1023))
        real, imag = real * scale, imag * scale
        step = turn_parts(jnp.bitwise_and(angle * (factor * LANES), 1023))
        for tile in range(piece_count * piece_tiles):
            index = piece_count - 1 - jnp.bitwise_xor(pulse_place, tile // piece_tiles)
            start = tile % piece_tiles * LANES
            phase_ref[index, slot, 0, :, start : start + LANES] = real
            phase_ref[index, slot, 1, :, start : start + LANES] = imag
            real, imag = turned(real, imag, *step)


def outer_levels(piece_count):
    return [piece_count >> level for level in range(piece_count.bit_length() - 1)]


def outer_tables_kernel(sizes, angle_ref, codes_ref, after_ref, outer_ref, phase_ref):
    rx_count, width, piece_count = sizes
    rng_place = lax.axis_index("rng")
    rx_place = lax.axis_index("rx")
    pulse_place = lax.axis_index("pulse")
    piece_width = phase_ref.shape[3]
    angle = as_column(angle_ref[...])
    lane = lax.broadcasted_iota(jnp.int32, (1, piece_width), 1)
    block = (rng_place * rx_count + rx_place) * width + 1
    base = jnp.bitwise_and(angle * (block + pulse_place * piece_width + lane), 1023)
    rows = [row + level for level in outer_levels(piece_count) for row in range(level)]
    codes = code_columns(codes_ref, rows)
    slot = 0
    now = piece_count
    while now > 1:
        for index in range(now):
            outer_ref[slot] = interp_matrix(codes[:, slot : slot + 1])
            real, imag = turn_parts(jnp.bitwise_and(base * (now + index + 1), 1023))
            phase_ref[slot, 0] = real * half_root
            phase_ref[slot, 1] = imag * half_root
            slot += 1
        now //= 2


ROWS = 8


def inner_kernel(index, other, keep_ref, other_ref, first_ref, inner_ref, phase_ref, *rest):
    out_ref, moved_ref, picture_ref, level_ref = rest[-4:]
    pulses = keep_ref.shape[1]
    beams = inner_ref.shape[1]
    columns = keep_ref.shape[3]
    for image in range(pulses):
        rows = jnp.concatenate([keep_ref[index, image], other_ref[other, image]], axis=0)
        moved_ref[image] = jnp.dot(
            first_ref[image],
            jnp.concatenate([rows, rows], axis=0),
            preferred_element_type=jnp.float32,
        )

    def merge(count, level, read, write):
        for row in range(0, beams, ROWS):
            span = slice(row, row + ROWS)
            step = (phase_ref[index, 0, 0, span], phase_ref[index, 0, 1, span])
            phase = (phase_ref[index, level, 0, span], phase_ref[index, level, 1, span])
            for image in range(count):
                term = turned(*read(image, row), *phase)
                if image & 1:
                    write(image // 2, row, left[0] + term[0], left[1] + term[1])
                left = term
                if image < count - 1:
                    phase = turned(*phase, *step)

    def write_picture(image, row, real, imag):
        picture_ref[image, row : row + ROWS, :columns] = real
        picture_ref[image, row : row + ROWS, columns:] = imag

    def write_out(image, row, real, imag):
        picture_ref[0, row : row + ROWS, :columns] = real
        picture_ref[0, row : row + ROWS, columns:] = imag

    merge(
        pulses,
        1,
        lambda image, row: (
            moved_ref[image, row : row + ROWS],
            moved_ref[image, beams + row : beams + row + ROWS],
        ),
        write_picture,
    )
    slot = 0
    level = 2
    count = pulses // 2
    while count > 1:
        for image in range(count):
            level_ref[image] = jnp.dot(
                inner_ref[slot],
                picture_ref[image].astype(jnp.bfloat16),
                preferred_element_type=jnp.float32,
            )
            slot += 1
        merge(
            count,
            level,
            lambda image, row: (
                level_ref[image, row : row + ROWS, :columns],
                level_ref[image, row : row + ROWS, columns:],
            ),
            write_picture,
        )
        count //= 2
        level += 1
    out_ref[0] = picture_ref[0, :, :columns].astype(jnp.bfloat16)
    out_ref[1] = picture_ref[0, :, columns:].astype(jnp.bfloat16)


def outer_kernel(outer_ref, phase_ref, *rest):
    image_refs, out_ref = rest[-2::-1], rest[-1]
    pulse_place = lax.axis_index("pulse")
    pictures = [(ref[0], ref[1]) for ref in image_refs]
    base = 0
    level = 0
    while len(pictures) > 1:
        count = len(pictures)
        place = jnp.right_shift(pulse_place, level)
        merged = []
        for distance, (real, imag) in enumerate(pictures):
            slot = base + jnp.bitwise_xor(place, distance)
            matrix = outer_ref[slot]
            moved_re = jnp.dot(
                matrix, real.astype(jnp.bfloat16), preferred_element_type=jnp.float32
            )
            moved_im = jnp.dot(
                matrix, imag.astype(jnp.bfloat16), preferred_element_type=jnp.float32
            )
            merged.append(turned(moved_re, moved_im, phase_ref[slot, 0], phase_ref[slot, 1]))
            if distance & 1:
                right, left = merged.pop(), merged.pop()
                merged.append((left[0] + right[0], left[1] + right[1]))
        pictures = merged
        base += count
        level += 1
    out_ref[0] = pictures[0][0]
    out_ref[1] = pictures[0][1]


def cost(micros):
    return pl.CostEstimate(
        flops=int(micros * 1.1e9), bytes_accessed=int(micros * 3.6e6), transcendentals=0
    )


PARAMS = dict(compiler_params=pltpu.CompilerParams(vmem_limit_bytes=40 * 1024 * 1024))


def send_groups(pulse_count):
    last = pulse_count - 1
    if pulse_count < 4:
        return [[distance] for distance in range(last, -1, -1)]
    return [[last, last - 1], list(range(last - 2, -1, -1))]


def fast(echoes, beam_angle, interp_table):
    rx_count = lax.axis_size("rx")
    pulse_count = lax.axis_size("pulse")
    _, pulses, channels, length = echoes.shape
    beams = beam_angle.shape[0]
    width = length // rx_count
    piece_width = width // pulse_count
    piece_tiles = piece_width // LANES
    rows = 2 * channels
    group = 2 * pulses
    bands = jnp.asarray(rx_bands_table(channels * rx_count))
    chirp = jnp.asarray(chirp_bands_table())
    angles = beam_angle.reshape(1, beams)
    codes = interp_table.reshape(-1, beams)
    bf16 = jnp.bfloat16
    f32 = jnp.float32
    shape = jax.ShapeDtypeStruct
    across = swapped(echoes, "rng", 0)
    mask = pl.pallas_call(
        mask_kernel,
        out_shape=shape((pulses, LANES), f32),
        out_specs=vmem(),
        name="mask",
        cost_estimate=cost(10.0),
        **PARAMS,
    )()
    tiles = length // LANES
    filtered_shape = shape((rows * pulses, (tiles + 2 * HALO_TILES - 1) * LANES), bf16)
    filtered = pl.pallas_call(
        interior_kernel,
        out_shape=filtered_shape,
        in_specs=[vmem()] * 3,
        out_specs=vmem(),
        scratch_shapes=[
            pltpu.VMEM((tiles + 2, channels * group, LANES), f32),
            pltpu.VMEM((tiles + 1, rows * pulses, LANES), f32),
        ],
        name="interior",
        **PARAMS,
    )(echoes, bands, mask)

    def pieces(count):
        return shape((count, pulses, rows, piece_width), bf16)

    last = pulse_count - 1
    groups = send_groups(pulse_count)
    filtered, first_sent = pl.pallas_call(
        functools.partial(edges_kernel, (pulse_count, groups[:1])),
        out_shape=[filtered_shape, pieces(len(groups[0]))],
        in_specs=[vmem()] * 5,
        out_specs=[vmem()] * 2,
        scratch_shapes=[
            pltpu.VMEM((HALO_TILES + 1, channels * group, LANES), f32),
            pltpu.VMEM((HALO_TILES, rows * pulses, LANES), f32),
        ],
        input_output_aliases={0: 0},
        name="edges",
        **PARAMS,
    )(filtered, echoes, across, bands, chirp)
    levels = pulses.bit_length() - 1
    first, inner, phase = pl.pallas_call(
        functools.partial(tables_kernel, (pulses, channels, rx_count, width)),
        out_shape=[
            shape((pulses, 2 * beams, 8 * channels), bf16),
            shape((pulses - 2, beams, beams), bf16),
            shape((pulse_count, levels + 1, 2, beams, piece_width), f32),
        ],
        in_specs=[vmem()] * 2,
        out_specs=[vmem()] * 3,
        name="tables",
        **PARAMS,
    )(angles, codes)
    kept, *sent = pl.pallas_call(
        functools.partial(rest_kernel, pulse_count, groups[1:]),
        out_shape=[pieces(pulse_count)] + [pieces(len(members)) for members in groups[1:]],
        in_specs=[vmem()] * 2 + [anywhere()],
        out_specs=[vmem()] * len(groups),
        name="rest",
        **PARAMS,
    )(filtered, chirp, first)
    received = {}
    for members, piece in zip(groups, [first_sent, *sent]):
        piece = swapped(piece, "rx", 0)
        for index, distance in enumerate(members):
            received[distance] = (piece, index)
    images = [None] * pulse_count

    def merge(distance):
        other, place = received[distance]
        return pl.pallas_call(
            functools.partial(inner_kernel, last - distance, place),
            out_shape=shape((2, beams, piece_width), bf16),
            in_specs=[vmem()] * 5,
            out_specs=vmem(),
            scratch_shapes=[
                pltpu.VMEM((pulses, 2 * beams, piece_width), f32),
                pltpu.VMEM((pulses // 2, beams, 2 * piece_width), f32),
                pltpu.VMEM((pulses // 2, beams, 2 * piece_width), f32),
            ],
            name="inner",
            **PARAMS,
        )(kept, other, first, inner, phase)

    for distance in [*range(1, pulse_count), 0]:
        images[distance] = merge(distance)
    for distance in range(1, pulse_count):
        pairs = [(i, i ^ distance) for i in range(pulse_count)]
        images[distance] = lax.ppermute(images[distance], "pulse", pairs)
    outer_count = 2 * pulse_count - 2
    outer, outer_phase = pl.pallas_call(
        functools.partial(outer_tables_kernel, (rx_count, width, pulse_count)),
        out_shape=[
            shape((outer_count, beams, beams), bf16),
            shape((outer_count, 2, beams, piece_width), f32),
        ],
        in_specs=[vmem(), vmem(), anywhere()],
        out_specs=[vmem()] * 2,
        name="outer_tables",
        **PARAMS,
    )(angles, codes, images[0])
    return pl.pallas_call(
        outer_kernel,
        out_shape=shape((2, beams, piece_width), f32),
        in_specs=[vmem()] * (2 + pulse_count),
        out_specs=vmem(),
        name="outer",
        **PARAMS,
    )(outer, outer_phase, *images[::-1])


def power_of_two(count):
    return count > 0 and count & (count - 1) == 0


def per_device(echoes, beam_angle, interp_table):
    _, pulses, channels, length = echoes.shape
    rx_count = lax.axis_size("rx")
    pulse_count = lax.axis_size("pulse")
    piece_width = length // (rx_count * pulse_count)
    if (
        lax.axis_size("rng") == 2
        and rx_count == 2
        and channels == 8
        and pulses == 8
        and power_of_two(pulse_count)
        and pulse_count > 1
        and power_of_two(beam_angle.shape[0])
        and beam_angle.shape[0] % 16 == 0
        and piece_width % LANES == 0
    ):
        return fast(echoes, beam_angle, interp_table)
    return local(echoes, beam_angle, interp_table)


def solution(mesh):
    placed = (P(None, ("slab", "pulse"), "rx", "rng"), P(), P())
    return jax.shard_map(
        per_device,
        mesh=mesh,
        in_specs=placed,
        out_specs=P(None, "slab", ("rng", "rx", "pulse")),
        check_vma=False,
    )
```

```python
import functools
import math

import jax
import jax.numpy as jnp
import ml_dtypes
import numpy as np
from jax import lax
from jax.experimental import pallas as pl
from jax.experimental.pallas import tpu as pltpu
from jax.sharding import PartitionSpec as P

RTAPS = 64
CTAPS = 512


half_root = 0.7071067811865476
full_turn = 2.0 * math.pi


def extended_2(block, sides, width):
    for axis, dim in sides:
        count = lax.axis_size(axis)
        forward = [(i, i + 1) for i in range(count - 1)]
        backward = [(target, source) for source, target in forward]
        low = lax.ppermute(
            lax.slice_in_dim(block, block.shape[dim] - width, None, axis=dim), axis, forward
        )
        high = lax.ppermute(lax.slice_in_dim(block, 0, width, axis=dim), axis, backward)
        block = jnp.concatenate([low, block, high], axis=dim)
    return block


def swapped(x, axis, distance):
    return lax.ppermute(x, axis, [(i, i ^ 1 << distance) for i in range(lax.axis_size(axis))])


def receiver_taps(channel_ids, tap_count):
    tap_index = jnp.arange(tap_count, dtype=jnp.float32)
    window = 0.5 - 0.5 * jnp.cos(full_turn * (tap_index + 0.5) / tap_count)
    window = window / jnp.sqrt(jnp.sum(window * window))
    channel = channel_ids.astype(jnp.float32)[:, None] + 1.0
    angle = full_turn * channel * (tap_index - tap_count // 2) / (4 * tap_count)
    return (
        (window * jnp.cos(angle)).astype(jnp.bfloat16),
        (window * jnp.sin(angle)).astype(jnp.bfloat16),
    )


def chirp_taps(tap_count):
    offset = jnp.arange(tap_count, dtype=jnp.int32) - tap_count // 2
    phase_step = jnp.mod(offset * offset, 2 * tap_count).astype(jnp.float32)
    angle = math.pi * phase_step / tap_count
    scale = 1.0 / math.sqrt(tap_count)
    return (
        (jnp.cos(angle) * scale).astype(jnp.bfloat16),
        (-jnp.sin(angle) * scale).astype(jnp.bfloat16),
    )


def steering(beam_angle, receivers):
    channel = jnp.arange(receivers, dtype=jnp.int32)
    turns = jnp.mod(beam_angle[:, None] * channel[None, :], 1024).astype(jnp.float32)
    angle = full_turn * turns / 1024.0
    scale = 1.0 / math.sqrt(receivers)
    return (
        (jnp.cos(angle) * scale).astype(jnp.bfloat16),
        (-jnp.sin(angle) * scale).astype(jnp.bfloat16),
    )


def interp_matrices(codes, beam_count):
    shifted = codes // 4 - 1
    fraction = jnp.mod(codes, 4).astype(jnp.float32) / 4.0
    weights = (
        -fraction * (fraction - 1.0) * (fraction - 2.0) / 6.0,
        (fraction + 1.0) * (fraction - 1.0) * (fraction - 2.0) / 2.0,
        -(fraction + 1.0) * fraction * (fraction - 2.0) / 2.0,
        (fraction + 1.0) * fraction * (fraction - 1.0) / 6.0,
    )
    columns = jnp.arange(beam_count, dtype=jnp.int32)
    matrices = jnp.zeros(codes.shape + (beam_count,), jnp.float32)
    for tap_index in range(4):
        target = jnp.mod(columns + shifted + tap_index - 1, beam_count)
        matrices = matrices + weights[tap_index][..., None] * (target[..., None] == columns).astype(
            jnp.float32
        )
    return matrices


def phases(node_ids, positions, beam_angle, side):
    base = jnp.mod(beam_angle[:, None] * (positions[None, :] + 1), 1024)
    factor = 2 * node_ids + side + 1
    turns = jnp.mod(base[:, None, :] * factor[None, :, None], 1024).astype(jnp.float32)
    angle = full_turn * turns / 1024.0
    return (jnp.cos(angle), jnp.sin(angle))


def side_term(picture, matrices, cosine, sine):
    moved = jnp.einsum("gqa,cagr->cqgr", matrices, picture, precision=lax.Precision.HIGHEST)
    return (cosine * moved[0] - sine * moved[1], sine * moved[0] + cosine * moved[1])


def merge_pair(left_image, right_image, node_ids, positions, beam_angle, interp_table):
    matrices = interp_matrices(interp_table[node_ids], left_image.shape[1])
    left_cos, left_sin = phases(node_ids, positions, beam_angle, 0)
    right_cos, right_sin = phases(node_ids, positions, beam_angle, 1)
    left_re, left_im = side_term(left_image, matrices[:, 0], left_cos, left_sin)
    right_re, right_im = side_term(right_image, matrices[:, 1], right_cos, right_sin)
    return jnp.stack([(left_re + right_re) * half_root, (left_im + right_im) * half_root])


def toeplitz_blocks(taps_re, taps_im):
    tap_count = taps_re.shape[-1]
    leading = taps_re.shape[:-1]

    def lay_out(taps):
        padded = jnp.concatenate([taps, jnp.zeros(leading + (tap_count + 1,), taps.dtype)], axis=-1)
        tiled = jnp.tile(padded, (1,) * len(leading) + (tap_count,))
        banded = tiled[..., : 2 * tap_count * tap_count].reshape(
            leading + (tap_count, 2 * tap_count)
        )
        return jnp.swapaxes(banded, -1, -2)

    real_band = lay_out(taps_re)
    imag_band = lay_out(taps_im)
    upper = jnp.concatenate([real_band, imag_band], axis=-1)
    lower = jnp.concatenate([-imag_band, real_band], axis=-1)
    return jnp.concatenate([upper, lower], axis=-2)


def block_filter(extended, matrices, tap_count, per_channel):
    pulses, channels, length = extended.shape[1:]
    blocks = length // tap_count - 1
    pieces = extended.reshape(2, pulses, channels, blocks + 1, tap_count)
    windows = jnp.concatenate([pieces[:, :, :, :-1], pieces[:, :, :, 1:]], axis=4)
    windows = jnp.transpose(windows, (1, 2, 3, 0, 4)).reshape(
        pulses, channels, blocks, 4 * tap_count
    )
    if per_channel:
        output = jnp.einsum("pcnw,cwo->pcno", windows, matrices, preferred_element_type=jnp.float32)
    else:
        output = jnp.einsum("pcnw,wo->pcno", windows, matrices, preferred_element_type=jnp.float32)
    output = output.reshape(pulses, channels, blocks, 2, tap_count)
    return jnp.transpose(output, (3, 0, 1, 2, 4)).reshape(2, pulses, channels, blocks * tap_count)


def local(echoes, beam_angle, interp_table):
    rx_count = lax.axis_size("rx")
    pulse_count = lax.axis_size("pulse")
    rng_place = lax.axis_index("rng")
    rx_place = lax.axis_index("rx")
    pulse_place = lax.axis_index("pulse")
    pulses, channels, length = echoes.shape[1:]
    beam_count = beam_angle.shape[0]
    receivers = channels * rx_count
    channel_ids = rx_place * channels + jnp.arange(channels, dtype=jnp.int32)
    rx_re, rx_im = receiver_taps(channel_ids, RTAPS)
    rx_bands = toeplitz_blocks(rx_re, rx_im)
    chirp_re, chirp_im = chirp_taps(CTAPS)
    chirp_band = toeplitz_blocks(chirp_re, chirp_im)
    extended = extended_2(echoes, (("rng", 3),), RTAPS // 2)
    filtered = block_filter(extended, rx_bands, RTAPS, True).astype(jnp.bfloat16)
    filtered = extended_2(filtered, (("rng", 3),), CTAPS // 2)
    compressed = block_filter(filtered, chirp_band, CTAPS, False).astype(jnp.bfloat16)
    steering_real, steering_imaginary = steering(beam_angle, receivers)
    steer_matrix = jnp.concatenate(
        [
            jnp.concatenate([steering_real, -steering_imaginary], axis=1),
            jnp.concatenate([steering_imaginary, steering_real], axis=1),
        ],
        axis=0,
    )
    arrived = lax.all_to_all(compressed, "rx", split_axis=3, concat_axis=2, tiled=True)
    item_count, recv_count, owned_cols = arrived.shape[1:]
    stacked = jnp.transpose(arrived, (0, 2, 1, 3)).reshape(2 * recv_count, item_count * owned_cols)
    formed = jnp.dot(steer_matrix, stacked, preferred_element_type=jnp.float32)
    picture = formed.reshape(2, beam_count, item_count, owned_cols)
    owned_width = length // rx_count
    positions = (
        rng_place * length + rx_place * owned_width + jnp.arange(owned_width, dtype=jnp.int32)
    )
    for level in range(pulses.bit_length() - 1):
        groups_now = pulses >> level + 1
        node_ids = (pulse_count + pulse_place) * groups_now + jnp.arange(
            groups_now, dtype=jnp.int32
        )
        paired = picture.reshape(2, beam_count, groups_now, 2, owned_width)
        picture = merge_pair(
            paired[:, :, :, 0], paired[:, :, :, 1], node_ids, positions, beam_angle, interp_table
        )
    picture = picture[:, :, 0]
    cross_levels = pulse_count.bit_length() - 1
    piece_width = owned_width // pulse_count
    pieces = picture.reshape(2, beam_count, pulse_count, piece_width)
    spots = positions.reshape(pulse_count, piece_width)
    for level in range(cross_levels):
        parity = jnp.right_shift(pulse_place, level) & 1
        count_now = pieces.shape[2]
        paired = pieces.reshape(2, beam_count, count_now // 2, 2, piece_width)
        kept_half = lax.dynamic_index_in_dim(paired, parity, 3, keepdims=False)
        sent_half = lax.dynamic_index_in_dim(paired, 1 - parity, 3, keepdims=False)
        partner = swapped(sent_half, "pulse", level)
        spot_pairs = spots.reshape(count_now // 2, 2, piece_width)
        spots = lax.dynamic_index_in_dim(spot_pairs, parity, 1, keepdims=False)
        own_part = kept_half.reshape(2, beam_count, -1)
        other_part = partner.reshape(2, beam_count, -1)
        left_image = jnp.where(parity == 0, own_part, other_part)
        right_image = jnp.where(parity == 0, other_part, own_part)
        combine_node_ids = jnp.reshape(
            (pulse_count >> level + 1) + jnp.right_shift(pulse_place, level + 1), (1,)
        )
        merged = merge_pair(
            left_image[:, :, None],
            right_image[:, :, None],
            combine_node_ids,
            spots.reshape(-1),
            beam_angle,
            interp_table,
        )
        flat = merged[:, :, 0]
        pieces = flat.reshape(2, beam_count, count_now // 2, piece_width)
    picture = pieces.reshape(2, beam_count, piece_width)
    return picture


LANES = 128
RX_TILE = 2 * LANES
CHIRP_TILE = 6 * LANES
HALO_TILES = 3
HALO = HALO_TILES * LANES


def vmem():
    return pl.BlockSpec(memory_space=pltpu.VMEM)


def hbm():
    return pl.BlockSpec(memory_space=pltpu.HBM)


def anywhere():
    return pl.BlockSpec(memory_space=pl.ANY)


def chirp_bands_table():
    offset = np.arange(CTAPS) - CTAPS // 2
    angle = math.pi * np.mod(offset * offset, 2 * CTAPS) / CTAPS
    scale = 1.0 / math.sqrt(CTAPS)
    offset = np.arange(CHIRP_TILE)[:, None] - np.arange(LANES)[None, :] - (LANES - RTAPS // 2)
    inside = (offset >= 0) & (offset < CTAPS)
    place = np.clip(offset, 0, CTAPS - 1)
    bands = [
        np.where(inside, taps[place], 0.0)
        for taps in (np.cos(angle) * scale, -np.sin(angle) * scale)
    ]
    return np.concatenate(bands, axis=-1).astype(ml_dtypes.bfloat16)


def filter_channel(windows, bands, pulses):
    product = jnp.dot(windows, bands, preferred_element_type=jnp.float32)
    product = product.reshape(-1, 2, pulses, 2 * LANES)
    real = product[:, 0, :, :LANES] - product[:, 1, :, LANES:]
    imag = product[:, 0, :, LANES:] + product[:, 1, :, :LANES]
    return real, imag


def bands_kernel(bands_ref):
    channels = bands_ref.shape[0]
    first_channel = lax.axis_index("rx") * channels
    lane = lax.broadcasted_iota(jnp.int32, (channels, LANES), 1)
    channel = lax.broadcasted_iota(jnp.int32, (channels, LANES), 0) + first_channel + 1
    tap = jnp.bitwise_and(LANES - lane, LANES - 1)
    unit = 1024 // RTAPS
    window = 0.5 - 0.5 * turn_parts(tap * unit + unit // 2)[0]
    window = jnp.where(tap < RTAPS, window * (1.0 / math.sqrt(RTAPS * 3 / 8)), 0.0)
    turn = channel * (tap - RTAPS // 2) * (1024 // (4 * RTAPS))
    row = lax.broadcasted_iota(jnp.int32, (LANES, LANES), 0)
    upper = lax.broadcasted_iota(jnp.int32, (LANES, LANES), 1) <= row
    for part, wave in enumerate(turn_parts(jnp.bitwise_and(turn, 1023))):
        taps = window * wave
        span = slice(part * LANES, (part + 1) * LANES)
        for index in range(channels):
            spread = jnp.broadcast_to(taps[index : index + 1], (LANES, LANES))
            rolled = pltpu.roll(spread, 0, 1, stride=1, stride_axis=0)
            bands_ref[index, :LANES, span] = jnp.where(upper, rolled, 0.0).astype(jnp.bfloat16)
            bands_ref[index, LANES:, span] = jnp.where(upper, 0.0, rolled).astype(jnp.bfloat16)


def interior_kernel(echo_ref, bands_ref, filtered_ref, rows_in, rows_out):
    _, pulses, channels, length = echo_ref.shape
    tiles = length // LANES
    group = 2 * pulses
    empty = jnp.zeros(rows_in.shape[1:], jnp.float32)
    rows_in[0] = empty
    rows_in[tiles + 1] = empty
    for part in range(2):
        for pulse in range(pulses):
            where = pl.ds(part * pulses + pulse, channels, stride=group)
            block = echo_ref[part, pulse].astype(jnp.float32)
            for tile in range(tiles):
                rows_in[tile + 1, where, :] = block[:, tile * LANES : (tile + 1) * LANES]
    lane = lax.broadcasted_iota(jnp.int32, (pulses, LANES), 1)
    mask = jnp.where(lane >= LANES - RTAPS // 2, 1.0, 0.0)
    for channel in range(channels):
        rows = rows_in[:, channel * group : (channel + 1) * group, :].astype(jnp.bfloat16)
        windows = jnp.concatenate(
            [rows[:-1].reshape(-1, LANES), rows[1:].reshape(-1, LANES)], axis=1
        )
        real, imag = filter_channel(windows, bands_ref[channel], pulses)
        for tile in range(tiles + 1):
            tile_re, tile_im = real[tile], imag[tile]
            if tile == 0:
                tile_re, tile_im = tile_re * mask, tile_im * mask
            if tile == tiles:
                tile_re, tile_im = tile_re * (1.0 - mask), tile_im * (1.0 - mask)
            rows_out[tile, pl.ds(channel, pulses, stride=2 * channels), :] = tile_re
            rows_out[tile, pl.ds(channels + channel, pulses, stride=2 * channels), :] = tile_im
    rows = filtered_ref.shape[0]
    nothing = jnp.zeros((rows, (HALO_TILES - 1) * LANES), jnp.bfloat16)
    filtered_ref[:, : (HALO_TILES - 1) * LANES] = nothing
    filtered_ref[:, (HALO_TILES + tiles) * LANES :] = nothing
    for tile in range(tiles + 1):
        spot = (HALO_TILES - 1 + tile) * LANES
        filtered_ref[:, spot : spot + LANES] = rows_out[tile].astype(jnp.bfloat16)


def chirp_piece(filtered_ref, chirp_ref, starts, out_ref):
    windows = [filtered_ref[:, pl.ds(start, CHIRP_TILE)] for start in starts]
    product = jnp.dot(
        jnp.concatenate(windows, axis=0), chirp_ref[...], preferred_element_type=jnp.float32
    )
    pulses, rows, _ = out_ref.shape
    channels = rows // 2
    product = product.reshape(len(starts), pulses, rows, 2 * LANES)
    for tile in range(len(starts)):
        block = product[tile]
        real = block[:, :channels, :LANES] - block[:, channels:, LANES:]
        imag = block[:, :channels, LANES:] + block[:, channels:, :LANES]
        out_ref[:, :, tile * LANES : (tile + 1) * LANES] = jnp.concatenate(
            [real, imag], axis=1
        ).astype(jnp.bfloat16)


def chirp_pieces(filtered_ref, chirp_ref, owner, piece_count, distances, out_ref):
    pulse_place = lax.axis_index("pulse")
    piece_tiles = out_ref.shape[3] // LANES
    for index, distance in enumerate(distances):
        piece = jnp.bitwise_xor(pulse_place, distance)
        first = (owner * piece_count + piece) * piece_tiles
        starts = [pl.multiple_of((first + t) * LANES, LANES) for t in range(piece_tiles)]
        chirp_piece(filtered_ref, chirp_ref, starts, out_ref.at[index])


def edges_kernel(
    plan, inner_ref, echo_ref, across_ref, bands_ref, chirp_ref, filtered_ref, *rest
):
    *send_refs, rows_in, rows_out = rest
    del inner_ref
    _, pulses, channels, length = echo_ref.shape
    tiles = length // LANES
    group = 2 * pulses
    lowest = lax.axis_index("rng") == 0
    far = pl.ds(pl.multiple_of(jnp.where(lowest, 0, length - HALO), LANES), HALO)
    for part in range(2):
        for pulse in range(pulses):
            where = pl.ds(part * pulses + pulse, channels, stride=group)
            edge = across_ref[part, pulse, :, far].astype(jnp.float32)
            near_low = echo_ref[part, pulse, :, :LANES].astype(jnp.float32)
            near_high = echo_ref[part, pulse, :, length - LANES :].astype(jnp.float32)
            pieces = [edge[:, t * LANES : (t + 1) * LANES] for t in range(HALO_TILES)]
            for tile in range(HALO_TILES + 1):
                high = near_high if tile == 0 else pieces[tile - 1]
                low = near_low if tile == HALO_TILES else pieces[tile]
                rows_in[tile, where, :] = jnp.where(lowest, high, low)
    for channel in range(channels):
        rows = rows_in[:, channel * group : (channel + 1) * group, :].astype(jnp.bfloat16)
        windows = jnp.concatenate(
            [rows[:-1].reshape(-1, LANES), rows[1:].reshape(-1, LANES)], axis=1
        )
        real, imag = filter_channel(windows, bands_ref[channel], pulses)
        for tile in range(HALO_TILES):
            rows_out[tile, pl.ds(channel, pulses, stride=2 * channels), :] = real[tile]
            rows_out[tile, pl.ds(channels + channel, pulses, stride=2 * channels), :] = imag[tile]
    first = jnp.where(lowest, tiles + HALO_TILES - 1, 0)
    for tile in range(HALO_TILES):
        start = pl.multiple_of((first + tile) * LANES, LANES)
        filtered_ref[:, pl.ds(start, LANES)] = rows_out[tile].astype(jnp.bfloat16)
    piece_count, groups = plan
    for distances, send_ref in zip(groups, send_refs):
        chirp_pieces(
            filtered_ref, chirp_ref, 1 - lax.axis_index("rx"), piece_count, distances, send_ref
        )


def rest_kernel(piece_count, groups, filtered_ref, chirp_ref, after_ref, keep_ref, *send_refs):
    rx_place = lax.axis_index("rx")
    own = list(range(piece_count - 1, -1, -1))
    chirp_pieces(filtered_ref, chirp_ref, rx_place, piece_count, own, keep_ref)
    for distances, send_ref in zip(groups, send_refs):
        chirp_pieces(filtered_ref, chirp_ref, 1 - rx_place, piece_count, distances, send_ref)


def turn_parts(step):
    shifted = step + 128
    angle = (jnp.bitwise_and(shifted, 255) - 128).astype(jnp.float32) * (full_turn / 1024.0)
    quarter = jnp.right_shift(shifted, 8)
    square = angle * angle
    cosine = 1.0 + square * (-1 / 2 + square * (1 / 24 + square * (-1 / 720 + square * (1 / 40320))))
    sine = angle * (1.0 + square * (-1 / 6 + square * (1 / 120 + square * (-1 / 5040))))
    odd = jnp.bitwise_and(quarter, 1) == 1
    real = jnp.where(odd, sine, cosine)
    imag = jnp.where(odd, cosine, sine)
    real = jnp.where(jnp.bitwise_and(quarter + 1, 2) == 2, -real, real)
    imag = jnp.where(jnp.bitwise_and(quarter, 2) == 2, -imag, imag)
    return real, imag


def turned(real, imag, phase_re, phase_im):
    return phase_re * real - phase_im * imag, phase_im * real + phase_re * imag


def as_column(row):
    count = row.shape[1]
    first = lax.broadcasted_iota(jnp.int32, (count, count), 0)
    second = lax.broadcasted_iota(jnp.int32, (count, count), 1)
    spread = jnp.where(first == second, row.astype(jnp.float32), 0.0)
    return jnp.sum(spread, axis=1, keepdims=True).astype(jnp.int32)


def interp_matrix(code):
    beams = code.shape[0]
    angle_bin = lax.broadcasted_iota(jnp.int32, (beams, beams), 0)
    column = lax.broadcasted_iota(jnp.int32, (beams, beams), 1)
    half = 2 * beams
    away = jnp.bitwise_and(4 * (column - angle_bin + 1) - code + half, 4 * beams - 1) - half
    away = jnp.abs(away.astype(jnp.float32)) * 0.25
    near = (1.0 - away * away) * (2.0 - away) * 0.5
    far = (1.0 - away) * (2.0 - away) * (3.0 - away) * (1.0 / 6.0)
    matrix = jnp.where(away < 1.0, near, jnp.where(away < 2.0, far, 0.0))
    return matrix.astype(jnp.bfloat16)


def code_columns(codes_ref, rows):
    picked = [codes_ref[pl.ds(row, 1), :] for row in rows]
    picked = jnp.concatenate(picked, axis=0).astype(jnp.float32)
    spare = -len(rows) % 8
    if spare:
        picked = jnp.concatenate([picked, jnp.zeros((spare, picked.shape[1]), jnp.float32)], axis=0)
    return picked.T.astype(jnp.int32)


def weights_kernel(sizes, angle_ref, codes_ref, after_ref, first_ref, inner_ref):
    pulses, channels, rx_count, piece_count = sizes
    rx_place = lax.axis_index("rx")
    pulse_place = lax.axis_index("pulse")
    beams = angle_ref.shape[1]
    angle = as_column(angle_ref[...])
    rows = []
    now = pulses
    while now > 1:
        base = now * piece_count + pulse_place * now
        rows.extend(base + index for index in range(now))
        now //= 2
    codes = code_columns(codes_ref, rows)
    column = lax.broadcasted_iota(jnp.int32, (1, 4 * channels * 2), 1)
    within = jnp.bitwise_and(column, 4 * channels - 1)
    owner = jnp.bitwise_xor(rx_place, jnp.where(within >= 2 * channels, 1, 0))
    receiver = owner * channels + jnp.bitwise_and(column, channels - 1)
    is_imag = jnp.bitwise_and(within, channels) != 0
    scale = 1.0 / math.sqrt(channels * rx_count)
    steer_re, steer_im = turn_parts(jnp.bitwise_and(angle * receiver, 1023))
    steer_re = (steer_re * scale).astype(jnp.bfloat16).astype(jnp.float32)
    steer_im = (-steer_im * scale).astype(jnp.bfloat16).astype(jnp.float32)
    steer = jnp.concatenate(
        [
            jnp.where(is_imag, -steer_im, steer_re).astype(jnp.bfloat16),
            jnp.where(is_imag, steer_re, steer_im).astype(jnp.bfloat16),
        ],
        axis=1,
    )
    low_half = column >= 4 * channels
    entries = 8 * channels
    matrices = [interp_matrix(codes[:, index : index + 1]) for index in range(len(rows))]
    composed = jnp.dot(
        jnp.concatenate(matrices[:pulses], axis=0), steer, preferred_element_type=jnp.float32
    )
    for index in range(pulses):
        for part in range(2):
            value = composed[
                index * beams : (index + 1) * beams, part * entries : (part + 1) * entries
            ]
            high = value.astype(jnp.bfloat16).astype(jnp.float32)
            first_ref[index, part * beams : (part + 1) * beams, :] = jnp.where(
                low_half, value - high, high
            ).astype(jnp.bfloat16)
    for index, matrix in enumerate(matrices[pulses:]):
        inner_ref[index] = matrix


def phases_kernel(sizes, angle_ref, phase_ref):
    pulses, rx_count, width = sizes
    rng_place = lax.axis_index("rng")
    rx_place = lax.axis_index("rx")
    pulse_place = lax.axis_index("pulse")
    piece_count = phase_ref.shape[0]
    piece_tiles = phase_ref.shape[4] // LANES
    angle = as_column(angle_ref[...])
    factors = []
    now = pulses
    while now > 1:
        base = now * piece_count + pulse_place * now
        factors.extend(base + 1 + index for index in range(0, now, 2))
        now //= 2
    lane = lax.broadcasted_iota(jnp.int32, (1, LANES), 1)
    block = (rng_place * rx_count + rx_place) * width + 1
    base = jnp.bitwise_and(angle * (block + lane), 1023)
    for slot, factor in enumerate([1, *factors]):
        scale = half_root if slot else 1.0
        real, imag = turn_parts(jnp.bitwise_and(base * factor, 1023))
        real, imag = real * scale, imag * scale
        step = turn_parts(jnp.bitwise_and(angle * (factor * LANES), 1023))
        for tile in range(piece_count * piece_tiles):
            index = piece_count - 1 - jnp.bitwise_xor(pulse_place, tile // piece_tiles)
            start = tile % piece_tiles * LANES
            phase_ref[index, slot, 0, :, start : start + LANES] = real
            phase_ref[index, slot, 1, :, start : start + LANES] = imag
            real, imag = turned(real, imag, *step)


def outer_levels(piece_count):
    return [piece_count >> level for level in range(piece_count.bit_length() - 1)]


def outer_tables_kernel(sizes, angle_ref, codes_ref, after_ref, outer_ref, phase_ref):
    rx_count, width, piece_count = sizes
    rng_place = lax.axis_index("rng")
    rx_place = lax.axis_index("rx")
    pulse_place = lax.axis_index("pulse")
    piece_width = phase_ref.shape[3]
    angle = as_column(angle_ref[...])
    lane = lax.broadcasted_iota(jnp.int32, (1, piece_width), 1)
    block = (rng_place * rx_count + rx_place) * width + 1
    base = jnp.bitwise_and(angle * (block + pulse_place * piece_width + lane), 1023)
    rows = [row + level for level in outer_levels(piece_count) for row in range(level)]
    codes = code_columns(codes_ref, rows)
    slot = 0
    now = piece_count
    while now > 1:
        for index in range(now):
            outer_ref[slot] = interp_matrix(codes[:, slot : slot + 1])
            real, imag = turn_parts(jnp.bitwise_and(base * (now + index + 1), 1023))
            phase_ref[slot, 0] = real * half_root
            phase_ref[slot, 1] = imag * half_root
            slot += 1
        now //= 2


ROWS = 8


def inner_kernel(indices, keep_ref, other_ref, first_ref, inner_ref, phase_ref, *rest):
    *out_refs, moved_ref, picture_ref, level_ref = rest
    pulses = keep_ref.shape[1]
    beams, columns = out_refs[0].shape[1:]
    pieces = range(len(indices))

    def merge(piece, count, base, read, write):
        index = indices[piece]
        for row in range(0, beams, ROWS):
            span = slice(row, row + ROWS)
            step = (phase_ref[index, 0, 0, span], phase_ref[index, 0, 1, span])
            for image in range(0, count, 2):
                slot = base + image // 2
                left = read(image, row)
                right = turned(*read(image + 1, row), *step)
                phase = (phase_ref[index, slot, 0, span], phase_ref[index, slot, 1, span])
                write(
                    image // 2, row, *turned(left[0] + right[0], left[1] + right[1], *phase)
                )

    def lift(piece, image, slot):
        level_ref[piece, image] = jnp.dot(
            inner_ref[slot],
            picture_ref[piece, image].astype(jnp.bfloat16),
            preferred_element_type=jnp.float32,
        )

    for piece in pieces:
        for image in range(pulses):
            rows = jnp.concatenate(
                [keep_ref[indices[piece], image], other_ref[piece, image]], axis=0
            )
            moved_ref[piece, image] = jnp.dot(
                first_ref[image],
                jnp.concatenate([rows, rows], axis=0),
                preferred_element_type=jnp.float32,
            )

    def read_first(piece):
        return lambda image, row: (
            moved_ref[piece, image, row : row + ROWS],
            moved_ref[piece, image, beams + row : beams + row + ROWS],
        )

    def read_level(piece):
        return lambda image, row: (
            level_ref[piece, image, row : row + ROWS, :columns],
            level_ref[piece, image, row : row + ROWS, columns:],
        )

    def write_picture(piece):
        def write(image, row, real, imag):
            picture_ref[piece, image, row : row + ROWS, :columns] = real
            picture_ref[piece, image, row : row + ROWS, columns:] = imag

        return write

    for piece in pieces:
        merge(piece, pulses, 1, read_first(piece), write_picture(piece))
        for image in range(pulses // 2):
            lift(piece, image, image)
    base = 1 + pulses // 2
    slot = pulses // 2
    count = pulses // 2
    while count > 1:
        for piece in pieces:
            merge(piece, count, base, read_level(piece), write_picture(piece))
            for image in range(count // 2 if count > 2 else 0):
                lift(piece, image, slot + image)
        count //= 2
        base += count
        slot += count
    for piece in pieces:
        out_refs[piece][0] = picture_ref[piece, 0, :, :columns].astype(jnp.bfloat16)
        out_refs[piece][1] = picture_ref[piece, 0, :, columns:].astype(jnp.bfloat16)


def outer_kernel(outer_ref, phase_ref, *rest):
    image_refs, out_ref = rest[-2::-1], rest[-1]
    pulse_place = lax.axis_index("pulse")
    pictures = [(ref[0], ref[1]) for ref in image_refs]
    base = 0
    level = 0
    while len(pictures) > 1:
        count = len(pictures)
        place = jnp.right_shift(pulse_place, level)
        merged = []
        for distance, (real, imag) in enumerate(pictures):
            slot = base + jnp.bitwise_xor(place, distance)
            matrix = outer_ref[slot]
            moved_re = jnp.dot(
                matrix, real.astype(jnp.bfloat16), preferred_element_type=jnp.float32
            )
            moved_im = jnp.dot(
                matrix, imag.astype(jnp.bfloat16), preferred_element_type=jnp.float32
            )
            merged.append(turned(moved_re, moved_im, phase_ref[slot, 0], phase_ref[slot, 1]))
            if distance & 1:
                right, left = merged.pop(), merged.pop()
                merged.append((left[0] + right[0], left[1] + right[1]))
        pictures = merged
        base += count
        level += 1
    out_ref[0] = pictures[0][0]
    out_ref[1] = pictures[0][1]


def cost(micros):
    return pl.CostEstimate(
        flops=int(micros * 1.1e9), bytes_accessed=int(micros * 3.6e6), transcendentals=0
    )


PARAMS = dict(compiler_params=pltpu.CompilerParams(vmem_limit_bytes=40 * 1024 * 1024))


def send_groups(pulse_count):
    last = pulse_count - 1
    if pulse_count < 4:
        return [[distance] for distance in range(last, -1, -1)]
    return [[last, last - 1], list(range(last - 2, -1, -1))]


def fast(echoes, beam_angle, interp_table):
    rx_count = lax.axis_size("rx")
    pulse_count = lax.axis_size("pulse")
    _, pulses, channels, length = echoes.shape
    beams = beam_angle.shape[0]
    width = length // rx_count
    piece_width = width // pulse_count
    piece_tiles = piece_width // LANES
    rows = 2 * channels
    group = 2 * pulses
    chirp = jnp.asarray(chirp_bands_table())
    angles = beam_angle.reshape(1, beams)
    codes = interp_table.reshape(-1, beams)
    bf16 = jnp.bfloat16
    f32 = jnp.float32
    shape = jax.ShapeDtypeStruct
    across = swapped(echoes, "rng", 0)
    bands = pl.pallas_call(
        bands_kernel,
        out_shape=shape((channels, RX_TILE, 2 * LANES), bf16),
        out_specs=vmem(),
        name="bands",
        cost_estimate=cost(10.0),
        **PARAMS,
    )()
    tiles = length // LANES
    filtered_shape = shape((rows * pulses, (tiles + 2 * HALO_TILES - 1) * LANES), bf16)
    filtered = pl.pallas_call(
        interior_kernel,
        out_shape=filtered_shape,
        in_specs=[vmem()] * 2,
        out_specs=vmem(),
        scratch_shapes=[
            pltpu.VMEM((tiles + 2, channels * group, LANES), f32),
            pltpu.VMEM((tiles + 1, rows * pulses, LANES), f32),
        ],
        name="interior",
        **PARAMS,
    )(echoes, bands)

    def pieces(count):
        return shape((count, pulses, rows, piece_width), bf16)

    last = pulse_count - 1
    groups = send_groups(pulse_count)
    filtered, first_sent = pl.pallas_call(
        functools.partial(edges_kernel, (pulse_count, groups[:1])),
        out_shape=[filtered_shape, pieces(len(groups[0]))],
        in_specs=[vmem()] * 5,
        out_specs=[vmem()] * 2,
        scratch_shapes=[
            pltpu.VMEM((HALO_TILES + 1, channels * group, LANES), f32),
            pltpu.VMEM((HALO_TILES, rows * pulses, LANES), f32),
        ],
        input_output_aliases={0: 0},
        name="edges",
        **PARAMS,
    )(filtered, echoes, across, bands, chirp)
    phase = pl.pallas_call(
        functools.partial(phases_kernel, (pulses, rx_count, width)),
        out_shape=shape((pulse_count, pulses, 2, beams, piece_width), f32),
        in_specs=[vmem()],
        out_specs=vmem(),
        name="phases",
        **PARAMS,
    )(angles)
    kept, *sent = pl.pallas_call(
        functools.partial(rest_kernel, pulse_count, groups[1:]),
        out_shape=[pieces(pulse_count)] + [pieces(len(members)) for members in groups[1:]],
        in_specs=[vmem()] * 2 + [anywhere()],
        out_specs=[vmem()] * len(groups),
        name="rest",
        **PARAMS,
    )(filtered, chirp, phase)
    first, inner = pl.pallas_call(
        functools.partial(weights_kernel, (pulses, channels, rx_count, pulse_count)),
        out_shape=[
            shape((pulses, 2 * beams, 8 * channels), bf16),
            shape((pulses - 2, beams, beams), bf16),
        ],
        in_specs=[vmem()] * 2 + [anywhere()],
        out_specs=[vmem()] * 2,
        name="weights",
        **PARAMS,
    )(angles, codes, kept)
    images = [None] * pulse_count
    for members, piece in zip(groups, [first_sent, *sent]):
        other = swapped(piece, "rx", 0)
        size = len(members)
        merged = pl.pallas_call(
            functools.partial(inner_kernel, [last - distance for distance in members]),
            out_shape=[shape((2, beams, piece_width), bf16)] * size,
            in_specs=[vmem()] * 5,
            out_specs=[vmem()] * size,
            scratch_shapes=[
                pltpu.VMEM((size, pulses, 2 * beams, piece_width), f32),
                pltpu.VMEM((size, pulses // 2, beams, 2 * piece_width), f32),
                pltpu.VMEM((size, pulses // 2, beams, 2 * piece_width), f32),
            ],
            name="inner",
            **PARAMS,
        )(kept, other, first, inner, phase)
        for distance, image in zip(members, merged):
            images[distance] = image
    for distance in range(1, pulse_count):
        pairs = [(i, i ^ distance) for i in range(pulse_count)]
        images[distance] = lax.ppermute(images[distance], "pulse", pairs)
    outer_count = 2 * pulse_count - 2
    outer, outer_phase = pl.pallas_call(
        functools.partial(outer_tables_kernel, (rx_count, width, pulse_count)),
        out_shape=[
            shape((outer_count, beams, beams), bf16),
            shape((outer_count, 2, beams, piece_width), f32),
        ],
        in_specs=[vmem(), vmem(), anywhere()],
        out_specs=[vmem()] * 2,
        name="outer_tables",
        **PARAMS,
    )(angles, codes, images[0])
    return pl.pallas_call(
        outer_kernel,
        out_shape=shape((2, beams, piece_width), f32),
        in_specs=[vmem()] * (2 + pulse_count),
        out_specs=vmem(),
        name="outer",
        **PARAMS,
    )(outer, outer_phase, *images[::-1])


def power_of_two(count):
    return count > 0 and count & (count - 1) == 0


def per_device(echoes, beam_angle, interp_table):
    _, pulses, channels, length = echoes.shape
    rx_count = lax.axis_size("rx")
    pulse_count = lax.axis_size("pulse")
    piece_width = length // (rx_count * pulse_count)
    if (
        lax.axis_size("rng") == 2
        and rx_count == 2
        and channels == 8
        and pulses == 8
        and power_of_two(pulse_count)
        and pulse_count > 1
        and power_of_two(beam_angle.shape[0])
        and beam_angle.shape[0] % 16 == 0
        and piece_width % LANES == 0
    ):
        return fast(echoes, beam_angle, interp_table)
    return local(echoes, beam_angle, interp_table)


def solution(mesh):
    placed = (P(None, ("slab", "pulse"), "rx", "rng"), P(), P())
    return jax.shard_map(
        per_device,
        mesh=mesh,
        in_specs=placed,
        out_specs=P(None, "slab", ("rng", "rx", "pulse")),
        check_vma=False,
    )
```

```python
import functools
import math

import jax
import jax.numpy as jnp
import ml_dtypes
import numpy as np
from jax import lax
from jax.experimental import pallas as pl
from jax.experimental.pallas import tpu as pltpu
from jax.sharding import PartitionSpec as P

RTAPS = 64
CTAPS = 512


half_root = 0.7071067811865476
full_turn = 2.0 * math.pi


def extended_2(block, sides, width):
    for axis, dim in sides:
        count = lax.axis_size(axis)
        forward = [(i, i + 1) for i in range(count - 1)]
        backward = [(target, source) for source, target in forward]
        low = lax.ppermute(
            lax.slice_in_dim(block, block.shape[dim] - width, None, axis=dim), axis, forward
        )
        high = lax.ppermute(lax.slice_in_dim(block, 0, width, axis=dim), axis, backward)
        block = jnp.concatenate([low, block, high], axis=dim)
    return block


def swapped(x, axis, distance):
    return lax.ppermute(x, axis, [(i, i ^ 1 << distance) for i in range(lax.axis_size(axis))])


def receiver_taps(channel_ids, tap_count):
    tap_index = jnp.arange(tap_count, dtype=jnp.float32)
    window = 0.5 - 0.5 * jnp.cos(full_turn * (tap_index + 0.5) / tap_count)
    window = window / jnp.sqrt(jnp.sum(window * window))
    channel = channel_ids.astype(jnp.float32)[:, None] + 1.0
    angle = full_turn * channel * (tap_index - tap_count // 2) / (4 * tap_count)
    return (
        (window * jnp.cos(angle)).astype(jnp.bfloat16),
        (window * jnp.sin(angle)).astype(jnp.bfloat16),
    )


def chirp_taps(tap_count):
    offset = jnp.arange(tap_count, dtype=jnp.int32) - tap_count // 2
    phase_step = jnp.mod(offset * offset, 2 * tap_count).astype(jnp.float32)
    angle = math.pi * phase_step / tap_count
    scale = 1.0 / math.sqrt(tap_count)
    return (
        (jnp.cos(angle) * scale).astype(jnp.bfloat16),
        (-jnp.sin(angle) * scale).astype(jnp.bfloat16),
    )


def steering(beam_angle, receivers):
    channel = jnp.arange(receivers, dtype=jnp.int32)
    turns = jnp.mod(beam_angle[:, None] * channel[None, :], 1024).astype(jnp.float32)
    angle = full_turn * turns / 1024.0
    scale = 1.0 / math.sqrt(receivers)
    return (
        (jnp.cos(angle) * scale).astype(jnp.bfloat16),
        (-jnp.sin(angle) * scale).astype(jnp.bfloat16),
    )


def interp_matrices(codes, beam_count):
    shifted = codes // 4 - 1
    fraction = jnp.mod(codes, 4).astype(jnp.float32) / 4.0
    weights = (
        -fraction * (fraction - 1.0) * (fraction - 2.0) / 6.0,
        (fraction + 1.0) * (fraction - 1.0) * (fraction - 2.0) / 2.0,
        -(fraction + 1.0) * fraction * (fraction - 2.0) / 2.0,
        (fraction + 1.0) * fraction * (fraction - 1.0) / 6.0,
    )
    columns = jnp.arange(beam_count, dtype=jnp.int32)
    matrices = jnp.zeros(codes.shape + (beam_count,), jnp.float32)
    for tap_index in range(4):
        target = jnp.mod(columns + shifted + tap_index - 1, beam_count)
        matrices = matrices + weights[tap_index][..., None] * (target[..., None] == columns).astype(
            jnp.float32
        )
    return matrices


def phases(node_ids, positions, beam_angle, side):
    base = jnp.mod(beam_angle[:, None] * (positions[None, :] + 1), 1024)
    factor = 2 * node_ids + side + 1
    turns = jnp.mod(base[:, None, :] * factor[None, :, None], 1024).astype(jnp.float32)
    angle = full_turn * turns / 1024.0
    return (jnp.cos(angle), jnp.sin(angle))


def side_term(picture, matrices, cosine, sine):
    moved = jnp.einsum("gqa,cagr->cqgr", matrices, picture, precision=lax.Precision.HIGHEST)
    return (cosine * moved[0] - sine * moved[1], sine * moved[0] + cosine * moved[1])


def merge_pair(left_image, right_image, node_ids, positions, beam_angle, interp_table):
    matrices = interp_matrices(interp_table[node_ids], left_image.shape[1])
    left_cos, left_sin = phases(node_ids, positions, beam_angle, 0)
    right_cos, right_sin = phases(node_ids, positions, beam_angle, 1)
    left_re, left_im = side_term(left_image, matrices[:, 0], left_cos, left_sin)
    right_re, right_im = side_term(right_image, matrices[:, 1], right_cos, right_sin)
    return jnp.stack([(left_re + right_re) * half_root, (left_im + right_im) * half_root])


def toeplitz_blocks(taps_re, taps_im):
    tap_count = taps_re.shape[-1]
    leading = taps_re.shape[:-1]

    def lay_out(taps):
        padded = jnp.concatenate([taps, jnp.zeros(leading + (tap_count + 1,), taps.dtype)], axis=-1)
        tiled = jnp.tile(padded, (1,) * len(leading) + (tap_count,))
        banded = tiled[..., : 2 * tap_count * tap_count].reshape(
            leading + (tap_count, 2 * tap_count)
        )
        return jnp.swapaxes(banded, -1, -2)

    real_band = lay_out(taps_re)
    imag_band = lay_out(taps_im)
    upper = jnp.concatenate([real_band, imag_band], axis=-1)
    lower = jnp.concatenate([-imag_band, real_band], axis=-1)
    return jnp.concatenate([upper, lower], axis=-2)


def block_filter(extended, matrices, tap_count, per_channel):
    pulses, channels, length = extended.shape[1:]
    blocks = length // tap_count - 1
    pieces = extended.reshape(2, pulses, channels, blocks + 1, tap_count)
    windows = jnp.concatenate([pieces[:, :, :, :-1], pieces[:, :, :, 1:]], axis=4)
    windows = jnp.transpose(windows, (1, 2, 3, 0, 4)).reshape(
        pulses, channels, blocks, 4 * tap_count
    )
    if per_channel:
        output = jnp.einsum("pcnw,cwo->pcno", windows, matrices, preferred_element_type=jnp.float32)
    else:
        output = jnp.einsum("pcnw,wo->pcno", windows, matrices, preferred_element_type=jnp.float32)
    output = output.reshape(pulses, channels, blocks, 2, tap_count)
    return jnp.transpose(output, (3, 0, 1, 2, 4)).reshape(2, pulses, channels, blocks * tap_count)


def local(echoes, beam_angle, interp_table):
    rx_count = lax.axis_size("rx")
    pulse_count = lax.axis_size("pulse")
    rng_place = lax.axis_index("rng")
    rx_place = lax.axis_index("rx")
    pulse_place = lax.axis_index("pulse")
    pulses, channels, length = echoes.shape[1:]
    beam_count = beam_angle.shape[0]
    receivers = channels * rx_count
    channel_ids = rx_place * channels + jnp.arange(channels, dtype=jnp.int32)
    rx_re, rx_im = receiver_taps(channel_ids, RTAPS)
    rx_bands = toeplitz_blocks(rx_re, rx_im)
    chirp_re, chirp_im = chirp_taps(CTAPS)
    chirp_band = toeplitz_blocks(chirp_re, chirp_im)
    extended = extended_2(echoes, (("rng", 3),), RTAPS // 2)
    filtered = block_filter(extended, rx_bands, RTAPS, True).astype(jnp.bfloat16)
    filtered = extended_2(filtered, (("rng", 3),), CTAPS // 2)
    compressed = block_filter(filtered, chirp_band, CTAPS, False).astype(jnp.bfloat16)
    steering_real, steering_imaginary = steering(beam_angle, receivers)
    steer_matrix = jnp.concatenate(
        [
            jnp.concatenate([steering_real, -steering_imaginary], axis=1),
            jnp.concatenate([steering_imaginary, steering_real], axis=1),
        ],
        axis=0,
    )
    arrived = lax.all_to_all(compressed, "rx", split_axis=3, concat_axis=2, tiled=True)
    item_count, recv_count, owned_cols = arrived.shape[1:]
    stacked = jnp.transpose(arrived, (0, 2, 1, 3)).reshape(2 * recv_count, item_count * owned_cols)
    formed = jnp.dot(steer_matrix, stacked, preferred_element_type=jnp.float32)
    picture = formed.reshape(2, beam_count, item_count, owned_cols)
    owned_width = length // rx_count
    positions = (
        rng_place * length + rx_place * owned_width + jnp.arange(owned_width, dtype=jnp.int32)
    )
    for level in range(pulses.bit_length() - 1):
        groups_now = pulses >> level + 1
        node_ids = (pulse_count + pulse_place) * groups_now + jnp.arange(
            groups_now, dtype=jnp.int32
        )
        paired = picture.reshape(2, beam_count, groups_now, 2, owned_width)
        picture = merge_pair(
            paired[:, :, :, 0], paired[:, :, :, 1], node_ids, positions, beam_angle, interp_table
        )
    picture = picture[:, :, 0]
    cross_levels = pulse_count.bit_length() - 1
    piece_width = owned_width // pulse_count
    pieces = picture.reshape(2, beam_count, pulse_count, piece_width)
    spots = positions.reshape(pulse_count, piece_width)
    for level in range(cross_levels):
        parity = jnp.right_shift(pulse_place, level) & 1
        count_now = pieces.shape[2]
        paired = pieces.reshape(2, beam_count, count_now // 2, 2, piece_width)
        kept_half = lax.dynamic_index_in_dim(paired, parity, 3, keepdims=False)
        sent_half = lax.dynamic_index_in_dim(paired, 1 - parity, 3, keepdims=False)
        partner = swapped(sent_half, "pulse", level)
        spot_pairs = spots.reshape(count_now // 2, 2, piece_width)
        spots = lax.dynamic_index_in_dim(spot_pairs, parity, 1, keepdims=False)
        own_part = kept_half.reshape(2, beam_count, -1)
        other_part = partner.reshape(2, beam_count, -1)
        left_image = jnp.where(parity == 0, own_part, other_part)
        right_image = jnp.where(parity == 0, other_part, own_part)
        combine_node_ids = jnp.reshape(
            (pulse_count >> level + 1) + jnp.right_shift(pulse_place, level + 1), (1,)
        )
        merged = merge_pair(
            left_image[:, :, None],
            right_image[:, :, None],
            combine_node_ids,
            spots.reshape(-1),
            beam_angle,
            interp_table,
        )
        flat = merged[:, :, 0]
        pieces = flat.reshape(2, beam_count, count_now // 2, piece_width)
    picture = pieces.reshape(2, beam_count, piece_width)
    return picture


LANES = 128
RX_TILE = LANES + RTAPS
CHIRP_TILE = 6 * LANES
HALO_TILES = 3
HALO = HALO_TILES * LANES


def vmem():
    return pl.BlockSpec(memory_space=pltpu.VMEM)


def hbm():
    return pl.BlockSpec(memory_space=pltpu.HBM)


def anywhere():
    return pl.BlockSpec(memory_space=pl.ANY)


def chirp_bands_table():
    offset = np.arange(CTAPS) - CTAPS // 2
    angle = math.pi * np.mod(offset * offset, 2 * CTAPS) / CTAPS
    scale = 1.0 / math.sqrt(CTAPS)
    offset = np.arange(CHIRP_TILE)[:, None] - np.arange(LANES)[None, :] - (LANES - RTAPS // 2)
    inside = (offset >= 0) & (offset < CTAPS)
    place = np.clip(offset, 0, CTAPS - 1)
    bands = [
        np.where(inside, taps[place], 0.0)
        for taps in (np.cos(angle) * scale, -np.sin(angle) * scale)
    ]
    return np.concatenate(bands, axis=-1).astype(ml_dtypes.bfloat16)


def filter_channel(windows, bands, pulses):
    product = jnp.dot(windows, bands, preferred_element_type=jnp.float32)
    product = product.reshape(-1, 2, pulses, 2 * LANES)
    real = product[:, 0, :, :LANES] - product[:, 1, :, LANES:]
    imag = product[:, 0, :, LANES:] + product[:, 1, :, :LANES]
    return real, imag


def bands_kernel(bands_ref):
    channels = bands_ref.shape[0]
    first_channel = lax.axis_index("rx") * channels
    lane = lax.broadcasted_iota(jnp.int32, (channels, LANES), 1)
    channel = lax.broadcasted_iota(jnp.int32, (channels, LANES), 0) + first_channel + 1
    tap = jnp.bitwise_and(LANES - lane, LANES - 1)
    unit = 1024 // RTAPS
    window = 0.5 - 0.5 * turn_parts(tap * unit + unit // 2)[0]
    window = jnp.where(tap < RTAPS, window * (1.0 / math.sqrt(RTAPS * 3 / 8)), 0.0)
    turn = channel * (tap - RTAPS // 2) * (1024 // (4 * RTAPS))
    row = lax.broadcasted_iota(jnp.int32, (LANES, LANES), 0)
    upper = lax.broadcasted_iota(jnp.int32, (LANES, LANES), 1) <= row
    for part, wave in enumerate(turn_parts(jnp.bitwise_and(turn, 1023))):
        taps = window * wave
        span = slice(part * LANES, (part + 1) * LANES)
        for index in range(channels):
            spread = jnp.broadcast_to(taps[index : index + 1], (LANES, LANES))
            rolled = pltpu.roll(spread, 0, 1, stride=1, stride_axis=0)
            bands_ref[index, :LANES, span] = jnp.where(upper, rolled, 0.0).astype(jnp.bfloat16)
            lower = jnp.where(upper, 0.0, rolled)[:RTAPS]
            bands_ref[index, LANES:, span] = lower.astype(jnp.bfloat16)


def interior_kernel(echo_ref, bands_ref, filtered_ref, rows_in, rows_out):
    _, pulses, channels, length = echo_ref.shape
    tiles = length // LANES
    group = 2 * pulses
    empty = jnp.zeros(rows_in.shape[1:], jnp.float32)
    rows_in[0] = empty
    rows_in[tiles + 1] = empty
    for part in range(2):
        for pulse in range(pulses):
            where = pl.ds(part * pulses + pulse, channels, stride=group)
            block = echo_ref[part, pulse].astype(jnp.float32)
            for tile in range(tiles):
                rows_in[tile + 1, where, :] = block[:, tile * LANES : (tile + 1) * LANES]
    lane = lax.broadcasted_iota(jnp.int32, (pulses, LANES), 1)
    mask = jnp.where(lane >= LANES - RTAPS // 2, 1.0, 0.0)
    for channel in range(channels):
        rows = rows_in[:, channel * group : (channel + 1) * group, :].astype(jnp.bfloat16)
        windows = jnp.concatenate(
            [rows[:-1].reshape(-1, LANES), rows[1:].reshape(-1, LANES)[:, :RTAPS]], axis=1
        )
        real, imag = filter_channel(windows, bands_ref[channel], pulses)
        for tile in range(tiles + 1):
            tile_re, tile_im = real[tile], imag[tile]
            if tile == 0:
                tile_re, tile_im = tile_re * mask, tile_im * mask
            if tile == tiles:
                tile_re, tile_im = tile_re * (1.0 - mask), tile_im * (1.0 - mask)
            rows_out[tile, pl.ds(channel, pulses, stride=2 * channels), :] = tile_re
            rows_out[tile, pl.ds(channels + channel, pulses, stride=2 * channels), :] = tile_im
    rows = filtered_ref.shape[0]
    nothing = jnp.zeros((rows, (HALO_TILES - 1) * LANES), jnp.bfloat16)
    filtered_ref[:, : (HALO_TILES - 1) * LANES] = nothing
    filtered_ref[:, (HALO_TILES + tiles) * LANES :] = nothing
    for tile in range(tiles + 1):
        spot = (HALO_TILES - 1 + tile) * LANES
        filtered_ref[:, spot : spot + LANES] = rows_out[tile].astype(jnp.bfloat16)


def chirp_pieces(filtered_ref, chirp_ref, owner, piece_count, distances, out_ref):
    pulse_place = lax.axis_index("pulse")
    _, pulses, rows, width = out_ref.shape
    tiles = width // LANES
    channels = rows // 2
    windows = []
    for distance in distances:
        piece = jnp.bitwise_xor(pulse_place, distance)
        first = (owner * piece_count + piece) * tiles
        for tile in range(tiles):
            start = pl.multiple_of((first + tile) * LANES, LANES)
            windows.append(filtered_ref[:, pl.ds(start, CHIRP_TILE)])
    product = jnp.dot(
        jnp.concatenate(windows, axis=0), chirp_ref[...], preferred_element_type=jnp.float32
    )
    product = product.reshape(len(windows), pulses, rows, 2 * LANES)
    for index in range(len(distances)):
        for tile in range(tiles):
            block = product[index * tiles + tile]
            real = block[:, :channels, :LANES] - block[:, channels:, LANES:]
            imag = block[:, :channels, LANES:] + block[:, channels:, :LANES]
            out_ref[index, :, :, tile * LANES : (tile + 1) * LANES] = jnp.concatenate(
                [real, imag], axis=1
            ).astype(jnp.bfloat16)


def edges_kernel(
    plan, inner_ref, echo_ref, across_ref, bands_ref, chirp_ref, filtered_ref, *rest
):
    *send_refs, rows_in, rows_out = rest
    del inner_ref
    _, pulses, channels, length = echo_ref.shape
    tiles = length // LANES
    group = 2 * pulses
    lowest = lax.axis_index("rng") == 0
    far = pl.ds(pl.multiple_of(jnp.where(lowest, 0, length - HALO), LANES), HALO)
    for part in range(2):
        for pulse in range(pulses):
            where = pl.ds(part * pulses + pulse, channels, stride=group)
            edge = across_ref[part, pulse, :, far].astype(jnp.float32)
            near_low = echo_ref[part, pulse, :, :LANES].astype(jnp.float32)
            near_high = echo_ref[part, pulse, :, length - LANES :].astype(jnp.float32)
            pieces = [edge[:, t * LANES : (t + 1) * LANES] for t in range(HALO_TILES)]
            for tile in range(HALO_TILES + 1):
                high = near_high if tile == 0 else pieces[tile - 1]
                low = near_low if tile == HALO_TILES else pieces[tile]
                rows_in[tile, where, :] = jnp.where(lowest, high, low)
    for channel in range(channels):
        rows = rows_in[:, channel * group : (channel + 1) * group, :].astype(jnp.bfloat16)
        windows = jnp.concatenate(
            [rows[:-1].reshape(-1, LANES), rows[1:].reshape(-1, LANES)[:, :RTAPS]], axis=1
        )
        real, imag = filter_channel(windows, bands_ref[channel], pulses)
        for tile in range(HALO_TILES):
            rows_out[tile, pl.ds(channel, pulses, stride=2 * channels), :] = real[tile]
            rows_out[tile, pl.ds(channels + channel, pulses, stride=2 * channels), :] = imag[tile]
    first = jnp.where(lowest, tiles + HALO_TILES - 1, 0)
    for tile in range(HALO_TILES):
        start = pl.multiple_of((first + tile) * LANES, LANES)
        filtered_ref[:, pl.ds(start, LANES)] = rows_out[tile].astype(jnp.bfloat16)
    piece_count, groups = plan
    for distances, send_ref in zip(groups, send_refs):
        chirp_pieces(
            filtered_ref, chirp_ref, 1 - lax.axis_index("rx"), piece_count, distances, send_ref
        )


def rest_kernel(piece_count, groups, filtered_ref, chirp_ref, after_ref, keep_ref, *send_refs):
    rx_place = lax.axis_index("rx")
    own = list(range(piece_count - 1, -1, -1))
    chirp_pieces(filtered_ref, chirp_ref, rx_place, piece_count, own, keep_ref)
    for distances, send_ref in zip(groups, send_refs):
        chirp_pieces(filtered_ref, chirp_ref, 1 - rx_place, piece_count, distances, send_ref)


def turn_parts(step):
    shifted = step + 128
    angle = (jnp.bitwise_and(shifted, 255) - 128).astype(jnp.float32) * (full_turn / 1024.0)
    quarter = jnp.right_shift(shifted, 8)
    square = angle * angle
    cosine = 1.0 + square * (-1 / 2 + square * (1 / 24 + square * (-1 / 720 + square * (1 / 40320))))
    sine = angle * (1.0 + square * (-1 / 6 + square * (1 / 120 + square * (-1 / 5040))))
    odd = jnp.bitwise_and(quarter, 1) == 1
    real = jnp.where(odd, sine, cosine)
    imag = jnp.where(odd, cosine, sine)
    real = jnp.where(jnp.bitwise_and(quarter + 1, 2) == 2, -real, real)
    imag = jnp.where(jnp.bitwise_and(quarter, 2) == 2, -imag, imag)
    return real, imag


def turned(real, imag, phase_re, phase_im):
    return phase_re * real - phase_im * imag, phase_im * real + phase_re * imag


def as_column(row):
    count = row.shape[1]
    first = lax.broadcasted_iota(jnp.int32, (count, count), 0)
    second = lax.broadcasted_iota(jnp.int32, (count, count), 1)
    spread = jnp.where(first == second, row.astype(jnp.float32), 0.0)
    return jnp.sum(spread, axis=1, keepdims=True).astype(jnp.int32)


def interp_matrix(code):
    beams = code.shape[0]
    angle_bin = lax.broadcasted_iota(jnp.int32, (beams, beams), 0)
    column = lax.broadcasted_iota(jnp.int32, (beams, beams), 1)
    half = 2 * beams
    away = jnp.bitwise_and(4 * (column - angle_bin + 1) - code + half, 4 * beams - 1) - half
    away = jnp.abs(away.astype(jnp.float32)) * 0.25
    near = (1.0 - away * away) * (2.0 - away) * 0.5
    far = (1.0 - away) * (2.0 - away) * (3.0 - away) * (1.0 / 6.0)
    matrix = jnp.where(away < 1.0, near, jnp.where(away < 2.0, far, 0.0))
    return matrix.astype(jnp.bfloat16)


def code_columns(codes_ref, rows):
    picked = [codes_ref[pl.ds(row, 1), :] for row in rows]
    picked = jnp.concatenate(picked, axis=0).astype(jnp.float32)
    spare = -len(rows) % 8
    if spare:
        picked = jnp.concatenate([picked, jnp.zeros((spare, picked.shape[1]), jnp.float32)], axis=0)
    return picked.T.astype(jnp.int32)


def weights_kernel(sizes, angle_ref, codes_ref, after_ref, first_ref, inner_ref):
    pulses, channels, rx_count, piece_count = sizes
    rx_place = lax.axis_index("rx")
    pulse_place = lax.axis_index("pulse")
    beams = angle_ref.shape[1]
    angle = as_column(angle_ref[...])
    rows = []
    now = pulses
    while now > 1:
        base = now * piece_count + pulse_place * now
        rows.extend(base + index for index in range(now))
        now //= 2
    codes = code_columns(codes_ref, rows)
    column = lax.broadcasted_iota(jnp.int32, (1, 4 * channels * 2), 1)
    within = jnp.bitwise_and(column, 4 * channels - 1)
    owner = jnp.bitwise_xor(rx_place, jnp.where(within >= 2 * channels, 1, 0))
    receiver = owner * channels + jnp.bitwise_and(column, channels - 1)
    is_imag = jnp.bitwise_and(within, channels) != 0
    scale = 1.0 / math.sqrt(channels * rx_count)
    steer_re, steer_im = turn_parts(jnp.bitwise_and(angle * receiver, 1023))
    steer_re = (steer_re * scale).astype(jnp.bfloat16).astype(jnp.float32)
    steer_im = (-steer_im * scale).astype(jnp.bfloat16).astype(jnp.float32)
    steer = jnp.concatenate(
        [
            jnp.where(is_imag, -steer_im, steer_re).astype(jnp.bfloat16),
            jnp.where(is_imag, steer_re, steer_im).astype(jnp.bfloat16),
        ],
        axis=1,
    )
    low_half = column >= 4 * channels
    entries = 8 * channels
    matrices = [interp_matrix(codes[:, index : index + 1]) for index in range(len(rows))]
    composed = jnp.dot(
        jnp.concatenate(matrices[:pulses], axis=0), steer, preferred_element_type=jnp.float32
    )
    for index in range(pulses):
        for part in range(2):
            value = composed[
                index * beams : (index + 1) * beams, part * entries : (part + 1) * entries
            ]
            high = value.astype(jnp.bfloat16).astype(jnp.float32)
            first_ref[index, part * beams : (part + 1) * beams, :] = jnp.where(
                low_half, value - high, high
            ).astype(jnp.bfloat16)
    for index, matrix in enumerate(matrices[pulses:]):
        inner_ref[index] = matrix


def phases_kernel(sizes, angle_ref, after_ref, phase_ref):
    pulses, rx_count, width = sizes
    rng_place = lax.axis_index("rng")
    rx_place = lax.axis_index("rx")
    pulse_place = lax.axis_index("pulse")
    piece_count = phase_ref.shape[0]
    piece_tiles = phase_ref.shape[4] // LANES
    angle = as_column(angle_ref[...])
    factors = []
    now = pulses
    while now > 1:
        base = now * piece_count + pulse_place * now
        factors.extend(base + 1 + index for index in range(0, now, 2))
        now //= 2
    lane = lax.broadcasted_iota(jnp.int32, (1, LANES), 1)
    block = (rng_place * rx_count + rx_place) * width + 1
    base = jnp.bitwise_and(angle * (block + lane), 1023)
    for slot, factor in enumerate([1, *factors]):
        scale = half_root if slot else 1.0
        real, imag = turn_parts(jnp.bitwise_and(base * factor, 1023))
        real, imag = real * scale, imag * scale
        step = turn_parts(jnp.bitwise_and(angle * (factor * LANES), 1023))
        for tile in range(piece_count * piece_tiles):
            index = piece_count - 1 - jnp.bitwise_xor(pulse_place, tile // piece_tiles)
            start = tile % piece_tiles * LANES
            phase_ref[index, slot, 0, :, start : start + LANES] = real
            phase_ref[index, slot, 1, :, start : start + LANES] = imag
            real, imag = turned(real, imag, *step)


def risen(outer_ref, phase_ref, slot, real, imag):
    matrix = outer_ref[slot]
    moved_re = jnp.dot(matrix, real.astype(jnp.bfloat16), preferred_element_type=jnp.float32)
    moved_im = jnp.dot(matrix, imag.astype(jnp.bfloat16), preferred_element_type=jnp.float32)
    return turned(moved_re, moved_im, phase_ref[slot, 0], phase_ref[slot, 1])


def outer_tables_kernel(sizes, angle_ref, codes_ref, image_ref, outer_ref, phase_ref, own_ref):
    rx_count, width, piece_count = sizes
    rng_place = lax.axis_index("rng")
    rx_place = lax.axis_index("rx")
    pulse_place = lax.axis_index("pulse")
    piece_width = phase_ref.shape[3]
    angle = as_column(angle_ref[...])
    lane = lax.broadcasted_iota(jnp.int32, (1, piece_width), 1)
    block = (rng_place * rx_count + rx_place) * width + 1
    base = jnp.bitwise_and(angle * (block + pulse_place * piece_width + lane), 1023)
    counts = [piece_count >> level for level in range(piece_count.bit_length() - 1)]
    rows = [count + index for count in counts for index in range(count)]
    codes = code_columns(codes_ref, rows)
    for slot, row in enumerate(rows):
        outer_ref[slot] = interp_matrix(codes[:, slot : slot + 1])
        real, imag = turn_parts(jnp.bitwise_and(base * (row + 1), 1023))
        phase_ref[slot, 0] = real * half_root
        phase_ref[slot, 1] = imag * half_root
    own_ref[0], own_ref[1] = risen(
        outer_ref, phase_ref, pulse_place, image_ref[0], image_ref[1]
    )


ROWS = 8


def inner_kernel(indices, keep_ref, other_ref, first_ref, inner_ref, phase_ref, *rest):
    *out_refs, moved_ref, picture_ref, level_ref = rest
    pulses = keep_ref.shape[1]
    beams, columns = out_refs[0].shape[1:]
    pieces = range(len(indices))

    def merge(piece, count, base, read, write):
        index = indices[piece]
        for row in range(0, beams, ROWS):
            span = slice(row, row + ROWS)
            step = (phase_ref[index, 0, 0, span], phase_ref[index, 0, 1, span])
            for image in range(0, count, 2):
                slot = base + image // 2
                left = read(image, row)
                right = turned(*read(image + 1, row), *step)
                phase = (phase_ref[index, slot, 0, span], phase_ref[index, slot, 1, span])
                write(
                    image // 2, row, *turned(left[0] + right[0], left[1] + right[1], *phase)
                )

    def lift(piece, image, slot):
        level_ref[piece, image] = jnp.dot(
            inner_ref[slot],
            picture_ref[piece, image].astype(jnp.bfloat16),
            preferred_element_type=jnp.float32,
        )

    for piece in pieces:
        for image in range(pulses):
            rows = jnp.concatenate(
                [keep_ref[indices[piece], image], other_ref[piece, image]], axis=0
            )
            moved_ref[piece, image] = jnp.dot(
                first_ref[image],
                jnp.concatenate([rows, rows], axis=0),
                preferred_element_type=jnp.float32,
            )

    def read_first(piece):
        return lambda image, row: (
            moved_ref[piece, image, row : row + ROWS],
            moved_ref[piece, image, beams + row : beams + row + ROWS],
        )

    def read_level(piece):
        return lambda image, row: (
            level_ref[piece, image, row : row + ROWS, :columns],
            level_ref[piece, image, row : row + ROWS, columns:],
        )

    def write_picture(piece):
        def write(image, row, real, imag):
            picture_ref[piece, image, row : row + ROWS, :columns] = real
            picture_ref[piece, image, row : row + ROWS, columns:] = imag

        return write

    for piece in pieces:
        merge(piece, pulses, 1, read_first(piece), write_picture(piece))
        for image in range(pulses // 2):
            lift(piece, image, image)
    base = 1 + pulses // 2
    slot = pulses // 2
    count = pulses // 2
    while count > 1:
        for piece in pieces:
            merge(piece, count, base, read_level(piece), write_picture(piece))
            for image in range(count // 2 if count > 2 else 0):
                lift(piece, image, slot + image)
        count //= 2
        base += count
        slot += count
    for piece in pieces:
        out_refs[piece][0] = picture_ref[piece, 0, :, :columns].astype(jnp.bfloat16)
        out_refs[piece][1] = picture_ref[piece, 0, :, columns:].astype(jnp.bfloat16)


def far_kernel(distances, *rest):
    *image_refs, outer_ref, phase_ref, far_ref = rest
    pulse_place = lax.axis_index("pulse")
    terms = [
        risen(outer_ref, phase_ref, jnp.bitwise_xor(pulse_place, distance), ref[0], ref[1])
        for distance, ref in zip(distances, image_refs)
    ]
    real = terms[0][0] + terms[1][0]
    imag = terms[0][1] + terms[1][1]
    half = jnp.bitwise_xor(jnp.right_shift(pulse_place, 1), 1)
    far_ref[0], far_ref[1] = risen(outer_ref, phase_ref, 4 + half, real, imag)


def near_kernel(far_ref, image_ref, own_ref, outer_ref, phase_ref, out_ref):
    pulse_place = lax.axis_index("pulse")
    near = risen(
        outer_ref, phase_ref, jnp.bitwise_xor(pulse_place, 1), image_ref[0], image_ref[1]
    )
    real = own_ref[0] + near[0]
    imag = own_ref[1] + near[1]
    half = jnp.right_shift(pulse_place, 1)
    real, imag = risen(outer_ref, phase_ref, 4 + half, real, imag)
    out_ref[0] = real + far_ref[0]
    out_ref[1] = imag + far_ref[1]


def cost(micros):
    return pl.CostEstimate(
        flops=int(micros * 1.1e9), bytes_accessed=int(micros * 3.6e6), transcendentals=0
    )


PARAMS = dict(compiler_params=pltpu.CompilerParams(vmem_limit_bytes=40 * 1024 * 1024))


def fast(echoes, beam_angle, interp_table):
    rx_count = lax.axis_size("rx")
    pulse_count = lax.axis_size("pulse")
    _, pulses, channels, length = echoes.shape
    beams = beam_angle.shape[0]
    width = length // rx_count
    piece_width = width // pulse_count
    piece_tiles = piece_width // LANES
    rows = 2 * channels
    group = 2 * pulses
    chirp = jnp.asarray(chirp_bands_table())
    angles = beam_angle.reshape(1, beams)
    codes = interp_table.reshape(-1, beams)
    bf16 = jnp.bfloat16
    f32 = jnp.float32
    shape = jax.ShapeDtypeStruct
    across = swapped(echoes, "rng", 0)
    bands = pl.pallas_call(
        bands_kernel,
        out_shape=shape((channels, RX_TILE, 2 * LANES), bf16),
        out_specs=vmem(),
        name="bands",
        cost_estimate=cost(10.0),
        **PARAMS,
    )()
    tiles = length // LANES
    filtered_shape = shape((rows * pulses, (tiles + 2 * HALO_TILES - 1) * LANES), bf16)
    filtered = pl.pallas_call(
        interior_kernel,
        out_shape=filtered_shape,
        in_specs=[vmem()] * 2,
        out_specs=vmem(),
        scratch_shapes=[
            pltpu.VMEM((tiles + 2, channels * group, LANES), f32),
            pltpu.VMEM((tiles + 1, rows * pulses, LANES), f32),
        ],
        name="interior",
        **PARAMS,
    )(echoes, bands)

    def pieces(count):
        return shape((count, pulses, rows, piece_width), bf16)

    last = pulse_count - 1
    groups = [[3, 2], [1, 0]]
    filtered, first_sent = pl.pallas_call(
        functools.partial(edges_kernel, (pulse_count, groups[:1])),
        out_shape=[filtered_shape, pieces(len(groups[0]))],
        in_specs=[vmem()] * 5,
        out_specs=[vmem()] * 2,
        scratch_shapes=[
            pltpu.VMEM((HALO_TILES + 1, channels * group, LANES), f32),
            pltpu.VMEM((HALO_TILES, rows * pulses, LANES), f32),
        ],
        input_output_aliases={0: 0},
        name="edges",
        **PARAMS,
    )(filtered, echoes, across, bands, chirp)
    phase = pl.pallas_call(
        functools.partial(phases_kernel, (pulses, rx_count, width)),
        out_shape=shape((pulse_count, pulses, 2, beams, piece_width), f32),
        in_specs=[vmem(), anywhere()],
        out_specs=vmem(),
        name="phases",
        **PARAMS,
    )(angles, first_sent)
    kept, *sent = pl.pallas_call(
        functools.partial(rest_kernel, pulse_count, groups[1:2]),
        out_shape=[pieces(pulse_count), pieces(len(groups[1]))],
        in_specs=[vmem()] * 2 + [anywhere()],
        out_specs=[vmem()] * 2,
        name="rest",
        **PARAMS,
    )(filtered, chirp, phase)
    first, inner = pl.pallas_call(
        functools.partial(weights_kernel, (pulses, channels, rx_count, pulse_count)),
        out_shape=[
            shape((pulses, 2 * beams, 8 * channels), bf16),
            shape((pulses - 2, beams, beams), bf16),
        ],
        in_specs=[vmem()] * 2 + [anywhere()],
        out_specs=[vmem()] * 2,
        name="weights",
        **PARAMS,
    )(angles, codes, kept)
    images = [None] * pulse_count

    def merge(members, piece):
        other = swapped(piece, "rx", 0)
        size = len(members)
        merged = pl.pallas_call(
            functools.partial(inner_kernel, [last - distance for distance in members]),
            out_shape=[shape((2, beams, piece_width), bf16)] * size,
            in_specs=[vmem()] * 5,
            out_specs=[vmem()] * size,
            scratch_shapes=[
                pltpu.VMEM((size, pulses, 2 * beams, piece_width), f32),
                pltpu.VMEM((size, pulses // 2, beams, 2 * piece_width), f32),
                pltpu.VMEM((size, pulses // 2, beams, 2 * piece_width), f32),
            ],
            name="inner",
            cost_estimate=cost(3.0),
            **PARAMS,
        )(kept, other, first, inner, phase)
        for distance, image in zip(members, merged):
            images[distance] = image

    merge(groups[0], first_sent)
    merge(groups[1], sent[0])
    for distance in range(1, pulse_count):
        pairs = [(i, i ^ distance) for i in range(pulse_count)]
        images[distance] = lax.ppermute(images[distance], "pulse", pairs)
    outer_count = 2 * pulse_count - 2
    picture_shape = shape((2, beams, piece_width), f32)
    outer, outer_phase, own = pl.pallas_call(
        functools.partial(outer_tables_kernel, (rx_count, width, pulse_count)),
        out_shape=[
            shape((outer_count, beams, beams), bf16),
            shape((outer_count, 2, beams, piece_width), f32),
            picture_shape,
        ],
        in_specs=[vmem()] * 3,
        out_specs=[vmem()] * 3,
        name="outer_tables",
        **PARAMS,
    )(angles, codes, images[0])
    far = pl.pallas_call(
        functools.partial(far_kernel, (3, 2)),
        out_shape=picture_shape,
        in_specs=[vmem()] * 4,
        out_specs=vmem(),
        name="far",
        **PARAMS,
    )(images[3], images[2], outer, outer_phase)
    return pl.pallas_call(
        near_kernel,
        out_shape=picture_shape,
        in_specs=[vmem()] * 5,
        out_specs=vmem(),
        name="near",
        **PARAMS,
    )(far, images[1], own, outer, outer_phase)


def power_of_two(count):
    return count > 0 and count & (count - 1) == 0


def per_device(echoes, beam_angle, interp_table):
    _, pulses, channels, length = echoes.shape
    rx_count = lax.axis_size("rx")
    pulse_count = lax.axis_size("pulse")
    piece_width = length // (rx_count * pulse_count)
    if (
        lax.axis_size("rng") == 2
        and rx_count == 2
        and channels == 8
        and pulses == 8
        and pulse_count == 4
        and power_of_two(beam_angle.shape[0])
        and beam_angle.shape[0] % 16 == 0
        and piece_width % LANES == 0
    ):
        return fast(echoes, beam_angle, interp_table)
    return local(echoes, beam_angle, interp_table)


def solution(mesh):
    placed = (P(None, ("slab", "pulse"), "rx", "rng"), P(), P())
    return jax.shard_map(
        per_device,
        mesh=mesh,
        in_specs=placed,
        out_specs=P(None, "slab", ("rng", "rx", "pulse")),
        check_vma=False,
    )
```

```python
import functools
import math

import jax
import jax.numpy as jnp
import ml_dtypes
import numpy as np
from jax import lax
from jax.experimental import pallas as pl
from jax.experimental.pallas import tpu as pltpu
from jax.sharding import PartitionSpec as P

RTAPS = 64
CTAPS = 512


half_root = 0.7071067811865476
full_turn = 2.0 * math.pi


def extended_2(block, sides, width):
    for axis, dim in sides:
        count = lax.axis_size(axis)
        forward = [(i, i + 1) for i in range(count - 1)]
        backward = [(target, source) for source, target in forward]
        low = lax.ppermute(
            lax.slice_in_dim(block, block.shape[dim] - width, None, axis=dim), axis, forward
        )
        high = lax.ppermute(lax.slice_in_dim(block, 0, width, axis=dim), axis, backward)
        block = jnp.concatenate([low, block, high], axis=dim)
    return block


def swapped(x, axis, distance):
    return lax.ppermute(x, axis, [(i, i ^ 1 << distance) for i in range(lax.axis_size(axis))])


def receiver_taps(channel_ids, tap_count):
    tap_index = jnp.arange(tap_count, dtype=jnp.float32)
    window = 0.5 - 0.5 * jnp.cos(full_turn * (tap_index + 0.5) / tap_count)
    window = window / jnp.sqrt(jnp.sum(window * window))
    channel = channel_ids.astype(jnp.float32)[:, None] + 1.0
    angle = full_turn * channel * (tap_index - tap_count // 2) / (4 * tap_count)
    return (
        (window * jnp.cos(angle)).astype(jnp.bfloat16),
        (window * jnp.sin(angle)).astype(jnp.bfloat16),
    )


def chirp_taps(tap_count):
    offset = jnp.arange(tap_count, dtype=jnp.int32) - tap_count // 2
    phase_step = jnp.mod(offset * offset, 2 * tap_count).astype(jnp.float32)
    angle = math.pi * phase_step / tap_count
    scale = 1.0 / math.sqrt(tap_count)
    return (
        (jnp.cos(angle) * scale).astype(jnp.bfloat16),
        (-jnp.sin(angle) * scale).astype(jnp.bfloat16),
    )


def steering(beam_angle, receivers):
    channel = jnp.arange(receivers, dtype=jnp.int32)
    turns = jnp.mod(beam_angle[:, None] * channel[None, :], 1024).astype(jnp.float32)
    angle = full_turn * turns / 1024.0
    scale = 1.0 / math.sqrt(receivers)
    return (
        (jnp.cos(angle) * scale).astype(jnp.bfloat16),
        (-jnp.sin(angle) * scale).astype(jnp.bfloat16),
    )


def interp_matrices(codes, beam_count):
    shifted = codes // 4 - 1
    fraction = jnp.mod(codes, 4).astype(jnp.float32) / 4.0
    weights = (
        -fraction * (fraction - 1.0) * (fraction - 2.0) / 6.0,
        (fraction + 1.0) * (fraction - 1.0) * (fraction - 2.0) / 2.0,
        -(fraction + 1.0) * fraction * (fraction - 2.0) / 2.0,
        (fraction + 1.0) * fraction * (fraction - 1.0) / 6.0,
    )
    columns = jnp.arange(beam_count, dtype=jnp.int32)
    matrices = jnp.zeros(codes.shape + (beam_count,), jnp.float32)
    for tap_index in range(4):
        target = jnp.mod(columns + shifted + tap_index - 1, beam_count)
        matrices = matrices + weights[tap_index][..., None] * (target[..., None] == columns).astype(
            jnp.float32
        )
    return matrices


def phases(node_ids, positions, beam_angle, side):
    base = jnp.mod(beam_angle[:, None] * (positions[None, :] + 1), 1024)
    factor = 2 * node_ids + side + 1
    turns = jnp.mod(base[:, None, :] * factor[None, :, None], 1024).astype(jnp.float32)
    angle = full_turn * turns / 1024.0
    return (jnp.cos(angle), jnp.sin(angle))


def side_term(picture, matrices, cosine, sine):
    moved = jnp.einsum("gqa,cagr->cqgr", matrices, picture, precision=lax.Precision.HIGHEST)
    return (cosine * moved[0] - sine * moved[1], sine * moved[0] + cosine * moved[1])


def merge_pair(left_image, right_image, node_ids, positions, beam_angle, interp_table):
    matrices = interp_matrices(interp_table[node_ids], left_image.shape[1])
    left_cos, left_sin = phases(node_ids, positions, beam_angle, 0)
    right_cos, right_sin = phases(node_ids, positions, beam_angle, 1)
    left_re, left_im = side_term(left_image, matrices[:, 0], left_cos, left_sin)
    right_re, right_im = side_term(right_image, matrices[:, 1], right_cos, right_sin)
    return jnp.stack([(left_re + right_re) * half_root, (left_im + right_im) * half_root])


def toeplitz_blocks(taps_re, taps_im):
    tap_count = taps_re.shape[-1]
    leading = taps_re.shape[:-1]

    def lay_out(taps):
        padded = jnp.concatenate([taps, jnp.zeros(leading + (tap_count + 1,), taps.dtype)], axis=-1)
        tiled = jnp.tile(padded, (1,) * len(leading) + (tap_count,))
        banded = tiled[..., : 2 * tap_count * tap_count].reshape(
            leading + (tap_count, 2 * tap_count)
        )
        return jnp.swapaxes(banded, -1, -2)

    real_band = lay_out(taps_re)
    imag_band = lay_out(taps_im)
    upper = jnp.concatenate([real_band, imag_band], axis=-1)
    lower = jnp.concatenate([-imag_band, real_band], axis=-1)
    return jnp.concatenate([upper, lower], axis=-2)


def block_filter(extended, matrices, tap_count, per_channel):
    pulses, channels, length = extended.shape[1:]
    blocks = length // tap_count - 1
    pieces = extended.reshape(2, pulses, channels, blocks + 1, tap_count)
    windows = jnp.concatenate([pieces[:, :, :, :-1], pieces[:, :, :, 1:]], axis=4)
    windows = jnp.transpose(windows, (1, 2, 3, 0, 4)).reshape(
        pulses, channels, blocks, 4 * tap_count
    )
    if per_channel:
        output = jnp.einsum("pcnw,cwo->pcno", windows, matrices, preferred_element_type=jnp.float32)
    else:
        output = jnp.einsum("pcnw,wo->pcno", windows, matrices, preferred_element_type=jnp.float32)
    output = output.reshape(pulses, channels, blocks, 2, tap_count)
    return jnp.transpose(output, (3, 0, 1, 2, 4)).reshape(2, pulses, channels, blocks * tap_count)


def local(echoes, beam_angle, interp_table):
    rx_count = lax.axis_size("rx")
    pulse_count = lax.axis_size("pulse")
    rng_place = lax.axis_index("rng")
    rx_place = lax.axis_index("rx")
    pulse_place = lax.axis_index("pulse")
    pulses, channels, length = echoes.shape[1:]
    beam_count = beam_angle.shape[0]
    receivers = channels * rx_count
    channel_ids = rx_place * channels + jnp.arange(channels, dtype=jnp.int32)
    rx_re, rx_im = receiver_taps(channel_ids, RTAPS)
    rx_bands = toeplitz_blocks(rx_re, rx_im)
    chirp_re, chirp_im = chirp_taps(CTAPS)
    chirp_band = toeplitz_blocks(chirp_re, chirp_im)
    extended = extended_2(echoes, (("rng", 3),), RTAPS // 2)
    filtered = block_filter(extended, rx_bands, RTAPS, True).astype(jnp.bfloat16)
    filtered = extended_2(filtered, (("rng", 3),), CTAPS // 2)
    compressed = block_filter(filtered, chirp_band, CTAPS, False).astype(jnp.bfloat16)
    steering_real, steering_imaginary = steering(beam_angle, receivers)
    steer_matrix = jnp.concatenate(
        [
            jnp.concatenate([steering_real, -steering_imaginary], axis=1),
            jnp.concatenate([steering_imaginary, steering_real], axis=1),
        ],
        axis=0,
    )
    arrived = lax.all_to_all(compressed, "rx", split_axis=3, concat_axis=2, tiled=True)
    item_count, recv_count, owned_cols = arrived.shape[1:]
    stacked = jnp.transpose(arrived, (0, 2, 1, 3)).reshape(2 * recv_count, item_count * owned_cols)
    formed = jnp.dot(steer_matrix, stacked, preferred_element_type=jnp.float32)
    picture = formed.reshape(2, beam_count, item_count, owned_cols)
    owned_width = length // rx_count
    positions = (
        rng_place * length + rx_place * owned_width + jnp.arange(owned_width, dtype=jnp.int32)
    )
    for level in range(pulses.bit_length() - 1):
        groups_now = pulses >> level + 1
        node_ids = (pulse_count + pulse_place) * groups_now + jnp.arange(
            groups_now, dtype=jnp.int32
        )
        paired = picture.reshape(2, beam_count, groups_now, 2, owned_width)
        picture = merge_pair(
            paired[:, :, :, 0], paired[:, :, :, 1], node_ids, positions, beam_angle, interp_table
        )
    picture = picture[:, :, 0]
    cross_levels = pulse_count.bit_length() - 1
    piece_width = owned_width // pulse_count
    pieces = picture.reshape(2, beam_count, pulse_count, piece_width)
    spots = positions.reshape(pulse_count, piece_width)
    for level in range(cross_levels):
        parity = jnp.right_shift(pulse_place, level) & 1
        count_now = pieces.shape[2]
        paired = pieces.reshape(2, beam_count, count_now // 2, 2, piece_width)
        kept_half = lax.dynamic_index_in_dim(paired, parity, 3, keepdims=False)
        sent_half = lax.dynamic_index_in_dim(paired, 1 - parity, 3, keepdims=False)
        partner = swapped(sent_half, "pulse", level)
        spot_pairs = spots.reshape(count_now // 2, 2, piece_width)
        spots = lax.dynamic_index_in_dim(spot_pairs, parity, 1, keepdims=False)
        own_part = kept_half.reshape(2, beam_count, -1)
        other_part = partner.reshape(2, beam_count, -1)
        left_image = jnp.where(parity == 0, own_part, other_part)
        right_image = jnp.where(parity == 0, other_part, own_part)
        combine_node_ids = jnp.reshape(
            (pulse_count >> level + 1) + jnp.right_shift(pulse_place, level + 1), (1,)
        )
        merged = merge_pair(
            left_image[:, :, None],
            right_image[:, :, None],
            combine_node_ids,
            spots.reshape(-1),
            beam_angle,
            interp_table,
        )
        flat = merged[:, :, 0]
        pieces = flat.reshape(2, beam_count, count_now // 2, piece_width)
    picture = pieces.reshape(2, beam_count, piece_width)
    return picture


LANES = 128
RX_TILE = LANES + RTAPS
CHIRP_TILE = 6 * LANES
HALO_TILES = 3
HALO = HALO_TILES * LANES


def vmem():
    return pl.BlockSpec(memory_space=pltpu.VMEM)


def hbm():
    return pl.BlockSpec(memory_space=pltpu.HBM)


def anywhere():
    return pl.BlockSpec(memory_space=pl.ANY)


def chirp_bands_table():
    offset = np.arange(CTAPS) - CTAPS // 2
    angle = math.pi * np.mod(offset * offset, 2 * CTAPS) / CTAPS
    scale = 1.0 / math.sqrt(CTAPS)
    offset = np.arange(CHIRP_TILE)[:, None] - np.arange(LANES)[None, :] - (LANES - RTAPS // 2)
    inside = (offset >= 0) & (offset < CTAPS)
    place = np.clip(offset, 0, CTAPS - 1)
    bands = [
        np.where(inside, taps[place], 0.0)
        for taps in (np.cos(angle) * scale, -np.sin(angle) * scale)
    ]
    return np.concatenate(bands, axis=-1).astype(ml_dtypes.bfloat16)


def filter_channel(windows, bands, pulses):
    product = jnp.dot(windows, bands, preferred_element_type=jnp.float32)
    product = product.reshape(-1, 2, pulses, 2 * LANES)
    real = product[:, 0, :, :LANES] - product[:, 1, :, LANES:]
    imag = product[:, 0, :, LANES:] + product[:, 1, :, :LANES]
    return real, imag


def bands_kernel(bands_ref):
    channels = bands_ref.shape[0]
    first_channel = lax.axis_index("rx") * channels
    lane = lax.broadcasted_iota(jnp.int32, (channels, LANES), 1)
    channel = lax.broadcasted_iota(jnp.int32, (channels, LANES), 0) + first_channel + 1
    tap = jnp.bitwise_and(LANES - lane, LANES - 1)
    unit = 1024 // RTAPS
    window = 0.5 - 0.5 * turn_parts(tap * unit + unit // 2)[0]
    window = jnp.where(tap < RTAPS, window * (1.0 / math.sqrt(RTAPS * 3 / 8)), 0.0)
    turn = channel * (tap - RTAPS // 2) * (1024 // (4 * RTAPS))
    row = lax.broadcasted_iota(jnp.int32, (LANES, LANES), 0)
    upper = lax.broadcasted_iota(jnp.int32, (LANES, LANES), 1) <= row
    for part, wave in enumerate(turn_parts(jnp.bitwise_and(turn, 1023))):
        taps = window * wave
        span = slice(part * LANES, (part + 1) * LANES)
        for index in range(channels):
            spread = jnp.broadcast_to(taps[index : index + 1], (LANES, LANES))
            rolled = pltpu.roll(spread, 0, 1, stride=1, stride_axis=0)
            bands_ref[index, :LANES, span] = jnp.where(upper, rolled, 0.0).astype(jnp.bfloat16)
            lower = jnp.where(upper, 0.0, rolled)[:RTAPS]
            bands_ref[index, LANES:, span] = lower.astype(jnp.bfloat16)


def interior_kernel(echo_ref, bands_ref, filtered_ref, rows_in, rows_out):
    _, pulses, channels, length = echo_ref.shape
    tiles = length // LANES
    group = 2 * pulses
    empty = jnp.zeros(rows_in.shape[1:], jnp.float32)
    rows_in[0] = empty
    rows_in[tiles + 1] = empty
    for part in range(2):
        for pulse in range(pulses):
            where = pl.ds(part * pulses + pulse, channels, stride=group)
            block = echo_ref[part, pulse].astype(jnp.float32)
            for tile in range(tiles):
                rows_in[tile + 1, where, :] = block[:, tile * LANES : (tile + 1) * LANES]
    lane = lax.broadcasted_iota(jnp.int32, (pulses, LANES), 1)
    mask = jnp.where(lane >= LANES - RTAPS // 2, 1.0, 0.0)
    for channel in range(channels):
        rows = rows_in[:, channel * group : (channel + 1) * group, :].astype(jnp.bfloat16)
        windows = jnp.concatenate(
            [rows[:-1].reshape(-1, LANES), rows[1:].reshape(-1, LANES)[:, :RTAPS]], axis=1
        )
        real, imag = filter_channel(windows, bands_ref[channel], pulses)
        for tile in range(tiles + 1):
            tile_re, tile_im = real[tile], imag[tile]
            if tile == 0:
                tile_re, tile_im = tile_re * mask, tile_im * mask
            if tile == tiles:
                tile_re, tile_im = tile_re * (1.0 - mask), tile_im * (1.0 - mask)
            rows_out[tile, pl.ds(channel, pulses, stride=2 * channels), :] = tile_re
            rows_out[tile, pl.ds(channels + channel, pulses, stride=2 * channels), :] = tile_im
    rows = filtered_ref.shape[0]
    nothing = jnp.zeros((rows, (HALO_TILES - 1) * LANES), jnp.bfloat16)
    filtered_ref[:, : (HALO_TILES - 1) * LANES] = nothing
    filtered_ref[:, (HALO_TILES + tiles) * LANES :] = nothing
    for tile in range(tiles + 1):
        spot = (HALO_TILES - 1 + tile) * LANES
        filtered_ref[:, spot : spot + LANES] = rows_out[tile].astype(jnp.bfloat16)


def chirp_pieces(filtered_ref, chirp_ref, owner, piece_count, distances, out_ref):
    pulse_place = lax.axis_index("pulse")
    _, pulses, rows, width = out_ref.shape
    tiles = width // LANES
    channels = rows // 2
    windows = []
    for distance in distances:
        piece = jnp.bitwise_xor(pulse_place, distance)
        first = (owner * piece_count + piece) * tiles
        for tile in range(tiles):
            start = pl.multiple_of((first + tile) * LANES, LANES)
            windows.append(filtered_ref[:, pl.ds(start, CHIRP_TILE)])
    product = jnp.dot(
        jnp.concatenate(windows, axis=0), chirp_ref[...], preferred_element_type=jnp.float32
    )
    product = product.reshape(len(windows), pulses, rows, 2 * LANES)
    for index in range(len(distances)):
        for tile in range(tiles):
            block = product[index * tiles + tile]
            real = block[:, :channels, :LANES] - block[:, channels:, LANES:]
            imag = block[:, :channels, LANES:] + block[:, channels:, :LANES]
            out_ref[index, :, :, tile * LANES : (tile + 1) * LANES] = jnp.concatenate(
                [real, imag], axis=1
            ).astype(jnp.bfloat16)


def edges_kernel(
    plan, inner_ref, echo_ref, across_ref, bands_ref, chirp_ref, filtered_ref, *rest
):
    *send_refs, rows_in, rows_out = rest
    del inner_ref
    _, pulses, channels, length = echo_ref.shape
    tiles = length // LANES
    group = 2 * pulses
    lowest = lax.axis_index("rng") == 0
    far = pl.ds(pl.multiple_of(jnp.where(lowest, 0, length - HALO), LANES), HALO)
    for part in range(2):
        for pulse in range(pulses):
            where = pl.ds(part * pulses + pulse, channels, stride=group)
            edge = across_ref[part, pulse, :, far].astype(jnp.float32)
            near_low = echo_ref[part, pulse, :, :LANES].astype(jnp.float32)
            near_high = echo_ref[part, pulse, :, length - LANES :].astype(jnp.float32)
            pieces = [edge[:, t * LANES : (t + 1) * LANES] for t in range(HALO_TILES)]
            for tile in range(HALO_TILES + 1):
                high = near_high if tile == 0 else pieces[tile - 1]
                low = near_low if tile == HALO_TILES else pieces[tile]
                rows_in[tile, where, :] = jnp.where(lowest, high, low)
    for channel in range(channels):
        rows = rows_in[:, channel * group : (channel + 1) * group, :].astype(jnp.bfloat16)
        windows = jnp.concatenate(
            [rows[:-1].reshape(-1, LANES), rows[1:].reshape(-1, LANES)[:, :RTAPS]], axis=1
        )
        real, imag = filter_channel(windows, bands_ref[channel], pulses)
        for tile in range(HALO_TILES):
            rows_out[tile, pl.ds(channel, pulses, stride=2 * channels), :] = real[tile]
            rows_out[tile, pl.ds(channels + channel, pulses, stride=2 * channels), :] = imag[tile]
    first = jnp.where(lowest, tiles + HALO_TILES - 1, 0)
    for tile in range(HALO_TILES):
        start = pl.multiple_of((first + tile) * LANES, LANES)
        filtered_ref[:, pl.ds(start, LANES)] = rows_out[tile].astype(jnp.bfloat16)
    piece_count, groups = plan
    for distances, send_ref in zip(groups, send_refs):
        chirp_pieces(
            filtered_ref, chirp_ref, 1 - lax.axis_index("rx"), piece_count, distances, send_ref
        )


def rest_kernel(piece_count, groups, filtered_ref, chirp_ref, after_ref, keep_ref, *send_refs):
    rx_place = lax.axis_index("rx")
    own = list(range(piece_count - 1, -1, -1))
    chirp_pieces(filtered_ref, chirp_ref, rx_place, piece_count, own, keep_ref)
    for distances, send_ref in zip(groups, send_refs):
        chirp_pieces(filtered_ref, chirp_ref, 1 - rx_place, piece_count, distances, send_ref)


def turn_parts(step):
    shifted = step + 128
    angle = (jnp.bitwise_and(shifted, 255) - 128).astype(jnp.float32) * (full_turn / 1024.0)
    quarter = jnp.right_shift(shifted, 8)
    square = angle * angle
    cosine = 1.0 + square * (-1 / 2 + square * (1 / 24 + square * (-1 / 720 + square * (1 / 40320))))
    sine = angle * (1.0 + square * (-1 / 6 + square * (1 / 120 + square * (-1 / 5040))))
    odd = jnp.bitwise_and(quarter, 1) == 1
    real = jnp.where(odd, sine, cosine)
    imag = jnp.where(odd, cosine, sine)
    real = jnp.where(jnp.bitwise_and(quarter + 1, 2) == 2, -real, real)
    imag = jnp.where(jnp.bitwise_and(quarter, 2) == 2, -imag, imag)
    return real, imag


def turned(real, imag, phase_re, phase_im):
    return phase_re * real - phase_im * imag, phase_im * real + phase_re * imag


def as_column(row):
    count = row.shape[1]
    first = lax.broadcasted_iota(jnp.int32, (count, count), 0)
    second = lax.broadcasted_iota(jnp.int32, (count, count), 1)
    spread = jnp.where(first == second, row.astype(jnp.float32), 0.0)
    return jnp.sum(spread, axis=1, keepdims=True).astype(jnp.int32)


def interp_matrix(code):
    beams = code.shape[0]
    angle_bin = lax.broadcasted_iota(jnp.int32, (beams, beams), 0)
    column = lax.broadcasted_iota(jnp.int32, (beams, beams), 1)
    half = 2 * beams
    away = jnp.bitwise_and(4 * (column - angle_bin + 1) - code + half, 4 * beams - 1) - half
    away = jnp.abs(away.astype(jnp.float32)) * 0.25
    near = (1.0 - away * away) * (2.0 - away) * 0.5
    far = (1.0 - away) * (2.0 - away) * (3.0 - away) * (1.0 / 6.0)
    matrix = jnp.where(away < 1.0, near, jnp.where(away < 2.0, far, 0.0))
    return matrix.astype(jnp.bfloat16)


def code_columns(codes_ref, rows):
    picked = [codes_ref[pl.ds(row, 1), :] for row in rows]
    picked = jnp.concatenate(picked, axis=0).astype(jnp.float32)
    spare = -len(rows) % 8
    if spare:
        picked = jnp.concatenate([picked, jnp.zeros((spare, picked.shape[1]), jnp.float32)], axis=0)
    return picked.T.astype(jnp.int32)


def weights_kernel(sizes, angle_ref, codes_ref, after_ref, first_ref, inner_ref):
    pulses, channels, rx_count, piece_count = sizes
    rx_place = lax.axis_index("rx")
    pulse_place = lax.axis_index("pulse")
    beams = angle_ref.shape[1]
    angle = as_column(angle_ref[...])
    rows = []
    now = pulses
    while now > 1:
        base = now * piece_count + pulse_place * now
        rows.extend(base + index for index in range(now))
        now //= 2
    codes = code_columns(codes_ref, rows)
    column = lax.broadcasted_iota(jnp.int32, (1, 4 * channels * 2), 1)
    within = jnp.bitwise_and(column, 4 * channels - 1)
    owner = jnp.bitwise_xor(rx_place, jnp.where(within >= 2 * channels, 1, 0))
    receiver = owner * channels + jnp.bitwise_and(column, channels - 1)
    is_imag = jnp.bitwise_and(within, channels) != 0
    scale = 1.0 / math.sqrt(channels * rx_count)
    steer_re, steer_im = turn_parts(jnp.bitwise_and(angle * receiver, 1023))
    steer_re = (steer_re * scale).astype(jnp.bfloat16).astype(jnp.float32)
    steer_im = (-steer_im * scale).astype(jnp.bfloat16).astype(jnp.float32)
    steer = jnp.concatenate(
        [
            jnp.where(is_imag, -steer_im, steer_re).astype(jnp.bfloat16),
            jnp.where(is_imag, steer_re, steer_im).astype(jnp.bfloat16),
        ],
        axis=1,
    )
    low_half = column >= 4 * channels
    entries = 8 * channels
    matrices = [interp_matrix(codes[:, index : index + 1]) for index in range(len(rows))]
    composed = jnp.dot(
        jnp.concatenate(matrices[:pulses], axis=0), steer, preferred_element_type=jnp.float32
    )
    for index in range(pulses):
        for part in range(2):
            value = composed[
                index * beams : (index + 1) * beams, part * entries : (part + 1) * entries
            ]
            high = value.astype(jnp.bfloat16).astype(jnp.float32)
            first_ref[index, part * beams : (part + 1) * beams, :] = jnp.where(
                low_half, value - high, high
            ).astype(jnp.bfloat16)
    for index, matrix in enumerate(matrices[pulses:]):
        inner_ref[index] = matrix


def phases_kernel(sizes, angle_ref, after_ref, phase_ref):
    pulses, rx_count, width = sizes
    rng_place = lax.axis_index("rng")
    rx_place = lax.axis_index("rx")
    pulse_place = lax.axis_index("pulse")
    piece_count = phase_ref.shape[0]
    piece_tiles = phase_ref.shape[4] // LANES
    angle = as_column(angle_ref[...])
    factors = []
    now = pulses
    while now > 1:
        base = now * piece_count + pulse_place * now
        factors.extend(base + 1 + index for index in range(0, now, 2))
        now //= 2
    lane = lax.broadcasted_iota(jnp.int32, (1, LANES), 1)
    block = (rng_place * rx_count + rx_place) * width + 1
    base = jnp.bitwise_and(angle * (block + lane), 1023)
    for slot, factor in enumerate([1, *factors]):
        scale = half_root if slot else 1.0
        real, imag = turn_parts(jnp.bitwise_and(base * factor, 1023))
        real, imag = real * scale, imag * scale
        step = turn_parts(jnp.bitwise_and(angle * (factor * LANES), 1023))
        for tile in range(piece_count * piece_tiles):
            index = piece_count - 1 - jnp.bitwise_xor(pulse_place, tile // piece_tiles)
            start = tile % piece_tiles * LANES
            phase_ref[index, slot, 0, :, start : start + LANES] = real
            phase_ref[index, slot, 1, :, start : start + LANES] = imag
            real, imag = turned(real, imag, *step)


def risen(outer_ref, phase_ref, slot, real, imag):
    matrix = outer_ref[slot]
    moved_re = jnp.dot(matrix, real.astype(jnp.bfloat16), preferred_element_type=jnp.float32)
    moved_im = jnp.dot(matrix, imag.astype(jnp.bfloat16), preferred_element_type=jnp.float32)
    return turned(moved_re, moved_im, phase_ref[slot, 0], phase_ref[slot, 1])


def outer_tables_kernel(sizes, angle_ref, codes_ref, image_ref, outer_ref, phase_ref, own_ref):
    rx_count, width, piece_count = sizes
    rng_place = lax.axis_index("rng")
    rx_place = lax.axis_index("rx")
    pulse_place = lax.axis_index("pulse")
    piece_width = phase_ref.shape[3]
    angle = as_column(angle_ref[...])
    lane = lax.broadcasted_iota(jnp.int32, (1, piece_width), 1)
    block = (rng_place * rx_count + rx_place) * width + 1
    base = jnp.bitwise_and(angle * (block + pulse_place * piece_width + lane), 1023)
    counts = [piece_count >> level for level in range(piece_count.bit_length() - 1)]
    rows = [count + index for count in counts for index in range(count)]
    codes = code_columns(codes_ref, rows)
    for slot, row in enumerate(rows):
        outer_ref[slot] = interp_matrix(codes[:, slot : slot + 1])
        real, imag = turn_parts(jnp.bitwise_and(base * (row + 1), 1023))
        phase_ref[slot, 0] = real * half_root
        phase_ref[slot, 1] = imag * half_root
    own_ref[0], own_ref[1] = risen(
        outer_ref, phase_ref, pulse_place, image_ref[0], image_ref[1]
    )


ROWS = 8


def inner_kernel(indices, keep_ref, other_ref, first_ref, inner_ref, phase_ref, *rest):
    *out_refs, moved_ref, picture_ref, level_ref = rest
    pulses = keep_ref.shape[1]
    beams, columns = out_refs[0].shape[1:]
    pieces = range(len(indices))

    def merge(piece, count, base, read, write):
        index = indices[piece]
        for row in range(0, beams, ROWS):
            span = slice(row, row + ROWS)
            step = (phase_ref[index, 0, 0, span], phase_ref[index, 0, 1, span])
            for image in range(0, count, 2):
                slot = base + image // 2
                left = read(image, row)
                right = turned(*read(image + 1, row), *step)
                phase = (phase_ref[index, slot, 0, span], phase_ref[index, slot, 1, span])
                write(
                    image // 2, row, *turned(left[0] + right[0], left[1] + right[1], *phase)
                )

    def lift(piece, image, slot):
        level_ref[piece, image] = jnp.dot(
            inner_ref[slot],
            picture_ref[piece, image].astype(jnp.bfloat16),
            preferred_element_type=jnp.float32,
        )

    for piece in pieces:
        for image in range(pulses):
            rows = jnp.concatenate(
                [keep_ref[indices[piece], image], other_ref[piece, image]], axis=0
            )
            moved_ref[piece, image] = jnp.dot(
                first_ref[image],
                jnp.concatenate([rows, rows], axis=0),
                preferred_element_type=jnp.float32,
            )

    def read_first(piece):
        return lambda image, row: (
            moved_ref[piece, image, row : row + ROWS],
            moved_ref[piece, image, beams + row : beams + row + ROWS],
        )

    def read_level(piece):
        return lambda image, row: (
            level_ref[piece, image, row : row + ROWS, :columns],
            level_ref[piece, image, row : row + ROWS, columns:],
        )

    def write_picture(piece):
        def write(image, row, real, imag):
            picture_ref[piece, image, row : row + ROWS, :columns] = real
            picture_ref[piece, image, row : row + ROWS, columns:] = imag

        return write

    for piece in pieces:
        merge(piece, pulses, 1, read_first(piece), write_picture(piece))
        for image in range(pulses // 2):
            lift(piece, image, image)
    base = 1 + pulses // 2
    slot = pulses // 2
    count = pulses // 2
    while count > 1:
        for piece in pieces:
            merge(piece, count, base, read_level(piece), write_picture(piece))
            for image in range(count // 2 if count > 2 else 0):
                lift(piece, image, slot + image)
        count //= 2
        base += count
        slot += count
    for piece in pieces:
        out_refs[piece][0] = picture_ref[piece, 0, :, :columns].astype(jnp.bfloat16)
        out_refs[piece][1] = picture_ref[piece, 0, :, columns:].astype(jnp.bfloat16)


def far_kernel(distances, *rest):
    *image_refs, outer_ref, phase_ref, far_ref = rest
    pulse_place = lax.axis_index("pulse")
    terms = [
        risen(outer_ref, phase_ref, jnp.bitwise_xor(pulse_place, distance), ref[0], ref[1])
        for distance, ref in zip(distances, image_refs)
    ]
    real = terms[0][0] + terms[1][0]
    imag = terms[0][1] + terms[1][1]
    half = jnp.bitwise_xor(jnp.right_shift(pulse_place, 1), 1)
    far_ref[0], far_ref[1] = risen(outer_ref, phase_ref, 4 + half, real, imag)


def near_kernel(far_ref, image_ref, own_ref, outer_ref, phase_ref, out_ref):
    pulse_place = lax.axis_index("pulse")
    near = risen(
        outer_ref, phase_ref, jnp.bitwise_xor(pulse_place, 1), image_ref[0], image_ref[1]
    )
    real = own_ref[0] + near[0]
    imag = own_ref[1] + near[1]
    half = jnp.right_shift(pulse_place, 1)
    real, imag = risen(outer_ref, phase_ref, 4 + half, real, imag)
    out_ref[0] = real + far_ref[0]
    out_ref[1] = imag + far_ref[1]


def cost(micros):
    return pl.CostEstimate(
        flops=int(micros * 1.1e9), bytes_accessed=int(micros * 3.6e6), transcendentals=0
    )


PARAMS = dict(compiler_params=pltpu.CompilerParams(vmem_limit_bytes=40 * 1024 * 1024))


def fast(echoes, beam_angle, interp_table):
    rx_count = lax.axis_size("rx")
    pulse_count = lax.axis_size("pulse")
    _, pulses, channels, length = echoes.shape
    beams = beam_angle.shape[0]
    width = length // rx_count
    piece_width = width // pulse_count
    piece_tiles = piece_width // LANES
    rows = 2 * channels
    group = 2 * pulses
    chirp = jnp.asarray(chirp_bands_table())
    angles = beam_angle.reshape(1, beams)
    codes = interp_table.reshape(-1, beams)
    bf16 = jnp.bfloat16
    f32 = jnp.float32
    shape = jax.ShapeDtypeStruct
    across = swapped(echoes, "rng", 0)
    bands = pl.pallas_call(
        bands_kernel,
        out_shape=shape((channels, RX_TILE, 2 * LANES), bf16),
        out_specs=vmem(),
        name="bands",
        cost_estimate=cost(10.0),
        **PARAMS,
    )()
    tiles = length // LANES
    filtered_shape = shape((rows * pulses, (tiles + 2 * HALO_TILES - 1) * LANES), bf16)
    filtered = pl.pallas_call(
        interior_kernel,
        out_shape=filtered_shape,
        in_specs=[vmem()] * 2,
        out_specs=vmem(),
        scratch_shapes=[
            pltpu.VMEM((tiles + 2, channels * group, LANES), f32),
            pltpu.VMEM((tiles + 1, rows * pulses, LANES), f32),
        ],
        name="interior",
        **PARAMS,
    )(echoes, bands)

    def pieces(count):
        return shape((count, pulses, rows, piece_width), bf16)

    last = pulse_count - 1
    groups = [[3, 2], [1, 0]]
    filtered, first_sent = pl.pallas_call(
        functools.partial(edges_kernel, (pulse_count, groups[:1])),
        out_shape=[filtered_shape, pieces(len(groups[0]))],
        in_specs=[vmem()] * 5,
        out_specs=[vmem()] * 2,
        scratch_shapes=[
            pltpu.VMEM((HALO_TILES + 1, channels * group, LANES), f32),
            pltpu.VMEM((HALO_TILES, rows * pulses, LANES), f32),
        ],
        input_output_aliases={0: 0},
        name="edges",
        **PARAMS,
    )(filtered, echoes, across, bands, chirp)
    phase = pl.pallas_call(
        functools.partial(phases_kernel, (pulses, rx_count, width)),
        out_shape=shape((pulse_count, pulses, 2, beams, piece_width), f32),
        in_specs=[vmem(), anywhere()],
        out_specs=vmem(),
        name="phases",
        **PARAMS,
    )(angles, first_sent)
    kept, *sent = pl.pallas_call(
        functools.partial(rest_kernel, pulse_count, groups[1:2]),
        out_shape=[pieces(pulse_count), pieces(len(groups[1]))],
        in_specs=[vmem()] * 2 + [anywhere()],
        out_specs=[vmem()] * 2,
        name="rest",
        **PARAMS,
    )(filtered, chirp, phase)
    first, inner = pl.pallas_call(
        functools.partial(weights_kernel, (pulses, channels, rx_count, pulse_count)),
        out_shape=[
            shape((pulses, 2 * beams, 8 * channels), bf16),
            shape((pulses - 2, beams, beams), bf16),
        ],
        in_specs=[vmem()] * 2 + [anywhere()],
        out_specs=[vmem()] * 2,
        name="weights",
        **PARAMS,
    )(angles, codes, kept)
    images = [None] * pulse_count

    def merge(members, piece):
        other = swapped(piece, "rx", 0)
        size = len(members)
        merged = pl.pallas_call(
            functools.partial(inner_kernel, [last - distance for distance in members]),
            out_shape=[shape((2, beams, piece_width), bf16)] * size,
            in_specs=[vmem()] * 5,
            out_specs=[vmem()] * size,
            scratch_shapes=[
                pltpu.VMEM((size, pulses, 2 * beams, piece_width), f32),
                pltpu.VMEM((size, pulses // 2, beams, 2 * piece_width), f32),
                pltpu.VMEM((size, pulses // 2, beams, 2 * piece_width), f32),
            ],
            name="inner",
            cost_estimate=cost(3.0),
            **PARAMS,
        )(kept, other, first, inner, phase)
        for distance, image in zip(members, merged):
            images[distance] = image

    merge(groups[0], first_sent)
    merge(groups[1], sent[0])
    for distance in range(1, pulse_count):
        pairs = [(i, i ^ distance) for i in range(pulse_count)]
        images[distance] = lax.ppermute(images[distance], "pulse", pairs)
    outer_count = 2 * pulse_count - 2
    picture_shape = shape((2, beams, piece_width), f32)
    outer, outer_phase, own = pl.pallas_call(
        functools.partial(outer_tables_kernel, (rx_count, width, pulse_count)),
        out_shape=[
            shape((outer_count, beams, beams), bf16),
            shape((outer_count, 2, beams, piece_width), f32),
            picture_shape,
        ],
        in_specs=[vmem()] * 3,
        out_specs=[vmem()] * 3,
        name="outer_tables",
        **PARAMS,
    )(angles, codes, images[0])
    far = pl.pallas_call(
        functools.partial(far_kernel, (2, 3)),
        out_shape=picture_shape,
        in_specs=[vmem()] * 4,
        out_specs=vmem(),
        name="far",
        **PARAMS,
    )(images[2], images[3], outer, outer_phase)
    return pl.pallas_call(
        near_kernel,
        out_shape=picture_shape,
        in_specs=[vmem()] * 5,
        out_specs=vmem(),
        name="near",
        **PARAMS,
    )(far, images[1], own, outer, outer_phase)


def power_of_two(count):
    return count > 0 and count & (count - 1) == 0


def per_device(echoes, beam_angle, interp_table):
    _, pulses, channels, length = echoes.shape
    rx_count = lax.axis_size("rx")
    pulse_count = lax.axis_size("pulse")
    piece_width = length // (rx_count * pulse_count)
    if (
        lax.axis_size("rng") == 2
        and rx_count == 2
        and channels == 8
        and pulses == 8
        and pulse_count == 4
        and power_of_two(beam_angle.shape[0])
        and beam_angle.shape[0] % 16 == 0
        and piece_width % LANES == 0
    ):
        return fast(echoes, beam_angle, interp_table)
    return local(echoes, beam_angle, interp_table)


def solution(mesh):
    placed = (P(None, ("slab", "pulse"), "rx", "rng"), P(), P())
    return jax.shard_map(
        per_device,
        mesh=mesh,
        in_specs=placed,
        out_specs=P(None, "slab", ("rng", "rx", "pulse")),
        check_vma=False,
    )
```

```python
import functools
import math

import jax
import jax.numpy as jnp
import ml_dtypes
import numpy as np
from jax import lax
from jax.experimental import pallas as pl
from jax.experimental.pallas import tpu as pltpu
from jax.sharding import PartitionSpec as P

RTAPS = 64
CTAPS = 512


half_root = 0.7071067811865476
full_turn = 2.0 * math.pi


def extended_2(block, sides, width):
    for axis, dim in sides:
        count = lax.axis_size(axis)
        forward = [(i, i + 1) for i in range(count - 1)]
        backward = [(target, source) for source, target in forward]
        low = lax.ppermute(
            lax.slice_in_dim(block, block.shape[dim] - width, None, axis=dim), axis, forward
        )
        high = lax.ppermute(lax.slice_in_dim(block, 0, width, axis=dim), axis, backward)
        block = jnp.concatenate([low, block, high], axis=dim)
    return block


def swapped(x, axis, distance):
    return lax.ppermute(x, axis, [(i, i ^ 1 << distance) for i in range(lax.axis_size(axis))])


def receiver_taps(channel_ids, tap_count):
    tap_index = jnp.arange(tap_count, dtype=jnp.float32)
    window = 0.5 - 0.5 * jnp.cos(full_turn * (tap_index + 0.5) / tap_count)
    window = window / jnp.sqrt(jnp.sum(window * window))
    channel = channel_ids.astype(jnp.float32)[:, None] + 1.0
    angle = full_turn * channel * (tap_index - tap_count // 2) / (4 * tap_count)
    return (
        (window * jnp.cos(angle)).astype(jnp.bfloat16),
        (window * jnp.sin(angle)).astype(jnp.bfloat16),
    )


def chirp_taps(tap_count):
    offset = jnp.arange(tap_count, dtype=jnp.int32) - tap_count // 2
    phase_step = jnp.mod(offset * offset, 2 * tap_count).astype(jnp.float32)
    angle = math.pi * phase_step / tap_count
    scale = 1.0 / math.sqrt(tap_count)
    return (
        (jnp.cos(angle) * scale).astype(jnp.bfloat16),
        (-jnp.sin(angle) * scale).astype(jnp.bfloat16),
    )


def steering(beam_angle, receivers):
    channel = jnp.arange(receivers, dtype=jnp.int32)
    turns = jnp.mod(beam_angle[:, None] * channel[None, :], 1024).astype(jnp.float32)
    angle = full_turn * turns / 1024.0
    scale = 1.0 / math.sqrt(receivers)
    return (
        (jnp.cos(angle) * scale).astype(jnp.bfloat16),
        (-jnp.sin(angle) * scale).astype(jnp.bfloat16),
    )


def interp_matrices(codes, beam_count):
    shifted = codes // 4 - 1
    fraction = jnp.mod(codes, 4).astype(jnp.float32) / 4.0
    weights = (
        -fraction * (fraction - 1.0) * (fraction - 2.0) / 6.0,
        (fraction + 1.0) * (fraction - 1.0) * (fraction - 2.0) / 2.0,
        -(fraction + 1.0) * fraction * (fraction - 2.0) / 2.0,
        (fraction + 1.0) * fraction * (fraction - 1.0) / 6.0,
    )
    columns = jnp.arange(beam_count, dtype=jnp.int32)
    matrices = jnp.zeros(codes.shape + (beam_count,), jnp.float32)
    for tap_index in range(4):
        target = jnp.mod(columns + shifted + tap_index - 1, beam_count)
        matrices = matrices + weights[tap_index][..., None] * (target[..., None] == columns).astype(
            jnp.float32
        )
    return matrices


def phases(node_ids, positions, beam_angle, side):
    base = jnp.mod(beam_angle[:, None] * (positions[None, :] + 1), 1024)
    factor = 2 * node_ids + side + 1
    turns = jnp.mod(base[:, None, :] * factor[None, :, None], 1024).astype(jnp.float32)
    angle = full_turn * turns / 1024.0
    return (jnp.cos(angle), jnp.sin(angle))


def side_term(picture, matrices, cosine, sine):
    moved = jnp.einsum("gqa,cagr->cqgr", matrices, picture, precision=lax.Precision.HIGHEST)
    return (cosine * moved[0] - sine * moved[1], sine * moved[0] + cosine * moved[1])


def merge_pair(left_image, right_image, node_ids, positions, beam_angle, interp_table):
    matrices = interp_matrices(interp_table[node_ids], left_image.shape[1])
    left_cos, left_sin = phases(node_ids, positions, beam_angle, 0)
    right_cos, right_sin = phases(node_ids, positions, beam_angle, 1)
    left_re, left_im = side_term(left_image, matrices[:, 0], left_cos, left_sin)
    right_re, right_im = side_term(right_image, matrices[:, 1], right_cos, right_sin)
    return jnp.stack([(left_re + right_re) * half_root, (left_im + right_im) * half_root])


def toeplitz_blocks(taps_re, taps_im):
    tap_count = taps_re.shape[-1]
    leading = taps_re.shape[:-1]

    def lay_out(taps):
        padded = jnp.concatenate([taps, jnp.zeros(leading + (tap_count + 1,), taps.dtype)], axis=-1)
        tiled = jnp.tile(padded, (1,) * len(leading) + (tap_count,))
        banded = tiled[..., : 2 * tap_count * tap_count].reshape(
            leading + (tap_count, 2 * tap_count)
        )
        return jnp.swapaxes(banded, -1, -2)

    real_band = lay_out(taps_re)
    imag_band = lay_out(taps_im)
    upper = jnp.concatenate([real_band, imag_band], axis=-1)
    lower = jnp.concatenate([-imag_band, real_band], axis=-1)
    return jnp.concatenate([upper, lower], axis=-2)


def block_filter(extended, matrices, tap_count, per_channel):
    pulses, channels, length = extended.shape[1:]
    blocks = length // tap_count - 1
    pieces = extended.reshape(2, pulses, channels, blocks + 1, tap_count)
    windows = jnp.concatenate([pieces[:, :, :, :-1], pieces[:, :, :, 1:]], axis=4)
    windows = jnp.transpose(windows, (1, 2, 3, 0, 4)).reshape(
        pulses, channels, blocks, 4 * tap_count
    )
    if per_channel:
        output = jnp.einsum("pcnw,cwo->pcno", windows, matrices, preferred_element_type=jnp.float32)
    else:
        output = jnp.einsum("pcnw,wo->pcno", windows, matrices, preferred_element_type=jnp.float32)
    output = output.reshape(pulses, channels, blocks, 2, tap_count)
    return jnp.transpose(output, (3, 0, 1, 2, 4)).reshape(2, pulses, channels, blocks * tap_count)


def local(echoes, beam_angle, interp_table):
    rx_count = lax.axis_size("rx")
    pulse_count = lax.axis_size("pulse")
    rng_place = lax.axis_index("rng")
    rx_place = lax.axis_index("rx")
    pulse_place = lax.axis_index("pulse")
    pulses, channels, length = echoes.shape[1:]
    beam_count = beam_angle.shape[0]
    receivers = channels * rx_count
    channel_ids = rx_place * channels + jnp.arange(channels, dtype=jnp.int32)
    rx_re, rx_im = receiver_taps(channel_ids, RTAPS)
    rx_bands = toeplitz_blocks(rx_re, rx_im)
    chirp_re, chirp_im = chirp_taps(CTAPS)
    chirp_band = toeplitz_blocks(chirp_re, chirp_im)
    extended = extended_2(echoes, (("rng", 3),), RTAPS // 2)
    filtered = block_filter(extended, rx_bands, RTAPS, True).astype(jnp.bfloat16)
    filtered = extended_2(filtered, (("rng", 3),), CTAPS // 2)
    compressed = block_filter(filtered, chirp_band, CTAPS, False).astype(jnp.bfloat16)
    steering_real, steering_imaginary = steering(beam_angle, receivers)
    steer_matrix = jnp.concatenate(
        [
            jnp.concatenate([steering_real, -steering_imaginary], axis=1),
            jnp.concatenate([steering_imaginary, steering_real], axis=1),
        ],
        axis=0,
    )
    arrived = lax.all_to_all(compressed, "rx", split_axis=3, concat_axis=2, tiled=True)
    item_count, recv_count, owned_cols = arrived.shape[1:]
    stacked = jnp.transpose(arrived, (0, 2, 1, 3)).reshape(2 * recv_count, item_count * owned_cols)
    formed = jnp.dot(steer_matrix, stacked, preferred_element_type=jnp.float32)
    picture = formed.reshape(2, beam_count, item_count, owned_cols)
    owned_width = length // rx_count
    positions = (
        rng_place * length + rx_place * owned_width + jnp.arange(owned_width, dtype=jnp.int32)
    )
    for level in range(pulses.bit_length() - 1):
        groups_now = pulses >> level + 1
        node_ids = (pulse_count + pulse_place) * groups_now + jnp.arange(
            groups_now, dtype=jnp.int32
        )
        paired = picture.reshape(2, beam_count, groups_now, 2, owned_width)
        picture = merge_pair(
            paired[:, :, :, 0], paired[:, :, :, 1], node_ids, positions, beam_angle, interp_table
        )
    picture = picture[:, :, 0]
    cross_levels = pulse_count.bit_length() - 1
    piece_width = owned_width // pulse_count
    pieces = picture.reshape(2, beam_count, pulse_count, piece_width)
    spots = positions.reshape(pulse_count, piece_width)
    for level in range(cross_levels):
        parity = jnp.right_shift(pulse_place, level) & 1
        count_now = pieces.shape[2]
        paired = pieces.reshape(2, beam_count, count_now // 2, 2, piece_width)
        kept_half = lax.dynamic_index_in_dim(paired, parity, 3, keepdims=False)
        sent_half = lax.dynamic_index_in_dim(paired, 1 - parity, 3, keepdims=False)
        partner = swapped(sent_half, "pulse", level)
        spot_pairs = spots.reshape(count_now // 2, 2, piece_width)
        spots = lax.dynamic_index_in_dim(spot_pairs, parity, 1, keepdims=False)
        own_part = kept_half.reshape(2, beam_count, -1)
        other_part = partner.reshape(2, beam_count, -1)
        left_image = jnp.where(parity == 0, own_part, other_part)
        right_image = jnp.where(parity == 0, other_part, own_part)
        combine_node_ids = jnp.reshape(
            (pulse_count >> level + 1) + jnp.right_shift(pulse_place, level + 1), (1,)
        )
        merged = merge_pair(
            left_image[:, :, None],
            right_image[:, :, None],
            combine_node_ids,
            spots.reshape(-1),
            beam_angle,
            interp_table,
        )
        flat = merged[:, :, 0]
        pieces = flat.reshape(2, beam_count, count_now // 2, piece_width)
    picture = pieces.reshape(2, beam_count, piece_width)
    return picture


LANES = 128
RX_TILE = LANES + RTAPS
CHIRP_TILE = 6 * LANES
HALO_TILES = 3
HALO = HALO_TILES * LANES


def vmem():
    return pl.BlockSpec(memory_space=pltpu.VMEM)


def hbm():
    return pl.BlockSpec(memory_space=pltpu.HBM)


def anywhere():
    return pl.BlockSpec(memory_space=pl.ANY)


def chirp_bands_table():
    offset = np.arange(CTAPS) - CTAPS // 2
    angle = math.pi * np.mod(offset * offset, 2 * CTAPS) / CTAPS
    scale = 1.0 / math.sqrt(CTAPS)
    offset = np.arange(CHIRP_TILE)[:, None] - np.arange(LANES)[None, :] - (LANES - RTAPS // 2)
    inside = (offset >= 0) & (offset < CTAPS)
    place = np.clip(offset, 0, CTAPS - 1)
    bands = [
        np.where(inside, taps[place], 0.0)
        for taps in (np.cos(angle) * scale, -np.sin(angle) * scale)
    ]
    return np.concatenate(bands, axis=-1).astype(ml_dtypes.bfloat16)


def filter_channel(windows, bands, pulses):
    product = jnp.dot(windows, bands, preferred_element_type=jnp.float32)
    product = product.reshape(-1, 2, pulses, 2 * LANES)
    real = product[:, 0, :, :LANES] - product[:, 1, :, LANES:]
    imag = product[:, 0, :, LANES:] + product[:, 1, :, :LANES]
    return real, imag


def bands_kernel(bands_ref):
    channels = bands_ref.shape[0]
    first_channel = lax.axis_index("rx") * channels
    lane = lax.broadcasted_iota(jnp.int32, (channels, LANES), 1)
    channel = lax.broadcasted_iota(jnp.int32, (channels, LANES), 0) + first_channel + 1
    tap = jnp.bitwise_and(LANES - lane, LANES - 1)
    unit = 1024 // RTAPS
    window = 0.5 - 0.5 * turn_parts(tap * unit + unit // 2)[0]
    window = jnp.where(tap < RTAPS, window * (1.0 / math.sqrt(RTAPS * 3 / 8)), 0.0)
    turn = channel * (tap - RTAPS // 2) * (1024 // (4 * RTAPS))
    row = lax.broadcasted_iota(jnp.int32, (LANES, LANES), 0)
    upper = lax.broadcasted_iota(jnp.int32, (LANES, LANES), 1) <= row
    for part, wave in enumerate(turn_parts(jnp.bitwise_and(turn, 1023))):
        taps = window * wave
        span = slice(part * LANES, (part + 1) * LANES)
        for index in range(channels):
            spread = jnp.broadcast_to(taps[index : index + 1], (LANES, LANES))
            rolled = pltpu.roll(spread, 0, 1, stride=1, stride_axis=0)
            bands_ref[index, :LANES, span] = jnp.where(upper, rolled, 0.0).astype(jnp.bfloat16)
            lower = jnp.where(upper, 0.0, rolled)[:RTAPS]
            bands_ref[index, LANES:, span] = lower.astype(jnp.bfloat16)


def interior_kernel(echo_ref, bands_ref, filtered_ref, rows_in, rows_out):
    _, pulses, channels, length = echo_ref.shape
    tiles = length // LANES
    group = 2 * pulses
    empty = jnp.zeros(rows_in.shape[1:], jnp.float32)
    rows_in[0] = empty
    rows_in[tiles + 1] = empty
    for part in range(2):
        for pulse in range(pulses):
            where = pl.ds(part * pulses + pulse, channels, stride=group)
            block = echo_ref[part, pulse].astype(jnp.float32)
            for tile in range(tiles):
                rows_in[tile + 1, where, :] = block[:, tile * LANES : (tile + 1) * LANES]
    lane = lax.broadcasted_iota(jnp.int32, (pulses, LANES), 1)
    mask = jnp.where(lane >= LANES - RTAPS // 2, 1.0, 0.0)
    for channel in range(channels):
        rows = rows_in[:, channel * group : (channel + 1) * group, :].astype(jnp.bfloat16)
        windows = jnp.concatenate(
            [rows[:-1].reshape(-1, LANES), rows[1:].reshape(-1, LANES)[:, :RTAPS]], axis=1
        )
        real, imag = filter_channel(windows, bands_ref[channel], pulses)
        for tile in range(tiles + 1):
            tile_re, tile_im = real[tile], imag[tile]
            if tile == 0:
                tile_re, tile_im = tile_re * mask, tile_im * mask
            if tile == tiles:
                tile_re, tile_im = tile_re * (1.0 - mask), tile_im * (1.0 - mask)
            rows_out[tile, pl.ds(channel, pulses, stride=2 * channels), :] = tile_re
            rows_out[tile, pl.ds(channels + channel, pulses, stride=2 * channels), :] = tile_im
    rows = filtered_ref.shape[0]
    nothing = jnp.zeros((rows, (HALO_TILES - 1) * LANES), jnp.bfloat16)
    filtered_ref[:, : (HALO_TILES - 1) * LANES] = nothing
    filtered_ref[:, (HALO_TILES + tiles) * LANES :] = nothing
    for tile in range(tiles + 1):
        spot = (HALO_TILES - 1 + tile) * LANES
        filtered_ref[:, spot : spot + LANES] = rows_out[tile].astype(jnp.bfloat16)


def chirp_pieces(filtered_ref, chirp_ref, owner, piece_count, distances, out_ref):
    pulse_place = lax.axis_index("pulse")
    _, pulses, rows, width = out_ref.shape
    tiles = width // LANES
    channels = rows // 2
    windows = []
    for distance in distances:
        piece = jnp.bitwise_xor(pulse_place, distance)
        first = (owner * piece_count + piece) * tiles
        for tile in range(tiles):
            start = pl.multiple_of((first + tile) * LANES, LANES)
            windows.append(filtered_ref[:, pl.ds(start, CHIRP_TILE)])
    product = jnp.dot(
        jnp.concatenate(windows, axis=0), chirp_ref[...], preferred_element_type=jnp.float32
    )
    product = product.reshape(len(windows), pulses, rows, 2 * LANES)
    for index in range(len(distances)):
        for tile in range(tiles):
            block = product[index * tiles + tile]
            real = block[:, :channels, :LANES] - block[:, channels:, LANES:]
            imag = block[:, :channels, LANES:] + block[:, channels:, :LANES]
            out_ref[index, :, :, tile * LANES : (tile + 1) * LANES] = jnp.concatenate(
                [real, imag], axis=1
            ).astype(jnp.bfloat16)


def edges_kernel(
    plan, inner_ref, echo_ref, across_ref, bands_ref, chirp_ref, filtered_ref, *rest
):
    *send_refs, rows_in, rows_out = rest
    del inner_ref
    _, pulses, channels, length = echo_ref.shape
    tiles = length // LANES
    group = 2 * pulses
    lowest = lax.axis_index("rng") == 0
    far = pl.ds(pl.multiple_of(jnp.where(lowest, 0, length - HALO), LANES), HALO)
    for part in range(2):
        for pulse in range(pulses):
            where = pl.ds(part * pulses + pulse, channels, stride=group)
            edge = across_ref[part, pulse, :, far].astype(jnp.float32)
            near_low = echo_ref[part, pulse, :, :LANES].astype(jnp.float32)
            near_high = echo_ref[part, pulse, :, length - LANES :].astype(jnp.float32)
            pieces = [edge[:, t * LANES : (t + 1) * LANES] for t in range(HALO_TILES)]
            for tile in range(HALO_TILES + 1):
                high = near_high if tile == 0 else pieces[tile - 1]
                low = near_low if tile == HALO_TILES else pieces[tile]
                rows_in[tile, where, :] = jnp.where(lowest, high, low)
    for channel in range(channels):
        rows = rows_in[:, channel * group : (channel + 1) * group, :].astype(jnp.bfloat16)
        windows = jnp.concatenate(
            [rows[:-1].reshape(-1, LANES), rows[1:].reshape(-1, LANES)[:, :RTAPS]], axis=1
        )
        real, imag = filter_channel(windows, bands_ref[channel], pulses)
        for tile in range(HALO_TILES):
            rows_out[tile, pl.ds(channel, pulses, stride=2 * channels), :] = real[tile]
            rows_out[tile, pl.ds(channels + channel, pulses, stride=2 * channels), :] = imag[tile]
    first = jnp.where(lowest, tiles + HALO_TILES - 1, 0)
    for tile in range(HALO_TILES):
        start = pl.multiple_of((first + tile) * LANES, LANES)
        filtered_ref[:, pl.ds(start, LANES)] = rows_out[tile].astype(jnp.bfloat16)
    piece_count, groups = plan
    for distances, send_ref in zip(groups, send_refs):
        chirp_pieces(
            filtered_ref, chirp_ref, 1 - lax.axis_index("rx"), piece_count, distances, send_ref
        )


def rest_kernel(piece_count, groups, filtered_ref, chirp_ref, after_ref, keep_ref, *send_refs):
    rx_place = lax.axis_index("rx")
    own = list(range(piece_count - 1, -1, -1))
    chirp_pieces(filtered_ref, chirp_ref, rx_place, piece_count, own, keep_ref)
    for distances, send_ref in zip(groups, send_refs):
        chirp_pieces(filtered_ref, chirp_ref, 1 - rx_place, piece_count, distances, send_ref)


def turn_parts(step):
    shifted = step + 128
    angle = (jnp.bitwise_and(shifted, 255) - 128).astype(jnp.float32) * (full_turn / 1024.0)
    quarter = jnp.right_shift(shifted, 8)
    square = angle * angle
    cosine = 1.0 + square * (-1 / 2 + square * (1 / 24 + square * (-1 / 720 + square * (1 / 40320))))
    sine = angle * (1.0 + square * (-1 / 6 + square * (1 / 120 + square * (-1 / 5040))))
    odd = jnp.bitwise_and(quarter, 1) == 1
    real = jnp.where(odd, sine, cosine)
    imag = jnp.where(odd, cosine, sine)
    real = jnp.where(jnp.bitwise_and(quarter + 1, 2) == 2, -real, real)
    imag = jnp.where(jnp.bitwise_and(quarter, 2) == 2, -imag, imag)
    return real, imag


def turned(real, imag, phase_re, phase_im):
    return phase_re * real - phase_im * imag, phase_im * real + phase_re * imag


def as_column(row):
    count = row.shape[1]
    first = lax.broadcasted_iota(jnp.int32, (count, count), 0)
    second = lax.broadcasted_iota(jnp.int32, (count, count), 1)
    spread = jnp.where(first == second, row.astype(jnp.float32), 0.0)
    return jnp.sum(spread, axis=1, keepdims=True).astype(jnp.int32)


def interp_matrix(code):
    beams = code.shape[0]
    angle_bin = lax.broadcasted_iota(jnp.int32, (beams, beams), 0)
    column = lax.broadcasted_iota(jnp.int32, (beams, beams), 1)
    half = 2 * beams
    away = jnp.bitwise_and(4 * (column - angle_bin + 1) - code + half, 4 * beams - 1) - half
    away = jnp.abs(away.astype(jnp.float32)) * 0.25
    near = (1.0 - away * away) * (2.0 - away) * 0.5
    far = (1.0 - away) * (2.0 - away) * (3.0 - away) * (1.0 / 6.0)
    matrix = jnp.where(away < 1.0, near, jnp.where(away < 2.0, far, 0.0))
    return matrix.astype(jnp.bfloat16)


def code_columns(codes_ref, rows):
    picked = [codes_ref[pl.ds(row, 1), :] for row in rows]
    picked = jnp.concatenate(picked, axis=0).astype(jnp.float32)
    spare = -len(rows) % 8
    if spare:
        picked = jnp.concatenate([picked, jnp.zeros((spare, picked.shape[1]), jnp.float32)], axis=0)
    return picked.T.astype(jnp.int32)


def weights_kernel(sizes, angle_ref, codes_ref, after_ref, first_ref, inner_ref):
    pulses, channels, rx_count, piece_count = sizes
    rx_place = lax.axis_index("rx")
    pulse_place = lax.axis_index("pulse")
    beams = angle_ref.shape[1]
    angle = as_column(angle_ref[...])
    rows = []
    now = pulses
    while now > 1:
        base = now * piece_count + pulse_place * now
        rows.extend(base + index for index in range(now))
        now //= 2
    codes = code_columns(codes_ref, rows)
    within = lax.broadcasted_iota(jnp.int32, (1, 4 * channels), 1)
    owner = jnp.bitwise_xor(rx_place, jnp.where(within >= 2 * channels, 1, 0))
    receiver = owner * channels + jnp.bitwise_and(within, channels - 1)
    is_imag = jnp.bitwise_and(within, channels) != 0
    scale = 1.0 / math.sqrt(channels * rx_count)
    steer_re, steer_im = turn_parts(jnp.bitwise_and(angle * receiver, 1023))
    steer_re = (steer_re * scale).astype(jnp.bfloat16).astype(jnp.float32)
    steer_im = (-steer_im * scale).astype(jnp.bfloat16).astype(jnp.float32)
    steer = jnp.concatenate(
        [
            jnp.where(is_imag, -steer_im, steer_re).astype(jnp.bfloat16),
            jnp.where(is_imag, steer_re, steer_im).astype(jnp.bfloat16),
        ],
        axis=1,
    )
    entries = 4 * channels
    matrices = [interp_matrix(codes[:, index : index + 1]) for index in range(len(rows))]
    composed = jnp.dot(
        jnp.concatenate(matrices[:pulses], axis=0), steer, preferred_element_type=jnp.float32
    )
    for index in range(pulses):
        for part in range(2):
            value = composed[
                index * beams : (index + 1) * beams, part * entries : (part + 1) * entries
            ]
            first_ref[index, part * beams : (part + 1) * beams, :] = value.astype(jnp.bfloat16)
    for index, matrix in enumerate(matrices[pulses:]):
        inner_ref[index] = matrix


def phases_kernel(sizes, angle_ref, after_ref, phase_ref):
    pulses, rx_count, width = sizes
    rng_place = lax.axis_index("rng")
    rx_place = lax.axis_index("rx")
    pulse_place = lax.axis_index("pulse")
    piece_count = phase_ref.shape[0]
    piece_tiles = phase_ref.shape[4] // LANES
    angle = as_column(angle_ref[...])
    factors = []
    now = pulses
    while now > 1:
        base = now * piece_count + pulse_place * now
        factors.extend(base + 1 + index for index in range(0, now, 2))
        now //= 2
    lane = lax.broadcasted_iota(jnp.int32, (1, LANES), 1)
    block = (rng_place * rx_count + rx_place) * width + 1
    base = jnp.bitwise_and(angle * (block + lane), 1023)
    for slot, factor in enumerate([1, *factors]):
        scale = half_root if slot else 1.0
        real, imag = turn_parts(jnp.bitwise_and(base * factor, 1023))
        real, imag = real * scale, imag * scale
        step = turn_parts(jnp.bitwise_and(angle * (factor * LANES), 1023))
        for tile in range(piece_count * piece_tiles):
            index = piece_count - 1 - jnp.bitwise_xor(pulse_place, tile // piece_tiles)
            start = tile % piece_tiles * LANES
            phase_ref[index, slot, 0, :, start : start + LANES] = real
            phase_ref[index, slot, 1, :, start : start + LANES] = imag
            real, imag = turned(real, imag, *step)


def risen(outer_ref, phase_ref, slot, real, imag):
    matrix = outer_ref[slot]
    moved_re = jnp.dot(matrix, real.astype(jnp.bfloat16), preferred_element_type=jnp.float32)
    moved_im = jnp.dot(matrix, imag.astype(jnp.bfloat16), preferred_element_type=jnp.float32)
    return turned(moved_re, moved_im, phase_ref[slot, 0], phase_ref[slot, 1])


def outer_tables_kernel(sizes, angle_ref, codes_ref, image_ref, outer_ref, phase_ref, own_ref):
    rx_count, width, piece_count = sizes
    rng_place = lax.axis_index("rng")
    rx_place = lax.axis_index("rx")
    pulse_place = lax.axis_index("pulse")
    piece_width = phase_ref.shape[3]
    angle = as_column(angle_ref[...])
    lane = lax.broadcasted_iota(jnp.int32, (1, piece_width), 1)
    block = (rng_place * rx_count + rx_place) * width + 1
    base = jnp.bitwise_and(angle * (block + pulse_place * piece_width + lane), 1023)
    counts = [piece_count >> level for level in range(piece_count.bit_length() - 1)]
    rows = [count + index for count in counts for index in range(count)]
    codes = code_columns(codes_ref, rows)
    for slot, row in enumerate(rows):
        outer_ref[slot] = interp_matrix(codes[:, slot : slot + 1])
        real, imag = turn_parts(jnp.bitwise_and(base * (row + 1), 1023))
        phase_ref[slot, 0] = real * half_root
        phase_ref[slot, 1] = imag * half_root
    own_ref[0], own_ref[1] = risen(
        outer_ref, phase_ref, pulse_place, image_ref[0], image_ref[1]
    )


ROWS = 8


def inner_kernel(indices, keep_ref, other_ref, first_ref, inner_ref, phase_ref, *rest):
    *out_refs, moved_ref, picture_ref, level_ref = rest
    pulses = keep_ref.shape[1]
    beams, columns = out_refs[0].shape[1:]
    pieces = range(len(indices))

    def merge(piece, count, base, read, write):
        index = indices[piece]
        for row in range(0, beams, ROWS):
            span = slice(row, row + ROWS)
            step = (phase_ref[index, 0, 0, span], phase_ref[index, 0, 1, span])
            for image in range(0, count, 2):
                slot = base + image // 2
                left = read(image, row)
                right = turned(*read(image + 1, row), *step)
                phase = (phase_ref[index, slot, 0, span], phase_ref[index, slot, 1, span])
                write(
                    image // 2, row, *turned(left[0] + right[0], left[1] + right[1], *phase)
                )

    def lift(piece, image, slot):
        level_ref[piece, image] = jnp.dot(
            inner_ref[slot],
            picture_ref[piece, image].astype(jnp.bfloat16),
            preferred_element_type=jnp.float32,
        )

    for piece in pieces:
        for image in range(pulses):
            rows = jnp.concatenate(
                [keep_ref[indices[piece], image], other_ref[piece, image]], axis=0
            )
            moved_ref[piece, image] = jnp.dot(
                first_ref[image],
                rows,
                preferred_element_type=jnp.float32,
            )

    def read_first(piece):
        return lambda image, row: (
            moved_ref[piece, image, row : row + ROWS],
            moved_ref[piece, image, beams + row : beams + row + ROWS],
        )

    def read_level(piece):
        return lambda image, row: (
            level_ref[piece, image, row : row + ROWS, :columns],
            level_ref[piece, image, row : row + ROWS, columns:],
        )

    def write_picture(piece):
        def write(image, row, real, imag):
            picture_ref[piece, image, row : row + ROWS, :columns] = real
            picture_ref[piece, image, row : row + ROWS, columns:] = imag

        return write

    for piece in pieces:
        merge(piece, pulses, 1, read_first(piece), write_picture(piece))
        for image in range(pulses // 2):
            lift(piece, image, image)
    base = 1 + pulses // 2
    slot = pulses // 2
    count = pulses // 2
    while count > 1:
        for piece in pieces:
            merge(piece, count, base, read_level(piece), write_picture(piece))
            for image in range(count // 2 if count > 2 else 0):
                lift(piece, image, slot + image)
        count //= 2
        base += count
        slot += count
    for piece in pieces:
        out_refs[piece][0] = picture_ref[piece, 0, :, :columns].astype(jnp.bfloat16)
        out_refs[piece][1] = picture_ref[piece, 0, :, columns:].astype(jnp.bfloat16)


def far_kernel(distances, *rest):
    *image_refs, outer_ref, phase_ref, far_ref = rest
    pulse_place = lax.axis_index("pulse")
    terms = [
        risen(outer_ref, phase_ref, jnp.bitwise_xor(pulse_place, distance), ref[0], ref[1])
        for distance, ref in zip(distances, image_refs)
    ]
    real = terms[0][0] + terms[1][0]
    imag = terms[0][1] + terms[1][1]
    half = jnp.bitwise_xor(jnp.right_shift(pulse_place, 1), 1)
    far_ref[0], far_ref[1] = risen(outer_ref, phase_ref, 4 + half, real, imag)


def near_kernel(far_ref, image_ref, own_ref, outer_ref, phase_ref, out_ref):
    pulse_place = lax.axis_index("pulse")
    near = risen(
        outer_ref, phase_ref, jnp.bitwise_xor(pulse_place, 1), image_ref[0], image_ref[1]
    )
    real = own_ref[0] + near[0]
    imag = own_ref[1] + near[1]
    half = jnp.right_shift(pulse_place, 1)
    real, imag = risen(outer_ref, phase_ref, 4 + half, real, imag)
    out_ref[0] = real + far_ref[0]
    out_ref[1] = imag + far_ref[1]


def cost(micros):
    return pl.CostEstimate(
        flops=int(micros * 1.1e9), bytes_accessed=int(micros * 3.6e6), transcendentals=0
    )


PARAMS = dict(compiler_params=pltpu.CompilerParams(vmem_limit_bytes=40 * 1024 * 1024))


def fast(echoes, beam_angle, interp_table):
    rx_count = lax.axis_size("rx")
    pulse_count = lax.axis_size("pulse")
    _, pulses, channels, length = echoes.shape
    beams = beam_angle.shape[0]
    width = length // rx_count
    piece_width = width // pulse_count
    piece_tiles = piece_width // LANES
    rows = 2 * channels
    group = 2 * pulses
    chirp = jnp.asarray(chirp_bands_table())
    angles = beam_angle.reshape(1, beams)
    codes = interp_table.reshape(-1, beams)
    bf16 = jnp.bfloat16
    f32 = jnp.float32
    shape = jax.ShapeDtypeStruct
    across = swapped(echoes, "rng", 0)
    bands = pl.pallas_call(
        bands_kernel,
        out_shape=shape((channels, RX_TILE, 2 * LANES), bf16),
        out_specs=vmem(),
        name="bands",
        cost_estimate=cost(10.0),
        **PARAMS,
    )()
    tiles = length // LANES
    filtered_shape = shape((rows * pulses, (tiles + 2 * HALO_TILES - 1) * LANES), bf16)
    filtered = pl.pallas_call(
        interior_kernel,
        out_shape=filtered_shape,
        in_specs=[vmem()] * 2,
        out_specs=vmem(),
        scratch_shapes=[
            pltpu.VMEM((tiles + 2, channels * group, LANES), f32),
            pltpu.VMEM((tiles + 1, rows * pulses, LANES), f32),
        ],
        name="interior",
        **PARAMS,
    )(echoes, bands)

    def pieces(count):
        return shape((count, pulses, rows, piece_width), bf16)

    last = pulse_count - 1
    groups = [[3, 2], [1, 0]]
    filtered, first_sent = pl.pallas_call(
        functools.partial(edges_kernel, (pulse_count, groups[:1])),
        out_shape=[filtered_shape, pieces(len(groups[0]))],
        in_specs=[vmem()] * 5,
        out_specs=[vmem()] * 2,
        scratch_shapes=[
            pltpu.VMEM((HALO_TILES + 1, channels * group, LANES), f32),
            pltpu.VMEM((HALO_TILES, rows * pulses, LANES), f32),
        ],
        input_output_aliases={0: 0},
        name="edges",
        **PARAMS,
    )(filtered, echoes, across, bands, chirp)
    phase = pl.pallas_call(
        functools.partial(phases_kernel, (pulses, rx_count, width)),
        out_shape=shape((pulse_count, pulses, 2, beams, piece_width), f32),
        in_specs=[vmem(), anywhere()],
        out_specs=vmem(),
        name="phases",
        **PARAMS,
    )(angles, first_sent)
    kept, *sent = pl.pallas_call(
        functools.partial(rest_kernel, pulse_count, groups[1:2]),
        out_shape=[pieces(pulse_count), pieces(len(groups[1]))],
        in_specs=[vmem()] * 2 + [anywhere()],
        out_specs=[vmem()] * 2,
        name="rest",
        **PARAMS,
    )(filtered, chirp, phase)
    first, inner = pl.pallas_call(
        functools.partial(weights_kernel, (pulses, channels, rx_count, pulse_count)),
        out_shape=[
            shape((pulses, 2 * beams, 4 * channels), bf16),
            shape((pulses - 2, beams, beams), bf16),
        ],
        in_specs=[vmem()] * 2 + [anywhere()],
        out_specs=[vmem()] * 2,
        name="weights",
        **PARAMS,
    )(angles, codes, kept)
    images = [None] * pulse_count

    def merge(members, piece):
        other = swapped(piece, "rx", 0)
        size = len(members)
        merged = pl.pallas_call(
            functools.partial(inner_kernel, [last - distance for distance in members]),
            out_shape=[shape((2, beams, piece_width), bf16)] * size,
            in_specs=[vmem()] * 5,
            out_specs=[vmem()] * size,
            scratch_shapes=[
                pltpu.VMEM((size, pulses, 2 * beams, piece_width), f32),
                pltpu.VMEM((size, pulses // 2, beams, 2 * piece_width), f32),
                pltpu.VMEM((size, pulses // 2, beams, 2 * piece_width), f32),
            ],
            name="inner",
            cost_estimate=cost(3.0),
            **PARAMS,
        )(kept, other, first, inner, phase)
        for distance, image in zip(members, merged):
            images[distance] = image

    merge(groups[0], first_sent)
    merge(groups[1], sent[0])
    for distance in range(1, pulse_count):
        pairs = [(i, i ^ distance) for i in range(pulse_count)]
        images[distance] = lax.ppermute(images[distance], "pulse", pairs)
    outer_count = 2 * pulse_count - 2
    picture_shape = shape((2, beams, piece_width), f32)
    outer, outer_phase, own = pl.pallas_call(
        functools.partial(outer_tables_kernel, (rx_count, width, pulse_count)),
        out_shape=[
            shape((outer_count, beams, beams), bf16),
            shape((outer_count, 2, beams, piece_width), f32),
            picture_shape,
        ],
        in_specs=[vmem()] * 3,
        out_specs=[vmem()] * 3,
        name="outer_tables",
        **PARAMS,
    )(angles, codes, images[0])
    far = pl.pallas_call(
        functools.partial(far_kernel, (3, 2)),
        out_shape=picture_shape,
        in_specs=[vmem()] * 4,
        out_specs=vmem(),
        name="far",
        **PARAMS,
    )(images[3], images[2], outer, outer_phase)
    return pl.pallas_call(
        near_kernel,
        out_shape=picture_shape,
        in_specs=[vmem()] * 5,
        out_specs=vmem(),
        name="near",
        **PARAMS,
    )(far, images[1], own, outer, outer_phase)


def power_of_two(count):
    return count > 0 and count & (count - 1) == 0


def per_device(echoes, beam_angle, interp_table):
    _, pulses, channels, length = echoes.shape
    rx_count = lax.axis_size("rx")
    pulse_count = lax.axis_size("pulse")
    piece_width = length // (rx_count * pulse_count)
    if (
        lax.axis_size("rng") == 2
        and rx_count == 2
        and channels == 8
        and pulses == 8
        and pulse_count == 4
        and power_of_two(beam_angle.shape[0])
        and beam_angle.shape[0] % 16 == 0
        and piece_width % LANES == 0
    ):
        return fast(echoes, beam_angle, interp_table)
    return local(echoes, beam_angle, interp_table)


def solution(mesh):
    placed = (P(None, ("slab", "pulse"), "rx", "rng"), P(), P())
    return jax.shard_map(
        per_device,
        mesh=mesh,
        in_specs=placed,
        out_specs=P(None, "slab", ("rng", "rx", "pulse")),
        check_vma=False,
    )
```

```python
import functools
import math

import jax
import jax.numpy as jnp
import ml_dtypes
import numpy as np
from jax import lax
from jax.experimental import pallas as pl
from jax.experimental.pallas import tpu as pltpu
from jax.sharding import PartitionSpec as P

RTAPS = 64
CTAPS = 512


half_root = 0.7071067811865476
full_turn = 2.0 * math.pi


def extended_2(block, sides, width):
    for axis, dim in sides:
        count = lax.axis_size(axis)
        forward = [(i, i + 1) for i in range(count - 1)]
        backward = [(target, source) for source, target in forward]
        low = lax.ppermute(
            lax.slice_in_dim(block, block.shape[dim] - width, None, axis=dim), axis, forward
        )
        high = lax.ppermute(lax.slice_in_dim(block, 0, width, axis=dim), axis, backward)
        block = jnp.concatenate([low, block, high], axis=dim)
    return block


def swapped(x, axis, distance):
    return lax.ppermute(x, axis, [(i, i ^ 1 << distance) for i in range(lax.axis_size(axis))])


def receiver_taps(channel_ids, tap_count):
    tap_index = jnp.arange(tap_count, dtype=jnp.float32)
    window = 0.5 - 0.5 * jnp.cos(full_turn * (tap_index + 0.5) / tap_count)
    window = window / jnp.sqrt(jnp.sum(window * window))
    channel = channel_ids.astype(jnp.float32)[:, None] + 1.0
    angle = full_turn * channel * (tap_index - tap_count // 2) / (4 * tap_count)
    return (
        (window * jnp.cos(angle)).astype(jnp.bfloat16),
        (window * jnp.sin(angle)).astype(jnp.bfloat16),
    )


def chirp_taps(tap_count):
    offset = jnp.arange(tap_count, dtype=jnp.int32) - tap_count // 2
    phase_step = jnp.mod(offset * offset, 2 * tap_count).astype(jnp.float32)
    angle = math.pi * phase_step / tap_count
    scale = 1.0 / math.sqrt(tap_count)
    return (
        (jnp.cos(angle) * scale).astype(jnp.bfloat16),
        (-jnp.sin(angle) * scale).astype(jnp.bfloat16),
    )


def steering(beam_angle, receivers):
    channel = jnp.arange(receivers, dtype=jnp.int32)
    turns = jnp.mod(beam_angle[:, None] * channel[None, :], 1024).astype(jnp.float32)
    angle = full_turn * turns / 1024.0
    scale = 1.0 / math.sqrt(receivers)
    return (
        (jnp.cos(angle) * scale).astype(jnp.bfloat16),
        (-jnp.sin(angle) * scale).astype(jnp.bfloat16),
    )


def interp_matrices(codes, beam_count):
    shifted = codes // 4 - 1
    fraction = jnp.mod(codes, 4).astype(jnp.float32) / 4.0
    weights = (
        -fraction * (fraction - 1.0) * (fraction - 2.0) / 6.0,
        (fraction + 1.0) * (fraction - 1.0) * (fraction - 2.0) / 2.0,
        -(fraction + 1.0) * fraction * (fraction - 2.0) / 2.0,
        (fraction + 1.0) * fraction * (fraction - 1.0) / 6.0,
    )
    columns = jnp.arange(beam_count, dtype=jnp.int32)
    matrices = jnp.zeros(codes.shape + (beam_count,), jnp.float32)
    for tap_index in range(4):
        target = jnp.mod(columns + shifted + tap_index - 1, beam_count)
        matrices = matrices + weights[tap_index][..., None] * (target[..., None] == columns).astype(
            jnp.float32
        )
    return matrices


def phases(node_ids, positions, beam_angle, side):
    base = jnp.mod(beam_angle[:, None] * (positions[None, :] + 1), 1024)
    factor = 2 * node_ids + side + 1
    turns = jnp.mod(base[:, None, :] * factor[None, :, None], 1024).astype(jnp.float32)
    angle = full_turn * turns / 1024.0
    return (jnp.cos(angle), jnp.sin(angle))


def side_term(picture, matrices, cosine, sine):
    moved = jnp.einsum("gqa,cagr->cqgr", matrices, picture, precision=lax.Precision.HIGHEST)
    return (cosine * moved[0] - sine * moved[1], sine * moved[0] + cosine * moved[1])


def merge_pair(left_image, right_image, node_ids, positions, beam_angle, interp_table):
    matrices = interp_matrices(interp_table[node_ids], left_image.shape[1])
    left_cos, left_sin = phases(node_ids, positions, beam_angle, 0)
    right_cos, right_sin = phases(node_ids, positions, beam_angle, 1)
    left_re, left_im = side_term(left_image, matrices[:, 0], left_cos, left_sin)
    right_re, right_im = side_term(right_image, matrices[:, 1], right_cos, right_sin)
    return jnp.stack([(left_re + right_re) * half_root, (left_im + right_im) * half_root])


def toeplitz_blocks(taps_re, taps_im):
    tap_count = taps_re.shape[-1]
    leading = taps_re.shape[:-1]

    def lay_out(taps):
        padded = jnp.concatenate([taps, jnp.zeros(leading + (tap_count + 1,), taps.dtype)], axis=-1)
        tiled = jnp.tile(padded, (1,) * len(leading) + (tap_count,))
        banded = tiled[..., : 2 * tap_count * tap_count].reshape(
            leading + (tap_count, 2 * tap_count)
        )
        return jnp.swapaxes(banded, -1, -2)

    real_band = lay_out(taps_re)
    imag_band = lay_out(taps_im)
    upper = jnp.concatenate([real_band, imag_band], axis=-1)
    lower = jnp.concatenate([-imag_band, real_band], axis=-1)
    return jnp.concatenate([upper, lower], axis=-2)


def block_filter(extended, matrices, tap_count, per_channel):
    pulses, channels, length = extended.shape[1:]
    blocks = length // tap_count - 1
    pieces = extended.reshape(2, pulses, channels, blocks + 1, tap_count)
    windows = jnp.concatenate([pieces[:, :, :, :-1], pieces[:, :, :, 1:]], axis=4)
    windows = jnp.transpose(windows, (1, 2, 3, 0, 4)).reshape(
        pulses, channels, blocks, 4 * tap_count
    )
    if per_channel:
        output = jnp.einsum("pcnw,cwo->pcno", windows, matrices, preferred_element_type=jnp.float32)
    else:
        output = jnp.einsum("pcnw,wo->pcno", windows, matrices, preferred_element_type=jnp.float32)
    output = output.reshape(pulses, channels, blocks, 2, tap_count)
    return jnp.transpose(output, (3, 0, 1, 2, 4)).reshape(2, pulses, channels, blocks * tap_count)


def local(echoes, beam_angle, interp_table):
    rx_count = lax.axis_size("rx")
    pulse_count = lax.axis_size("pulse")
    rng_place = lax.axis_index("rng")
    rx_place = lax.axis_index("rx")
    pulse_place = lax.axis_index("pulse")
    pulses, channels, length = echoes.shape[1:]
    beam_count = beam_angle.shape[0]
    receivers = channels * rx_count
    channel_ids = rx_place * channels + jnp.arange(channels, dtype=jnp.int32)
    rx_re, rx_im = receiver_taps(channel_ids, RTAPS)
    rx_bands = toeplitz_blocks(rx_re, rx_im)
    chirp_re, chirp_im = chirp_taps(CTAPS)
    chirp_band = toeplitz_blocks(chirp_re, chirp_im)
    extended = extended_2(echoes, (("rng", 3),), RTAPS // 2)
    filtered = block_filter(extended, rx_bands, RTAPS, True).astype(jnp.bfloat16)
    filtered = extended_2(filtered, (("rng", 3),), CTAPS // 2)
    compressed = block_filter(filtered, chirp_band, CTAPS, False).astype(jnp.bfloat16)
    steering_real, steering_imaginary = steering(beam_angle, receivers)
    steer_matrix = jnp.concatenate(
        [
            jnp.concatenate([steering_real, -steering_imaginary], axis=1),
            jnp.concatenate([steering_imaginary, steering_real], axis=1),
        ],
        axis=0,
    )
    arrived = lax.all_to_all(compressed, "rx", split_axis=3, concat_axis=2, tiled=True)
    item_count, recv_count, owned_cols = arrived.shape[1:]
    stacked = jnp.transpose(arrived, (0, 2, 1, 3)).reshape(2 * recv_count, item_count * owned_cols)
    formed = jnp.dot(steer_matrix, stacked, preferred_element_type=jnp.float32)
    picture = formed.reshape(2, beam_count, item_count, owned_cols)
    owned_width = length // rx_count
    positions = (
        rng_place * length + rx_place * owned_width + jnp.arange(owned_width, dtype=jnp.int32)
    )
    for level in range(pulses.bit_length() - 1):
        groups_now = pulses >> level + 1
        node_ids = (pulse_count + pulse_place) * groups_now + jnp.arange(
            groups_now, dtype=jnp.int32
        )
        paired = picture.reshape(2, beam_count, groups_now, 2, owned_width)
        picture = merge_pair(
            paired[:, :, :, 0], paired[:, :, :, 1], node_ids, positions, beam_angle, interp_table
        )
    picture = picture[:, :, 0]
    cross_levels = pulse_count.bit_length() - 1
    piece_width = owned_width // pulse_count
    pieces = picture.reshape(2, beam_count, pulse_count, piece_width)
    spots = positions.reshape(pulse_count, piece_width)
    for level in range(cross_levels):
        parity = jnp.right_shift(pulse_place, level) & 1
        count_now = pieces.shape[2]
        paired = pieces.reshape(2, beam_count, count_now // 2, 2, piece_width)
        kept_half = lax.dynamic_index_in_dim(paired, parity, 3, keepdims=False)
        sent_half = lax.dynamic_index_in_dim(paired, 1 - parity, 3, keepdims=False)
        partner = swapped(sent_half, "pulse", level)
        spot_pairs = spots.reshape(count_now // 2, 2, piece_width)
        spots = lax.dynamic_index_in_dim(spot_pairs, parity, 1, keepdims=False)
        own_part = kept_half.reshape(2, beam_count, -1)
        other_part = partner.reshape(2, beam_count, -1)
        left_image = jnp.where(parity == 0, own_part, other_part)
        right_image = jnp.where(parity == 0, other_part, own_part)
        combine_node_ids = jnp.reshape(
            (pulse_count >> level + 1) + jnp.right_shift(pulse_place, level + 1), (1,)
        )
        merged = merge_pair(
            left_image[:, :, None],
            right_image[:, :, None],
            combine_node_ids,
            spots.reshape(-1),
            beam_angle,
            interp_table,
        )
        flat = merged[:, :, 0]
        pieces = flat.reshape(2, beam_count, count_now // 2, piece_width)
    picture = pieces.reshape(2, beam_count, piece_width)
    return picture


LANES = 128
RX_TILE = LANES + RTAPS
CHIRP_TILE = 6 * LANES
HALO_TILES = 3
HALO = HALO_TILES * LANES


def vmem():
    return pl.BlockSpec(memory_space=pltpu.VMEM)


def hbm():
    return pl.BlockSpec(memory_space=pltpu.HBM)


def anywhere():
    return pl.BlockSpec(memory_space=pl.ANY)


def chirp_bands_table():
    offset = np.arange(CTAPS) - CTAPS // 2
    angle = math.pi * np.mod(offset * offset, 2 * CTAPS) / CTAPS
    scale = 1.0 / math.sqrt(CTAPS)
    offset = np.arange(CHIRP_TILE)[:, None] - np.arange(LANES)[None, :] - (LANES - RTAPS // 2)
    inside = (offset >= 0) & (offset < CTAPS)
    place = np.clip(offset, 0, CTAPS - 1)
    bands = [
        np.where(inside, taps[place], 0.0)
        for taps in (np.cos(angle) * scale, -np.sin(angle) * scale)
    ]
    return np.concatenate(bands, axis=-1).astype(ml_dtypes.bfloat16)


def filter_channel(windows, bands, pulses):
    product = jnp.dot(windows, bands, preferred_element_type=jnp.float32)
    product = product.reshape(-1, 2, pulses, 2 * LANES)
    real = product[:, 0, :, :LANES] - product[:, 1, :, LANES:]
    imag = product[:, 0, :, LANES:] + product[:, 1, :, :LANES]
    return real, imag


def bands_kernel(bands_ref):
    channels = bands_ref.shape[0]
    first_channel = lax.axis_index("rx") * channels
    lane = lax.broadcasted_iota(jnp.int32, (channels, LANES), 1)
    channel = lax.broadcasted_iota(jnp.int32, (channels, LANES), 0) + first_channel + 1
    tap = jnp.bitwise_and(LANES - lane, LANES - 1)
    unit = 1024 // RTAPS
    window = 0.5 - 0.5 * turn_parts(tap * unit + unit // 2)[0]
    window = jnp.where(tap < RTAPS, window * (1.0 / math.sqrt(RTAPS * 3 / 8)), 0.0)
    turn = channel * (tap - RTAPS // 2) * (1024 // (4 * RTAPS))
    row = lax.broadcasted_iota(jnp.int32, (LANES, LANES), 0)
    upper = lax.broadcasted_iota(jnp.int32, (LANES, LANES), 1) <= row
    for part, wave in enumerate(turn_parts(jnp.bitwise_and(turn, 1023))):
        taps = window * wave
        span = slice(part * LANES, (part + 1) * LANES)
        for index in range(channels):
            spread = jnp.broadcast_to(taps[index : index + 1], (LANES, LANES))
            rolled = pltpu.roll(spread, 0, 1, stride=1, stride_axis=0)
            bands_ref[index, :LANES, span] = jnp.where(upper, rolled, 0.0).astype(jnp.bfloat16)
            lower = jnp.where(upper, 0.0, rolled)[:RTAPS]
            bands_ref[index, LANES:, span] = lower.astype(jnp.bfloat16)


def interior_kernel(echo_ref, bands_ref, filtered_ref, rows_in, rows_out):
    _, pulses, channels, length = echo_ref.shape
    tiles = length // LANES
    group = 2 * pulses
    empty = jnp.zeros(rows_in.shape[1:], jnp.float32)
    rows_in[0] = empty
    rows_in[tiles + 1] = empty
    for part in range(2):
        for pulse in range(pulses):
            where = pl.ds(part * pulses + pulse, channels, stride=group)
            block = echo_ref[part, pulse].astype(jnp.float32)
            for tile in range(tiles):
                rows_in[tile + 1, where, :] = block[:, tile * LANES : (tile + 1) * LANES]
    lane = lax.broadcasted_iota(jnp.int32, (pulses, LANES), 1)
    mask = jnp.where(lane >= LANES - RTAPS // 2, 1.0, 0.0)
    for channel in range(channels):
        rows = rows_in[:, channel * group : (channel + 1) * group, :].astype(jnp.bfloat16)
        windows = jnp.concatenate(
            [rows[:-1].reshape(-1, LANES), rows[1:].reshape(-1, LANES)[:, :RTAPS]], axis=1
        )
        real, imag = filter_channel(windows, bands_ref[channel], pulses)
        for tile in range(tiles + 1):
            tile_re, tile_im = real[tile], imag[tile]
            if tile == 0:
                tile_re, tile_im = tile_re * mask, tile_im * mask
            if tile == tiles:
                tile_re, tile_im = tile_re * (1.0 - mask), tile_im * (1.0 - mask)
            rows_out[tile, pl.ds(channel, pulses, stride=2 * channels), :] = tile_re
            rows_out[tile, pl.ds(channels + channel, pulses, stride=2 * channels), :] = tile_im
    rows = filtered_ref.shape[0]
    nothing = jnp.zeros((rows, (HALO_TILES - 1) * LANES), jnp.bfloat16)
    filtered_ref[:, : (HALO_TILES - 1) * LANES] = nothing
    filtered_ref[:, (HALO_TILES + tiles) * LANES :] = nothing
    for tile in range(tiles + 1):
        spot = (HALO_TILES - 1 + tile) * LANES
        filtered_ref[:, spot : spot + LANES] = rows_out[tile].astype(jnp.bfloat16)


def chirp_pieces(filtered_ref, chirp_ref, owner, piece_count, distances, out_ref):
    pulse_place = lax.axis_index("pulse")
    _, pulses, rows, width = out_ref.shape
    tiles = width // LANES
    channels = rows // 2
    windows = []
    for distance in distances:
        piece = jnp.bitwise_xor(pulse_place, distance)
        first = (owner * piece_count + piece) * tiles
        for tile in range(tiles):
            start = pl.multiple_of((first + tile) * LANES, LANES)
            windows.append(filtered_ref[:, pl.ds(start, CHIRP_TILE)])
    product = jnp.dot(
        jnp.concatenate(windows, axis=0), chirp_ref[...], preferred_element_type=jnp.float32
    )
    product = product.reshape(len(windows), pulses, rows, 2 * LANES)
    for index in range(len(distances)):
        for tile in range(tiles):
            block = product[index * tiles + tile]
            real = block[:, :channels, :LANES] - block[:, channels:, LANES:]
            imag = block[:, :channels, LANES:] + block[:, channels:, :LANES]
            out_ref[index, :, :, tile * LANES : (tile + 1) * LANES] = jnp.concatenate(
                [real, imag], axis=1
            ).astype(jnp.bfloat16)


def edges_kernel(
    plan, inner_ref, echo_ref, across_ref, bands_ref, chirp_ref, filtered_ref, *rest
):
    *send_refs, rows_in, rows_out = rest
    del inner_ref
    _, pulses, channels, length = echo_ref.shape
    tiles = length // LANES
    group = 2 * pulses
    lowest = lax.axis_index("rng") == 0
    far = pl.ds(pl.multiple_of(jnp.where(lowest, 0, length - HALO), LANES), HALO)
    for part in range(2):
        for pulse in range(pulses):
            where = pl.ds(part * pulses + pulse, channels, stride=group)
            edge = across_ref[part, pulse, :, far].astype(jnp.float32)
            near_low = echo_ref[part, pulse, :, :LANES].astype(jnp.float32)
            near_high = echo_ref[part, pulse, :, length - LANES :].astype(jnp.float32)
            pieces = [edge[:, t * LANES : (t + 1) * LANES] for t in range(HALO_TILES)]
            for tile in range(HALO_TILES + 1):
                high = near_high if tile == 0 else pieces[tile - 1]
                low = near_low if tile == HALO_TILES else pieces[tile]
                rows_in[tile, where, :] = jnp.where(lowest, high, low)
    for channel in range(channels):
        rows = rows_in[:, channel * group : (channel + 1) * group, :].astype(jnp.bfloat16)
        windows = jnp.concatenate(
            [rows[:-1].reshape(-1, LANES), rows[1:].reshape(-1, LANES)[:, :RTAPS]], axis=1
        )
        real, imag = filter_channel(windows, bands_ref[channel], pulses)
        for tile in range(HALO_TILES):
            rows_out[tile, pl.ds(channel, pulses, stride=2 * channels), :] = real[tile]
            rows_out[tile, pl.ds(channels + channel, pulses, stride=2 * channels), :] = imag[tile]
    first = jnp.where(lowest, tiles + HALO_TILES - 1, 0)
    for tile in range(HALO_TILES):
        start = pl.multiple_of((first + tile) * LANES, LANES)
        filtered_ref[:, pl.ds(start, LANES)] = rows_out[tile].astype(jnp.bfloat16)
    piece_count, groups = plan
    for distances, send_ref in zip(groups, send_refs):
        chirp_pieces(
            filtered_ref, chirp_ref, 1 - lax.axis_index("rx"), piece_count, distances, send_ref
        )


def rest_kernel(piece_count, groups, filtered_ref, chirp_ref, after_ref, keep_ref, *send_refs):
    rx_place = lax.axis_index("rx")
    own = list(range(piece_count - 1, -1, -1))
    chirp_pieces(filtered_ref, chirp_ref, rx_place, piece_count, own, keep_ref)
    for distances, send_ref in zip(groups, send_refs):
        chirp_pieces(filtered_ref, chirp_ref, 1 - rx_place, piece_count, distances, send_ref)


def turn_parts(step):
    shifted = step + 128
    angle = (jnp.bitwise_and(shifted, 255) - 128).astype(jnp.float32) * (full_turn / 1024.0)
    quarter = jnp.right_shift(shifted, 8)
    square = angle * angle
    cosine = 1.0 + square * (-1 / 2 + square * (1 / 24 + square * (-1 / 720 + square * (1 / 40320))))
    sine = angle * (1.0 + square * (-1 / 6 + square * (1 / 120 + square * (-1 / 5040))))
    odd = jnp.bitwise_and(quarter, 1) == 1
    real = jnp.where(odd, sine, cosine)
    imag = jnp.where(odd, cosine, sine)
    real = jnp.where(jnp.bitwise_and(quarter + 1, 2) == 2, -real, real)
    imag = jnp.where(jnp.bitwise_and(quarter, 2) == 2, -imag, imag)
    return real, imag


def turned(real, imag, phase_re, phase_im):
    return phase_re * real - phase_im * imag, phase_im * real + phase_re * imag


def as_column(row):
    count = row.shape[1]
    first = lax.broadcasted_iota(jnp.int32, (count, count), 0)
    second = lax.broadcasted_iota(jnp.int32, (count, count), 1)
    spread = jnp.where(first == second, row.astype(jnp.float32), 0.0)
    return jnp.sum(spread, axis=1, keepdims=True).astype(jnp.int32)


def interp_matrix(code):
    beams = code.shape[0]
    angle_bin = lax.broadcasted_iota(jnp.int32, (beams, beams), 0)
    column = lax.broadcasted_iota(jnp.int32, (beams, beams), 1)
    half = 2 * beams
    away = jnp.bitwise_and(4 * (column - angle_bin + 1) - code + half, 4 * beams - 1) - half
    away = jnp.abs(away.astype(jnp.float32)) * 0.25
    near = (1.0 - away * away) * (2.0 - away) * 0.5
    far = (1.0 - away) * (2.0 - away) * (3.0 - away) * (1.0 / 6.0)
    matrix = jnp.where(away < 1.0, near, jnp.where(away < 2.0, far, 0.0))
    return matrix.astype(jnp.bfloat16)


def code_columns(codes_ref, rows):
    picked = [codes_ref[pl.ds(row, 1), :] for row in rows]
    picked = jnp.concatenate(picked, axis=0).astype(jnp.float32)
    spare = -len(rows) % 8
    if spare:
        picked = jnp.concatenate([picked, jnp.zeros((spare, picked.shape[1]), jnp.float32)], axis=0)
    return picked.T.astype(jnp.int32)


def weights_kernel(sizes, angle_ref, codes_ref, after_ref, first_ref, inner_ref):
    pulses, channels, rx_count, piece_count = sizes
    rx_place = lax.axis_index("rx")
    pulse_place = lax.axis_index("pulse")
    beams = angle_ref.shape[1]
    angle = as_column(angle_ref[...])
    rows = []
    now = pulses
    while now > 1:
        base = now * piece_count + pulse_place * now
        rows.extend(base + index for index in range(now))
        now //= 2
    codes = code_columns(codes_ref, rows)
    within = lax.broadcasted_iota(jnp.int32, (1, 4 * channels), 1)
    owner = jnp.bitwise_xor(rx_place, jnp.where(within >= 2 * channels, 1, 0))
    receiver = owner * channels + jnp.bitwise_and(within, channels - 1)
    is_imag = jnp.bitwise_and(within, channels) != 0
    scale = 1.0 / math.sqrt(channels * rx_count)
    steer_re, steer_im = turn_parts(jnp.bitwise_and(angle * receiver, 1023))
    steer_re = (steer_re * scale).astype(jnp.bfloat16).astype(jnp.float32)
    steer_im = (-steer_im * scale).astype(jnp.bfloat16).astype(jnp.float32)
    steer = jnp.concatenate(
        [
            jnp.where(is_imag, -steer_im, steer_re).astype(jnp.bfloat16),
            jnp.where(is_imag, steer_re, steer_im).astype(jnp.bfloat16),
        ],
        axis=1,
    )
    entries = 4 * channels
    matrices = [interp_matrix(codes[:, index : index + 1]) for index in range(len(rows))]
    composed = jnp.dot(
        jnp.concatenate(matrices[:pulses], axis=0), steer, preferred_element_type=jnp.float32
    )
    for index in range(pulses):
        for part in range(2):
            value = composed[
                index * beams : (index + 1) * beams, part * entries : (part + 1) * entries
            ]
            first_ref[index, part * beams : (part + 1) * beams, :] = value.astype(jnp.bfloat16)
    for index, matrix in enumerate(matrices[pulses:]):
        inner_ref[index] = matrix


def phases_kernel(sizes, angle_ref, after_ref, phase_ref):
    pulses, rx_count, width = sizes
    rng_place = lax.axis_index("rng")
    rx_place = lax.axis_index("rx")
    pulse_place = lax.axis_index("pulse")
    piece_count = phase_ref.shape[0]
    piece_tiles = phase_ref.shape[4] // LANES
    angle = as_column(angle_ref[...])
    factors = []
    now = pulses
    while now > 1:
        base = now * piece_count + pulse_place * now
        factors.extend(base + 1 + index for index in range(0, now, 2))
        now //= 2
    lane = lax.broadcasted_iota(jnp.int32, (1, LANES), 1)
    block = (rng_place * rx_count + rx_place) * width + 1
    base = jnp.bitwise_and(angle * (block + lane), 1023)
    for slot, factor in enumerate([1, *factors]):
        scale = half_root if slot else 1.0
        real, imag = turn_parts(jnp.bitwise_and(base * factor, 1023))
        real, imag = real * scale, imag * scale
        step = turn_parts(jnp.bitwise_and(angle * (factor * LANES), 1023))
        for tile in range(piece_count * piece_tiles):
            index = piece_count - 1 - jnp.bitwise_xor(pulse_place, tile // piece_tiles)
            start = tile % piece_tiles * LANES
            phase_ref[index, slot, 0, :, start : start + LANES] = real
            phase_ref[index, slot, 1, :, start : start + LANES] = imag
            real, imag = turned(real, imag, *step)


def risen(outer_ref, phase_ref, slot, real, imag):
    matrix = outer_ref[slot]
    moved_re = jnp.dot(matrix, real.astype(jnp.bfloat16), preferred_element_type=jnp.float32)
    moved_im = jnp.dot(matrix, imag.astype(jnp.bfloat16), preferred_element_type=jnp.float32)
    return turned(moved_re, moved_im, phase_ref[slot, 0], phase_ref[slot, 1])


def outer_tables_kernel(sizes, angle_ref, codes_ref, image_ref, outer_ref, phase_ref, own_ref):
    rx_count, width, piece_count = sizes
    rng_place = lax.axis_index("rng")
    rx_place = lax.axis_index("rx")
    pulse_place = lax.axis_index("pulse")
    piece_width = phase_ref.shape[3]
    angle = as_column(angle_ref[...])
    lane = lax.broadcasted_iota(jnp.int32, (1, piece_width), 1)
    block = (rng_place * rx_count + rx_place) * width + 1
    base = jnp.bitwise_and(angle * (block + pulse_place * piece_width + lane), 1023)
    counts = [piece_count >> level for level in range(piece_count.bit_length() - 1)]
    rows = [count + index for count in counts for index in range(count)]
    codes = code_columns(codes_ref, rows)
    for slot, row in enumerate(rows):
        outer_ref[slot] = interp_matrix(codes[:, slot : slot + 1])
        real, imag = turn_parts(jnp.bitwise_and(base * (row + 1), 1023))
        phase_ref[slot, 0] = real * half_root
        phase_ref[slot, 1] = imag * half_root
    own_ref[0], own_ref[1] = risen(
        outer_ref, phase_ref, pulse_place, image_ref[0], image_ref[1]
    )


ROWS = 16


def inner_kernel(indices, keep_ref, other_ref, first_ref, inner_ref, phase_ref, *rest):
    *out_refs, moved_ref, picture_ref, level_ref = rest
    pulses = keep_ref.shape[1]
    beams, columns = out_refs[0].shape[1:]
    pieces = range(len(indices))

    def merge(piece, count, base, read, write):
        index = indices[piece]
        for row in range(0, beams, ROWS):
            span = slice(row, row + ROWS)
            step = (phase_ref[index, 0, 0, span], phase_ref[index, 0, 1, span])
            for image in range(0, count, 2):
                slot = base + image // 2
                left = read(image, row)
                right = turned(*read(image + 1, row), *step)
                phase = (phase_ref[index, slot, 0, span], phase_ref[index, slot, 1, span])
                write(
                    image // 2, row, *turned(left[0] + right[0], left[1] + right[1], *phase)
                )

    def lift(piece, image, slot):
        level_ref[piece, image] = jnp.dot(
            inner_ref[slot],
            picture_ref[piece, image],
            preferred_element_type=jnp.float32,
        )

    for piece in pieces:
        for image in range(pulses):
            rows = jnp.concatenate(
                [keep_ref[indices[piece], image], other_ref[piece, image]], axis=0
            )
            moved_ref[piece, image] = jnp.dot(
                first_ref[image],
                rows,
                preferred_element_type=jnp.float32,
            )

    def read_first(piece):
        return lambda image, row: (
            moved_ref[piece, image, row : row + ROWS],
            moved_ref[piece, image, beams + row : beams + row + ROWS],
        )

    def read_level(piece):
        return lambda image, row: (
            level_ref[piece, image, row : row + ROWS, :columns],
            level_ref[piece, image, row : row + ROWS, columns:],
        )

    def write_picture(piece):
        def write(image, row, real, imag):
            picture_ref[piece, image, row : row + ROWS, :columns] = real.astype(jnp.bfloat16)
            picture_ref[piece, image, row : row + ROWS, columns:] = imag.astype(jnp.bfloat16)

        return write

    for piece in pieces:
        merge(piece, pulses, 1, read_first(piece), write_picture(piece))
        for image in range(pulses // 2):
            lift(piece, image, image)
    base = 1 + pulses // 2
    slot = pulses // 2
    count = pulses // 2
    while count > 1:
        for piece in pieces:
            merge(piece, count, base, read_level(piece), write_picture(piece))
            for image in range(count // 2 if count > 2 else 0):
                lift(piece, image, slot + image)
        count //= 2
        base += count
        slot += count
    for piece in pieces:
        out_refs[piece][0] = picture_ref[piece, 0, :, :columns]
        out_refs[piece][1] = picture_ref[piece, 0, :, columns:]


def far_kernel(distances, *rest):
    *image_refs, outer_ref, phase_ref, far_ref = rest
    pulse_place = lax.axis_index("pulse")
    terms = [
        risen(outer_ref, phase_ref, jnp.bitwise_xor(pulse_place, distance), ref[0], ref[1])
        for distance, ref in zip(distances, image_refs)
    ]
    real = terms[0][0] + terms[1][0]
    imag = terms[0][1] + terms[1][1]
    half = jnp.bitwise_xor(jnp.right_shift(pulse_place, 1), 1)
    far_ref[0], far_ref[1] = risen(outer_ref, phase_ref, 4 + half, real, imag)


def near_kernel(far_ref, image_ref, own_ref, outer_ref, phase_ref, out_ref):
    pulse_place = lax.axis_index("pulse")
    near = risen(
        outer_ref, phase_ref, jnp.bitwise_xor(pulse_place, 1), image_ref[0], image_ref[1]
    )
    real = own_ref[0] + near[0]
    imag = own_ref[1] + near[1]
    half = jnp.right_shift(pulse_place, 1)
    real, imag = risen(outer_ref, phase_ref, 4 + half, real, imag)
    out_ref[0] = real + far_ref[0]
    out_ref[1] = imag + far_ref[1]


def cost(micros):
    return pl.CostEstimate(
        flops=int(micros * 1.1e9), bytes_accessed=int(micros * 3.6e6), transcendentals=0
    )


PARAMS = dict(compiler_params=pltpu.CompilerParams(vmem_limit_bytes=40 * 1024 * 1024))


def fast(echoes, beam_angle, interp_table):
    rx_count = lax.axis_size("rx")
    pulse_count = lax.axis_size("pulse")
    _, pulses, channels, length = echoes.shape
    beams = beam_angle.shape[0]
    width = length // rx_count
    piece_width = width // pulse_count
    piece_tiles = piece_width // LANES
    rows = 2 * channels
    group = 2 * pulses
    chirp = jnp.asarray(chirp_bands_table())
    angles = beam_angle.reshape(1, beams)
    codes = interp_table.reshape(-1, beams)
    bf16 = jnp.bfloat16
    f32 = jnp.float32
    shape = jax.ShapeDtypeStruct
    across = swapped(echoes, "rng", 0)
    bands = pl.pallas_call(
        bands_kernel,
        out_shape=shape((channels, RX_TILE, 2 * LANES), bf16),
        out_specs=vmem(),
        name="bands",
        cost_estimate=cost(10.0),
        **PARAMS,
    )()
    tiles = length // LANES
    filtered_shape = shape((rows * pulses, (tiles + 2 * HALO_TILES - 1) * LANES), bf16)
    filtered = pl.pallas_call(
        interior_kernel,
        out_shape=filtered_shape,
        in_specs=[vmem()] * 2,
        out_specs=vmem(),
        scratch_shapes=[
            pltpu.VMEM((tiles + 2, channels * group, LANES), f32),
            pltpu.VMEM((tiles + 1, rows * pulses, LANES), f32),
        ],
        name="interior",
        **PARAMS,
    )(echoes, bands)

    def pieces(count):
        return shape((count, pulses, rows, piece_width), bf16)

    last = pulse_count - 1
    groups = [[3, 2], [1, 0]]
    filtered, first_sent = pl.pallas_call(
        functools.partial(edges_kernel, (pulse_count, groups[:1])),
        out_shape=[filtered_shape, pieces(len(groups[0]))],
        in_specs=[vmem()] * 5,
        out_specs=[vmem()] * 2,
        scratch_shapes=[
            pltpu.VMEM((HALO_TILES + 1, channels * group, LANES), f32),
            pltpu.VMEM((HALO_TILES, rows * pulses, LANES), f32),
        ],
        input_output_aliases={0: 0},
        name="edges",
        **PARAMS,
    )(filtered, echoes, across, bands, chirp)
    phase = pl.pallas_call(
        functools.partial(phases_kernel, (pulses, rx_count, width)),
        out_shape=shape((pulse_count, pulses, 2, beams, piece_width), f32),
        in_specs=[vmem(), anywhere()],
        out_specs=vmem(),
        name="phases",
        **PARAMS,
    )(angles, first_sent)
    kept, *sent = pl.pallas_call(
        functools.partial(rest_kernel, pulse_count, groups[1:2]),
        out_shape=[pieces(pulse_count), pieces(len(groups[1]))],
        in_specs=[vmem()] * 2 + [anywhere()],
        out_specs=[vmem()] * 2,
        name="rest",
        **PARAMS,
    )(filtered, chirp, phase)
    first, inner = pl.pallas_call(
        functools.partial(weights_kernel, (pulses, channels, rx_count, pulse_count)),
        out_shape=[
            shape((pulses, 2 * beams, 4 * channels), bf16),
            shape((pulses - 2, beams, beams), bf16),
        ],
        in_specs=[vmem()] * 2 + [anywhere()],
        out_specs=[vmem()] * 2,
        name="weights",
        **PARAMS,
    )(angles, codes, kept)
    images = [None] * pulse_count

    def merge(members, piece):
        other = swapped(piece, "rx", 0)
        size = len(members)
        merged = pl.pallas_call(
            functools.partial(inner_kernel, [last - distance for distance in members]),
            out_shape=[shape((2, beams, piece_width), bf16)] * size,
            in_specs=[vmem()] * 5,
            out_specs=[vmem()] * size,
            scratch_shapes=[
                pltpu.VMEM((size, pulses, 2 * beams, piece_width), f32),
                pltpu.VMEM((size, pulses // 2, beams, 2 * piece_width), bf16),
                pltpu.VMEM((size, pulses // 2, beams, 2 * piece_width), f32),
            ],
            name="inner",
            cost_estimate=cost(3.0),
            **PARAMS,
        )(kept, other, first, inner, phase)
        for distance, image in zip(members, merged):
            images[distance] = image

    merge(groups[0], first_sent)
    merge(groups[1], sent[0])
    for distance in range(1, pulse_count):
        pairs = [(i, i ^ distance) for i in range(pulse_count)]
        images[distance] = lax.ppermute(images[distance], "pulse", pairs)
    outer_count = 2 * pulse_count - 2
    picture_shape = shape((2, beams, piece_width), f32)
    outer, outer_phase, own = pl.pallas_call(
        functools.partial(outer_tables_kernel, (rx_count, width, pulse_count)),
        out_shape=[
            shape((outer_count, beams, beams), bf16),
            shape((outer_count, 2, beams, piece_width), f32),
            picture_shape,
        ],
        in_specs=[vmem()] * 3,
        out_specs=[vmem()] * 3,
        name="outer_tables",
        **PARAMS,
    )(angles, codes, images[0])
    far = pl.pallas_call(
        functools.partial(far_kernel, (3, 2)),
        out_shape=picture_shape,
        in_specs=[vmem()] * 4,
        out_specs=vmem(),
        name="far",
        **PARAMS,
    )(images[3], images[2], outer, outer_phase)
    return pl.pallas_call(
        near_kernel,
        out_shape=picture_shape,
        in_specs=[vmem()] * 5,
        out_specs=vmem(),
        name="near",
        **PARAMS,
    )(far, images[1], own, outer, outer_phase)


def power_of_two(count):
    return count > 0 and count & (count - 1) == 0


def per_device(echoes, beam_angle, interp_table):
    _, pulses, channels, length = echoes.shape
    rx_count = lax.axis_size("rx")
    pulse_count = lax.axis_size("pulse")
    piece_width = length // (rx_count * pulse_count)
    if (
        lax.axis_size("rng") == 2
        and rx_count == 2
        and channels == 8
        and pulses == 8
        and pulse_count == 4
        and power_of_two(beam_angle.shape[0])
        and beam_angle.shape[0] % 16 == 0
        and piece_width % LANES == 0
    ):
        return fast(echoes, beam_angle, interp_table)
    return local(echoes, beam_angle, interp_table)


def solution(mesh):
    placed = (P(None, ("slab", "pulse"), "rx", "rng"), P(), P())
    return jax.shard_map(
        per_device,
        mesh=mesh,
        in_specs=placed,
        out_specs=P(None, "slab", ("rng", "rx", "pulse")),
        check_vma=False,
    )
```

```python
import functools
import math

import jax
import jax.numpy as jnp
import ml_dtypes
import numpy as np
from jax import lax
from jax.experimental import pallas as pl
from jax.experimental.pallas import tpu as pltpu
from jax.sharding import PartitionSpec as P

RTAPS = 64
CTAPS = 512


half_root = 0.7071067811865476
full_turn = 2.0 * math.pi


def extended_2(block, sides, width):
    for axis, dim in sides:
        count = lax.axis_size(axis)
        forward = [(i, i + 1) for i in range(count - 1)]
        backward = [(target, source) for source, target in forward]
        low = lax.ppermute(
            lax.slice_in_dim(block, block.shape[dim] - width, None, axis=dim), axis, forward
        )
        high = lax.ppermute(lax.slice_in_dim(block, 0, width, axis=dim), axis, backward)
        block = jnp.concatenate([low, block, high], axis=dim)
    return block


def swapped(x, axis, distance):
    return lax.ppermute(x, axis, [(i, i ^ 1 << distance) for i in range(lax.axis_size(axis))])


def receiver_taps(channel_ids, tap_count):
    tap_index = jnp.arange(tap_count, dtype=jnp.float32)
    window = 0.5 - 0.5 * jnp.cos(full_turn * (tap_index + 0.5) / tap_count)
    window = window / jnp.sqrt(jnp.sum(window * window))
    channel = channel_ids.astype(jnp.float32)[:, None] + 1.0
    angle = full_turn * channel * (tap_index - tap_count // 2) / (4 * tap_count)
    return (
        (window * jnp.cos(angle)).astype(jnp.bfloat16),
        (window * jnp.sin(angle)).astype(jnp.bfloat16),
    )


def chirp_taps(tap_count):
    offset = jnp.arange(tap_count, dtype=jnp.int32) - tap_count // 2
    phase_step = jnp.mod(offset * offset, 2 * tap_count).astype(jnp.float32)
    angle = math.pi * phase_step / tap_count
    scale = 1.0 / math.sqrt(tap_count)
    return (
        (jnp.cos(angle) * scale).astype(jnp.bfloat16),
        (-jnp.sin(angle) * scale).astype(jnp.bfloat16),
    )


def steering(beam_angle, receivers):
    channel = jnp.arange(receivers, dtype=jnp.int32)
    turns = jnp.mod(beam_angle[:, None] * channel[None, :], 1024).astype(jnp.float32)
    angle = full_turn * turns / 1024.0
    scale = 1.0 / math.sqrt(receivers)
    return (
        (jnp.cos(angle) * scale).astype(jnp.bfloat16),
        (-jnp.sin(angle) * scale).astype(jnp.bfloat16),
    )


def interp_matrices(codes, beam_count):
    shifted = codes // 4 - 1
    fraction = jnp.mod(codes, 4).astype(jnp.float32) / 4.0
    weights = (
        -fraction * (fraction - 1.0) * (fraction - 2.0) / 6.0,
        (fraction + 1.0) * (fraction - 1.0) * (fraction - 2.0) / 2.0,
        -(fraction + 1.0) * fraction * (fraction - 2.0) / 2.0,
        (fraction + 1.0) * fraction * (fraction - 1.0) / 6.0,
    )
    columns = jnp.arange(beam_count, dtype=jnp.int32)
    matrices = jnp.zeros(codes.shape + (beam_count,), jnp.float32)
    for tap_index in range(4):
        target = jnp.mod(columns + shifted + tap_index - 1, beam_count)
        matrices = matrices + weights[tap_index][..., None] * (target[..., None] == columns).astype(
            jnp.float32
        )
    return matrices


def phases(node_ids, positions, beam_angle, side):
    base = jnp.mod(beam_angle[:, None] * (positions[None, :] + 1), 1024)
    factor = 2 * node_ids + side + 1
    turns = jnp.mod(base[:, None, :] * factor[None, :, None], 1024).astype(jnp.float32)
    angle = full_turn * turns / 1024.0
    return (jnp.cos(angle), jnp.sin(angle))


def side_term(picture, matrices, cosine, sine):
    moved = jnp.einsum("gqa,cagr->cqgr", matrices, picture, precision=lax.Precision.HIGHEST)
    return (cosine * moved[0] - sine * moved[1], sine * moved[0] + cosine * moved[1])


def merge_pair(left_image, right_image, node_ids, positions, beam_angle, interp_table):
    matrices = interp_matrices(interp_table[node_ids], left_image.shape[1])
    left_cos, left_sin = phases(node_ids, positions, beam_angle, 0)
    right_cos, right_sin = phases(node_ids, positions, beam_angle, 1)
    left_re, left_im = side_term(left_image, matrices[:, 0], left_cos, left_sin)
    right_re, right_im = side_term(right_image, matrices[:, 1], right_cos, right_sin)
    return jnp.stack([(left_re + right_re) * half_root, (left_im + right_im) * half_root])


def toeplitz_blocks(taps_re, taps_im):
    tap_count = taps_re.shape[-1]
    leading = taps_re.shape[:-1]

    def lay_out(taps):
        padded = jnp.concatenate([taps, jnp.zeros(leading + (tap_count + 1,), taps.dtype)], axis=-1)
        tiled = jnp.tile(padded, (1,) * len(leading) + (tap_count,))
        banded = tiled[..., : 2 * tap_count * tap_count].reshape(
            leading + (tap_count, 2 * tap_count)
        )
        return jnp.swapaxes(banded, -1, -2)

    real_band = lay_out(taps_re)
    imag_band = lay_out(taps_im)
    upper = jnp.concatenate([real_band, imag_band], axis=-1)
    lower = jnp.concatenate([-imag_band, real_band], axis=-1)
    return jnp.concatenate([upper, lower], axis=-2)


def block_filter(extended, matrices, tap_count, per_channel):
    pulses, channels, length = extended.shape[1:]
    blocks = length // tap_count - 1
    pieces = extended.reshape(2, pulses, channels, blocks + 1, tap_count)
    windows = jnp.concatenate([pieces[:, :, :, :-1], pieces[:, :, :, 1:]], axis=4)
    windows = jnp.transpose(windows, (1, 2, 3, 0, 4)).reshape(
        pulses, channels, blocks, 4 * tap_count
    )
    if per_channel:
        output = jnp.einsum("pcnw,cwo->pcno", windows, matrices, preferred_element_type=jnp.float32)
    else:
        output = jnp.einsum("pcnw,wo->pcno", windows, matrices, preferred_element_type=jnp.float32)
    output = output.reshape(pulses, channels, blocks, 2, tap_count)
    return jnp.transpose(output, (3, 0, 1, 2, 4)).reshape(2, pulses, channels, blocks * tap_count)


def local(echoes, beam_angle, interp_table):
    rx_count = lax.axis_size("rx")
    pulse_count = lax.axis_size("pulse")
    rng_place = lax.axis_index("rng")
    rx_place = lax.axis_index("rx")
    pulse_place = lax.axis_index("pulse")
    pulses, channels, length = echoes.shape[1:]
    beam_count = beam_angle.shape[0]
    receivers = channels * rx_count
    channel_ids = rx_place * channels + jnp.arange(channels, dtype=jnp.int32)
    rx_re, rx_im = receiver_taps(channel_ids, RTAPS)
    rx_bands = toeplitz_blocks(rx_re, rx_im)
    chirp_re, chirp_im = chirp_taps(CTAPS)
    chirp_band = toeplitz_blocks(chirp_re, chirp_im)
    extended = extended_2(echoes, (("rng", 3),), RTAPS // 2)
    filtered = block_filter(extended, rx_bands, RTAPS, True).astype(jnp.bfloat16)
    filtered = extended_2(filtered, (("rng", 3),), CTAPS // 2)
    compressed = block_filter(filtered, chirp_band, CTAPS, False).astype(jnp.bfloat16)
    steering_real, steering_imaginary = steering(beam_angle, receivers)
    steer_matrix = jnp.concatenate(
        [
            jnp.concatenate([steering_real, -steering_imaginary], axis=1),
            jnp.concatenate([steering_imaginary, steering_real], axis=1),
        ],
        axis=0,
    )
    arrived = lax.all_to_all(compressed, "rx", split_axis=3, concat_axis=2, tiled=True)
    item_count, recv_count, owned_cols = arrived.shape[1:]
    stacked = jnp.transpose(arrived, (0, 2, 1, 3)).reshape(2 * recv_count, item_count * owned_cols)
    formed = jnp.dot(steer_matrix, stacked, preferred_element_type=jnp.float32)
    picture = formed.reshape(2, beam_count, item_count, owned_cols)
    owned_width = length // rx_count
    positions = (
        rng_place * length + rx_place * owned_width + jnp.arange(owned_width, dtype=jnp.int32)
    )
    for level in range(pulses.bit_length() - 1):
        groups_now = pulses >> level + 1
        node_ids = (pulse_count + pulse_place) * groups_now + jnp.arange(
            groups_now, dtype=jnp.int32
        )
        paired = picture.reshape(2, beam_count, groups_now, 2, owned_width)
        picture = merge_pair(
            paired[:, :, :, 0], paired[:, :, :, 1], node_ids, positions, beam_angle, interp_table
        )
    picture = picture[:, :, 0]
    cross_levels = pulse_count.bit_length() - 1
    piece_width = owned_width // pulse_count
    pieces = picture.reshape(2, beam_count, pulse_count, piece_width)
    spots = positions.reshape(pulse_count, piece_width)
    for level in range(cross_levels):
        parity = jnp.right_shift(pulse_place, level) & 1
        count_now = pieces.shape[2]
        paired = pieces.reshape(2, beam_count, count_now // 2, 2, piece_width)
        kept_half = lax.dynamic_index_in_dim(paired, parity, 3, keepdims=False)
        sent_half = lax.dynamic_index_in_dim(paired, 1 - parity, 3, keepdims=False)
        partner = swapped(sent_half, "pulse", level)
        spot_pairs = spots.reshape(count_now // 2, 2, piece_width)
        spots = lax.dynamic_index_in_dim(spot_pairs, parity, 1, keepdims=False)
        own_part = kept_half.reshape(2, beam_count, -1)
        other_part = partner.reshape(2, beam_count, -1)
        left_image = jnp.where(parity == 0, own_part, other_part)
        right_image = jnp.where(parity == 0, other_part, own_part)
        combine_node_ids = jnp.reshape(
            (pulse_count >> level + 1) + jnp.right_shift(pulse_place, level + 1), (1,)
        )
        merged = merge_pair(
            left_image[:, :, None],
            right_image[:, :, None],
            combine_node_ids,
            spots.reshape(-1),
            beam_angle,
            interp_table,
        )
        flat = merged[:, :, 0]
        pieces = flat.reshape(2, beam_count, count_now // 2, piece_width)
    picture = pieces.reshape(2, beam_count, piece_width)
    return picture


LANES = 128
RX_TILE = LANES + RTAPS
CHIRP_TILE = 6 * LANES
HALO_TILES = 3
HALO = HALO_TILES * LANES


def vmem():
    return pl.BlockSpec(memory_space=pltpu.VMEM)


def hbm():
    return pl.BlockSpec(memory_space=pltpu.HBM)


def anywhere():
    return pl.BlockSpec(memory_space=pl.ANY)


def chirp_bands_table():
    offset = np.arange(CTAPS) - CTAPS // 2
    angle = math.pi * np.mod(offset * offset, 2 * CTAPS) / CTAPS
    scale = 1.0 / math.sqrt(CTAPS)
    offset = np.arange(CHIRP_TILE)[:, None] - np.arange(LANES)[None, :] - (LANES - RTAPS // 2)
    inside = (offset >= 0) & (offset < CTAPS)
    place = np.clip(offset, 0, CTAPS - 1)
    bands = [
        np.where(inside, taps[place], 0.0)
        for taps in (np.cos(angle) * scale, -np.sin(angle) * scale)
    ]
    return np.concatenate(bands, axis=-1).astype(ml_dtypes.bfloat16)


def filter_channel(windows, bands, pulses):
    product = jnp.dot(windows, bands, preferred_element_type=jnp.float32)
    product = product.reshape(-1, 2, pulses, 2 * LANES)
    real = product[:, 0, :, :LANES] - product[:, 1, :, LANES:]
    imag = product[:, 0, :, LANES:] + product[:, 1, :, :LANES]
    return real, imag


def bands_kernel(bands_ref):
    channels = bands_ref.shape[0]
    first_channel = lax.axis_index("rx") * channels
    lane = lax.broadcasted_iota(jnp.int32, (channels, LANES), 1)
    channel = lax.broadcasted_iota(jnp.int32, (channels, LANES), 0) + first_channel + 1
    tap = jnp.bitwise_and(LANES - lane, LANES - 1)
    unit = 1024 // RTAPS
    window = 0.5 - 0.5 * turn_parts(tap * unit + unit // 2)[0]
    window = jnp.where(tap < RTAPS, window * (1.0 / math.sqrt(RTAPS * 3 / 8)), 0.0)
    turn = channel * (tap - RTAPS // 2) * (1024 // (4 * RTAPS))
    row = lax.broadcasted_iota(jnp.int32, (LANES, LANES), 0)
    upper = lax.broadcasted_iota(jnp.int32, (LANES, LANES), 1) <= row
    for part, wave in enumerate(turn_parts(jnp.bitwise_and(turn, 1023))):
        taps = window * wave
        span = slice(part * LANES, (part + 1) * LANES)
        for index in range(channels):
            spread = jnp.broadcast_to(taps[index : index + 1], (LANES, LANES))
            rolled = pltpu.roll(spread, 0, 1, stride=1, stride_axis=0)
            bands_ref[index, :LANES, span] = jnp.where(upper, rolled, 0.0).astype(jnp.bfloat16)
            lower = jnp.where(upper, 0.0, rolled)[:RTAPS]
            bands_ref[index, LANES:, span] = lower.astype(jnp.bfloat16)


def interior_kernel(echo_ref, bands_ref, filtered_ref, rows_in, rows_out):
    _, pulses, channels, length = echo_ref.shape
    tiles = length // LANES
    group = 2 * pulses
    empty = jnp.zeros(rows_in.shape[1:], jnp.float32)
    rows_in[0] = empty
    rows_in[tiles + 1] = empty
    for part in range(2):
        for pulse in range(pulses):
            where = pl.ds(part * pulses + pulse, channels, stride=group)
            block = echo_ref[part, pulse].astype(jnp.float32)
            for tile in range(tiles):
                rows_in[tile + 1, where, :] = block[:, tile * LANES : (tile + 1) * LANES]
    lane = lax.broadcasted_iota(jnp.int32, (pulses, LANES), 1)
    mask = jnp.where(lane >= LANES - RTAPS // 2, 1.0, 0.0)
    for channel in range(channels):
        rows = rows_in[:, channel * group : (channel + 1) * group, :].astype(jnp.bfloat16)
        windows = jnp.concatenate(
            [rows[:-1].reshape(-1, LANES), rows[1:].reshape(-1, LANES)[:, :RTAPS]], axis=1
        )
        real, imag = filter_channel(windows, bands_ref[channel], pulses)
        for tile in range(tiles + 1):
            tile_re, tile_im = real[tile], imag[tile]
            if tile == 0:
                tile_re, tile_im = tile_re * mask, tile_im * mask
            if tile == tiles:
                tile_re, tile_im = tile_re * (1.0 - mask), tile_im * (1.0 - mask)
            rows_out[tile, pl.ds(channel, pulses, stride=2 * channels), :] = tile_re
            rows_out[tile, pl.ds(channels + channel, pulses, stride=2 * channels), :] = tile_im
    rows = filtered_ref.shape[0]
    nothing = jnp.zeros((rows, (HALO_TILES - 1) * LANES), jnp.bfloat16)
    filtered_ref[:, : (HALO_TILES - 1) * LANES] = nothing
    filtered_ref[:, (HALO_TILES + tiles) * LANES :] = nothing
    for tile in range(tiles + 1):
        spot = (HALO_TILES - 1 + tile) * LANES
        filtered_ref[:, spot : spot + LANES] = rows_out[tile].astype(jnp.bfloat16)


def chirp_pieces(filtered_ref, chirp_ref, owner, piece_count, distances, out_ref):
    pulse_place = lax.axis_index("pulse")
    _, pulses, rows, width = out_ref.shape
    tiles = width // LANES
    channels = rows // 2
    windows = []
    for distance in distances:
        piece = jnp.bitwise_xor(pulse_place, distance)
        first = (owner * piece_count + piece) * tiles
        for tile in range(tiles):
            start = pl.multiple_of((first + tile) * LANES, LANES)
            windows.append(filtered_ref[:, pl.ds(start, CHIRP_TILE)])
    product = jnp.dot(
        jnp.concatenate(windows, axis=0), chirp_ref[...], preferred_element_type=jnp.float32
    )
    product = product.reshape(len(windows), pulses, rows, 2 * LANES)
    for index in range(len(distances)):
        for tile in range(tiles):
            block = product[index * tiles + tile]
            real = block[:, :channels, :LANES] - block[:, channels:, LANES:]
            imag = block[:, :channels, LANES:] + block[:, channels:, :LANES]
            out_ref[index, :, :, tile * LANES : (tile + 1) * LANES] = jnp.concatenate(
                [real, imag], axis=1
            ).astype(jnp.bfloat16)


def edges_kernel(
    plan, inner_ref, echo_ref, across_ref, bands_ref, chirp_ref, filtered_ref, *rest
):
    *send_refs, rows_in, rows_out = rest
    del inner_ref
    _, pulses, channels, length = echo_ref.shape
    tiles = length // LANES
    group = 2 * pulses
    lowest = lax.axis_index("rng") == 0
    far = pl.ds(pl.multiple_of(jnp.where(lowest, 0, length - HALO), LANES), HALO)
    beside = pl.ds(pl.multiple_of(jnp.where(lowest, length - LANES, 0), LANES), LANES)
    near_tile = jnp.where(lowest, 0, HALO_TILES)
    far_tile = jnp.where(lowest, 1, 0)
    for part in range(2):
        for pulse in range(pulses):
            where = pl.ds(part * pulses + pulse, channels, stride=group)
            edge = across_ref[part, pulse, :, far].astype(jnp.float32)
            near = echo_ref[part, pulse, :, beside].astype(jnp.float32)
            rows_in[near_tile, where, :] = near
            for tile in range(HALO_TILES):
                rows_in[far_tile + tile, where, :] = edge[:, tile * LANES : (tile + 1) * LANES]
    for channel in range(channels):
        rows = rows_in[:, channel * group : (channel + 1) * group, :].astype(jnp.bfloat16)
        windows = jnp.concatenate(
            [rows[:-1].reshape(-1, LANES), rows[1:].reshape(-1, LANES)[:, :RTAPS]], axis=1
        )
        real, imag = filter_channel(windows, bands_ref[channel], pulses)
        for tile in range(HALO_TILES):
            rows_out[tile, pl.ds(channel, pulses, stride=2 * channels), :] = real[tile]
            rows_out[tile, pl.ds(channels + channel, pulses, stride=2 * channels), :] = imag[tile]
    first = jnp.where(lowest, tiles + HALO_TILES - 1, 0)
    for tile in range(HALO_TILES):
        start = pl.multiple_of((first + tile) * LANES, LANES)
        filtered_ref[:, pl.ds(start, LANES)] = rows_out[tile].astype(jnp.bfloat16)
    piece_count, groups = plan
    for distances, send_ref in zip(groups, send_refs):
        chirp_pieces(
            filtered_ref, chirp_ref, 1 - lax.axis_index("rx"), piece_count, distances, send_ref
        )


def rest_kernel(piece_count, groups, filtered_ref, chirp_ref, after_ref, keep_ref, *send_refs):
    rx_place = lax.axis_index("rx")
    own = list(range(piece_count - 1, -1, -1))
    chirp_pieces(filtered_ref, chirp_ref, rx_place, piece_count, own, keep_ref)
    for distances, send_ref in zip(groups, send_refs):
        chirp_pieces(filtered_ref, chirp_ref, 1 - rx_place, piece_count, distances, send_ref)


def turn_parts(step):
    shifted = step + 128
    angle = (jnp.bitwise_and(shifted, 255) - 128).astype(jnp.float32) * (full_turn / 1024.0)
    quarter = jnp.right_shift(shifted, 8)
    square = angle * angle
    cosine = 1.0 + square * (-1 / 2 + square * (1 / 24 + square * (-1 / 720 + square * (1 / 40320))))
    sine = angle * (1.0 + square * (-1 / 6 + square * (1 / 120 + square * (-1 / 5040))))
    odd = jnp.bitwise_and(quarter, 1) == 1
    real = jnp.where(odd, sine, cosine)
    imag = jnp.where(odd, cosine, sine)
    real = jnp.where(jnp.bitwise_and(quarter + 1, 2) == 2, -real, real)
    imag = jnp.where(jnp.bitwise_and(quarter, 2) == 2, -imag, imag)
    return real, imag


def turned(real, imag, phase_re, phase_im):
    return phase_re * real - phase_im * imag, phase_im * real + phase_re * imag


def as_column(row):
    count = row.shape[1]
    first = lax.broadcasted_iota(jnp.int32, (count, count), 0)
    second = lax.broadcasted_iota(jnp.int32, (count, count), 1)
    spread = jnp.where(first == second, row.astype(jnp.float32), 0.0)
    return jnp.sum(spread, axis=1, keepdims=True).astype(jnp.int32)


def interp_matrix(code):
    beams = code.shape[0]
    angle_bin = lax.broadcasted_iota(jnp.int32, (beams, beams), 0)
    column = lax.broadcasted_iota(jnp.int32, (beams, beams), 1)
    half = 2 * beams
    away = jnp.bitwise_and(4 * (column - angle_bin + 1) - code + half, 4 * beams - 1) - half
    away = jnp.abs(away.astype(jnp.float32)) * 0.25
    near = (1.0 - away * away) * (2.0 - away) * 0.5
    far = (1.0 - away) * (2.0 - away) * (3.0 - away) * (1.0 / 6.0)
    matrix = jnp.where(away < 1.0, near, jnp.where(away < 2.0, far, 0.0))
    return matrix.astype(jnp.bfloat16)


def code_columns(codes_ref, rows):
    picked = [codes_ref[pl.ds(row, 1), :] for row in rows]
    picked = jnp.concatenate(picked, axis=0).astype(jnp.float32)
    spare = -len(rows) % 8
    if spare:
        picked = jnp.concatenate([picked, jnp.zeros((spare, picked.shape[1]), jnp.float32)], axis=0)
    return picked.T.astype(jnp.int32)


def weights_kernel(sizes, angle_ref, codes_ref, after_ref, first_ref, inner_ref):
    pulses, channels, rx_count, piece_count = sizes
    rx_place = lax.axis_index("rx")
    pulse_place = lax.axis_index("pulse")
    beams = angle_ref.shape[1]
    angle = as_column(angle_ref[...])
    rows = []
    now = pulses
    while now > 1:
        base = now * piece_count + pulse_place * now
        rows.extend(base + index for index in range(now))
        now //= 2
    codes = code_columns(codes_ref, rows)
    column = lax.broadcasted_iota(jnp.int32, (1, 4 * channels * 2), 1)
    within = jnp.bitwise_and(column, 4 * channels - 1)
    owner = jnp.bitwise_xor(rx_place, jnp.where(within >= 2 * channels, 1, 0))
    receiver = owner * channels + jnp.bitwise_and(column, channels - 1)
    is_imag = jnp.bitwise_and(within, channels) != 0
    scale = 1.0 / math.sqrt(channels * rx_count)
    steer_re, steer_im = turn_parts(jnp.bitwise_and(angle * receiver, 1023))
    steer_re = (steer_re * scale).astype(jnp.bfloat16).astype(jnp.float32)
    steer_im = (-steer_im * scale).astype(jnp.bfloat16).astype(jnp.float32)
    steer = jnp.concatenate(
        [
            jnp.where(is_imag, -steer_im, steer_re).astype(jnp.bfloat16),
            jnp.where(is_imag, steer_re, steer_im).astype(jnp.bfloat16),
        ],
        axis=1,
    )
    low_half = column >= 4 * channels
    entries = 8 * channels
    matrices = [interp_matrix(codes[:, index : index + 1]) for index in range(len(rows))]
    composed = jnp.dot(
        jnp.concatenate(matrices[:pulses], axis=0), steer, preferred_element_type=jnp.float32
    )
    for index in range(pulses):
        for part in range(2):
            value = composed[
                index * beams : (index + 1) * beams, part * entries : (part + 1) * entries
            ]
            high = value.astype(jnp.bfloat16).astype(jnp.float32)
            first_ref[index, part * beams : (part + 1) * beams, :] = jnp.where(
                low_half, value - high, high
            ).astype(jnp.bfloat16)
    for index, matrix in enumerate(matrices[pulses:]):
        inner_ref[index] = matrix


def phases_kernel(sizes, angle_ref, after_ref, phase_ref):
    pulses, rx_count, width = sizes
    rng_place = lax.axis_index("rng")
    rx_place = lax.axis_index("rx")
    pulse_place = lax.axis_index("pulse")
    piece_count = phase_ref.shape[0]
    piece_tiles = phase_ref.shape[4] // LANES
    angle = as_column(angle_ref[...])
    factors = []
    now = pulses
    while now > 1:
        base = now * piece_count + pulse_place * now
        factors.extend(base + 1 + index for index in range(0, now, 2))
        now //= 2
    lane = lax.broadcasted_iota(jnp.int32, (1, LANES), 1)
    block = (rng_place * rx_count + rx_place) * width + 1
    base = jnp.bitwise_and(angle * (block + lane), 1023)
    for slot, factor in enumerate([1, *factors]):
        scale = half_root if slot else 1.0
        real, imag = turn_parts(jnp.bitwise_and(base * factor, 1023))
        real, imag = real * scale, imag * scale
        step = turn_parts(jnp.bitwise_and(angle * (factor * LANES), 1023))
        for tile in range(piece_count * piece_tiles):
            index = piece_count - 1 - jnp.bitwise_xor(pulse_place, tile // piece_tiles)
            start = tile % piece_tiles * LANES
            phase_ref[index, slot, 0, :, start : start + LANES] = real
            phase_ref[index, slot, 1, :, start : start + LANES] = imag
            real, imag = turned(real, imag, *step)


def risen(outer_ref, phase_ref, slot, real, imag):
    matrix = outer_ref[slot]
    moved_re = jnp.dot(matrix, real.astype(jnp.bfloat16), preferred_element_type=jnp.float32)
    moved_im = jnp.dot(matrix, imag.astype(jnp.bfloat16), preferred_element_type=jnp.float32)
    return turned(moved_re, moved_im, phase_ref[slot, 0], phase_ref[slot, 1])


def outer_tables_kernel(sizes, angle_ref, codes_ref, image_ref, outer_ref, phase_ref, own_ref):
    rx_count, width, piece_count = sizes
    rng_place = lax.axis_index("rng")
    rx_place = lax.axis_index("rx")
    pulse_place = lax.axis_index("pulse")
    piece_width = phase_ref.shape[3]
    angle = as_column(angle_ref[...])
    lane = lax.broadcasted_iota(jnp.int32, (1, piece_width), 1)
    block = (rng_place * rx_count + rx_place) * width + 1
    base = jnp.bitwise_and(angle * (block + pulse_place * piece_width + lane), 1023)
    counts = [piece_count >> level for level in range(piece_count.bit_length() - 1)]
    rows = [count + index for count in counts for index in range(count)]
    codes = code_columns(codes_ref, rows)
    for slot, row in enumerate(rows):
        outer_ref[slot] = interp_matrix(codes[:, slot : slot + 1])
        real, imag = turn_parts(jnp.bitwise_and(base * (row + 1), 1023))
        phase_ref[slot, 0] = real * half_root
        phase_ref[slot, 1] = imag * half_root
    own_ref[0], own_ref[1] = risen(
        outer_ref, phase_ref, pulse_place, image_ref[0], image_ref[1]
    )


ROWS = 8


def inner_kernel(indices, keep_ref, other_ref, first_ref, inner_ref, phase_ref, *rest):
    *out_refs, moved_ref, picture_ref, level_ref = rest
    pulses = keep_ref.shape[1]
    beams, columns = out_refs[0].shape[1:]
    pieces = range(len(indices))

    def merge(piece, count, base, read, write):
        index = indices[piece]
        for row in range(0, beams, ROWS):
            span = slice(row, row + ROWS)
            step = (phase_ref[index, 0, 0, span], phase_ref[index, 0, 1, span])
            for image in range(0, count, 2):
                slot = base + image // 2
                left = read(image, row)
                right = turned(*read(image + 1, row), *step)
                phase = (phase_ref[index, slot, 0, span], phase_ref[index, slot, 1, span])
                write(
                    image // 2, row, *turned(left[0] + right[0], left[1] + right[1], *phase)
                )

    def lift(piece, image, slot):
        level_ref[piece, image] = jnp.dot(
            inner_ref[slot],
            picture_ref[piece, image].astype(jnp.bfloat16),
            preferred_element_type=jnp.float32,
        )

    for piece in pieces:
        for image in range(pulses):
            rows = jnp.concatenate(
                [keep_ref[indices[piece], image], other_ref[piece, image]], axis=0
            )
            moved_ref[piece, image] = jnp.dot(
                first_ref[image],
                jnp.concatenate([rows, rows], axis=0),
                preferred_element_type=jnp.float32,
            )

    def read_first(piece):
        return lambda image, row: (
            moved_ref[piece, image, row : row + ROWS],
            moved_ref[piece, image, beams + row : beams + row + ROWS],
        )

    def read_level(piece):
        return lambda image, row: (
            level_ref[piece, image, row : row + ROWS, :columns],
            level_ref[piece, image, row : row + ROWS, columns:],
        )

    def write_picture(piece):
        def write(image, row, real, imag):
            picture_ref[piece, image, row : row + ROWS, :columns] = real
            picture_ref[piece, image, row : row + ROWS, columns:] = imag

        return write

    for piece in pieces:
        merge(piece, pulses, 1, read_first(piece), write_picture(piece))
        for image in range(pulses // 2):
            lift(piece, image, image)
    base = 1 + pulses // 2
    slot = pulses // 2
    count = pulses // 2
    while count > 1:
        for piece in pieces:
            merge(piece, count, base, read_level(piece), write_picture(piece))
            for image in range(count // 2 if count > 2 else 0):
                lift(piece, image, slot + image)
        count //= 2
        base += count
        slot += count
    for piece in pieces:
        out_refs[piece][0] = picture_ref[piece, 0, :, :columns].astype(jnp.bfloat16)
        out_refs[piece][1] = picture_ref[piece, 0, :, columns:].astype(jnp.bfloat16)


def far_kernel(distances, *rest):
    *image_refs, outer_ref, phase_ref, far_ref = rest
    pulse_place = lax.axis_index("pulse")
    terms = [
        risen(outer_ref, phase_ref, jnp.bitwise_xor(pulse_place, distance), ref[0], ref[1])
        for distance, ref in zip(distances, image_refs)
    ]
    real = terms[0][0] + terms[1][0]
    imag = terms[0][1] + terms[1][1]
    half = jnp.bitwise_xor(jnp.right_shift(pulse_place, 1), 1)
    far_ref[0], far_ref[1] = risen(outer_ref, phase_ref, 4 + half, real, imag)


def near_kernel(far_ref, image_ref, own_ref, outer_ref, phase_ref, out_ref):
    pulse_place = lax.axis_index("pulse")
    near = risen(
        outer_ref, phase_ref, jnp.bitwise_xor(pulse_place, 1), image_ref[0], image_ref[1]
    )
    real = own_ref[0] + near[0]
    imag = own_ref[1] + near[1]
    half = jnp.right_shift(pulse_place, 1)
    real, imag = risen(outer_ref, phase_ref, 4 + half, real, imag)
    out_ref[0] = real + far_ref[0]
    out_ref[1] = imag + far_ref[1]


def cost(micros):
    return pl.CostEstimate(
        flops=int(micros * 1.1e9), bytes_accessed=int(micros * 3.6e6), transcendentals=0
    )


PARAMS = dict(compiler_params=pltpu.CompilerParams(vmem_limit_bytes=40 * 1024 * 1024))


def fast(echoes, beam_angle, interp_table):
    rx_count = lax.axis_size("rx")
    pulse_count = lax.axis_size("pulse")
    _, pulses, channels, length = echoes.shape
    beams = beam_angle.shape[0]
    width = length // rx_count
    piece_width = width // pulse_count
    piece_tiles = piece_width // LANES
    rows = 2 * channels
    group = 2 * pulses
    chirp = jnp.asarray(chirp_bands_table())
    angles = beam_angle.reshape(1, beams)
    codes = interp_table.reshape(-1, beams)
    bf16 = jnp.bfloat16
    f32 = jnp.float32
    shape = jax.ShapeDtypeStruct
    across = swapped(echoes, "rng", 0)
    bands = pl.pallas_call(
        bands_kernel,
        out_shape=shape((channels, RX_TILE, 2 * LANES), bf16),
        out_specs=vmem(),
        name="bands",
        cost_estimate=cost(10.0),
        **PARAMS,
    )()
    tiles = length // LANES
    filtered_shape = shape((rows * pulses, (tiles + 2 * HALO_TILES - 1) * LANES), bf16)
    filtered = pl.pallas_call(
        interior_kernel,
        out_shape=filtered_shape,
        in_specs=[vmem()] * 2,
        out_specs=vmem(),
        scratch_shapes=[
            pltpu.VMEM((tiles + 2, channels * group, LANES), f32),
            pltpu.VMEM((tiles + 1, rows * pulses, LANES), f32),
        ],
        name="interior",
        **PARAMS,
    )(echoes, bands)

    def pieces(count):
        return shape((count, pulses, rows, piece_width), bf16)

    last = pulse_count - 1
    groups = [[3, 2], [1, 0]]
    filtered, first_sent = pl.pallas_call(
        functools.partial(edges_kernel, (pulse_count, groups[:1])),
        out_shape=[filtered_shape, pieces(len(groups[0]))],
        in_specs=[vmem()] * 5,
        out_specs=[vmem()] * 2,
        scratch_shapes=[
            pltpu.VMEM((HALO_TILES + 1, channels * group, LANES), f32),
            pltpu.VMEM((HALO_TILES, rows * pulses, LANES), f32),
        ],
        input_output_aliases={0: 0},
        name="edges",
        **PARAMS,
    )(filtered, echoes, across, bands, chirp)
    phase = pl.pallas_call(
        functools.partial(phases_kernel, (pulses, rx_count, width)),
        out_shape=shape((pulse_count, pulses, 2, beams, piece_width), f32),
        in_specs=[vmem(), anywhere()],
        out_specs=vmem(),
        name="phases",
        **PARAMS,
    )(angles, first_sent)
    kept, *sent = pl.pallas_call(
        functools.partial(rest_kernel, pulse_count, groups[1:2]),
        out_shape=[pieces(pulse_count), pieces(len(groups[1]))],
        in_specs=[vmem()] * 2 + [anywhere()],
        out_specs=[vmem()] * 2,
        name="rest",
        **PARAMS,
    )(filtered, chirp, phase)
    first, inner = pl.pallas_call(
        functools.partial(weights_kernel, (pulses, channels, rx_count, pulse_count)),
        out_shape=[
            shape((pulses, 2 * beams, 8 * channels), bf16),
            shape((pulses - 2, beams, beams), bf16),
        ],
        in_specs=[vmem()] * 2 + [anywhere()],
        out_specs=[vmem()] * 2,
        name="weights",
        **PARAMS,
    )(angles, codes, kept)
    images = [None] * pulse_count

    def merge(members, piece):
        other = swapped(piece, "rx", 0)
        size = len(members)
        merged = pl.pallas_call(
            functools.partial(inner_kernel, [last - distance for distance in members]),
            out_shape=[shape((2, beams, piece_width), bf16)] * size,
            in_specs=[vmem()] * 5,
            out_specs=[vmem()] * size,
            scratch_shapes=[
                pltpu.VMEM((size, pulses, 2 * beams, piece_width), f32),
                pltpu.VMEM((size, pulses // 2, beams, 2 * piece_width), f32),
                pltpu.VMEM((size, pulses // 2, beams, 2 * piece_width), f32),
            ],
            name="inner",
            cost_estimate=cost(3.0),
            **PARAMS,
        )(kept, other, first, inner, phase)
        for distance, image in zip(members, merged):
            images[distance] = image

    merge(groups[0], first_sent)
    merge(groups[1], sent[0])
    for distance in range(1, pulse_count):
        pairs = [(i, i ^ distance) for i in range(pulse_count)]
        images[distance] = lax.ppermute(images[distance], "pulse", pairs)
    outer_count = 2 * pulse_count - 2
    picture_shape = shape((2, beams, piece_width), f32)
    outer, outer_phase, own = pl.pallas_call(
        functools.partial(outer_tables_kernel, (rx_count, width, pulse_count)),
        out_shape=[
            shape((outer_count, beams, beams), bf16),
            shape((outer_count, 2, beams, piece_width), f32),
            picture_shape,
        ],
        in_specs=[vmem()] * 3,
        out_specs=[vmem()] * 3,
        name="outer_tables",
        **PARAMS,
    )(angles, codes, images[0])
    far = pl.pallas_call(
        functools.partial(far_kernel, (3, 2)),
        out_shape=picture_shape,
        in_specs=[vmem()] * 4,
        out_specs=vmem(),
        name="far",
        **PARAMS,
    )(images[3], images[2], outer, outer_phase)
    return pl.pallas_call(
        near_kernel,
        out_shape=picture_shape,
        in_specs=[vmem()] * 5,
        out_specs=vmem(),
        name="near",
        **PARAMS,
    )(far, images[1], own, outer, outer_phase)


def power_of_two(count):
    return count > 0 and count & (count - 1) == 0


def per_device(echoes, beam_angle, interp_table):
    _, pulses, channels, length = echoes.shape
    rx_count = lax.axis_size("rx")
    pulse_count = lax.axis_size("pulse")
    piece_width = length // (rx_count * pulse_count)
    if (
        lax.axis_size("rng") == 2
        and rx_count == 2
        and channels == 8
        and pulses == 8
        and pulse_count == 4
        and power_of_two(beam_angle.shape[0])
        and beam_angle.shape[0] % 16 == 0
        and piece_width % LANES == 0
    ):
        return fast(echoes, beam_angle, interp_table)
    return local(echoes, beam_angle, interp_table)


def solution(mesh):
    placed = (P(None, ("slab", "pulse"), "rx", "rng"), P(), P())
    return jax.shard_map(
        per_device,
        mesh=mesh,
        in_specs=placed,
        out_specs=P(None, "slab", ("rng", "rx", "pulse")),
        check_vma=False,
    )
```
